32 devices in a mesh: head: 4 (over y, x), seq: 8 (over z, core).
Axes of the slice: x: 2, y: 2, z: 4, core: 2. Of those that a mesh axis runs over, the one named last changes fastest.
Arguments:
- prompts: bfloat16 [16, 256, 4096], P('seq'), may hold values from -6 to 6
- prompt_len: int32 [16], replicated, may hold values from 32 to 256, as said below
- admitted: int32 [4], replicated, may hold values from -1 to 15, as said below
- cache_len: int32 [4], replicated, may hold values from 256 to 4096, as said below
- cache_kv: bfloat16 [4, 4, 4096, 256], P('head', None, 'seq'), may hold values from -12 to 12
- dec_tokens: bfloat16 [4, 4, 4096], replicated, may hold values from -6 to 6
- w_query: bfloat16 [4096, 4096], P(None, 'head'), may hold values from -0.09375 to 0.09375
- w_key: bfloat16 [4096, 512], P(None, 'head'), may hold values from -0.09375 to 0.09375
- w_value: bfloat16 [4096, 512], P(None, 'head'), may hold values from -0.09375 to 0.09375
- w_out: bfloat16 [4096, 4096], P('head'), may hold values from -0.09375 to 0.09375
- q_gain: float32 [128], replicated, may hold values from 0.25 to 16
- k_gain: float32 [128], replicated, may hold values from 0.25 to 16
Outputs:
- prefill_out: bfloat16 [16, 256, 4096], P('seq', None, 'head')
- handed_kv: bfloat16 [4, 16, 256, 256], P('head', None, 'seq')
- decode_out: bfloat16 [4, 4, 4096], P(None, None, 'head')
The draws below stay inside these ranges and needn't reach their ends.
Inputs may be any that keep to these rules, and one draw needn't show every extreme that they name: `prompt_len`: some prompt has exactly 256 live tokens. `admitted`: slots with an entry of 0 or more name distinct prompts; in every draw some slot keeps its cache and some slot takes prompt 16 - 1. `cache_len`: some slot has exactly 4096 live positions.
All inputs are finite; a program needn't handle non-finite values.
Results may differ from the reference program's by a relative error of at most 0.02.
The reference program's roundings to bfloat16 on the way count: a program that leaves them out, or rounds other values in their place, can miss the bound.
Values may be sent and summed in bfloat16 or wider, within the bound.
No kernel may reach another device: no remote copies, remote signals or barrier semaphores. Data moves between devices by JAX's collectives and lax.ppermute only.
A program may use at most 128 MiB of HBM per device.

```python
import jax
import jax.numpy as jnp
from jax import lax

D = 4096
HQ = 32
KVH = 4
HD = 128
LP = 256
SLOTS = 4
CACHE_DEV = 512
STEPS = 4
PROMPTS = 16
CACHE_LEN = 4096
N_HEAD = 4
N_SEQ = 8


def draw_prompt_len(key, part):
    key = jax.random.fold_in(key, 11)
    first, second = jax.random.split(key)
    values = jax.random.randint(first, (PROMPTS,), max(1, LP // 8), LP + 1, dtype=jnp.int32)
    where = jax.random.randint(second, (), 0, PROMPTS, dtype=jnp.int32)
    return values.at[where].set(LP)


def draw_admitted(key, part):
    key = jax.random.fold_in(key, 13)
    first, second, third = jax.random.split(key, 3)
    order = jax.random.permutation(first, SLOTS).astype(jnp.int32)
    rank = jnp.argsort(order, stable=True).astype(jnp.int32)
    chosen = jax.random.permutation(second, PROMPTS - 1)[:SLOTS].astype(jnp.int32)
    chosen = jnp.where(rank == 1, PROMPTS - 1, chosen).astype(jnp.int32)
    coin = jax.random.randint(third, (SLOTS,), 0, 2, dtype=jnp.int32)
    taken = jnp.where(rank == 0, 0, jnp.where(rank == 1, 1, coin))
    return jnp.where(taken == 1, chosen, -1).astype(jnp.int32)


def draw_cache_len(key, part):
    key = jax.random.fold_in(key, 17)
    first, second = jax.random.split(key)
    values = jax.random.randint(first, (SLOTS,), max(1, CACHE_LEN // 16), CACHE_LEN + 1, dtype=jnp.int32)
    where = jax.random.randint(second, (), 0, SLOTS, dtype=jnp.int32)
    return values.at[where].set(CACHE_LEN)


def draw_cache_kv(key, part):
    key = jax.random.fold_in(key, 19)
    shape = (KVH, SLOTS, CACHE_LEN, 2 * HD)
    values = jax.random.normal(key, shape, jnp.float32)
    return jnp.clip(values, -12.0, 12.0).astype(jnp.bfloat16)


def draw_q_gain(key, part):
    key = jax.random.fold_in(key, 23)
    values = jax.random.uniform(key, (HD,), jnp.float32, 0.6, 1.6)
    return values


def draw_k_gain(key, part):
    key = jax.random.fold_in(key, 29)
    values = jax.random.uniform(key, (HD,), jnp.float32, 0.6, 1.6)
    return values


def steps_of(stream_key, shape, pieces, least, high):
    def one(dim, parts):
        draws = jax.random.uniform(jax.random.fold_in(jax.random.fold_in(stream_key, 6), dim), (parts,), jnp.float32, least / len(pieces), high / len(pieces))
        return jnp.repeat(jnp.exp(draws), shape[dim] // parts).reshape((-1,) + (1,) * (len(shape) - dim - 1))

    loudness = one(*pieces[0])
    for cut in pieces[1:]:
        loudness = loudness * one(*cut)
    return loudness


def centred(rng, dims, scale, limit, cuts=(), held_as=jnp.bfloat16):
    array = scale * jax.random.normal(rng, dims, jnp.float32)
    if cuts:
        array = array * steps_of(rng, dims, cuts, -0.22, 0.18)
    return jnp.clip(array, -limit, limit).astype(held_as)


def setup_inputs(seed: int = 0) -> dict:
    splits = jax.random.split(jax.random.key(seed), 13)
    return {
        "prompts": centred(splits[0], (PROMPTS, LP, D), 1.0, 6.0, ((0, 8),)),
        "prompt_len": draw_prompt_len(jax.random.fold_in(splits[12], 71), 0),
        "admitted": draw_admitted(jax.random.fold_in(splits[12], 71), 0),
        "cache_len": draw_cache_len(jax.random.fold_in(splits[12], 71), 0),
        "cache_kv": draw_cache_kv(jax.random.fold_in(splits[12], 71), 0),
        "dec_tokens": centred(splits[5], (STEPS, SLOTS, D), 1.0, 6.0),
        "w_query": centred(splits[6], (D, HQ * HD), D ** -0.5, 0.09375, ((1, 4),)),
        "w_key": centred(splits[7], (D, KVH * HD), D ** -0.5, 0.09375, ((1, 4),)),
        "w_value": centred(splits[8], (D, KVH * HD), D ** -0.5, 0.09375, ((1, 4),)),
        "w_out": centred(splits[9], (HQ * HD, D), (HQ * HD) ** -0.5, 0.09375, ((0, 4),)),
        "q_gain": draw_q_gain(jax.random.fold_in(splits[12], 71), 0),
        "k_gain": draw_k_gain(jax.random.fold_in(splits[12], 71), 0),
    }


EPS = 1e-06
THETA = 1000000.0
NEG = -1e+30

def rotate(values, positions):
    half = values.shape[-1] // 2
    freq = THETA ** (-jnp.arange(half, dtype=jnp.float32) / half)
    angle = positions.astype(jnp.float32)[..., None, None] * freq
    cosine = jnp.cos(angle)
    sine = jnp.sin(angle)
    first = values[..., :half]
    second = values[..., half:]
    return jnp.concatenate([first * cosine - second * sine, second * cosine + first * sine], axis=-1)

def normalize(values, gain):
    return values * lax.rsqrt(lax.optimization_barrier(jnp.mean(values * values, axis=-1, keepdims=True)) + EPS) * gain

def reference(prompts, prompt_len, admitted, cache_len, cache_kv, dec_tokens, w_query, w_key, w_value, w_out, q_gain, k_gain):
    group = HQ // KVH
    scale = HD ** (-0.5)
    flat = prompts.reshape(PROMPTS * LP, D)
    spots = jnp.arange(LP, dtype=jnp.int32)
    query = jnp.dot(flat, w_query, preferred_element_type=jnp.float32).reshape(PROMPTS, LP, HQ, HD)
    key = jnp.dot(flat, w_key, preferred_element_type=jnp.float32).reshape(PROMPTS, LP, KVH, HD)
    value = jnp.dot(flat, w_value, preferred_element_type=jnp.float32).reshape(PROMPTS, LP, KVH, HD)
    query = rotate(normalize(query, q_gain), spots).astype(jnp.bfloat16)
    key = rotate(normalize(key, k_gain), spots).astype(jnp.bfloat16)
    value = value.astype(jnp.bfloat16)

    def attend(item):
        q_one, k_one, v_one, length = item
        grouped = q_one.reshape(LP, KVH, group, HD).astype(jnp.float32)
        scores = jnp.einsum('skgd,tkd->kgst', grouped, k_one.astype(jnp.float32)) * scale
        allowed = (spots[None, :] <= spots[:, None]) & (spots[None, :] < length)
        scores = jnp.where(allowed, scores, NEG)
        weights = jax.nn.softmax(scores, axis=-1).astype(jnp.bfloat16)
        mixed = jnp.einsum('kgst,tkd->skgd', weights.astype(jnp.float32), v_one.astype(jnp.float32))
        return mixed.reshape(LP, HQ * HD).astype(jnp.bfloat16)
    attn = lax.map(attend, (query, key, value, prompt_len)).reshape(PROMPTS * LP, HQ * HD)
    width = HQ * HD // N_HEAD
    total = jnp.zeros((PROMPTS * LP, D), jnp.float32)
    for index in range(N_HEAD):
        part = jnp.dot(attn[:, index * width:(index + 1) * width], w_out[index * width:(index + 1) * width], preferred_element_type=jnp.float32)
        rounded = lax.optimization_barrier(part.astype(jnp.bfloat16))
        total = total + rounded.astype(jnp.float32)
    prefill_out = total.astype(jnp.bfloat16).reshape(PROMPTS, LP, D)
    kv_pos = jnp.concatenate([key, value], axis=-1).transpose(2, 0, 1, 3)
    rows_each = LP // N_SEQ
    handed_kv = kv_pos.reshape(KVH, PROMPTS, rows_each, N_SEQ, 2 * HD).transpose(0, 1, 3, 2, 4).reshape(KVH, PROMPTS, LP, 2 * HD)
    is_new = admitted >= 0
    pick = jnp.maximum(admitted, 0).astype(jnp.int32)
    eff_len = jnp.where(is_new, prompt_len[pick], cache_len).astype(jnp.int32)
    cache_pos = cache_kv.reshape(KVH, SLOTS, N_SEQ, CACHE_DEV, 2 * HD).transpose(0, 1, 3, 2, 4).reshape(KVH, SLOTS, CACHE_LEN, 2 * HD)
    replaced = kv_pos[:, pick]
    head_part = jnp.where(is_new[None, :, None, None], replaced, cache_pos[:, :, :LP])
    cache_pos = jnp.concatenate([head_part, cache_pos[:, :, LP:]], axis=2)
    rows = dec_tokens.reshape(STEPS * SLOTS, D)
    order = jnp.arange(STEPS, dtype=jnp.int32)
    places = eff_len[None, :] + order[:, None]
    dq = jnp.dot(rows, w_query, preferred_element_type=jnp.float32).reshape(STEPS, SLOTS, HQ, HD)
    dk = jnp.dot(rows, w_key, preferred_element_type=jnp.float32).reshape(STEPS, SLOTS, KVH, HD)
    dv = jnp.dot(rows, w_value, preferred_element_type=jnp.float32).reshape(STEPS, SLOTS, KVH, HD)
    dq = rotate(normalize(dq, q_gain), places).astype(jnp.bfloat16)
    dk = rotate(normalize(dk, k_gain), places).astype(jnp.bfloat16)
    dv = dv.astype(jnp.bfloat16)
    grouped = dq.reshape(STEPS, SLOTS, KVH, group, HD).astype(jnp.float32)
    stored_keys = cache_pos[..., :HD].astype(jnp.float32)
    stored_values = cache_pos[..., HD:].astype(jnp.float32)
    cache_scores = jnp.einsum('trkgd,krcd->trkgc', grouped, stored_keys) * scale
    live = jnp.arange(CACHE_LEN, dtype=jnp.int32)[None, :] < eff_len[:, None]
    cache_scores = jnp.where(live[None, :, None, None, :], cache_scores, NEG)
    new_scores = jnp.einsum('trkgd,urkd->trkgu', grouped, dk.astype(jnp.float32)) * scale
    causal = order[None, :] <= order[:, None]
    new_scores = jnp.where(causal[:, None, None, None, :], new_scores, NEG)
    weights = jax.nn.softmax(jnp.concatenate([cache_scores, new_scores], axis=-1), axis=-1)
    mixed = jnp.einsum('trkgc,krcd->trkgd', weights[..., :CACHE_LEN], stored_values)
    mixed = mixed + jnp.einsum('trkgu,urkd->trkgd', weights[..., CACHE_LEN:], dv.astype(jnp.float32))
    mixed = mixed.astype(jnp.bfloat16).reshape(STEPS * SLOTS, HQ * HD)
    decode_out = jnp.dot(mixed, w_out, preferred_element_type=jnp.float32).astype(jnp.bfloat16).reshape(STEPS, SLOTS, D)
    return (prefill_out, handed_kv, decode_out)
```

```python
import functools

import jax
import jax.numpy as jnp
import numpy as np
from jax import lax
from jax.experimental import pallas as pl
from jax.experimental.pallas import tpu as pltpu
from jax.sharding import PartitionSpec as P

HD = 128
EPS = 1e-06
THETA = 1000000.0
NEG = -1e30
LOG2E = 1.4426950408889634
SCALE = HD**-0.5
C2 = SCALE * LOG2E
BF = jnp.bfloat16
F32 = jnp.float32
ANY = pl.BlockSpec(memory_space=pl.ANY)
VM = pl.BlockSpec(memory_space=pltpu.VMEM)
SM = pl.BlockSpec(memory_space=pltpu.SMEM)
MIB = 1024 * 1024


def frequencies():
    half = HD // 2
    freq = np.float32(THETA) ** (-np.arange(half, dtype=np.float32) / np.float32(half))
    return freq.astype(np.float32)


def prompt_table(length):
    angle = np.arange(length, dtype=np.float32)[:, None] * frequencies()[None, :]
    cosine, sine = np.cos(angle), np.sin(angle)
    return np.concatenate([cosine, cosine, -sine, sine], axis=1).astype(np.float32)


def dot(a, b):
    return jnp.dot(a, b, preferred_element_type=F32)


def dot_nt(a, b):
    return lax.dot_general(a, b, (((1,), (1,)), ((), ())), preferred_element_type=F32)


def norm(values, gain):
    square = jnp.mean(values * values, axis=-1, keepdims=True)
    return values * lax.rsqrt(square + EPS) * gain


def rope(values, cos2, sin2):
    return values * cos2 + pltpu.roll(values, HD // 2, 1) * sin2


def effective_lengths(plen, adm, clen, slots):
    out = []
    for r in range(slots):
        taken = adm[r]
        out.append(jnp.where(taken >= 0, plen[jnp.maximum(taken, 0)], clen[r]))
    return out


def by_slot(index, values):
    result = jnp.full(index.shape, values[0])
    for r in range(1, len(values)):
        result = jnp.where(index == r, values[r], result)
    return result


def prefill_kernel(which, dec_rows, slots, n_head, *refs):
    it = iter(refs)
    plen, adm, clen = next(it), next(it), next(it)
    x_hbm = next(it)
    dec_hbm = next(it) if dec_rows else None
    wq_hbm, wk_hbm, wv_hbm, wo_hbm = next(it), next(it), next(it), next(it)
    qg, kg, table, freq = next(it), next(it), next(it), next(it)
    send_a, send_b, attn, kv_out = next(it), next(it), next(it), next(it)
    if dec_rows:
        dq_out, dkv_out = next(it), next(it)
    x_v, wkv_v, wq_v, wo_v, x_sem, wkv_sem, wq_sem, wo_sem = it

    rows, width = kv_out.shape[0], x_hbm.shape[2]
    tiles = wq_v.shape[0]
    nb = width // n_head
    hb = nb // 2
    head = lax.axis_index("head")
    flip_x = head + 1 - 2 * lax.rem(head, 2)
    flip_y = lax.rem(head + 2, 4)
    flip_xy = 3 - head

    copies = []
    copies.append(pltpu.make_async_copy(x_hbm.at[which], x_v.at[pl.ds(0, rows)], x_sem.at[0]))
    if dec_rows:
        copies.append(
            pltpu.make_async_copy(dec_hbm, x_v.at[pl.ds(rows, dec_rows)], x_sem.at[1])
        )
    copies.append(pltpu.make_async_copy(wk_hbm, wkv_v.at[:, pl.ds(0, HD)], wkv_sem.at[0]))
    copies.append(pltpu.make_async_copy(wv_hbm, wkv_v.at[:, pl.ds(HD, HD)], wkv_sem.at[1]))
    q_copies = [
        pltpu.make_async_copy(
            wq_hbm.at[:, pl.ds(j * 2 * HD, 2 * HD)], wq_v.at[j], wq_sem.at[j]
        )
        for j in range(tiles)
    ]
    offsets = [
        flip_xy * nb,
        flip_xy * nb + hb,
        flip_x * nb,
        flip_y * nb + hb,
    ]
    o_copies = [
        pltpu.make_async_copy(
            wo_hbm.at[:, pl.ds(pl.multiple_of(offset, hb), hb)], wo_v.at[j], wo_sem.at[j]
        )
        for j, offset in enumerate(offsets)
    ]
    for copy in copies:
        copy.start()
    later = q_copies + o_copies
    ahead = 2
    for copy in later[:ahead]:
        copy.start()

    length = plen[lax.axis_index("seq") * x_hbm.shape[0] + which]
    row_at = lax.broadcasted_iota(jnp.int32, (rows, rows), 0)
    col_at = lax.broadcasted_iota(jnp.int32, (rows, rows), 1)
    bias = jnp.where((col_at <= row_at) & (col_at < length), 0.0, NEG).astype(F32)
    cos2, sin2 = table[:, :HD], table[:, HD:]
    if dec_rows:
        eff = effective_lengths(plen, adm, clen, slots)
        row = lax.broadcasted_iota(jnp.int32, (dec_rows, HD), 0)
        places = by_slot(lax.rem(row, slots), eff) + row // slots
        angle = places.astype(F32) * freq[...]
        lane = lax.broadcasted_iota(jnp.int32, (dec_rows, HD), 1)
        dcos2 = jnp.cos(angle)
        dsin2 = jnp.where(lane < HD // 2, -1.0, 1.0) * jnp.sin(angle)

    for copy in copies:
        copy.wait()
    kv = dot(x_v[...], wkv_v[...])
    key = rope(norm(kv[:rows, :HD], kg[...]), cos2, sin2).astype(BF)
    value = kv[:rows, HD:].astype(BF)
    kv_out[:, :HD] = key
    kv_out[:, HD:] = value
    if dec_rows:
        dkv_out[:, :HD] = rope(norm(kv[rows:, :HD], kg[...]), dcos2, dsin2).astype(BF)
        dkv_out[:, HD:] = kv[rows:, HD:].astype(BF)

    for j in range(tiles):
        q_copies[j].wait()
        if j + ahead < len(later):
            later[j + ahead].start()
        projected = dot(x_v[...], wq_v[j])
        for i in range(2):
            h = 2 * j + i
            piece = projected[:, i * HD : (i + 1) * HD]
            query = rope(norm(piece[:rows], qg[...]), cos2, sin2).astype(BF)
            if dec_rows:
                dq_out[h * dec_rows : (h + 1) * dec_rows, :] = rope(
                    norm(piece[rows:], qg[...]), dcos2, dsin2
                ).astype(BF)
            scores = dot_nt(query, key) + bias
            top = jnp.max(scores, axis=-1, keepdims=True)
            expo = jnp.exp2((scores - top) * C2)
            total = jnp.sum(expo, axis=-1, keepdims=True)
            weights = (expo * (1.0 / total)).astype(BF)
            attn[:, h * HD : (h + 1) * HD] = dot(weights, value).astype(BF)

    for j in range(len(o_copies)):
        o_copies[j].wait()
        if tiles + j + ahead < len(later):
            later[tiles + j + ahead].start()
        part = dot(attn[...], wo_v[j]).astype(BF)
        dest = send_b if j % 2 else send_a
        at = (j // 2) * hb
        dest[:, at : at + hb] = part


def prefill(which, with_dec, n_head, plen, adm, clen, x, dec, wq, wk, wv, wo, qg, kg, table, freq):
    _, rows, width = x.shape
    slots = adm.shape[0]
    dec_rows = dec.shape[0] if with_dec else 0
    local = wq.shape[1]
    tiles = local // (2 * HD)
    nb = width // n_head
    hb = nb // 2
    outs = [
        jax.ShapeDtypeStruct((rows, nb), BF),
        jax.ShapeDtypeStruct((rows, nb), BF),
        jax.ShapeDtypeStruct((rows, local), BF),
        jax.ShapeDtypeStruct((rows, 2 * HD), BF),
    ]
    if with_dec:
        outs += [
            jax.ShapeDtypeStruct((dec_rows * (local // HD), HD), BF),
            jax.ShapeDtypeStruct((dec_rows, 2 * HD), BF),
        ]
    args = [plen, adm, clen, x] + ([dec] if with_dec else []) + [wq, wk, wv, wo, qg, kg, table, freq]
    specs = [SM, SM, SM, ANY] + ([ANY] if with_dec else []) + [ANY] * 4 + [VM] * 4
    total_rows = rows + dec_rows
    flops = 2 * total_rows * width * (local + 2 * HD) + rows * local * width
    return pl.pallas_call(
        functools.partial(prefill_kernel, which, dec_rows, slots, n_head),
        out_shape=outs,
        in_specs=specs,
        out_specs=[VM] * len(outs),
        scratch_shapes=[
            pltpu.VMEM((total_rows, width), BF),
            pltpu.VMEM((width, 2 * HD), BF),
            pltpu.VMEM((tiles, width, 2 * HD), BF),
            pltpu.VMEM((4, local, hb), BF),
            pltpu.SemaphoreType.DMA((2,)),
            pltpu.SemaphoreType.DMA((2,)),
            pltpu.SemaphoreType.DMA((tiles,)),
            pltpu.SemaphoreType.DMA((4,)),
        ],
        compiler_params=pltpu.CompilerParams(vmem_limit_bytes=40 * MIB),
        cost_estimate=pl.CostEstimate(
            flops=flops, bytes_accessed=18 * MIB, transcendentals=local // HD * rows * rows
        ),
        name="prefill_%d" % which,
    )(*args)


def own_kernel(n_head, attn0, attn1, wo_hbm, o_fa, o_fb, o_keep, wo_v, sems):
    width = wo_hbm.shape[1]
    nb = width // n_head
    hb = nb // 2
    head = lax.axis_index("head")
    flip_x = head + 1 - 2 * lax.rem(head, 2)
    flip_y = lax.rem(head + 2, 4)
    offsets = [flip_y * nb, flip_x * nb + hb, head * nb, head * nb + hb]
    copies = [
        pltpu.make_async_copy(
            wo_hbm.at[:, pl.ds(pl.multiple_of(offset, hb), hb)], wo_v.at[j], sems.at[j]
        )
        for j, offset in enumerate(offsets)
    ]
    for copy in copies:
        copy.start()
    for j in range(4):
        copies[j].wait()
        for p, attn in enumerate((attn0, attn1)):
            part = dot(attn[...], wo_v[j])
            if j == 0:
                o_fa[p] = part
            elif j == 1:
                o_fb[p] = part
            else:
                o_keep[p, :, (j - 2) * hb : (j - 1) * hb] = part


def own_parts(n_head, attn0, attn1, wo):
    rows, local = attn0.shape
    width = wo.shape[1]
    nb = width // n_head
    hb = nb // 2
    return pl.pallas_call(
        functools.partial(own_kernel, n_head),
        out_shape=[
            jax.ShapeDtypeStruct((2, rows, hb), F32),
            jax.ShapeDtypeStruct((2, rows, hb), F32),
            jax.ShapeDtypeStruct((2, rows, nb), F32),
        ],
        in_specs=[VM, VM, ANY],
        out_specs=[VM] * 3,
        scratch_shapes=[pltpu.VMEM((4, local, hb), BF), pltpu.SemaphoreType.DMA((4,))],
        compiler_params=pltpu.CompilerParams(vmem_limit_bytes=32 * MIB),
        cost_estimate=pl.CostEstimate(
            flops=2 * rows * local * width, bytes_accessed=9 * MIB, transcendentals=0
        ),
        name="own_parts",
    )(attn0, attn1, wo)


def decode_kernel(n_seq, plen, adm, clen, dq, dkv, cache, *refs):
    kvs, (part, handed) = refs[:-2], refs[-2:]
    seq = lax.axis_index("seq")
    slots, width = cache.shape[0], cache.shape[1]
    queries = dq[...]
    count = queries.shape[0]
    dec_rows = dkv.shape[0]
    rows = kvs[0].shape[0]
    each = rows // n_seq

    row = lax.rem(lax.broadcasted_iota(jnp.int32, (count, 1), 0), dec_rows)
    slot, step = lax.rem(row, slots), row // slots
    taken = by_slot(slot, [adm[r] for r in range(slots)])
    scores, masks, values = [], [], []
    at = lax.broadcasted_iota(jnp.int32, (1, width), 1) * n_seq + seq
    for r in range(slots):
        limit = jnp.where(adm[r] >= 0, 0, clen[r])
        masks.append((slot == r) & (at < limit))
        scores.append(dot_nt(queries, cache[r, :, :HD]))
        values.append(cache[r, :, HD:])
    spot = lax.broadcasted_iota(jnp.int32, (1, rows), 1)
    for p, kv in enumerate(kvs):
        prompt = seq * len(kvs) + p
        masks.append((taken == prompt) & (spot < plen[prompt]))
        scores.append(dot_nt(queries, kv[:, :HD]))
        values.append(kv[:, HD:])
    other = lax.broadcasted_iota(jnp.int32, (1, dec_rows), 1)
    first = jnp.where(seq == 0, 1, 0)
    masks.append(
        (lax.rem(other, slots) == slot) & (other // slots <= step) & (first + 0 * other > 0)
    )
    scores.append(dot_nt(queries, dkv[:, :HD]))
    values.append(dkv[:, HD:])

    top = jnp.full((count, 1), NEG, F32)
    scores = [jnp.where(mask, score, NEG) for mask, score in zip(masks, scores)]
    for score in scores:
        top = jnp.maximum(top, jnp.max(score, axis=-1, keepdims=True))
    total = jnp.zeros((count, 1), F32)
    acc = jnp.zeros((count, HD), F32)
    for mask, score, value in zip(masks, scores, values):
        expo = jnp.where(mask, jnp.exp2((score - top) * C2), 0.0)
        total = total + jnp.sum(expo, axis=-1, keepdims=True)
        acc = acc + dot(expo.astype(BF), value)
    some = total > 0.0
    safe = jnp.where(some, total, 1.0)
    part[:count, :] = acc * (1.0 / safe)
    level = jnp.where(some, top * C2 + jnp.log2(safe), NEG)
    eye = lax.broadcasted_iota(jnp.int32, (count, count), 0) == lax.broadcasted_iota(
        jnp.int32, (count, count), 1
    )
    part[count : count + 1, :] = jnp.sum(jnp.where(eye, level, 0.0), axis=0, keepdims=True)

    new = lax.broadcasted_iota(jnp.int32, (rows, rows), 0)
    old = lax.broadcasted_iota(jnp.int32, (rows, rows), 1)
    move = jnp.where(old == lax.rem(new, each) * n_seq + new // each, 1.0, 0.0).astype(BF)
    for p, kv in enumerate(kvs):
        handed[p] = dot(move, kv[...]).astype(BF)


def decode_attention(n_seq, plen, adm, clen, dq, dkv, cache, kvs):
    count = dq.shape[0]
    rows = kvs[0].shape[0]
    return pl.pallas_call(
        functools.partial(decode_kernel, n_seq),
        out_shape=[
            jax.ShapeDtypeStruct((count + 8, HD), F32),
            jax.ShapeDtypeStruct((len(kvs), rows, 2 * HD), BF),
        ],
        in_specs=[SM] * 3 + [VM] * (3 + len(kvs)),
        out_specs=[VM] * 2,
        compiler_params=pltpu.CompilerParams(vmem_limit_bytes=32 * MIB),
        cost_estimate=pl.CostEstimate(
            flops=400 * MIB, bytes_accessed=2 * MIB, transcendentals=count * 2600
        ),
        name="decode_attention",
    )(plen, adm, clen, dq, dkv, cache, *kvs)


def joined(bit, mine, other):
    count = mine.shape[0] - 8
    swap = lax.rem(lax.axis_index("seq") // bit, 2) == 1
    one, two = mine[...], other[...]
    low = jnp.where(swap, two, one)
    high = jnp.where(swap, one, two)
    eye = lax.broadcasted_iota(jnp.int32, (count, count), 0) == lax.broadcasted_iota(
        jnp.int32, (count, count), 1
    )

    def column(row):
        return jnp.sum(jnp.where(eye, row, 0.0), axis=1, keepdims=True)

    row_a, row_b = low[count : count + 1, :], high[count : count + 1, :]
    best = jnp.maximum(row_a, row_b)
    scale_a, scale_b = jnp.exp2(row_a - best), jnp.exp2(row_b - best)
    total = scale_a + scale_b
    inverse = 1.0 / total
    mixed = low[:count] * column(scale_a * inverse) + high[:count] * column(scale_b * inverse)
    return mixed, best + jnp.log2(total)


def join_kernel(bit, mine, other, out):
    count = mine.shape[0] - 8
    mixed, level = joined(bit, mine, other)
    out[:count, :] = mixed
    out[count : count + 1, :] = level


def join(bit, mine, other):
    return pl.pallas_call(
        functools.partial(join_kernel, bit),
        out_shape=jax.ShapeDtypeStruct(mine.shape, F32),
        in_specs=[VM, VM],
        out_specs=VM,
        name="join_%d" % bit,
    )(mine, other)


def decode_out_kernel(bit, n_head, mine, other, wo, *outs):
    count = mine.shape[0] - 8
    rows = outs[0].shape[0]
    nb = outs[0].shape[1]
    mixed, _ = joined(bit, mine, other)
    mixed = mixed.astype(BF)
    flat = jnp.concatenate([mixed[i * rows : (i + 1) * rows] for i in range(count // rows)], axis=1)
    head = lax.axis_index("head")
    for d in range(n_head):
        dest = head + 1 - 2 * lax.rem(head, 2) if d == 1 else lax.rem(head + 2, 4)
        if d == 0:
            dest = head
        elif d == 3:
            dest = 3 - head
        at = pl.multiple_of(dest * nb, nb)
        outs[d][...] = dot(flat, wo[:, pl.ds(at, nb)]).astype(BF)


def decode_project(bit, n_head, dec_rows, mine, other, wo):
    local, width = wo.shape
    nb = width // n_head
    return pl.pallas_call(
        functools.partial(decode_out_kernel, bit, n_head),
        out_shape=[jax.ShapeDtypeStruct((dec_rows, nb), BF)] * n_head,
        in_specs=[VM] * 3,
        out_specs=[VM] * n_head,
        compiler_params=pltpu.CompilerParams(vmem_limit_bytes=32 * MIB),
        cost_estimate=pl.CostEstimate(
            flops=2 * 256 * local * width, bytes_accessed=8 * MIB, transcendentals=0
        ),
        name="decode_project",
    )(mine, other, wo)


def local(
    prompts, prompt_len, admitted, cache_len, cache_kv, dec_tokens, w_query, w_key, w_value, w_out, q_gain, k_gain
):
    n_seq = lax.axis_size("seq")
    n_head = lax.axis_size("head")
    pr_dev, rows, width = prompts.shape
    steps, slots, _ = dec_tokens.shape
    nb = width // n_head
    hb = nb // 2
    qg, kg = q_gain.reshape(1, HD), k_gain.reshape(1, HD)
    table = jnp.asarray(prompt_table(rows))
    freq = jnp.asarray(np.tile(frequencies(), 2)[None, :])
    dec = dec_tokens.reshape(steps * slots, width)
    scalars = (prompt_len, admitted, cache_len)
    weights = (w_query, w_key, w_value, w_out, qg, kg, table, freq)

    across_x = [(i, i ^ 1) for i in range(n_head)]
    across_y = [(i, i ^ 2) for i in range(n_head)]
    across_xy = [(i, i ^ 3) for i in range(n_head)]

    def head_move(value, pairs):
        return lax.ppermute(value, "head", pairs)

    got, attns, kvs = [], [], []
    for p in range(pr_dev):
        last = p == pr_dev - 1
        out = prefill(p, last, n_head, *scalars, prompts, dec, *weights)
        got.append((head_move(out[0], across_x), head_move(out[1], across_y)))
        attns.append(out[2])
        kvs.append(out[3])
    dq, dkv = out[4], out[5]
    own_fa, own_fb, own_keep = own_parts(n_head, *attns, w_out)

    part, handed = decode_attention(n_seq, *scalars, dq, dkv, cache_kv[0], kvs)
    bit = 1
    while bit < n_seq:
        other = lax.ppermute(part, "seq", [(i, i ^ bit) for i in range(n_seq)])
        if 2 * bit < n_seq:
            part = join(bit, part, other)
        else:
            pieces = decode_project(bit, n_head, steps * slots, part, other, w_out)
        bit *= 2
    total = pieces[0].astype(F32)
    for piece, pairs in zip(pieces[1:], (across_x, across_y, across_xy)):
        total = total + head_move(piece, pairs).astype(F32)
    decode_out = total.astype(BF).reshape(steps, slots, nb)

    each = rows // n_seq
    sending = handed.reshape(pr_dev, n_seq, each, 2 * HD)
    handed = lax.all_to_all(sending, "seq", split_axis=1, concat_axis=0, tiled=True)
    handed = handed.reshape(1, pr_dev * n_seq, each, 2 * HD)

    finals = []
    for p in range(pr_dev):
        a, b = got[p]
        a, b = a.astype(F32), b.astype(F32)
        on_a = head_move((own_fa[p] + a[:, :hb]).astype(BF), across_y)
        on_b = head_move((own_fb[p] + b[:, :hb]).astype(BF), across_x)
        finals.append(
            jnp.concatenate(
                [
                    own_keep[p, :, :hb] + a[:, hb:] + on_a.astype(F32),
                    own_keep[p, :, hb:] + b[:, hb:] + on_b.astype(F32),
                ],
                axis=1,
            ).astype(BF)
        )
    prefill_out = jnp.stack(finals)
    return (prefill_out, handed, decode_out)


def solution(mesh):
    placed = (
        P("seq", None, None),
        P(),
        P(),
        P(),
        P("head", None, "seq", None),
        P(),
        P(None, "head"),
        P(None, "head"),
        P(None, "head"),
        P("head", None),
        P(),
        P(),
    )
    return jax.shard_map(
        local,
        mesh=mesh,
        in_specs=placed,
        out_specs=(P("seq", None, "head"), P("head", None, "seq", None), P(None, None, "head")),
        check_vma=False,
    )
```

```python
import functools

import jax
import jax.numpy as jnp
import numpy as np
from jax import lax
from jax.experimental import pallas as pl
from jax.experimental.pallas import tpu as pltpu
from jax.sharding import PartitionSpec as P

HD = 128
EPS = 1e-06
THETA = 1000000.0
NEG = -1e30
LOG2E = 1.4426950408889634
SCALE = HD**-0.5
C2 = SCALE * LOG2E
BF = jnp.bfloat16
F32 = jnp.float32
HB = pl.BlockSpec(memory_space=pltpu.HBM)
BRIEF = pl.CostEstimate(flops=1, bytes_accessed=1, transcendentals=0)
VM = pl.BlockSpec(memory_space=pltpu.VMEM)
SM = pl.BlockSpec(memory_space=pltpu.SMEM)
MIB = 1024 * 1024


def frequencies():
    half = HD // 2
    freq = np.float32(THETA) ** (-np.arange(half, dtype=np.float32) / np.float32(half))
    return freq.astype(np.float32)


def prompt_table(length):
    angle = np.arange(length, dtype=np.float32)[:, None] * frequencies()[None, :]
    cosine, sine = np.cos(angle), np.sin(angle)
    return np.concatenate([cosine, cosine, -sine, sine], axis=1).astype(np.float32)


def dot(a, b):
    return jnp.dot(a, b, preferred_element_type=F32)


def dot_nt(a, b):
    return lax.dot_general(a, b, (((1,), (1,)), ((), ())), preferred_element_type=F32)


def norm(values, gain):
    square = jnp.mean(values * values, axis=-1, keepdims=True)
    return values * lax.rsqrt(square + EPS) * gain


def rope(values, cos2, sin2):
    return values * cos2 + pltpu.roll(values, HD // 2, 1) * sin2


def effective_lengths(plen, adm, clen, slots):
    out = []
    for r in range(slots):
        taken = adm[r]
        out.append(jnp.where(taken >= 0, plen[jnp.maximum(taken, 0)], clen[r]))
    return out


def by_slot(index, values):
    result = jnp.full(index.shape, values[0])
    for r in range(1, len(values)):
        result = jnp.where(index == r, values[r], result)
    return result


def prefill_kernel(which, dec_rows, slots, n_head, *refs):
    it = iter(refs)
    plen_h, adm_h, clen_h = next(it), next(it), next(it)
    x_hbm = next(it)
    dec_hbm = next(it) if dec_rows else None
    wq_hbm, wk_hbm, wv_hbm, wo_hbm = next(it), next(it), next(it), next(it)
    smalls_h = [next(it) for _ in range(4)]
    send_a, send_b, attn, kv_out = next(it), next(it), next(it), next(it)
    if dec_rows:
        dq_out, dkv_out = next(it), next(it)
    x_v, wkv_v, wq_v, wo_v, acc = next(it), next(it), next(it), next(it), next(it)
    plen, adm, clen = next(it), next(it), next(it)
    qg, kg, table, freq = next(it), next(it), next(it), next(it)
    x_sem, dec_sem, wkv_sem, wq_sem, wo_sem, small_sem = it

    rows, width = kv_out.shape[0], x_hbm.shape[2]
    chunks, _, depth = x_v.shape
    local = wq_v.shape[1]
    nb = width // n_head
    hb = nb // 2
    head = lax.axis_index("head")
    flip_x = head + 1 - 2 * lax.rem(head, 2)
    flip_y = lax.rem(head + 2, 4)
    flip_xy = 3 - head

    steps = []
    for c in range(chunks):
        at = pl.ds(c * depth, depth)
        group = [
            pltpu.make_async_copy(
                x_hbm.at[which, :, at], x_v.at[c, pl.ds(0, rows)], x_sem.at[c]
            ),
            pltpu.make_async_copy(wk_hbm.at[at], wkv_v.at[at, pl.ds(0, HD)], wkv_sem.at[0, c]),
            pltpu.make_async_copy(wv_hbm.at[at], wkv_v.at[at, pl.ds(HD, HD)], wkv_sem.at[1, c]),
            pltpu.make_async_copy(wq_hbm.at[at], wq_v.at[at], wq_sem.at[c]),
        ]
        if dec_rows:
            group.append(
                pltpu.make_async_copy(
                    dec_hbm.at[:, at], x_v.at[c, pl.ds(rows, dec_rows)], dec_sem.at[c]
                )
            )
        steps.append(group)
    small = [
        pltpu.make_async_copy(src, dst, small_sem.at[i])
        for i, (src, dst) in enumerate(
            zip([plen_h, adm_h, clen_h] + smalls_h, [plen, adm, clen, qg, kg, table, freq])
        )
    ]
    places = [(flip_xy * nb, 0, nb), (flip_x * nb, nb, hb), (flip_y * nb + hb, nb + hb, hb)]
    o_copies = [
        pltpu.make_async_copy(
            wo_hbm.at[:, pl.ds(pl.multiple_of(src, hb), size)],
            wo_v.at[:, pl.ds(dst, size)],
            wo_sem.at[j],
        )
        for j, (src, dst, size) in enumerate(places)
    ]
    queue = steps + [[copy] for copy in o_copies]
    ahead = 4
    for copy in queue[0]:
        copy.start()
    for copy in small:
        copy.start()
    for group in queue[1:ahead]:
        for copy in group:
            copy.start()

    for c in range(chunks):
        for copy in steps[c]:
            copy.wait()
        if c + ahead < len(queue):
            for copy in queue[c + ahead]:
                copy.start()
        at = slice(c * depth, (c + 1) * depth)
        block = x_v[c]
        kv_part = dot(block, wkv_v[at, :])
        q_part = dot(block, wq_v[at, :])
        if c == 0:
            acc[:, local:] = kv_part
            acc[:, :local] = q_part
        else:
            acc[:, local:] += kv_part
            acc[:, :local] += q_part

    for copy in small:
        copy.wait()
    length = plen[lax.axis_index("seq") * x_hbm.shape[0] + which]
    row_at = lax.broadcasted_iota(jnp.int32, (rows, rows), 0)
    col_at = lax.broadcasted_iota(jnp.int32, (rows, rows), 1)
    bias = jnp.where((col_at <= row_at) & (col_at < length), 0.0, NEG).astype(F32)
    cos2, sin2 = table[:, :HD], table[:, HD:]
    key = rope(norm(acc[:rows, local : local + HD], kg[...]), cos2, sin2).astype(BF)
    value = acc[:rows, local + HD :].astype(BF)
    kv_out[:, :HD] = key
    kv_out[:, HD:] = value
    if dec_rows:
        eff = effective_lengths(plen, adm, clen, slots)
        row = lax.broadcasted_iota(jnp.int32, (dec_rows, HD), 0)
        spots = by_slot(lax.rem(row, slots), eff) + row // slots
        angle = spots.astype(F32) * freq[...]
        lane = lax.broadcasted_iota(jnp.int32, (dec_rows, HD), 1)
        dcos2 = jnp.cos(angle)
        dsin2 = jnp.where(lane < HD // 2, -1.0, 1.0) * jnp.sin(angle)
        dkv_out[:, :HD] = rope(norm(acc[rows:, local : local + HD], kg[...]), dcos2, dsin2).astype(BF)
        dkv_out[:, HD:] = acc[rows:, local + HD :].astype(BF)

    for h in range(local // HD):
        at = slice(h * HD, (h + 1) * HD)
        query = rope(norm(acc[:rows, at], qg[...]), cos2, sin2).astype(BF)
        if dec_rows:
            dq_out[h * dec_rows : (h + 1) * dec_rows, :] = rope(
                norm(acc[rows:, at], qg[...]), dcos2, dsin2
            ).astype(BF)
        scores = dot_nt(query, key) + bias
        top = jnp.max(scores, axis=-1, keepdims=True)
        expo = jnp.exp2((scores - top) * C2)
        total = jnp.sum(expo, axis=-1, keepdims=True)
        weights = (expo * (1.0 / total)).astype(BF)
        attn[:, at] = dot(weights, value).astype(BF)

    for copy in o_copies:
        copy.wait()
    mixed = attn[...]
    diag = dot(mixed, wo_v[:, :nb]).astype(BF)
    send_a[:, :hb] = diag[:, :hb]
    send_b[:, :hb] = diag[:, hb:]
    rest = dot(mixed, wo_v[:, nb:]).astype(BF)
    send_a[:, hb:] = rest[:, :hb]
    send_b[:, hb:] = rest[:, hb:]


def prefill(which, with_dec, n_head, plen, adm, clen, x, dec, wq, wk, wv, wo, qg, kg, table, freq):
    _, rows, width = x.shape
    slots = adm.shape[0]
    dec_rows = dec.shape[0] if with_dec else 0
    local = wq.shape[1]
    chunks = 8
    nb = width // n_head
    hb = nb // 2
    outs = [
        jax.ShapeDtypeStruct((rows, nb), BF),
        jax.ShapeDtypeStruct((rows, nb), BF),
        jax.ShapeDtypeStruct((rows, local), BF),
        jax.ShapeDtypeStruct((rows, 2 * HD), BF),
    ]
    if with_dec:
        outs += [
            jax.ShapeDtypeStruct((dec_rows * (local // HD), HD), BF),
            jax.ShapeDtypeStruct((dec_rows, 2 * HD), BF),
        ]
    args = [plen, adm, clen, x] + ([dec] if with_dec else []) + [wq, wk, wv, wo, qg, kg, table, freq]
    total_rows = rows + dec_rows
    return pl.pallas_call(
        functools.partial(prefill_kernel, which, dec_rows, slots, n_head),
        out_shape=outs,
        in_specs=[HB] * len(args),
        out_specs=[VM] * len(outs),
        scratch_shapes=[
            pltpu.VMEM((chunks, total_rows, width // chunks), BF),
            pltpu.VMEM((width, 2 * HD), BF),
            pltpu.VMEM((width, local), BF),
            pltpu.VMEM((local, 2 * nb), BF),
            pltpu.VMEM((total_rows, local + 2 * HD), F32),
            pltpu.SMEM(plen.shape, jnp.int32),
            pltpu.SMEM(adm.shape, jnp.int32),
            pltpu.SMEM(clen.shape, jnp.int32),
            pltpu.VMEM(qg.shape, F32),
            pltpu.VMEM(kg.shape, F32),
            pltpu.VMEM(table.shape, F32),
            pltpu.VMEM(freq.shape, F32),
            pltpu.SemaphoreType.DMA((chunks,)),
            pltpu.SemaphoreType.DMA((chunks,)),
            pltpu.SemaphoreType.DMA((2, chunks)),
            pltpu.SemaphoreType.DMA((chunks,)),
            pltpu.SemaphoreType.DMA((3,)),
            pltpu.SemaphoreType.DMA((7,)),
        ],
        compiler_params=pltpu.CompilerParams(vmem_limit_bytes=60 * MIB),
        cost_estimate=BRIEF,
        name="prefill_%d" % which,
    )(*args)


def own_kernel(n_head, attn0, attn1, wo_hbm, own0, own1, wo_v, sems):
    width = wo_hbm.shape[1]
    nb = width // n_head
    hb = nb // 2
    head = lax.axis_index("head")
    flip_x = head + 1 - 2 * lax.rem(head, 2)
    flip_y = lax.rem(head + 2, 4)
    places = [(head * nb, 0, nb), (flip_y * nb, nb, hb), (flip_x * nb + hb, nb + hb, hb)]
    copies = [
        pltpu.make_async_copy(
            wo_hbm.at[:, pl.ds(pl.multiple_of(src, hb), size)],
            wo_v.at[:, pl.ds(dst, size)],
            sems.at[j],
        )
        for j, (src, dst, size) in enumerate(places)
    ]
    for copy in copies:
        copy.start()
    copies[0].wait()
    for attn, own in ((attn0, own0), (attn1, own1)):
        own[:, :nb] = dot(attn[...], wo_v[:, :nb]).astype(BF)
    copies[1].wait()
    copies[2].wait()
    for attn, own in ((attn0, own0), (attn1, own1)):
        own[:, nb:] = dot(attn[...], wo_v[:, nb:]).astype(BF)


def own_parts(n_head, attn0, attn1, wo):
    rows, local = attn0.shape
    nb = wo.shape[1] // n_head
    return pl.pallas_call(
        functools.partial(own_kernel, n_head),
        out_shape=[jax.ShapeDtypeStruct((rows, 2 * nb), BF)] * 2,
        in_specs=[VM, VM, HB],
        out_specs=[VM, VM],
        scratch_shapes=[pltpu.VMEM((local, 2 * nb), BF), pltpu.SemaphoreType.DMA((3,))],
        compiler_params=pltpu.CompilerParams(vmem_limit_bytes=50 * MIB),
        cost_estimate=BRIEF,
        name="own_parts",
    )(attn0, attn1, wo)


def pass_on_kernel(own, got_a, got_b, on_a, on_b):
    nb = got_a.shape[1]
    hb = nb // 2
    on_a[...] = (own[:, nb : nb + hb].astype(F32) + got_a[:, :hb].astype(F32)).astype(BF)
    on_b[...] = (own[:, nb + hb :].astype(F32) + got_b[:, :hb].astype(F32)).astype(BF)


def pass_on(p, own, got_a, got_b):
    rows, nb = got_a.shape
    return pl.pallas_call(
        pass_on_kernel,
        out_shape=[jax.ShapeDtypeStruct((rows, nb // 2), BF)] * 2,
        in_specs=[VM] * 3,
        out_specs=[VM] * 2,
        compiler_params=pltpu.CompilerParams(vmem_limit_bytes=32 * MIB),
        cost_estimate=BRIEF,
        name="pass_on_%d" % p,
    )(own, got_a, got_b)


def sum_parts(stage, own, got_a, got_b, in_a, in_b):
    hb = in_a.shape[1]
    stage[:, :hb] = (
        own[:, :hb].astype(F32) + got_a[:, hb:].astype(F32) + in_a[...].astype(F32)
    ).astype(BF)
    stage[:, hb:] = (
        own[:, hb : 2 * hb].astype(F32) + got_b[:, hb:].astype(F32) + in_b[...].astype(F32)
    ).astype(BF)


def finish_first_kernel(p, own, got_a, got_b, in_a, in_b, moved, out, handed, stage, sems):
    keep = pltpu.make_async_copy(moved, handed, sems.at[1])
    keep.start()
    sum_parts(stage, own, got_a, got_b, in_a, in_b)
    copy = pltpu.make_async_copy(stage, out.at[p], sems.at[0])
    copy.start()
    copy.wait()
    keep.wait()


def finish_first(p, prompts, own, got_a, got_b, in_a, in_b, moved):
    rows, nb = got_a.shape
    return pl.pallas_call(
        functools.partial(finish_first_kernel, p),
        out_shape=[
            jax.ShapeDtypeStruct((prompts, rows, nb), BF),
            jax.ShapeDtypeStruct(moved.shape, BF),
        ],
        in_specs=[VM] * 6,
        out_specs=[HB] * 2,
        scratch_shapes=[pltpu.VMEM((rows, nb), BF), pltpu.SemaphoreType.DMA((2,))],
        compiler_params=pltpu.CompilerParams(vmem_limit_bytes=32 * MIB),
        cost_estimate=BRIEF,
        name="finish_%d" % p,
    )(own, got_a, got_b, in_a, in_b, moved)


def finish_last_kernel(p, slots, own, got_a, got_b, in_a, in_b, mine, *refs):
    others, (_, out, dec_out, stage, sem) = refs[:-5], refs[-5:]
    sum_parts(stage, own, got_a, got_b, in_a, in_b)
    copy = pltpu.make_async_copy(stage, out.at[p], sem)
    copy.start()
    total = mine[...].astype(F32)
    for other in others:
        total = total + other[...].astype(F32)
    for t in range(dec_out.shape[0]):
        dec_out[t] = total[t * slots : (t + 1) * slots].astype(BF)
    copy.wait()


def finish_last(p, steps, slots, own, got_a, got_b, in_a, in_b, pieces, partial):
    rows, nb = got_a.shape
    return pl.pallas_call(
        functools.partial(finish_last_kernel, p, slots),
        out_shape=[
            jax.ShapeDtypeStruct(partial.shape, BF),
            jax.ShapeDtypeStruct((steps, slots, nb), BF),
        ],
        in_specs=[VM] * (5 + len(pieces)) + [HB],
        out_specs=[HB, VM],
        scratch_shapes=[pltpu.VMEM((rows, nb), BF), pltpu.SemaphoreType.DMA],
        input_output_aliases={5 + len(pieces): 0},
        compiler_params=pltpu.CompilerParams(vmem_limit_bytes=32 * MIB),
        cost_estimate=BRIEF,
        name="finish_%d" % p,
    )(own, got_a, got_b, in_a, in_b, *pieces, partial)


def decode_kernel(n_seq, plen, adm, clen, dq, dkv, cache, *refs):
    kvs, (part, handed) = refs[:-2], refs[-2:]
    seq = lax.axis_index("seq")
    slots, width = cache.shape[0], cache.shape[1]
    queries = dq[...]
    count = queries.shape[0]
    dec_rows = dkv.shape[0]
    rows = kvs[0].shape[0]
    each = rows // n_seq

    row = lax.rem(lax.broadcasted_iota(jnp.int32, (count, 1), 0), dec_rows)
    slot, step = lax.rem(row, slots), row // slots
    taken = by_slot(slot, [adm[r] for r in range(slots)])
    scores, masks, values = [], [], []
    at = lax.broadcasted_iota(jnp.int32, (1, width), 1) * n_seq + seq
    for r in range(slots):
        limit = jnp.where(adm[r] >= 0, 0, clen[r])
        masks.append((slot == r) & (at < limit))
        scores.append(dot_nt(queries, cache[r, :, :HD]))
        values.append(cache[r, :, HD:])
    spot = lax.broadcasted_iota(jnp.int32, (1, rows), 1)
    for p, kv in enumerate(kvs):
        prompt = seq * len(kvs) + p
        masks.append((taken == prompt) & (spot < plen[prompt]))
        scores.append(dot_nt(queries, kv[:, :HD]))
        values.append(kv[:, HD:])
    other = lax.broadcasted_iota(jnp.int32, (1, dec_rows), 1)
    first = jnp.where(seq == 0, 1, 0)
    masks.append(
        (lax.rem(other, slots) == slot) & (other // slots <= step) & (first + 0 * other > 0)
    )
    scores.append(dot_nt(queries, dkv[:, :HD]))
    values.append(dkv[:, HD:])

    top = jnp.full((count, 1), NEG, F32)
    scores = [jnp.where(mask, score, NEG) for mask, score in zip(masks, scores)]
    for score in scores:
        top = jnp.maximum(top, jnp.max(score, axis=-1, keepdims=True))
    total = jnp.zeros((count, 1), F32)
    acc = jnp.zeros((count, HD), F32)
    for mask, score, value in zip(masks, scores, values):
        expo = jnp.where(mask, jnp.exp2((score - top) * C2), 0.0)
        total = total + jnp.sum(expo, axis=-1, keepdims=True)
        acc = acc + dot(expo.astype(BF), value)
    some = total > 0.0
    safe = jnp.where(some, total, 1.0)
    part[:count, :] = acc * (1.0 / safe)
    level = jnp.where(some, top * C2 + jnp.log2(safe), NEG)
    eye = lax.broadcasted_iota(jnp.int32, (count, count), 0) == lax.broadcasted_iota(
        jnp.int32, (count, count), 1
    )
    part[count : count + 1, :] = jnp.sum(jnp.where(eye, level, 0.0), axis=0, keepdims=True)

    new = lax.broadcasted_iota(jnp.int32, (rows, rows), 0)
    old = lax.broadcasted_iota(jnp.int32, (rows, rows), 1)
    move = jnp.where(old == lax.rem(new, each) * n_seq + new // each, 1.0, 0.0).astype(BF)
    for p, kv in enumerate(kvs):
        handed[p] = dot(move, kv[...]).astype(BF)


def decode_attention(n_seq, plen, adm, clen, dq, dkv, cache, kvs):
    count = dq.shape[0]
    rows = kvs[0].shape[0]
    return pl.pallas_call(
        functools.partial(decode_kernel, n_seq),
        out_shape=[
            jax.ShapeDtypeStruct((count + 8, HD), F32),
            jax.ShapeDtypeStruct((len(kvs), rows, 2 * HD), BF),
        ],
        in_specs=[SM] * 3 + [VM] * (3 + len(kvs)),
        out_specs=[VM] * 2,
        compiler_params=pltpu.CompilerParams(vmem_limit_bytes=60 * MIB),
        cost_estimate=BRIEF,
        name="decode_attention",
    )(plen, adm, clen, dq, dkv, cache, *kvs)


def joined(bit, mine, other):
    count = mine.shape[0] - 8
    swap = lax.rem(lax.axis_index("seq") // bit, 2) == 1
    one, two = mine[...], other[...]
    low = jnp.where(swap, two, one)
    high = jnp.where(swap, one, two)
    eye = lax.broadcasted_iota(jnp.int32, (count, count), 0) == lax.broadcasted_iota(
        jnp.int32, (count, count), 1
    )

    def column(row):
        return jnp.sum(jnp.where(eye, row, 0.0), axis=1, keepdims=True)

    row_a, row_b = low[count : count + 1, :], high[count : count + 1, :]
    best = jnp.maximum(row_a, row_b)
    scale_a, scale_b = jnp.exp2(row_a - best), jnp.exp2(row_b - best)
    total = scale_a + scale_b
    inverse = 1.0 / total
    mixed = low[:count] * column(scale_a * inverse) + high[:count] * column(scale_b * inverse)
    return mixed, best + jnp.log2(total)


def join_kernel(bit, mine, other, out):
    count = mine.shape[0] - 8
    mixed, level = joined(bit, mine, other)
    out[:count, :] = mixed
    out[count : count + 1, :] = level


def join(bit, mine, other):
    return pl.pallas_call(
        functools.partial(join_kernel, bit),
        out_shape=jax.ShapeDtypeStruct(mine.shape, F32),
        in_specs=[VM, VM],
        out_specs=VM,
        cost_estimate=BRIEF,
        name="join_%d" % bit,
    )(mine, other)


def decode_out_kernel(bit, n_head, mine, other, wo_hbm, *refs):
    outs, (wo_v, sems) = refs[:n_head], refs[n_head:]
    count = mine.shape[0] - 8
    rows = outs[0].shape[0]
    nb = outs[0].shape[1]
    head = lax.axis_index("head")
    flip_x = head + 1 - 2 * lax.rem(head, 2)
    flip_y = lax.rem(head + 2, 4)
    copies = [
        pltpu.make_async_copy(
            wo_hbm.at[:, pl.ds(pl.multiple_of(dest * nb, nb), nb)], wo_v.at[d], sems.at[d]
        )
        for d, dest in enumerate((head, flip_x, flip_y, 3 - head))
    ]
    for copy in reversed(copies):
        copy.start()
    mixed, _ = joined(bit, mine, other)
    mixed = mixed.astype(BF)
    flat = jnp.concatenate([mixed[i * rows : (i + 1) * rows] for i in range(count // rows)], axis=1)
    for d in reversed(range(n_head)):
        copies[d].wait()
        outs[d][...] = dot(flat, wo_v[d]).astype(BF)


def decode_project(bit, n_head, dec_rows, mine, other, wo):
    local, width = wo.shape
    nb = width // n_head
    return pl.pallas_call(
        functools.partial(decode_out_kernel, bit, n_head),
        out_shape=[jax.ShapeDtypeStruct((dec_rows, nb), BF)] * n_head,
        in_specs=[VM, VM, HB],
        out_specs=[VM] * n_head,
        scratch_shapes=[pltpu.VMEM((n_head, local, nb), BF), pltpu.SemaphoreType.DMA((n_head,))],
        compiler_params=pltpu.CompilerParams(vmem_limit_bytes=50 * MIB),
        cost_estimate=BRIEF,
        name="decode_project",
    )(mine, other, wo)


def local(
    prompts, prompt_len, admitted, cache_len, cache_kv, dec_tokens, w_query, w_key, w_value, w_out, q_gain, k_gain
):
    n_seq = lax.axis_size("seq")
    n_head = lax.axis_size("head")
    pr_dev, rows, width = prompts.shape
    steps, slots, _ = dec_tokens.shape
    nb = width // n_head
    qg, kg = q_gain.reshape(1, HD), k_gain.reshape(1, HD)
    table = jnp.asarray(prompt_table(rows))
    freq = jnp.asarray(np.tile(frequencies(), 2)[None, :])
    scalars = (prompt_len, admitted, cache_len)
    weights = (w_query, w_key, w_value, w_out, qg, kg, table, freq)

    across_x = [(i, i ^ 1) for i in range(n_head)]
    across_y = [(i, i ^ 2) for i in range(n_head)]
    across_xy = [(i, i ^ 3) for i in range(n_head)]

    def head_move(value, pairs):
        return lax.ppermute(value, "head", pairs)

    got, attns, kvs = [None] * pr_dev, [None] * pr_dev, [None] * pr_dev
    for p in reversed(range(pr_dev)):
        dec = dec_tokens
        if p < pr_dev - 1:
            dec = lax.optimization_barrier((dec_tokens, kvs[p + 1]))[0]
        dec = dec.reshape(steps * slots, width)
        out = prefill(p, p == 0, n_head, *scalars, prompts, dec, *weights)
        got[p] = (head_move(out[0], across_x), head_move(out[1], across_y))
        attns[p], kvs[p] = out[2], out[3]
    dq, dkv = out[4], out[5]
    part, handed = decode_attention(n_seq, *scalars, dq, dkv, cache_kv[0], kvs)
    own = own_parts(n_head, *attns, w_out)

    sums = [None] * pr_dev

    def after(value, other):
        return lax.optimization_barrier((value, other))[0]

    def send_on(p, before=None):
        if before is not None:
            got[p] = (after(got[p][0], before), got[p][1])
        on_a, on_b = pass_on(p, own[p], *got[p])
        sums[p] = (own[p], *got[p], head_move(on_a, across_y), head_move(on_b, across_x))
        return on_a

    def hand_over():
        each = rows // n_seq
        sending = handed.reshape(pr_dev, n_seq, each, 2 * HD)
        moved = lax.all_to_all(sending, "seq", split_axis=1, concat_axis=0, tiled=True)
        return moved.reshape(1, pr_dev * n_seq, each, 2 * HD)

    bit = 1
    while bit < n_seq:
        other = lax.ppermute(part, "seq", [(i, i ^ bit) for i in range(n_seq)])
        if bit == 1:
            other = after(other, send_on(1))
        if bit == 2:
            moved = hand_over()
            other = after(other, moved)
        if 2 * bit < n_seq:
            part = join(bit, part, other)
        else:
            other = after(other, send_on(0, part))
            partial, handed_out = finish_first(1, pr_dev, *sums[1], moved)
            other = after(other, partial)
            pieces = decode_project(bit, n_head, steps * slots, part, other, w_out)
        bit *= 2
    pieces = [pieces[0]] + [
        head_move(piece, pairs)
        for piece, pairs in zip(pieces[1:], (across_x, across_y, across_xy))
    ]
    prefill_out, decode_out = finish_last(0, steps, slots, *sums[0], pieces, partial)
    return (prefill_out, handed_out, decode_out)


def solution(mesh):
    placed = (
        P("seq", None, None),
        P(),
        P(),
        P(),
        P("head", None, "seq", None),
        P(),
        P(None, "head"),
        P(None, "head"),
        P(None, "head"),
        P("head", None),
        P(),
        P(),
    )
    return jax.shard_map(
        local,
        mesh=mesh,
        in_specs=placed,
        out_specs=(P("seq", None, "head"), P("head", None, "seq", None), P(None, None, "head")),
        check_vma=False,
    )
```

```python
import functools

import jax
import jax.numpy as jnp
import numpy as np
from jax import lax
from jax.experimental import pallas as pl
from jax.experimental.pallas import tpu as pltpu
from jax.sharding import PartitionSpec as P

HD = 128
EPS = 1e-06
THETA = 1000000.0
NEG = -1e30
LOG2E = 1.4426950408889634
SCALE = HD**-0.5
C2 = SCALE * LOG2E
BF = jnp.bfloat16
F32 = jnp.float32
HB = pl.BlockSpec(memory_space=pltpu.HBM)
VM = pl.BlockSpec(memory_space=pltpu.VMEM)
BRIEF = pl.CostEstimate(flops=1, bytes_accessed=1, transcendentals=0)
MIB = 1024 * 1024


def frequencies():
    half = HD // 2
    freq = np.float32(THETA) ** (-np.arange(half, dtype=np.float32) / np.float32(half))
    return freq.astype(np.float32)


def prompt_table(length):
    angle = np.arange(length, dtype=np.float32)[:, None] * frequencies()[None, :]
    cosine, sine = np.cos(angle), np.sin(angle)
    return np.concatenate([cosine, cosine, -sine, sine], axis=1).astype(np.float32)


def dot(a, b):
    return jnp.dot(a, b, preferred_element_type=F32)


def dot_nt(a, b):
    return lax.dot_general(a, b, (((1,), (1,)), ((), ())), preferred_element_type=F32)


def norm(values, gain):
    square = jnp.mean(values * values, axis=-1, keepdims=True)
    return values * lax.rsqrt(square + EPS) * gain


def rope(values, cos2, sin2):
    return values * cos2 + pltpu.roll(values, HD // 2, 1) * sin2


def effective_lengths(plen, adm, clen, slots):
    out = []
    for r in range(slots):
        taken = adm[r]
        out.append(jnp.where(taken >= 0, plen[jnp.maximum(taken, 0)], clen[r]))
    return out


def by_slot(index, values):
    result = jnp.full(index.shape, values[0])
    for r in range(1, len(values)):
        result = jnp.where(index == r, values[r], result)
    return result


def partners():
    head, seq = lax.axis_index("head"), lax.axis_index("seq")
    flip_x = head + 1 - 2 * lax.rem(head, 2)
    flip_y = lax.rem(head + 2, 4)
    even = lax.rem(seq, 2) == 0
    return jnp.where(even, flip_x, flip_y), jnp.where(even, flip_y, flip_x)


def out_copy(wo_hbm, block, nb, dest, sem):
    return pltpu.make_async_copy(
        wo_hbm.at[:, pl.ds(pl.multiple_of(block * nb, nb), nb)], dest, sem
    )


def attention(raw, kv, length, qg, table, bias_v, q_v, s_v, w_v, attn):
    rows = kv.shape[0]
    heads = attn.shape[1] // HD
    half = rows // 2
    quarter = rows // 4
    cos2, sin2 = table[:, :HD], table[:, HD:]
    row_at = lax.broadcasted_iota(jnp.int32, (rows, rows), 0)
    col_at = lax.broadcasted_iota(jnp.int32, (rows, rows), 1)
    bias_v[...] = jnp.where((col_at <= row_at) & (col_at < length), 0.0, NEG).astype(F32)
    for h in range(heads):
        q_v[h] = rope(norm(raw[:rows, h * HD : (h + 1) * HD], qg[...]), cos2, sin2).astype(BF)
    for h in range(heads):
        s_v[h, :half, :half] = dot_nt(q_v[h, :half], kv[:half, :HD])
        s_v[h, half:, :] = dot_nt(q_v[h, half:], kv[:, :HD])
    for h in range(heads):
        for block in range(4):
            at = slice(block * quarter, (block + 1) * quarter)
            keys = half if block < 2 else rows
            scores = s_v[h, at, :keys] + bias_v[at, :keys]
            top = jnp.max(scores, axis=-1, keepdims=True)
            expo = jnp.exp2((scores - top) * C2)
            total = jnp.sum(expo, axis=-1, keepdims=True)
            w_v[h, at, :keys] = (expo * (1.0 / total)).astype(BF)
    for h in range(heads):
        at = slice(h * HD, (h + 1) * HD)
        attn[:half, at] = dot(w_v[h, :half, :half], kv[:half, HD:]).astype(BF)
        attn[half:, at] = dot(w_v[h, half:, :], kv[:, HD:]).astype(BF)


def attention_scratch(rows, heads):
    return [
        pltpu.VMEM((rows, rows), F32),
        pltpu.VMEM((heads, rows, HD), BF),
        pltpu.VMEM((heads, rows, rows), F32),
        pltpu.VMEM((heads, rows, rows), BF),
    ]


def project_kernel(n_head, plen_h, x_hbm, dec_hbm, wq_hbm, wk_hbm, wv_hbm, wo_hbm, qg_h, kg_h, table_h, *refs):
    send, attn, kv, raw = refs[:4]
    x_v, wkv_v, wq_v, wo_v, acc, plen, qg, kg, table = refs[4:13]
    bias_v, q_v, s_v, w_v = refs[13:17]
    x_sem, dec_sem, wkv_sem, wq_sem, wo_sem, small_sem = refs[17:]
    prompts, rows, width = x_hbm.shape
    dec_rows = dec_hbm.shape[0]
    chunks, _, depth = x_v.shape
    local = wq_v.shape[1]
    nb = width // n_head
    lead = prompts - 1
    first, _ = partners()
    diag = 3 - lax.axis_index("head")

    queue = []
    for c in range(chunks):
        at = pl.ds(c * depth, depth)
        group = [
            pltpu.make_async_copy(
                x_hbm.at[p, :, at], x_v.at[c, pl.ds((lead - p) * rows, rows)], x_sem.at[p, c]
            )
            for p in range(prompts)
        ]
        group += [
            pltpu.make_async_copy(
                dec_hbm.at[:, at], x_v.at[c, pl.ds(prompts * rows, dec_rows)], dec_sem.at[c]
            ),
            pltpu.make_async_copy(wk_hbm.at[at], wkv_v.at[at, pl.ds(0, HD)], wkv_sem.at[0, c]),
            pltpu.make_async_copy(wv_hbm.at[at], wkv_v.at[at, pl.ds(HD, HD)], wkv_sem.at[1, c]),
            pltpu.make_async_copy(wq_hbm.at[at], wq_v.at[at], wq_sem.at[c]),
        ]
        queue.append(group)
    small = [
        pltpu.make_async_copy(src, dst, small_sem.at[i])
        for i, (src, dst) in enumerate(
            [(plen_h, plen), (qg_h, qg), (kg_h, kg), (table_h, table)]
        )
    ]
    o_copies = [
        out_copy(wo_hbm, block, nb, wo_v.at[j], wo_sem.at[j]) for j, block in enumerate((diag, first))
    ]
    queue += [[copy] for copy in o_copies]
    ahead = 4
    for copy in queue[0] + small:
        copy.start()
    for group in queue[1:ahead]:
        for copy in group:
            copy.start()
    for c in range(chunks):
        for copy in queue[c]:
            copy.wait()
        if c + ahead < len(queue):
            for copy in queue[c + ahead]:
                copy.start()
        at = slice(c * depth, (c + 1) * depth)
        lead_at, rest_at = slice(0, rows), slice(rows, prompts * rows + dec_rows)
        for dest, part in ((acc, lead_at), (raw, rest_at)):
            kv_part = dot(x_v[c, part], wkv_v[at, :])
            q_part = dot(x_v[c, part], wq_v[at, :])
            if c == 0:
                dest[:, local:] = kv_part
                dest[:, :local] = q_part
            else:
                dest[:, local:] += kv_part
                dest[:, :local] += q_part

    for copy in small:
        copy.wait()
    cos2, sin2 = table[:, :HD], table[:, HD:]
    kv[:, :HD] = rope(norm(acc[:, local : local + HD], kg[...]), cos2, sin2).astype(BF)
    kv[:, HD:] = acc[:, local + HD :].astype(BF)
    length = plen[lax.axis_index("seq") * prompts + lead]
    attention(acc, kv, length, qg, table, bias_v, q_v, s_v, w_v, attn)
    for j, copy in enumerate(o_copies):
        copy.wait()
        send[:, j * nb : (j + 1) * nb] = dot(attn[...], wo_v[j]).astype(BF)


def project(n_head, plen, x, dec, wq, wk, wv, wo, qg, kg, table):
    prompts, rows, width = x.shape
    dec_rows = dec.shape[0]
    local = wq.shape[1]
    chunks = 8
    nb = width // n_head
    return pl.pallas_call(
        functools.partial(project_kernel, n_head),
        out_shape=[
            jax.ShapeDtypeStruct((rows, 2 * nb), BF),
            jax.ShapeDtypeStruct((rows, local), BF),
            jax.ShapeDtypeStruct((rows, 2 * HD), BF),
            jax.ShapeDtypeStruct(((prompts - 1) * rows + dec_rows, local + 2 * HD), F32),
        ],
        in_specs=[HB] * 10,
        out_specs=[VM] * 4,
        scratch_shapes=[
            pltpu.VMEM((chunks, prompts * rows + dec_rows, width // chunks), BF),
            pltpu.VMEM((width, 2 * HD), BF),
            pltpu.VMEM((width, local), BF),
            pltpu.VMEM((2, local, nb), BF),
            pltpu.VMEM((rows, local + 2 * HD), F32),
            pltpu.SMEM(plen.shape, jnp.int32),
            pltpu.VMEM(qg.shape, F32),
            pltpu.VMEM(kg.shape, F32),
            pltpu.VMEM(table.shape, F32),
        ]
        + attention_scratch(rows, local // HD)
        + [
            pltpu.SemaphoreType.DMA((prompts, chunks)),
            pltpu.SemaphoreType.DMA((chunks,)),
            pltpu.SemaphoreType.DMA((2, chunks)),
            pltpu.SemaphoreType.DMA((chunks,)),
            pltpu.SemaphoreType.DMA((2,)),
            pltpu.SemaphoreType.DMA((4,)),
        ],
        compiler_params=pltpu.CompilerParams(vmem_limit_bytes=60 * MIB),
        cost_estimate=BRIEF,
        name="project",
    )(plen, x, dec, wq, wk, wv, wo, qg, kg, table)


def decode_attention(n_seq, slots, plen, adm, clen, raw, local, kvs, cache, qg, kg, freq, part):
    seq = lax.axis_index("seq")
    dec_rows = raw.shape[0]
    width = cache.shape[1]
    rows = kvs[0].shape[0]
    eff = effective_lengths(plen, adm, clen, slots)
    row = lax.broadcasted_iota(jnp.int32, (dec_rows, HD), 0)
    places = by_slot(lax.rem(row, slots), eff) + row // slots
    angle = places.astype(F32) * freq[...]
    lane = lax.broadcasted_iota(jnp.int32, (dec_rows, HD), 1)
    cos2 = jnp.cos(angle)
    sin2 = jnp.where(lane < HD // 2, -1.0, 1.0) * jnp.sin(angle)
    new_key = rope(norm(raw[:, local : local + HD], kg[...]), cos2, sin2).astype(BF)
    new_value = raw[:, local + HD :].astype(BF)
    queries = jnp.concatenate(
        [
            rope(norm(raw[:, h * HD : (h + 1) * HD], qg[...]), cos2, sin2).astype(BF)
            for h in range(local // HD)
        ],
        axis=0,
    )
    count = queries.shape[0]

    row = lax.rem(lax.broadcasted_iota(jnp.int32, (count, 1), 0), dec_rows)
    slot, step = lax.rem(row, slots), row // slots
    taken = by_slot(slot, [adm[r] for r in range(slots)])
    scores, masks, values = [], [], []
    at = lax.broadcasted_iota(jnp.int32, (1, width), 1) * n_seq + seq
    for r in range(slots):
        limit = jnp.where(adm[r] >= 0, 0, clen[r])
        masks.append((slot == r) & (at < limit))
        scores.append(dot_nt(queries, cache[r, :, :HD]))
        values.append(cache[r, :, HD:])
    spot = lax.broadcasted_iota(jnp.int32, (1, rows), 1)
    for p, kv in enumerate(kvs):
        prompt = seq * len(kvs) + p
        masks.append((taken == prompt) & (spot < plen[prompt]))
        scores.append(dot_nt(queries, kv[:, :HD]))
        values.append(kv[:, HD:])
    other = lax.broadcasted_iota(jnp.int32, (1, dec_rows), 1)
    first = jnp.where(seq == 0, 1, 0)
    masks.append(
        (lax.rem(other, slots) == slot) & (other // slots <= step) & (first + 0 * other > 0)
    )
    scores.append(dot_nt(queries, new_key))
    values.append(new_value)

    top = jnp.full((count, 1), NEG, F32)
    scores = [jnp.where(mask, score, NEG) for mask, score in zip(masks, scores)]
    for score in scores:
        top = jnp.maximum(top, jnp.max(score, axis=-1, keepdims=True))
    total = jnp.zeros((count, 1), F32)
    acc = jnp.zeros((count, HD), F32)
    for mask, score, value in zip(masks, scores, values):
        expo = jnp.where(mask, jnp.exp2((score - top) * C2), 0.0)
        total = total + jnp.sum(expo, axis=-1, keepdims=True)
        acc = acc + dot(expo.astype(BF), value)
    some = total > 0.0
    safe = jnp.where(some, total, 1.0)
    mixed = acc * (1.0 / safe)
    level = jnp.where(some, top * C2 + jnp.log2(safe), NEG) + jnp.zeros((count, HD), F32)
    each = part.shape[1]
    for d in range(n_seq):
        part[d, :, :HD] = mixed[d * each : (d + 1) * each]
        part[d, :, HD:] = level[d * each : (d + 1) * each]


def second_kernel(n_head, n_seq, prompts, plen_h, adm_h, clen_h, raw, kv1, attn1, cache_h, wo_hbm, *refs):
    smalls_h = refs[:4]
    send, own0, own1, part, handed = refs[4:9]
    cache, wo_v, attns, kv0, plen, adm, clen, qg, kg, table, freq = refs[9:20]
    bias_v, q_v, s_v, w_v = refs[20:24]
    cache_sem, wo_sem, small_sem = refs[24:]
    rows, local = attn1.shape
    nb = wo_v.shape[2]
    slots = cache.shape[0]
    first, second = partners()
    head = lax.axis_index("head")
    small = [
        pltpu.make_async_copy(src, dst, small_sem.at[i])
        for i, (src, dst) in enumerate(
            zip((plen_h, adm_h, clen_h) + smalls_h, (plen, adm, clen, qg, kg, table, freq))
        )
    ]
    o_copies = [
        out_copy(wo_hbm, block, nb, wo_v.at[j], wo_sem.at[j])
        for j, block in enumerate((3 - head, first, head, second))
    ]
    cache_copy = pltpu.make_async_copy(cache_h, cache, cache_sem)
    for copy in small + [cache_copy] + o_copies:
        copy.start()
    for copy in small:
        copy.wait()
    cos2, sin2 = table[:, :HD], table[:, HD:]
    kv0[:, :HD] = rope(norm(raw[:rows, local : local + HD], kg[...]), cos2, sin2).astype(BF)
    kv0[:, HD:] = raw[:rows, local + HD :].astype(BF)
    length = plen[lax.axis_index("seq") * prompts]
    mine = attns.at[pl.ds(0, rows)]
    attention(raw, kv0, length, qg, table, bias_v, q_v, s_v, w_v, mine)
    attns[rows:, :] = attn1[...]

    each = rows // n_seq
    total = 2 * rows
    new = lax.broadcasted_iota(jnp.int32, (total, total), 0)
    old = lax.broadcasted_iota(jnp.int32, (total, total), 1)
    dest, rest = new // (2 * each), lax.rem(new, 2 * each)
    source = (rest // each) * rows + lax.rem(rest, each) * n_seq + dest
    move = jnp.where(old == source, 1.0, 0.0).astype(BF)
    handed[...] = (dot(move[:, :rows], kv0[...]) + dot(move[:, rows:], kv1[...])).astype(BF)

    cache_copy.wait()
    decode_attention(
        n_seq, slots, plen, adm, clen, raw.at[pl.ds(rows, raw.shape[0] - rows)], local,
        [kv0, kv1], cache, qg, kg, freq, part,
    )
    for copy in o_copies:
        copy.wait()
    for j in range(2):
        send[:, j * nb : (j + 1) * nb] = dot(attns[:rows], wo_v[j]).astype(BF)
    for j in range(2):
        both = dot(attns[...], wo_v[2 + j]).astype(BF)
        own0[:, j * nb : (j + 1) * nb] = both[:rows]
        own1[:, j * nb : (j + 1) * nb] = both[rows:]


def second(n_head, n_seq, prompts, plen, adm, clen, raw, kv1, attn1, cache, wo, qg, kg, table, freq):
    rows, local = attn1.shape
    nb = wo.shape[1] // n_head
    dec_rows = raw.shape[0] - rows
    count = dec_rows * (local // HD)
    return pl.pallas_call(
        functools.partial(second_kernel, n_head, n_seq, prompts),
        out_shape=[jax.ShapeDtypeStruct((rows, 2 * nb), BF)] * 3
        + [
            jax.ShapeDtypeStruct((n_seq, count // n_seq, 2 * HD), F32),
            jax.ShapeDtypeStruct((prompts * rows, 2 * HD), BF),
        ],
        in_specs=[HB] * 3 + [VM] * 3 + [HB] * 6,
        out_specs=[VM] * 5,
        scratch_shapes=[
            pltpu.VMEM(cache.shape, BF),
            pltpu.VMEM((4, local, nb), BF),
            pltpu.VMEM((prompts * rows, local), BF),
            pltpu.VMEM((rows, 2 * HD), BF),
            pltpu.SMEM(plen.shape, jnp.int32),
            pltpu.SMEM(adm.shape, jnp.int32),
            pltpu.SMEM(clen.shape, jnp.int32),
            pltpu.VMEM(qg.shape, F32),
            pltpu.VMEM(kg.shape, F32),
            pltpu.VMEM(table.shape, F32),
            pltpu.VMEM(freq.shape, F32),
        ]
        + attention_scratch(rows, local // HD)
        + [
            pltpu.SemaphoreType.DMA,
            pltpu.SemaphoreType.DMA((4,)),
            pltpu.SemaphoreType.DMA((7,)),
        ],
        compiler_params=pltpu.CompilerParams(vmem_limit_bytes=48 * MIB),
        cost_estimate=BRIEF,
        name="second",
    )(plen, adm, clen, raw, kv1, attn1, cache, wo, qg, kg, table, freq)


def pass_on_kernel(own, got, on):
    nb = on.shape[1]
    on[...] = (own[:, nb:].astype(F32) + got[:, :nb].astype(F32)).astype(BF)


def pass_on(p, own, got):
    rows, both = got.shape
    return pl.pallas_call(
        pass_on_kernel,
        out_shape=jax.ShapeDtypeStruct((rows, both // 2), BF),
        in_specs=[VM] * 2,
        out_specs=VM,
        cost_estimate=BRIEF,
        name="pass_on_%d" % p,
    )(own, got)


def combine_kernel(parts, out):
    n_seq = parts.shape[0]
    levels = [parts[i, :, HD:] for i in range(n_seq)]
    best = functools.reduce(jnp.maximum, levels)
    total = jnp.zeros_like(best)
    mixed = jnp.zeros_like(best)
    for i in range(n_seq):
        weight = jnp.exp2(levels[i] - best)
        total = total + weight
        mixed = mixed + weight * parts[i, :, :HD]
    mixed = (mixed * (1.0 / total)).astype(BF)
    for i in range(n_seq):
        out[i] = mixed


def combine(parts):
    n_seq, each, _ = parts.shape
    return pl.pallas_call(
        combine_kernel,
        out_shape=jax.ShapeDtypeStruct((n_seq, each, HD), BF),
        in_specs=[VM],
        out_specs=VM,
        cost_estimate=BRIEF,
        name="combine",
    )(parts)


def decode_out_kernel(mixed, wo_hbm, out, wo_v, sems):
    n_head, rows, nb = out.shape
    count = mixed.shape[0]
    copies = [out_copy(wo_hbm, d, nb, wo_v.at[d], sems.at[d]) for d in range(n_head)]
    for copy in copies:
        copy.start()
    flat = jnp.concatenate([mixed[i * rows : (i + 1) * rows] for i in range(count // rows)], axis=1)
    for d in range(n_head):
        copies[d].wait()
        out[d] = dot(flat, wo_v[d]).astype(BF)


def decode_project(n_head, dec_rows, mixed, wo):
    local, width = wo.shape
    nb = width // n_head
    return pl.pallas_call(
        decode_out_kernel,
        out_shape=jax.ShapeDtypeStruct((n_head, dec_rows, nb), BF),
        in_specs=[VM, HB],
        out_specs=VM,
        scratch_shapes=[pltpu.VMEM((n_head, local, nb), BF), pltpu.SemaphoreType.DMA((n_head,))],
        compiler_params=pltpu.CompilerParams(vmem_limit_bytes=50 * MIB),
        cost_estimate=BRIEF,
        name="decode_project",
    )(mixed, wo)


def sum_parts(stage, own, got, last):
    nb = last.shape[1]
    stage[...] = (
        own[:, :nb].astype(F32) + got[:, nb:].astype(F32) + last[...].astype(F32)
    ).astype(BF)


def finish_first_kernel(p, own, got, last, moved, out, handed, stage, sems):
    keep = pltpu.make_async_copy(moved, handed, sems.at[1])
    keep.start()
    sum_parts(stage, own, got, last)
    copy = pltpu.make_async_copy(stage, out.at[p], sems.at[0])
    copy.start()
    copy.wait()
    keep.wait()


def finish_first(p, prompts, own, got, last, moved):
    rows, nb = last.shape
    return pl.pallas_call(
        functools.partial(finish_first_kernel, p),
        out_shape=[
            jax.ShapeDtypeStruct((prompts, rows, nb), BF),
            jax.ShapeDtypeStruct(moved.shape, BF),
        ],
        in_specs=[VM] * 4,
        out_specs=[HB] * 2,
        scratch_shapes=[pltpu.VMEM((rows, nb), BF), pltpu.SemaphoreType.DMA((2,))],
        cost_estimate=BRIEF,
        name="finish_%d" % p,
    )(own, got, last, moved)


def finish_last_kernel(p, slots, own, got, last, pieces, _, out, dec_out, stage, sem):
    sum_parts(stage, own, got, last)
    copy = pltpu.make_async_copy(stage, out.at[p], sem)
    copy.start()
    total = pieces[0].astype(F32)
    for i in range(1, pieces.shape[0]):
        total = total + pieces[i].astype(F32)
    for t in range(dec_out.shape[0]):
        dec_out[t] = total[t * slots : (t + 1) * slots].astype(BF)
    copy.wait()


def finish_last(p, steps, slots, own, got, last, pieces, partial):
    rows, nb = last.shape
    return pl.pallas_call(
        functools.partial(finish_last_kernel, p, slots),
        out_shape=[
            jax.ShapeDtypeStruct(partial.shape, BF),
            jax.ShapeDtypeStruct((steps, slots, nb), BF),
        ],
        in_specs=[VM] * 4 + [HB],
        out_specs=[HB, VM],
        scratch_shapes=[pltpu.VMEM((rows, nb), BF), pltpu.SemaphoreType.DMA],
        input_output_aliases={4: 0},
        cost_estimate=BRIEF,
        name="finish_%d" % p,
    )(own, got, last, pieces, partial)


def after(value, other):
    return lax.optimization_barrier((value, other))[0]


def exchange(value, axis):
    return lax.all_to_all(value, axis, split_axis=0, concat_axis=0, tiled=True)


def local(
    prompts, prompt_len, admitted, cache_len, cache_kv, dec_tokens, w_query, w_key, w_value, w_out, q_gain, k_gain
):
    n_seq = lax.axis_size("seq")
    n_head = lax.axis_size("head")
    pr_dev, rows, width = prompts.shape
    steps, slots, _ = dec_tokens.shape
    dec_rows = steps * slots
    each = rows // n_seq
    qg, kg = q_gain.reshape(1, HD), k_gain.reshape(1, HD)
    table = jnp.asarray(prompt_table(rows))
    freq = jnp.asarray(np.tile(frequencies(), 2)[None, :])
    dec = dec_tokens.reshape(dec_rows, width)

    def head_move(value, masks):
        pairs = [
            (h * n_seq + s, (h ^ masks[s % 2]) * n_seq + s)
            for h in range(n_head)
            for s in range(n_seq)
        ]
        return lax.ppermute(value, ("head", "seq"), pairs)

    send1, attn1, kv1, raw = project(
        n_head, prompt_len, prompts, dec, w_query, w_key, w_value, w_out, qg, kg, table
    )
    got1 = head_move(send1, (1, 2))
    send0, own0, own1, part, handed = second(
        n_head, n_seq, pr_dev, prompt_len, admitted, cache_len, raw, kv1, attn1, cache_kv[0], w_out,
        qg, kg, table, freq,
    )
    got0 = head_move(send0, (1, 2))
    parts = exchange(part, "seq")
    on1 = pass_on(1, own1, after(got1, parts))
    last1 = head_move(on1, (2, 1))
    mixed = exchange(combine(after(parts, on1)), "seq").reshape(-1, HD)
    on0 = pass_on(0, own0, after(got0, mixed))
    last0 = head_move(on0, (2, 1))
    pieces = exchange(decode_project(n_head, dec_rows, after(mixed, on0), w_out), "head")
    handed = handed.reshape(n_seq, pr_dev * each, 2 * HD)
    moved = exchange(after(handed, pieces), "seq").reshape(1, pr_dev * n_seq, each, 2 * HD)
    partial, handed_out = finish_first(1, pr_dev, own1, got1, last1, moved)
    prefill_out, decode_out = finish_last(0, steps, slots, own0, got0, last0, pieces, partial)
    return (prefill_out, handed_out, decode_out)


def solution(mesh):
    placed = (
        P("seq", None, None),
        P(),
        P(),
        P(),
        P("head", None, "seq", None),
        P(),
        P(None, "head"),
        P(None, "head"),
        P(None, "head"),
        P("head", None),
        P(),
        P(),
    )
    return jax.shard_map(
        local,
        mesh=mesh,
        in_specs=placed,
        out_specs=(P("seq", None, "head"), P("head", None, "seq", None), P(None, None, "head")),
        check_vma=False,
    )
```

```python
import functools

import jax
import jax.numpy as jnp
import numpy as np
from jax import lax
from jax.experimental import pallas as pl
from jax.experimental.pallas import tpu as pltpu
from jax.sharding import PartitionSpec as P

HD = 128
EPS = 1e-06
THETA = 1000000.0
NEG = -1e30
LOG2E = 1.4426950408889634
SCALE = HD**-0.5
C2 = SCALE * LOG2E
BF = jnp.bfloat16
F32 = jnp.float32
HB = pl.BlockSpec(memory_space=pltpu.HBM)
VM = pl.BlockSpec(memory_space=pltpu.VMEM)
BRIEF = pl.CostEstimate(flops=1, bytes_accessed=1, transcendentals=0)
MIB = 1024 * 1024
LIMIT_A = 60
LIMIT_B = 50
LIMIT_C = 50


def frequencies():
    half = HD // 2
    freq = np.float32(THETA) ** (-np.arange(half, dtype=np.float32) / np.float32(half))
    return freq.astype(np.float32)


def turns(places):
    lane = lax.broadcasted_iota(jnp.int32, places.shape, 1)
    freq = jnp.zeros(places.shape, F32)
    spot = lax.rem(lane, HD // 2)
    for i, value in enumerate(frequencies()):
        freq = jnp.where(spot == i, float(value), freq)
    return freq


def cos_sin(places, freq):
    angle = places.astype(F32) * freq
    lane = lax.broadcasted_iota(jnp.int32, places.shape, 1)
    return jnp.cos(angle), jnp.where(lane < HD // 2, -1.0, 1.0) * jnp.sin(angle)


def dot(a, b):
    return jnp.dot(a, b, preferred_element_type=F32)


def dot_nt(a, b):
    return lax.dot_general(a, b, (((1,), (1,)), ((), ())), preferred_element_type=F32)


def norm(values, gain):
    square = jnp.mean(values * values, axis=-1, keepdims=True)
    return values * lax.rsqrt(square + EPS) * gain


def rope(values, cos2, sin2):
    return values * cos2 + pltpu.roll(values, HD // 2, 1) * sin2


def effective_lengths(plen, adm, clen, slots):
    out = []
    for r in range(slots):
        taken = adm[r]
        out.append(jnp.where(taken >= 0, plen[jnp.maximum(taken, 0)], clen[r]))
    return out


def by_slot(index, values):
    result = jnp.full(index.shape, values[0])
    for r in range(1, len(values)):
        result = jnp.where(index == r, values[r], result)
    return result


def partners():
    head, seq = lax.axis_index("head"), lax.axis_index("seq")
    flip_x = head + 1 - 2 * lax.rem(head, 2)
    flip_y = lax.rem(head + 2, 4)
    even = lax.rem(seq, 2) == 0
    return jnp.where(even, flip_x, flip_y), jnp.where(even, flip_y, flip_x)


def out_copy(wo_hbm, block, nb, dest, sem):
    return pltpu.make_async_copy(
        wo_hbm.at[:, pl.ds(pl.multiple_of(block * nb, nb), nb)], dest, sem
    )


def attention(queries, kv, length, bias_v, s_v, w_v, attn):
    rows = kv.shape[0]
    heads = attn.shape[1] // HD
    half = rows // 2
    quarter = rows // 4
    row_at = lax.broadcasted_iota(jnp.int32, (rows, rows), 0)
    col_at = lax.broadcasted_iota(jnp.int32, (rows, rows), 1)
    bias_v[...] = jnp.where((col_at <= row_at) & (col_at < length), 0.0, NEG).astype(F32)
    for h in range(heads):
        at = slice(h * HD, (h + 1) * HD)
        s_v[h, :half, :half] = dot_nt(queries[:half, at], kv[:half, :HD])
        s_v[h, half:, :] = dot_nt(queries[half:, at], kv[:, :HD])
    for h in range(heads):
        for block in range(4):
            at = slice(block * quarter, (block + 1) * quarter)
            keys = half if block < 2 else rows
            scores = s_v[h, at, :keys] + bias_v[at, :keys]
            top = jnp.max(scores, axis=-1, keepdims=True)
            expo = jnp.exp2((scores - top) * C2)
            total = jnp.sum(expo, axis=-1, keepdims=True)
            w_v[h, at, :keys] = (expo * (1.0 / total)).astype(BF)
    for h in range(heads):
        at = slice(h * HD, (h + 1) * HD)
        attn[:half, at] = dot(w_v[h, :half, :half], kv[:half, HD:]).astype(BF)
        attn[half:, at] = dot(w_v[h, half:, :], kv[:, HD:]).astype(BF)


def attention_scratch(rows, heads):
    return [
        pltpu.VMEM((rows, rows), F32),
        pltpu.VMEM((heads, rows, rows), F32),
        pltpu.VMEM((heads, rows, rows), BF),
    ]


def unit(count):
    return lax.broadcasted_iota(jnp.int32, (count, count), 0) == lax.broadcasted_iota(
        jnp.int32, (count, count), 1
    )


def decode_attention(n_seq, slots, plen, adm, clen, raw, local, kvs, cache, qg, kg, part):
    seq = lax.axis_index("seq")
    dec_rows = raw.shape[0]
    width = cache.shape[1]
    rows = kvs[0].shape[0]
    eff = effective_lengths(plen, adm, clen, slots)
    row = lax.broadcasted_iota(jnp.int32, (dec_rows, HD), 0)
    places = by_slot(lax.rem(row, slots), eff) + row // slots
    cos2, sin2 = cos_sin(places, turns(row))
    new_key = rope(norm(raw[:, local : local + HD], kg[...]), cos2, sin2).astype(BF)
    new_value = raw[:, local + HD :].astype(BF)
    queries = jnp.concatenate(
        [
            rope(norm(raw[:, h * HD : (h + 1) * HD], qg[...]), cos2, sin2).astype(BF)
            for h in range(local // HD)
        ],
        axis=0,
    )
    count = queries.shape[0]

    row = lax.rem(lax.broadcasted_iota(jnp.int32, (count, 1), 0), dec_rows)
    slot, step = lax.rem(row, slots), row // slots
    taken = by_slot(slot, [adm[r] for r in range(slots)])
    scores, masks, values = [], [], []
    at = lax.broadcasted_iota(jnp.int32, (1, width), 1) * n_seq + seq
    for r in range(slots):
        limit = jnp.where(adm[r] >= 0, 0, clen[r])
        masks.append((slot == r) & (at < limit))
        scores.append(dot_nt(queries, cache[r, :, :HD]))
        values.append(cache[r, :, HD:])
    spot = lax.broadcasted_iota(jnp.int32, (1, rows), 1)
    for p, kv in enumerate(kvs):
        prompt = seq * len(kvs) + p
        masks.append((taken == prompt) & (spot < plen[prompt]))
        scores.append(dot_nt(queries, kv[:, :HD]))
        values.append(kv[:, HD:])
    other = lax.broadcasted_iota(jnp.int32, (1, dec_rows), 1)
    first = jnp.where(seq == 0, 1, 0)
    masks.append(
        (lax.rem(other, slots) == slot) & (other // slots <= step) & (first + 0 * other > 0)
    )
    scores.append(dot_nt(queries, new_key))
    values.append(new_value)

    top = jnp.full((count, 1), NEG, F32)
    scores = [jnp.where(mask, score, NEG) for mask, score in zip(masks, scores)]
    for score in scores:
        top = jnp.maximum(top, jnp.max(score, axis=-1, keepdims=True))
    total = jnp.zeros((count, 1), F32)
    acc = jnp.zeros((count, HD), F32)
    for mask, score, value in zip(masks, scores, values):
        expo = jnp.where(mask, jnp.exp2((score - top) * C2), 0.0)
        total = total + jnp.sum(expo, axis=-1, keepdims=True)
        acc = acc + dot(expo.astype(BF), value)
    some = total > 0.0
    safe = jnp.where(some, total, 1.0)
    part[:count, :] = acc * (1.0 / safe)
    level = jnp.where(some, top * C2 + jnp.log2(safe), NEG)
    part[count : count + 1, :] = jnp.sum(jnp.where(unit(count), level, 0.0), axis=0, keepdims=True)


def project_kernel(n_head, n_seq, *refs):
    plen_h, adm_h, clen_h, qg_h, kg_h, x_hbm, dec_hbm, cache_h, wq_hbm, wk_hbm, wv_hbm, wo_hbm = refs[:12]
    send_h, pack_h, part_h = refs[12:15]
    x_v, dec_v, flat_v, wkv_v, wq_v, wo_v, raw, send, pack, part = refs[15:25]
    cache, plen, adm, clen, qg, kg, cos_v, sin_v = refs[25:33]
    bias_v, s_v, w_v = refs[33:36]
    x_sem, dec_sem, wkv_sem, wq_sem, wo_sem, cache_sem, small_sem, out_sem = refs[36:]
    prompts, rows, width = x_hbm.shape
    steps, slots, _ = dec_hbm.shape
    dec_rows = steps * slots
    chunks, _, depth = x_v.shape
    local = wq_v.shape[1]
    nb = width // n_head
    first, _ = partners()
    diag = 3 - lax.axis_index("head")

    queue = []
    for c in range(chunks):
        at = pl.ds(c * depth, depth)
        group = [
            pltpu.make_async_copy(
                x_hbm.at[p, :, at], x_v.at[c, pl.ds(p * rows, rows)], x_sem.at[p, c]
            )
            for p in range(prompts)
        ]
        group += [
            pltpu.make_async_copy(wk_hbm.at[at], wkv_v.at[at, pl.ds(0, HD)], wkv_sem.at[0, c]),
            pltpu.make_async_copy(wv_hbm.at[at], wkv_v.at[at, pl.ds(HD, HD)], wkv_sem.at[1, c]),
            pltpu.make_async_copy(wq_hbm.at[at], wq_v.at[at], wq_sem.at[c]),
        ]
        queue.append(group)
    small = [
        pltpu.make_async_copy(src, dst, small_sem.at[i])
        for i, (src, dst) in enumerate(
            [(plen_h, plen), (adm_h, adm), (clen_h, clen), (qg_h, qg), (kg_h, kg)]
        )
    ]
    dec_copy = pltpu.make_async_copy(dec_hbm, dec_v, dec_sem)
    cache_copy = pltpu.make_async_copy(cache_h, cache, cache_sem)
    o_copies = [
        out_copy(wo_hbm, block, nb, wo_v.at[j], wo_sem.at[j]) for j, block in enumerate((diag, first))
    ]
    queue += [[cache_copy]] + [[copy] for copy in o_copies]
    ahead = 4
    for copy in [dec_copy] + queue[0] + small:
        copy.start()
    for group in queue[1:ahead]:
        for copy in group:
            copy.start()
    row = lax.broadcasted_iota(jnp.int32, (rows, HD), 0)
    freq = turns(lax.broadcasted_iota(jnp.int32, (1, HD), 0))
    cos_v[...], sin_v[...] = cos_sin(row, freq)
    dec_copy.wait()
    for t in range(steps):
        flat_v[t * slots : (t + 1) * slots, :] = dec_v[t].astype(F32)
    for c in range(chunks):
        x_v[c, prompts * rows :, :] = flat_v[:, c * depth : (c + 1) * depth].astype(BF)
    for c in range(chunks):
        for copy in queue[c]:
            copy.wait()
        if c + ahead < len(queue):
            for copy in queue[c + ahead]:
                copy.start()
        at = slice(c * depth, (c + 1) * depth)
        kv_part = dot(x_v[c], wkv_v[at, :])
        q_part = dot(x_v[c], wq_v[at, :])
        if c == 0:
            raw[:, local:] = kv_part
            raw[:, :local] = q_part
        else:
            raw[:, local:] += kv_part
            raw[:, :local] += q_part

    for copy in small:
        copy.wait()
    cos2, sin2 = cos_v[...], sin_v[...]
    lead = prompts - 1
    both = 2 * HD
    for p in range(prompts):
        at = slice(p * rows, (p + 1) * rows)
        col = p * both
        pack[:, col : col + HD] = rope(norm(raw[at, local : local + HD], kg[...]), cos2, sin2).astype(BF)
        pack[:, col + HD : col + both] = raw[at, local + HD :].astype(BF)
        for h in range(local // HD):
            col = prompts * both + (lead - p) * local + h * HD
            piece = raw[at, h * HD : (h + 1) * HD]
            pack[:, col : col + HD] = rope(norm(piece, qg[...]), cos2, sin2).astype(BF)
    kvs = [pack.at[:, pl.ds(p * both, both)] for p in range(prompts)]
    mine = pack.at[:, pl.ds(prompts * both, local)]
    length = plen[lax.axis_index("seq") * prompts + lead]
    for copy in [cache_copy] + o_copies:
        copy.wait()
    attention(mine, kvs[lead], length, bias_v, s_v, w_v, mine)
    pack_out = pltpu.make_async_copy(pack, pack_h, out_sem.at[0])
    pack_out.start()
    decode_attention(
        n_seq, slots, plen, adm, clen, raw.at[pl.ds(prompts * rows, dec_rows)], local,
        kvs, cache, qg, kg, part,
    )
    part_out = pltpu.make_async_copy(part, part_h, out_sem.at[1])
    part_out.start()
    outs = [pack_out, part_out]
    for j in range(2):
        at = pl.ds(j * nb, nb)
        send[:, at] = dot(mine[...], wo_v[j]).astype(BF)
        outs.append(pltpu.make_async_copy(send.at[:, at], send_h.at[:, at], out_sem.at[2 + j]))
        outs[-1].start()
    for copy in outs:
        copy.wait()


def project(n_head, n_seq, plen, adm, clen, qg, kg, x, dec, cache, wq, wk, wv, wo):
    prompts, rows, width = x.shape
    dec_rows = dec.shape[0] * dec.shape[1]
    local = wq.shape[1]
    chunks = 8
    nb = width // n_head
    every = prompts * rows + dec_rows
    send = (rows, 2 * nb)
    pack = (rows, 2 * prompts * HD + prompts * local)
    part = (dec_rows * (local // HD) + 8, HD)
    return pl.pallas_call(
        functools.partial(project_kernel, n_head, n_seq),
        out_shape=[
            jax.ShapeDtypeStruct(send, BF),
            jax.ShapeDtypeStruct(pack, BF),
            jax.ShapeDtypeStruct(part, F32),
        ],
        in_specs=[HB] * 12,
        out_specs=[HB] * 3,
        scratch_shapes=[
            pltpu.VMEM((chunks, every, width // chunks), BF),
            pltpu.VMEM(dec.shape, BF),
            pltpu.VMEM((dec_rows, width), F32),
            pltpu.VMEM((width, 2 * HD), BF),
            pltpu.VMEM((width, local), BF),
            pltpu.VMEM((2, local, nb), BF),
            pltpu.VMEM((every, local + 2 * HD), F32),
            pltpu.VMEM(send, BF),
            pltpu.VMEM(pack, BF),
            pltpu.VMEM(part, F32),
            pltpu.VMEM(cache.shape, BF),
            pltpu.SMEM(plen.shape, jnp.int32),
            pltpu.SMEM(adm.shape, jnp.int32),
            pltpu.SMEM(clen.shape, jnp.int32),
            pltpu.VMEM(qg.shape, F32),
            pltpu.VMEM(kg.shape, F32),
            pltpu.VMEM((rows, HD), F32),
            pltpu.VMEM((rows, HD), F32),
        ]
        + attention_scratch(rows, local // HD)
        + [
            pltpu.SemaphoreType.DMA((prompts, chunks)),
            pltpu.SemaphoreType.DMA,
            pltpu.SemaphoreType.DMA((2, chunks)),
            pltpu.SemaphoreType.DMA((chunks,)),
            pltpu.SemaphoreType.DMA((2,)),
            pltpu.SemaphoreType.DMA,
            pltpu.SemaphoreType.DMA((5,)),
            pltpu.SemaphoreType.DMA((4,)),
        ],
        compiler_params=pltpu.CompilerParams(vmem_limit_bytes=LIMIT_A * MIB),
        cost_estimate=BRIEF,
        name="project",
    )(plen, adm, clen, qg, kg, x, dec, cache, wq, wk, wv, wo)


def second_kernel(n_seq, prompts, plen_h, pack_h, wo_hbm, send, own0, own1, handed, *refs):
    pack, wo_v, both_v, plen = refs[:4]
    bias_v, s_v, w_v = refs[4:7]
    pack_sem, plen_sem, wo_sem = refs[7:]
    rows = pack.shape[0]
    local, nb = wo_v.shape[1:]
    first, second = partners()
    head = lax.axis_index("head")
    pack_copy = pltpu.make_async_copy(pack_h, pack, pack_sem)
    plen_copy = pltpu.make_async_copy(plen_h, plen, plen_sem)
    copies = [
        out_copy(wo_hbm, block, nb, wo_v.at[j], wo_sem.at[j])
        for j, block in enumerate((3 - head, first, head, second))
    ]
    for copy in [plen_copy, pack_copy] + copies:
        copy.start()
    plen_copy.wait()
    pack_copy.wait()
    both = 2 * HD
    base = prompts * both
    length = plen[lax.axis_index("seq") * prompts]
    kvs = [pack.at[:, pl.ds(p * both, both)] for p in range(prompts)]
    both_v[rows:] = pack[:, base : base + local]
    queries = pack.at[:, pl.ds(base + local, local)]
    attention(queries, kvs[0], length, bias_v, s_v, w_v, both_v.at[pl.ds(0, rows)])
    each = rows // n_seq
    total = 2 * rows
    new = lax.broadcasted_iota(jnp.int32, (total, total), 0)
    old = lax.broadcasted_iota(jnp.int32, (total, total), 1)
    dest, rest = new // (2 * each), lax.rem(new, 2 * each)
    source = (rest // each) * rows + lax.rem(rest, each) * n_seq + dest
    move = jnp.where(old == source, 1.0, 0.0).astype(BF)
    handed[...] = (dot(move[:, :rows], kvs[0][...]) + dot(move[:, rows:], kvs[1][...])).astype(BF)
    for j in range(2):
        copies[j].wait()
        send[:, j * nb : (j + 1) * nb] = dot(both_v[:rows], wo_v[j]).astype(BF)
    for j in range(2):
        copies[2 + j].wait()
        mixed = dot(both_v[...], wo_v[2 + j]).astype(BF)
        own0[:, j * nb : (j + 1) * nb] = mixed[:rows]
        own1[:, j * nb : (j + 1) * nb] = mixed[rows:]


def second(n_head, n_seq, prompts, plen, pack, wo):
    rows = pack.shape[0]
    local, width = wo.shape
    nb = width // n_head
    return pl.pallas_call(
        functools.partial(second_kernel, n_seq, prompts),
        out_shape=[jax.ShapeDtypeStruct((rows, 2 * nb), BF)] * 3
        + [jax.ShapeDtypeStruct((prompts * rows, 2 * HD), BF)],
        in_specs=[HB] * 3,
        out_specs=[VM] * 4,
        scratch_shapes=[
            pltpu.VMEM(pack.shape, BF),
            pltpu.VMEM((4, local, nb), BF),
            pltpu.VMEM((prompts * rows, local), BF),
            pltpu.SMEM(plen.shape, jnp.int32),
        ]
        + attention_scratch(rows, local // HD)
        + [
            pltpu.SemaphoreType.DMA,
            pltpu.SemaphoreType.DMA,
            pltpu.SemaphoreType.DMA((4,)),
        ],
        compiler_params=pltpu.CompilerParams(vmem_limit_bytes=LIMIT_B * MIB),
        cost_estimate=BRIEF,
        name="second",
    )(plen, pack, wo)


def joined(bit, mine, other):
    count = mine.shape[0] - 8
    swap = lax.rem(lax.axis_index("seq") // bit, 2) == 1
    one, two = mine[...], other[...]
    low = jnp.where(swap, two, one)
    high = jnp.where(swap, one, two)
    eye = unit(count)

    def column(row):
        return jnp.sum(jnp.where(eye, row, 0.0), axis=1, keepdims=True)

    row_a, row_b = low[count : count + 1, :], high[count : count + 1, :]
    best = jnp.maximum(row_a, row_b)
    scale_a, scale_b = jnp.exp2(row_a - best), jnp.exp2(row_b - best)
    total = scale_a + scale_b
    inverse = 1.0 / total
    mixed = low[:count] * column(scale_a * inverse) + high[:count] * column(scale_b * inverse)
    return mixed, best + jnp.log2(total)


def join_kernel(bit, mine, other, *refs):
    out = refs[-1] if len(refs) == 1 else refs[2]
    count = mine.shape[0] - 8
    mixed, level = joined(bit, mine, other)
    out[:count, :] = mixed
    out[count : count + 1, :] = level
    if len(refs) > 1:
        own, got, _, on = refs
        nb = on.shape[1]
        on[...] = (own[:, nb:].astype(F32) + got[:, :nb].astype(F32)).astype(BF)


def join(bit, mine, other, own=None, got=None):
    outs = [jax.ShapeDtypeStruct(mine.shape, F32)]
    args = [mine, other]
    if own is not None:
        rows, both = got.shape
        outs.append(jax.ShapeDtypeStruct((rows, both // 2), BF))
        args += [own, got]
    out = pl.pallas_call(
        functools.partial(join_kernel, bit),
        out_shape=outs,
        in_specs=[VM] * len(args),
        out_specs=[VM] * len(outs),
        compiler_params=pltpu.CompilerParams(vmem_limit_bytes=8 * MIB),
        cost_estimate=BRIEF,
        name="join_%d" % bit,
    )(*args)
    return out if own is not None else out[0]


def pass_on_kernel(own, got, on):
    nb = on.shape[1]
    on[...] = (own[:, nb:].astype(F32) + got[:, :nb].astype(F32)).astype(BF)


def pass_on(p, own, got):
    rows, both = got.shape
    return pl.pallas_call(
        pass_on_kernel,
        out_shape=jax.ShapeDtypeStruct((rows, both // 2), BF),
        in_specs=[VM] * 2,
        out_specs=VM,
        compiler_params=pltpu.CompilerParams(vmem_limit_bytes=8 * MIB),
        cost_estimate=BRIEF,
        name="pass_on_%d" % p,
    )(own, got)


def decode_out_kernel(bit, mine, other, wo_hbm, *refs):
    outs, (wo_v, sems) = refs[:4], refs[4:]
    count = mine.shape[0] - 8
    rows, nb = outs[0].shape
    first, second = partners()
    head = lax.axis_index("head")
    copies = [
        out_copy(wo_hbm, block, nb, wo_v.at[j], sems.at[j])
        for j, block in enumerate((3 - head, first, second, head))
    ]
    for copy in copies:
        copy.start()
    mixed, _ = joined(bit, mine, other)
    mixed = mixed.astype(BF)
    flat = jnp.concatenate([mixed[i * rows : (i + 1) * rows] for i in range(count // rows)], axis=1)
    for j, out in enumerate(outs):
        copies[j].wait()
        out[...] = dot(flat, wo_v[j]).astype(BF)


def decode_project(bit, n_head, dec_rows, mine, other, wo):
    local, width = wo.shape
    nb = width // n_head
    return pl.pallas_call(
        functools.partial(decode_out_kernel, bit),
        out_shape=[jax.ShapeDtypeStruct((dec_rows, nb), BF)] * 4,
        in_specs=[VM, VM, HB],
        out_specs=[VM] * 4,
        scratch_shapes=[pltpu.VMEM((4, local, nb), BF), pltpu.SemaphoreType.DMA((4,))],
        compiler_params=pltpu.CompilerParams(vmem_limit_bytes=LIMIT_C * MIB),
        cost_estimate=BRIEF,
        name="decode_project",
    )(mine, other, wo)


def sum_parts(stage, out, sems, own, got, last):
    rows, nb = last.shape
    step = rows // 2
    copies = []
    for i in range(2):
        at = pl.ds(i * step, step)
        stage[at] = (
            own[at, :nb].astype(F32) + got[at, nb:].astype(F32) + last[at].astype(F32)
        ).astype(BF)
        copies.append(pltpu.make_async_copy(stage.at[at], out.at[at], sems.at[i]))
        copies[-1].start()
    return copies


def finish_first_kernel(p, own, got, last, moved, out, handed, stage, sems):
    keep = pltpu.make_async_copy(moved, handed, sems.at[2])
    keep.start()
    for copy in sum_parts(stage, out.at[p], sems, own, got, last) + [keep]:
        copy.wait()


def finish_first(p, prompts, own, got, last, moved):
    rows, nb = last.shape
    return pl.pallas_call(
        functools.partial(finish_first_kernel, p),
        out_shape=[
            jax.ShapeDtypeStruct((prompts, rows, nb), BF),
            jax.ShapeDtypeStruct(moved.shape, BF),
        ],
        in_specs=[VM] * 4,
        out_specs=[HB] * 2,
        scratch_shapes=[pltpu.VMEM((rows, nb), BF), pltpu.SemaphoreType.DMA((3,))],
        compiler_params=pltpu.CompilerParams(vmem_limit_bytes=8 * MIB),
        cost_estimate=BRIEF,
        name="finish_%d" % p,
    )(own, got, last, moved)


def finish_last_kernel(p, slots, own, got, last, mine, *refs):
    others, (_, out, dec_out, stage, sems) = refs[:-5], refs[-5:]
    copies = sum_parts(stage, out.at[p], sems, own, got, last)
    total = mine[...].astype(F32)
    for other in others:
        total = total + other[...].astype(F32)
    for t in range(dec_out.shape[0]):
        dec_out[t] = total[t * slots : (t + 1) * slots].astype(BF)
    for copy in copies:
        copy.wait()


def finish_last(p, steps, slots, own, got, last, pieces, partial):
    rows, nb = last.shape
    return pl.pallas_call(
        functools.partial(finish_last_kernel, p, slots),
        out_shape=[
            jax.ShapeDtypeStruct(partial.shape, BF),
            jax.ShapeDtypeStruct((steps, slots, nb), BF),
        ],
        in_specs=[VM] * (3 + len(pieces)) + [HB],
        out_specs=[HB, VM],
        scratch_shapes=[pltpu.VMEM((rows, nb), BF), pltpu.SemaphoreType.DMA((2,))],
        input_output_aliases={3 + len(pieces): 0},
        compiler_params=pltpu.CompilerParams(vmem_limit_bytes=8 * MIB),
        cost_estimate=BRIEF,
        name="finish_%d" % p,
    )(own, got, last, *pieces, partial)


def after(value, other):
    return lax.optimization_barrier((value, other))[0]


def local(
    prompts, prompt_len, admitted, cache_len, cache_kv, dec_tokens, w_query, w_key, w_value, w_out, q_gain, k_gain
):
    n_seq = lax.axis_size("seq")
    n_head = lax.axis_size("head")
    pr_dev, rows, width = prompts.shape
    steps, slots, _ = dec_tokens.shape
    dec_rows = steps * slots
    each = rows // n_seq
    qg, kg = q_gain.reshape(1, HD), k_gain.reshape(1, HD)
    def head_move(value, masks):
        pairs = [
            (h * n_seq + s, (h ^ masks[s % 2]) * n_seq + s)
            for h in range(n_head)
            for s in range(n_seq)
        ]
        return lax.ppermute(value, ("head", "seq"), pairs)

    def seq_move(value, bit):
        return lax.ppermute(value, "seq", [(i, i ^ bit) for i in range(n_seq)])

    bits = []
    while 2 ** len(bits) < n_seq:
        bits.append(2 ** len(bits))
    bits = bits[::-1]

    send1, pack, part = project(
        n_head, n_seq, prompt_len, admitted, cache_len, qg, kg, prompts, dec_tokens, cache_kv[0],
        w_query, w_key, w_value, w_out,
    )
    got1 = head_move(send1, (1, 2))
    other = seq_move(part, bits[0])
    send0, own0, own1, handed = second(n_head, n_seq, pr_dev, prompt_len, pack, w_out)
    other, send0 = lax.optimization_barrier((other, send0))
    got0 = head_move(send0, (1, 2))
    for i, bit in enumerate(bits[:-2]):
        part = join(bit, part, other)
        other = seq_move(part, bits[i + 1])
    sending = handed.reshape(n_seq, pr_dev * each, 2 * HD)
    moved = lax.all_to_all(after(sending, part), "seq", split_axis=0, concat_axis=0, tiled=True)
    part, on1 = join(bits[-2], part, after(other, moved), own1, got1)
    other = seq_move(part, bits[-1])
    last1 = head_move(on1, (2, 1))
    on0 = pass_on(0, own0, after(got0, on1))
    last0 = head_move(on0, (2, 1))
    pieces = decode_project(bits[-1], n_head, dec_rows, part, after(other, on0), w_out)
    pieces = [
        pieces[3],
        head_move(pieces[0], (3, 3)),
        head_move(pieces[1], (1, 2)),
        head_move(pieces[2], (2, 1)),
    ]
    moved = moved.reshape(1, pr_dev * n_seq, each, 2 * HD)
    partial, handed_out = finish_first(1, pr_dev, own1, got1, last1, moved)
    prefill_out, decode_out = finish_last(0, steps, slots, own0, got0, last0, pieces, partial)
    return (prefill_out, handed_out, decode_out)


def solution(mesh):
    placed = (
        P("seq", None, None),
        P(),
        P(),
        P(),
        P("head", None, "seq", None),
        P(),
        P(None, "head"),
        P(None, "head"),
        P(None, "head"),
        P("head", None),
        P(),
        P(),
    )
    return jax.shard_map(
        local,
        mesh=mesh,
        in_specs=placed,
        out_specs=(P("seq", None, "head"), P("head", None, "seq", None), P(None, None, "head")),
        check_vma=False,
    )
```

```python
import functools

import jax
import jax.numpy as jnp
import numpy as np
from jax import lax
from jax.experimental import pallas as pl
from jax.experimental.pallas import tpu as pltpu
from jax.sharding import PartitionSpec as P

HD = 128
EPS = 1e-06
THETA = 1000000.0
NEG = -1e30
LOG2E = 1.4426950408889634
SCALE = HD**-0.5
C2 = SCALE * LOG2E
BF = jnp.bfloat16
F32 = jnp.float32
HB = pl.BlockSpec(memory_space=pltpu.HBM)
VM = pl.BlockSpec(memory_space=pltpu.VMEM)
BRIEF = pl.CostEstimate(flops=1, bytes_accessed=1, transcendentals=0)
MIB = 1024 * 1024
LIMIT_A = 60
LIMIT_B = 36
LIMIT_C = 16


def frequencies():
    half = HD // 2
    freq = np.float32(THETA) ** (-np.arange(half, dtype=np.float32) / np.float32(half))
    return freq.astype(np.float32)


def turns(places):
    lane = lax.broadcasted_iota(jnp.int32, places.shape, 1)
    freq = jnp.zeros(places.shape, F32)
    spot = lax.rem(lane, HD // 2)
    for i, value in enumerate(frequencies()):
        freq = jnp.where(spot == i, float(value), freq)
    return freq


def cos_sin(places, freq):
    angle = places.astype(F32) * freq
    lane = lax.broadcasted_iota(jnp.int32, places.shape, 1)
    return jnp.cos(angle), jnp.where(lane < HD // 2, -1.0, 1.0) * jnp.sin(angle)


def dot(a, b):
    return jnp.dot(a, b, preferred_element_type=F32)


def dot_nt(a, b):
    return lax.dot_general(a, b, (((1,), (1,)), ((), ())), preferred_element_type=F32)


def norm(values, gain):
    square = jnp.mean(values * values, axis=-1, keepdims=True)
    return values * lax.rsqrt(square + EPS) * gain


def rope(values, cos2, sin2):
    return values * cos2 + pltpu.roll(values, HD // 2, 1) * sin2


def effective_lengths(plen, adm, clen, slots):
    out = []
    for r in range(slots):
        taken = adm[r]
        out.append(jnp.where(taken >= 0, plen[jnp.maximum(taken, 0)], clen[r]))
    return out


def by_slot(index, values):
    result = jnp.full(index.shape, values[0])
    for r in range(1, len(values)):
        result = jnp.where(index == r, values[r], result)
    return result


def partners():
    head, seq = lax.axis_index("head"), lax.axis_index("seq")
    flip_x = head + 1 - 2 * lax.rem(head, 2)
    flip_y = lax.rem(head + 2, 4)
    even = lax.rem(seq, 2) == 0
    return jnp.where(even, flip_x, flip_y), jnp.where(even, flip_y, flip_x)


def out_copy(wo_hbm, block, nb, dest, sem):
    return pltpu.make_async_copy(
        wo_hbm.at[:, pl.ds(pl.multiple_of(block * nb, nb), nb)], dest, sem
    )


def mask_bias(rows, length):
    row_at = lax.broadcasted_iota(jnp.int32, (rows, rows), 0)
    col_at = lax.broadcasted_iota(jnp.int32, (rows, rows), 1)
    return jnp.where((col_at <= row_at) & (col_at < length), 0.0, NEG).astype(F32)


def attention(heads, queries, kv, bias_v, s_v, w_v, attn):
    rows = kv.shape[0]
    half = rows // 2
    quarter = rows // 4
    for h in heads:
        at = slice(h * HD, (h + 1) * HD)
        s_v[h, :half, :half] = dot_nt(queries[:half, at], kv[:half, :HD])
        s_v[h, half:, :] = dot_nt(queries[half:, at], kv[:, :HD])
    for h in heads:
        for block in range(4):
            at = slice(block * quarter, (block + 1) * quarter)
            keys = half if block < 2 else rows
            scores = s_v[h, at, :keys] + bias_v[at, :keys]
            top = jnp.max(scores, axis=-1, keepdims=True)
            expo = jnp.exp2((scores - top) * C2)
            total = jnp.sum(expo, axis=-1, keepdims=True)
            w_v[h, at, :keys] = (expo * (1.0 / total)).astype(BF)
    for h in heads:
        at = slice(h * HD, (h + 1) * HD)
        attn[:half, at] = dot(w_v[h, :half, :half], kv[:half, HD:]).astype(BF)
        attn[half:, at] = dot(w_v[h, half:, :], kv[:, HD:]).astype(BF)


def attention_scratch(rows, heads):
    return [
        pltpu.VMEM((rows, rows), F32),
        pltpu.VMEM((heads, rows, rows), F32),
        pltpu.VMEM((heads, rows, rows), BF),
    ]


def unit(count):
    return lax.broadcasted_iota(jnp.int32, (count, count), 0) == lax.broadcasted_iota(
        jnp.int32, (count, count), 1
    )


def decode_attention(n_seq, slots, plen, adm, clen, raw, raw_kv, kvs, cache, qg, kg, part):
    seq = lax.axis_index("seq")
    dec_rows = raw.shape[0]
    width = cache.shape[1]
    rows = kvs[0].shape[0]
    eff = effective_lengths(plen, adm, clen, slots)
    row = lax.broadcasted_iota(jnp.int32, (dec_rows, HD), 0)
    places = by_slot(lax.rem(row, slots), eff) + row // slots
    cos2, sin2 = cos_sin(places, turns(row))
    new_key = rope(norm(raw_kv[:, :HD], kg[...]), cos2, sin2).astype(BF)
    new_value = raw_kv[:, HD:].astype(BF)
    queries = jnp.concatenate(
        [
            rope(norm(raw[:, h * HD : (h + 1) * HD], qg[...]), cos2, sin2).astype(BF)
            for h in range(raw.shape[1] // HD)
        ],
        axis=0,
    )
    count = queries.shape[0]

    row = lax.rem(lax.broadcasted_iota(jnp.int32, (count, 1), 0), dec_rows)
    slot, step = lax.rem(row, slots), row // slots
    taken = by_slot(slot, [adm[r] for r in range(slots)])
    scores, masks, values = [], [], []
    at = lax.broadcasted_iota(jnp.int32, (1, width), 1) * n_seq + seq
    for r in range(slots):
        limit = jnp.where(adm[r] >= 0, 0, clen[r])
        masks.append((slot == r) & (at < limit))
        scores.append(dot_nt(queries, cache[r, :, :HD]))
        values.append(cache[r, :, HD:])
    spot = lax.broadcasted_iota(jnp.int32, (1, rows), 1)
    for p, kv in enumerate(kvs):
        prompt = seq * len(kvs) + p
        masks.append((taken == prompt) & (spot < plen[prompt]))
        scores.append(dot_nt(queries, kv[:, :HD]))
        values.append(kv[:, HD:])
    other = lax.broadcasted_iota(jnp.int32, (1, dec_rows), 1)
    first = jnp.where(seq == 0, 1, 0)
    masks.append(
        (lax.rem(other, slots) == slot) & (other // slots <= step) & (first + 0 * other > 0)
    )
    scores.append(dot_nt(queries, new_key))
    values.append(new_value)

    top = jnp.full((count, 1), NEG, F32)
    scores = [jnp.where(mask, score, NEG) for mask, score in zip(masks, scores)]
    for score in scores:
        top = jnp.maximum(top, jnp.max(score, axis=-1, keepdims=True))
    total = jnp.zeros((count, 1), F32)
    acc = jnp.zeros((count, HD), F32)
    for mask, score, value in zip(masks, scores, values):
        expo = jnp.where(mask, jnp.exp2((score - top) * C2), 0.0)
        total = total + jnp.sum(expo, axis=-1, keepdims=True)
        acc = acc + dot(expo.astype(BF), value)
    some = total > 0.0
    safe = jnp.where(some, total, 1.0)
    part[:count, :] = acc * (1.0 / safe)
    level = jnp.where(some, top * C2 + jnp.log2(safe), NEG)
    part[count : count + 1, :] = jnp.sum(jnp.where(unit(count), level, 0.0), axis=0, keepdims=True)


def project_kernel(n_head, n_seq, *refs):
    plen_h, adm_h, clen_h, qg_h, kg_h, x_hbm, dec_hbm, cache_h, wq_hbm, wk_hbm, wv_hbm, wo_hbm = refs[:12]
    send_h, pack_h, part_h, blocks_h, leave_h = refs[12:17]
    x_v, dec_v, flat_v, wkv_v, wq_v, wo_v, raw, raw_kv, send, pack, part, blocks = refs[17:29]
    cache, plen, adm, clen, qg, kg, cos_v, sin_v = refs[29:37]
    bias_v, s_v, w_v = refs[37:40]
    x_sem, dec_sem, wkv_sem, wq_sem, wo_sem, cache_sem, small_sem, out_sem = refs[40:]
    prompts, rows, width = x_hbm.shape
    steps, slots, _ = dec_hbm.shape
    dec_rows = steps * slots
    local = wq_v.shape[1]
    nb = width // n_head
    lead = prompts - 1
    seq = lax.axis_index("seq")
    first, _ = partners()
    diag = 3 - lax.axis_index("head")
    front = rows + dec_rows
    starts = [0, rows + dec_rows]

    cuts = cut_points(width)
    queue = []
    for c in range(len(cuts) - 1):
        at = pl.ds(cuts[c], cuts[c + 1] - cuts[c])
        queue.append(
            [
                pltpu.make_async_copy(
                    x_hbm.at[lead, :, at], x_v.at[pl.ds(0, rows), at], x_sem.at[0, c]
                ),
                pltpu.make_async_copy(
                    x_hbm.at[0, :, at], x_v.at[pl.ds(front, rows), at], x_sem.at[1, c]
                ),
                pltpu.make_async_copy(wk_hbm.at[at], wkv_v.at[at, pl.ds(0, HD)], wkv_sem.at[0, c]),
                pltpu.make_async_copy(wv_hbm.at[at], wkv_v.at[at, pl.ds(HD, HD)], wkv_sem.at[1, c]),
                pltpu.make_async_copy(wq_hbm.at[at], wq_v.at[at], wq_sem.at[c]),
            ]
        )
    small = [
        pltpu.make_async_copy(src, dst, small_sem.at[i])
        for i, (src, dst) in enumerate(
            [(plen_h, plen), (adm_h, adm), (clen_h, clen), (qg_h, qg), (kg_h, kg)]
        )
    ]
    dec_copy = pltpu.make_async_copy(dec_hbm, dec_v, dec_sem)
    cache_copy = pltpu.make_async_copy(cache_h, cache, cache_sem)
    o_copies = [
        out_copy(wo_hbm, block, nb, wo_v.at[j], wo_sem.at[j]) for j, block in enumerate((diag, first))
    ]
    ahead = 3
    queue += [[cache_copy]] + [[copy] for copy in o_copies]
    for copy in [dec_copy] + queue[0] + small:
        copy.start()
    for group in queue[1:ahead]:
        for copy in group:
            copy.start()
    row = lax.broadcasted_iota(jnp.int32, (rows, HD), 0)
    freq = turns(lax.broadcasted_iota(jnp.int32, (1, HD), 0))
    cos_v[...], sin_v[...] = cos_sin(row, freq)
    for copy in small:
        copy.wait()
    bias_v[...] = mask_bias(rows, plen[seq * prompts + lead])
    dec_copy.wait()
    for t in range(steps):
        flat_v[t * slots : (t + 1) * slots, :] = dec_v[t].astype(F32)
    x_v[rows:front, :] = flat_v[...].astype(BF)
    for c in range(len(cuts) - 1):
        for copy in queue[c]:
            copy.wait()
        if c + ahead < len(queue):
            for copy in queue[c + ahead]:
                copy.start()
        at = slice(cuts[c], cuts[c + 1])
        kv_part = dot(x_v[:, at], wkv_v[at, :])
        q_part = dot(x_v[:front, at], wq_v[at, :])
        if c == 0:
            raw_kv[...] = kv_part
            raw[...] = q_part
        else:
            raw_kv[...] += kv_part
            raw[...] += q_part
    for group in queue[len(cuts) - 1 + ahead :]:
        for copy in group:
            copy.start()

    cos2, sin2 = cos_v[...], sin_v[...]
    both = 2 * HD
    kvs = [pack.at[:, pl.ds(p * both, both)] for p in range(prompts)]
    for p, start in ((lead, 0), (0, front)):
        at = slice(start, start + rows)
        kvs[p][:, :HD] = rope(norm(raw_kv[at, :HD], kg[...]), cos2, sin2).astype(BF)
        kvs[p][:, HD:] = raw_kv[at, HD:].astype(BF)
    for copy in [cache_copy] + o_copies:
        copy.wait()
    each = rows // n_seq
    new = lax.broadcasted_iota(jnp.int32, (rows, rows), 0)
    old = lax.broadcasted_iota(jnp.int32, (rows, rows), 1)
    move = jnp.where(old == lax.rem(new, each) * n_seq + new // each, 1.0, 0.0).astype(BF)
    for p, kv in enumerate(kvs):
        moved = dot(move, kv[...]).astype(BF)
        for d in range(n_seq):
            blocks[d, p * each : (p + 1) * each] = moved[d * each : (d + 1) * each]
    half = n_seq // 2
    away = (1 - seq // half) * half
    outs = [
        pltpu.make_async_copy(blocks, blocks_h, out_sem.at[0]),
        pltpu.make_async_copy(blocks.at[pl.ds(away, half)], leave_h, out_sem.at[1]),
    ]
    for copy in outs:
        copy.start()
    base = prompts * both
    mine = pack.at[:, pl.ds(base, local)]
    pair = 2 * HD
    for j in range(local // pair):
        later = dot(x_v[front:, :], wq_v[:, j * pair : (j + 1) * pair])
        for h in (2 * j, 2 * j + 1):
            piece = raw[:rows, h * HD : (h + 1) * HD]
            mine[:, h * HD : (h + 1) * HD] = rope(norm(piece, qg[...]), cos2, sin2).astype(BF)
        attention((2 * j, 2 * j + 1), mine, kvs[lead], bias_v, s_v, w_v, mine)
        for i in range(2):
            col = base + local + (2 * j + i) * HD
            piece = later[:, i * HD : (i + 1) * HD]
            pack[:, col : col + HD] = rope(norm(piece, qg[...]), cos2, sin2).astype(BF)
    outs.append(pltpu.make_async_copy(pack, pack_h, out_sem.at[2]))
    outs[-1].start()
    decode_attention(
        n_seq, slots, plen, adm, clen, raw.at[pl.ds(rows, dec_rows)],
        raw_kv.at[pl.ds(rows, dec_rows)], kvs, cache, qg, kg, part,
    )
    outs.append(pltpu.make_async_copy(part, part_h, out_sem.at[3]))
    outs[-1].start()
    for j in range(2):
        at = pl.ds(j * nb, nb)
        send[:, at] = dot(mine[...], wo_v[j]).astype(BF)
        outs.append(pltpu.make_async_copy(send.at[:, at], send_h.at[:, at], out_sem.at[4 + j]))
        outs[-1].start()
    for copy in outs:
        copy.wait()


def cut_points(width):
    step = width // 8
    return [0, step, 2 * step, 4 * step, 6 * step, 8 * step]


def project(n_head, n_seq, plen, adm, clen, qg, kg, x, dec, cache, wq, wk, wv, wo):
    prompts, rows, width = x.shape
    dec_rows = dec.shape[0] * dec.shape[1]
    local = wq.shape[1]
    nb = width // n_head
    every = prompts * rows + dec_rows
    send = (rows, 2 * nb)
    pack = (rows, 2 * prompts * HD + prompts * local)
    part = (dec_rows * (local // HD) + 8, HD)
    blocks = (n_seq, prompts * rows // n_seq, 2 * HD)
    chunks = len(cut_points(width)) - 1
    return pl.pallas_call(
        functools.partial(project_kernel, n_head, n_seq),
        out_shape=[
            jax.ShapeDtypeStruct(send, BF),
            jax.ShapeDtypeStruct(pack, BF),
            jax.ShapeDtypeStruct(part, F32),
            jax.ShapeDtypeStruct(blocks, BF),
            jax.ShapeDtypeStruct((n_seq // 2,) + blocks[1:], BF),
        ],
        in_specs=[HB] * 12,
        out_specs=[HB] * 5,
        scratch_shapes=[
            pltpu.VMEM((every, width), BF),
            pltpu.VMEM(dec.shape, BF),
            pltpu.VMEM((dec_rows, width), F32),
            pltpu.VMEM((width, 2 * HD), BF),
            pltpu.VMEM((width, local), BF),
            pltpu.VMEM((2, local, nb), BF),
            pltpu.VMEM((rows + dec_rows, local), F32),
            pltpu.VMEM((every, 2 * HD), F32),
            pltpu.VMEM(send, BF),
            pltpu.VMEM(pack, BF),
            pltpu.VMEM(part, F32),
            pltpu.VMEM(blocks, BF),
            pltpu.VMEM(cache.shape, BF),
            pltpu.SMEM(plen.shape, jnp.int32),
            pltpu.SMEM(adm.shape, jnp.int32),
            pltpu.SMEM(clen.shape, jnp.int32),
            pltpu.VMEM(qg.shape, F32),
            pltpu.VMEM(kg.shape, F32),
            pltpu.VMEM((rows, HD), F32),
            pltpu.VMEM((rows, HD), F32),
        ]
        + attention_scratch(rows, local // HD)
        + [
            pltpu.SemaphoreType.DMA((2, chunks)),
            pltpu.SemaphoreType.DMA,
            pltpu.SemaphoreType.DMA((2, chunks)),
            pltpu.SemaphoreType.DMA((chunks,)),
            pltpu.SemaphoreType.DMA((2,)),
            pltpu.SemaphoreType.DMA,
            pltpu.SemaphoreType.DMA((5,)),
            pltpu.SemaphoreType.DMA((6,)),
        ],
        compiler_params=pltpu.CompilerParams(vmem_limit_bytes=LIMIT_A * MIB),
        cost_estimate=BRIEF,
        name="project",
    )(plen, adm, clen, qg, kg, x, dec, cache, wq, wk, wv, wo)


def second_kernel(prompts, plen_h, pack_h, wo_hbm, send, own0, own1, wo_a, wo_b, *refs):
    pack, attn, plen = refs[:3]
    bias_v, s_v, w_v = refs[3:6]
    pack_sem, small_sem, wo_sem = refs[6:]
    rows = pack.shape[0]
    local, nb = wo_a.shape[1:]
    first, second = partners()
    head = lax.axis_index("head")
    wo_v = [wo_a.at[0], wo_a.at[1], wo_b.at[0], wo_b.at[1]]
    pack_copy = pltpu.make_async_copy(pack_h, pack, pack_sem)
    plen_copy = pltpu.make_async_copy(plen_h, plen, small_sem)
    copies = [
        out_copy(wo_hbm, block, nb, wo_v[j], wo_sem.at[j])
        for j, block in enumerate((head, second, 3 - head, first))
    ]
    for copy in [plen_copy, pack_copy] + copies:
        copy.start()
    plen_copy.wait()
    bias_v[...] = mask_bias(rows, plen[lax.axis_index("seq") * prompts])
    pack_copy.wait()
    both = 2 * HD
    base = prompts * both
    kv = pack.at[:, pl.ds(0, both)]
    other = pack.at[:, pl.ds(base, local)]
    queries = pack.at[:, pl.ds(base + local, local)]
    hb = nb // 2
    for j in range(local // both):
        if j in (1, 2):
            copies[j - 1].wait()
            for i in range(2):
                at = slice(i * hb, (i + 1) * hb)
                to = slice((j - 1) * nb + i * hb, (j - 1) * nb + (i + 1) * hb)
                own1[:, to] = dot(other[...], wo_v[j - 1][:, at]).astype(BF)
        attention((2 * j, 2 * j + 1), queries, kv, bias_v, s_v, w_v, attn)
    for copy in copies[2:]:
        copy.wait()
    for j in range(2):
        send[:, j * nb : (j + 1) * nb] = dot(attn[...], wo_v[2 + j][...]).astype(BF)
    for j in range(2):
        own0[:, j * nb : (j + 1) * nb] = dot(attn[...], wo_v[j][...]).astype(BF)


def second(n_head, prompts, plen, pack, wo):
    rows = pack.shape[0]
    local, width = wo.shape
    nb = width // n_head
    return pl.pallas_call(
        functools.partial(second_kernel, prompts),
        out_shape=[jax.ShapeDtypeStruct((rows, 2 * nb), BF)] * 3
        + [jax.ShapeDtypeStruct((2, local, nb), BF)] * 2,
        in_specs=[HB] * 3,
        out_specs=[VM] * 5,
        scratch_shapes=[
            pltpu.VMEM(pack.shape, BF),
            pltpu.VMEM((rows, local), BF),
            pltpu.SMEM(plen.shape, jnp.int32),
        ]
        + attention_scratch(rows, local // HD)
        + [
            pltpu.SemaphoreType.DMA,
            pltpu.SemaphoreType.DMA,
            pltpu.SemaphoreType.DMA((4,)),
        ],
        compiler_params=pltpu.CompilerParams(vmem_limit_bytes=LIMIT_B * MIB),
        cost_estimate=BRIEF,
        name="second",
    )(plen, pack, wo)


def joined(bit, mine, other):
    count = mine.shape[0] - 8
    swap = lax.rem(lax.axis_index("seq") // bit, 2) == 1
    one, two = mine[...], other[...]
    low = jnp.where(swap, two, one)
    high = jnp.where(swap, one, two)
    eye = unit(count)

    def column(row):
        return jnp.sum(jnp.where(eye, row, 0.0), axis=1, keepdims=True)

    row_a, row_b = low[count : count + 1, :], high[count : count + 1, :]
    best = jnp.maximum(row_a, row_b)
    scale_a, scale_b = jnp.exp2(row_a - best), jnp.exp2(row_b - best)
    total = scale_a + scale_b
    inverse = 1.0 / total
    mixed = low[:count] * column(scale_a * inverse) + high[:count] * column(scale_b * inverse)
    return mixed, best + jnp.log2(total)


def range_start(seq, size):
    return seq // size * size


def join_kernel(bit, mine, other, *refs):
    held, (out, leave) = refs[:-2], refs[-2:]
    count = mine.shape[0] - 8
    mixed, level = joined(bit, mine, other)
    out[:count, :] = mixed
    out[count : count + 1, :] = level
    seq = lax.axis_index("seq")
    size = bit // 2
    target = range_start(seq, bit) + size * (1 - lax.rem(seq // size, 2))
    at = 0
    for array in held:
        sources, dests = array.shape[:2]
        skip = target - range_start(seq, dests)
        for k in range(sources):
            leave[at] = array[k, pl.ds(skip, size)]
            at += 1


def join(bit, mine, other, held):
    sources = sum(array.shape[0] for array in held)
    return pl.pallas_call(
        functools.partial(join_kernel, bit),
        out_shape=[
            jax.ShapeDtypeStruct(mine.shape, F32),
            jax.ShapeDtypeStruct((sources, bit // 2) + held[0].shape[2:], BF),
        ],
        in_specs=[VM] * (2 + len(held)),
        out_specs=[VM] * 2,
        compiler_params=pltpu.CompilerParams(vmem_limit_bytes=8 * MIB),
        cost_estimate=BRIEF,
        name="join_%d" % bit,
    )(mine, other, *held)


def pass_on_kernel(own, got, on):
    nb = on.shape[1]
    on[...] = (own[:, nb:].astype(F32) + got[:, :nb].astype(F32)).astype(BF)


def pass_on(p, own, got):
    rows, both = got.shape
    return pl.pallas_call(
        pass_on_kernel,
        out_shape=jax.ShapeDtypeStruct((rows, both // 2), BF),
        in_specs=[VM] * 2,
        out_specs=VM,
        compiler_params=pltpu.CompilerParams(vmem_limit_bytes=8 * MIB),
        cost_estimate=BRIEF,
        name="pass_on_%d" % p,
    )(own, got)


def decode_out_kernel(bit, mine, other, wo_a, wo_b, *outs):
    count = mine.shape[0] - 8
    rows = outs[0].shape[0]
    mixed, _ = joined(bit, mine, other)
    mixed = mixed.astype(BF)
    flat = jnp.concatenate([mixed[i * rows : (i + 1) * rows] for i in range(count // rows)], axis=1)
    for j, out in enumerate(outs):
        out[...] = dot(flat, (wo_a, wo_b)[j // 2][j % 2]).astype(BF)


def decode_project(bit, dec_rows, mine, other, wo_a, wo_b):
    nb = wo_a.shape[2]
    return pl.pallas_call(
        functools.partial(decode_out_kernel, bit),
        out_shape=[jax.ShapeDtypeStruct((dec_rows, nb), BF)] * 4,
        in_specs=[VM] * 4,
        out_specs=[VM] * 4,
        compiler_params=pltpu.CompilerParams(vmem_limit_bytes=LIMIT_C * MIB),
        cost_estimate=BRIEF,
        name="decode_project",
    )(mine, other, wo_a, wo_b)


def sum_parts(stage, out, sems, own, got, last):
    rows, nb = last.shape
    step = rows // 2
    copies = []
    for i in range(2):
        at = pl.ds(i * step, step)
        stage[at] = (
            own[at, :nb].astype(F32) + got[at, nb:].astype(F32) + last[at].astype(F32)
        ).astype(BF)
        copies.append(pltpu.make_async_copy(stage.at[at], out.at[at], sems.at[i]))
        copies[-1].start()
    return copies


def finish_first_kernel(p, bits, own, got, last, *refs):
    held, (out, handed, stage, sems, keep_sem) = refs[: len(bits) + 1], refs[len(bits) + 1 :]
    seq = lax.axis_index("seq")
    copies = []
    sources = [0]
    for j, array in enumerate(held):
        if j:
            sources = sources + [bits[j - 1] ^ source for source in sources]
        for k in range(array.shape[0]):
            source = seq ^ sources[len(copies)]
            copies.append(
                pltpu.make_async_copy(
                    array.at[k, seq - range_start(seq, array.shape[1])],
                    handed.at[source],
                    keep_sem.at[len(copies)],
                )
            )
            copies[-1].start()
    for copy in sum_parts(stage, out.at[p], sems, own, got, last) + copies:
        copy.wait()


def finish_first(p, prompts, bits, own, got, last, held):
    rows, nb = last.shape
    n_seq = held[0].shape[1]
    return pl.pallas_call(
        functools.partial(finish_first_kernel, p, bits),
        out_shape=[
            jax.ShapeDtypeStruct((prompts, rows, nb), BF),
            jax.ShapeDtypeStruct((n_seq,) + held[0].shape[2:], BF),
        ],
        in_specs=[VM] * (3 + len(held)),
        out_specs=[HB] * 2,
        scratch_shapes=[
            pltpu.VMEM((rows, nb), BF),
            pltpu.SemaphoreType.DMA((2,)),
            pltpu.SemaphoreType.DMA((n_seq,)),
        ],
        compiler_params=pltpu.CompilerParams(vmem_limit_bytes=8 * MIB),
        cost_estimate=BRIEF,
        name="finish_%d" % p,
    )(own, got, last, *held)


def finish_last_kernel(p, slots, own, got, last, mine, *refs):
    others, (_, out, dec_out, stage, sems) = refs[:-5], refs[-5:]
    copies = sum_parts(stage, out.at[p], sems, own, got, last)
    total = mine[...].astype(F32)
    for other in others:
        total = total + other[...].astype(F32)
    for t in range(dec_out.shape[0]):
        dec_out[t] = total[t * slots : (t + 1) * slots].astype(BF)
    for copy in copies:
        copy.wait()


def finish_last(p, steps, slots, own, got, last, pieces, partial):
    rows, nb = last.shape
    return pl.pallas_call(
        functools.partial(finish_last_kernel, p, slots),
        out_shape=[
            jax.ShapeDtypeStruct(partial.shape, BF),
            jax.ShapeDtypeStruct((steps, slots, nb), BF),
        ],
        in_specs=[VM] * (3 + len(pieces)) + [HB],
        out_specs=[HB, VM],
        scratch_shapes=[pltpu.VMEM((rows, nb), BF), pltpu.SemaphoreType.DMA((2,))],
        input_output_aliases={3 + len(pieces): 0},
        compiler_params=pltpu.CompilerParams(vmem_limit_bytes=8 * MIB),
        cost_estimate=BRIEF,
        name="finish_%d" % p,
    )(own, got, last, *pieces, partial)


def after(value, other):
    return lax.optimization_barrier((value, other))[0]


def local(
    prompts, prompt_len, admitted, cache_len, cache_kv, dec_tokens, w_query, w_key, w_value, w_out, q_gain, k_gain
):
    n_seq = lax.axis_size("seq")
    n_head = lax.axis_size("head")
    pr_dev, rows, width = prompts.shape
    steps, slots, _ = dec_tokens.shape
    dec_rows = steps * slots
    each = rows // n_seq
    qg, kg = q_gain.reshape(1, HD), k_gain.reshape(1, HD)
    def head_move(value, masks):
        pairs = [
            (h * n_seq + s, (h ^ masks[s % 2]) * n_seq + s)
            for h in range(n_head)
            for s in range(n_seq)
        ]
        return lax.ppermute(value, ("head", "seq"), pairs)

    def seq_move(value, bit):
        return lax.ppermute(value, "seq", [(i, i ^ bit) for i in range(n_seq)])

    bits = []
    while 2 ** len(bits) < n_seq:
        bits.append(2 ** len(bits))
    bits = bits[::-1]

    send1, pack, part, blocks, leave = project(
        n_head, n_seq, prompt_len, admitted, cache_len, qg, kg, prompts, dec_tokens, cache_kv[0],
        w_query, w_key, w_value, w_out,
    )
    got1 = head_move(send1, (1, 2))
    other = seq_move(part, bits[0])
    arrived = seq_move(leave, bits[0])
    send0, own0, own1, *wo = second(n_head, pr_dev, prompt_len, pack, w_out)
    other, arrived, send0 = lax.optimization_barrier((other, arrived, send0))
    got0 = head_move(send0, (1, 2))
    held = [blocks[None], arrived[None]]
    for i, bit in enumerate(bits[:-1]):
        part, leave = join(bit, part, other, held)
        other = seq_move(part, bits[i + 1])
        held.append(seq_move(leave, bits[i + 1]))
    on1 = pass_on(1, own1, after(got1, part))
    last1 = head_move(on1, (2, 1))
    pieces = decode_project(bits[-1], dec_rows, part, after(other, on1), *wo)
    on0 = pass_on(0, own0, after(got0, pieces[0]))
    last0 = head_move(on0, (2, 1))
    pieces = [
        pieces[0],
        head_move(pieces[1], (2, 1)),
        head_move(pieces[2], (3, 3)),
        head_move(pieces[3], (1, 2)),
    ]
    partial, handed = finish_first(1, pr_dev, bits, own1, got1, after(last1, on0), held)
    handed_out = handed.reshape(1, pr_dev * n_seq, each, 2 * HD)
    prefill_out, decode_out = finish_last(0, steps, slots, own0, got0, last0, pieces, partial)
    return (prefill_out, handed_out, decode_out)


def solution(mesh):
    placed = (
        P("seq", None, None),
        P(),
        P(),
        P(),
        P("head", None, "seq", None),
        P(),
        P(None, "head"),
        P(None, "head"),
        P(None, "head"),
        P("head", None),
        P(),
        P(),
    )
    return jax.shard_map(
        local,
        mesh=mesh,
        in_specs=placed,
        out_specs=(P("seq", None, "head"), P("head", None, "seq", None), P(None, None, "head")),
        check_vma=False,
    )
```

```python
import functools

import jax
import jax.numpy as jnp
import numpy as np
from jax import lax
from jax.experimental import pallas as pl
from jax.experimental.pallas import tpu as pltpu
from jax.sharding import PartitionSpec as P

HD = 128
EPS = 1e-06
THETA = 1000000.0
NEG = -1e30
LOG2E = 1.4426950408889634
SCALE = HD**-0.5
C2 = SCALE * LOG2E
BF = jnp.bfloat16
F32 = jnp.float32
HB = pl.BlockSpec(memory_space=pltpu.HBM)
VM = pl.BlockSpec(memory_space=pltpu.VMEM)
BRIEF = pl.CostEstimate(flops=1, bytes_accessed=1, transcendentals=0)
MIB = 1024 * 1024
LIMIT_A = 60
LIMIT_B = 36
LIMIT_C = 16


def frequencies():
    half = HD // 2
    freq = np.float32(THETA) ** (-np.arange(half, dtype=np.float32) / np.float32(half))
    return freq.astype(np.float32)


def turns(places):
    lane = lax.broadcasted_iota(jnp.int32, places.shape, 1)
    freq = jnp.zeros(places.shape, F32)
    spot = lax.rem(lane, HD // 2)
    for i, value in enumerate(frequencies()):
        freq = jnp.where(spot == i, float(value), freq)
    return freq


def cos_sin(places, freq):
    angle = places.astype(F32) * freq
    lane = lax.broadcasted_iota(jnp.int32, places.shape, 1)
    return jnp.cos(angle), jnp.where(lane < HD // 2, -1.0, 1.0) * jnp.sin(angle)


def dot(a, b):
    return jnp.dot(a, b, preferred_element_type=F32)


def dot_nt(a, b):
    return lax.dot_general(a, b, (((1,), (1,)), ((), ())), preferred_element_type=F32)


def norm(values, gain):
    square = jnp.mean(values * values, axis=-1, keepdims=True)
    return values * lax.rsqrt(square + EPS) * gain


def rope(values, cos2, sin2):
    return values * cos2 + pltpu.roll(values, HD // 2, 1) * sin2


def effective_lengths(plen, adm, clen, slots):
    out = []
    for r in range(slots):
        taken = adm[r]
        out.append(jnp.where(taken >= 0, plen[jnp.maximum(taken, 0)], clen[r]))
    return out


def by_slot(index, values):
    result = jnp.full(index.shape, values[0])
    for r in range(1, len(values)):
        result = jnp.where(index == r, values[r], result)
    return result


def partners():
    head, seq = lax.axis_index("head"), lax.axis_index("seq")
    flip_x = head + 1 - 2 * lax.rem(head, 2)
    flip_y = lax.rem(head + 2, 4)
    even = lax.rem(seq, 2) == 0
    return jnp.where(even, flip_x, flip_y), jnp.where(even, flip_y, flip_x)


def out_copy(wo_hbm, block, nb, dest, sem):
    return pltpu.make_async_copy(
        wo_hbm.at[:, pl.ds(pl.multiple_of(block * nb, nb), nb)], dest, sem
    )


def mask_bias(rows, length):
    row_at = lax.broadcasted_iota(jnp.int32, (rows, rows), 0)
    col_at = lax.broadcasted_iota(jnp.int32, (rows, rows), 1)
    return jnp.where((col_at <= row_at) & (col_at < length), 0.0, NEG).astype(F32)


def attention(heads, queries, kv, bias_v, s_v, w_v, attn):
    rows = kv.shape[0]
    half = rows // 2
    quarter = rows // 4
    for h in heads:
        at = slice(h * HD, (h + 1) * HD)
        s_v[h, :half, :half] = dot_nt(queries[:half, at], kv[:half, :HD])
        s_v[h, half:, :] = dot_nt(queries[half:, at], kv[:, :HD])
    for h in heads:
        for block in range(4):
            at = slice(block * quarter, (block + 1) * quarter)
            keys = half if block < 2 else rows
            scores = s_v[h, at, :keys] + bias_v[at, :keys]
            top = jnp.max(scores, axis=-1, keepdims=True)
            expo = jnp.exp2((scores - top) * C2)
            total = jnp.sum(expo, axis=-1, keepdims=True)
            w_v[h, at, :keys] = (expo * (1.0 / total)).astype(BF)
    for h in heads:
        at = slice(h * HD, (h + 1) * HD)
        attn[:half, at] = dot(w_v[h, :half, :half], kv[:half, HD:]).astype(BF)
        attn[half:, at] = dot(w_v[h, half:, :], kv[:, HD:]).astype(BF)


def attention_scratch(rows, heads):
    return [
        pltpu.VMEM((rows, rows), F32),
        pltpu.VMEM((heads, rows, rows), F32),
        pltpu.VMEM((heads, rows, rows), BF),
    ]


def unit(count):
    return lax.broadcasted_iota(jnp.int32, (count, count), 0) == lax.broadcasted_iota(
        jnp.int32, (count, count), 1
    )


def decode_attention(n_seq, slots, plen, adm, clen, raw, raw_kv, kvs, cache, qg, kg, part):
    seq = lax.axis_index("seq")
    dec_rows = raw.shape[1]
    width = cache.shape[1]
    rows = kvs[0].shape[0]
    eff = effective_lengths(plen, adm, clen, slots)
    row = lax.broadcasted_iota(jnp.int32, (dec_rows, HD), 0)
    places = by_slot(lax.rem(row, slots), eff) + row // slots
    cos2, sin2 = cos_sin(places, turns(row))
    new_key = rope(norm(raw_kv[:, :HD], kg[...]), cos2, sin2).astype(BF)
    new_value = raw_kv[:, HD:].astype(BF)
    queries = jnp.concatenate(
        [
            rope(norm(raw[j, :, i * HD : (i + 1) * HD], qg[...]), cos2, sin2).astype(BF)
            for j in range(raw.shape[0])
            for i in range(2)
        ],
        axis=0,
    )
    count = queries.shape[0]

    row = lax.rem(lax.broadcasted_iota(jnp.int32, (count, 1), 0), dec_rows)
    slot, step = lax.rem(row, slots), row // slots
    taken = by_slot(slot, [adm[r] for r in range(slots)])
    scores, masks, values = [], [], []
    at = lax.broadcasted_iota(jnp.int32, (1, width), 1) * n_seq + seq
    for r in range(slots):
        limit = jnp.where(adm[r] >= 0, 0, clen[r])
        masks.append((slot == r) & (at < limit))
        scores.append(dot_nt(queries, cache[r, :, :HD]))
        values.append(cache[r, :, HD:])
    spot = lax.broadcasted_iota(jnp.int32, (1, rows), 1)
    for p, kv in enumerate(kvs):
        prompt = seq * len(kvs) + p
        masks.append((taken == prompt) & (spot < plen[prompt]))
        scores.append(dot_nt(queries, kv[:, :HD]))
        values.append(kv[:, HD:])
    other = lax.broadcasted_iota(jnp.int32, (1, dec_rows), 1)
    first = jnp.where(seq == 0, 1, 0)
    masks.append(
        (lax.rem(other, slots) == slot) & (other // slots <= step) & (first + 0 * other > 0)
    )
    scores.append(dot_nt(queries, new_key))
    values.append(new_value)

    top = jnp.full((count, 1), NEG, F32)
    scores = [jnp.where(mask, score, NEG) for mask, score in zip(masks, scores)]
    for score in scores:
        top = jnp.maximum(top, jnp.max(score, axis=-1, keepdims=True))
    total = jnp.zeros((count, 1), F32)
    acc = jnp.zeros((count, HD), F32)
    for mask, score, value in zip(masks, scores, values):
        expo = jnp.where(mask, jnp.exp2((score - top) * C2), 0.0)
        total = total + jnp.sum(expo, axis=-1, keepdims=True)
        acc = acc + dot(expo.astype(BF), value)
    some = total > 0.0
    safe = jnp.where(some, total, 1.0)
    part[:count, :] = acc * (1.0 / safe)
    level = jnp.where(some, top * C2 + jnp.log2(safe), NEG)
    part[count : count + 1, :] = jnp.sum(jnp.where(unit(count), level, 0.0), axis=0, keepdims=True)


def prompt_kernel(which, n_head, n_seq, with_dec, *refs):
    it = iter(refs)
    take = lambda count: [next(it) for _ in range(count)]
    plen_h, qg_h, kg_h, x_hbm, wq_hbm, wk_hbm, wv_hbm, wo_hbm = take(8)
    if with_dec:
        adm_h, clen_h, dec_hbm, cache_h, pack1_h = take(5)
    send_h, pack_h = take(2)
    part_h = next(it) if with_dec else None
    x_v, wkv_v, wq_v, wo_v, raw, raw_kv, send, pack, plen, qg, kg = take(11)
    bias_v, s_v, w_v = take(3)
    x_sem, wkv_sem, wq_sem, wo_sem, small_sem, out_sem = take(6)
    if with_dec:
        dec_v, flat_v, cache, kv1, part, adm, clen, dec_sem = take(8)
    prompts, rows, width = x_hbm.shape
    tiles, _, pair = wq_v.shape
    nb = width // n_head
    seq = lax.axis_index("seq")
    first, _ = partners()
    diag = 3 - lax.axis_index("head")
    half = width // 2
    every = x_v.shape[0]

    queue = []
    for c in range(2):
        at = pl.ds(c * half, half)
        queue.append(
            [
                pltpu.make_async_copy(
                    x_hbm.at[which, :, at], x_v.at[pl.ds(0, rows), at], x_sem.at[c]
                ),
                pltpu.make_async_copy(wk_hbm.at[at], wkv_v.at[at, pl.ds(0, HD)], wkv_sem.at[0, c]),
                pltpu.make_async_copy(wv_hbm.at[at], wkv_v.at[at, pl.ds(HD, HD)], wkv_sem.at[1, c]),
            ]
        )
    for j in range(tiles):
        queue.append(
            [pltpu.make_async_copy(wq_hbm.at[:, pl.ds(j * pair, pair)], wq_v.at[j], wq_sem.at[j])]
        )
    o_copies = [
        out_copy(wo_hbm, block, nb, wo_v.at[j], wo_sem.at[j]) for j, block in enumerate((diag, first))
    ]
    queue += [[copy] for copy in o_copies]
    small = [(plen_h, plen), (qg_h, qg), (kg_h, kg)]
    if with_dec:
        small += [(adm_h, adm), (clen_h, clen), (dec_hbm, dec_v)]
        late = [
            pltpu.make_async_copy(cache_h, cache, dec_sem.at[0]),
            pltpu.make_async_copy(pack1_h.at[:, pl.ds(0, 2 * HD)], kv1, dec_sem.at[1]),
        ]
        queue[-1] = queue[-1] + late
    small = [
        pltpu.make_async_copy(src, dst, small_sem.at[i]) for i, (src, dst) in enumerate(small)
    ]
    ahead = 4
    for copy in queue[0] + small:
        copy.start()
    for group in queue[1:ahead]:
        for copy in group:
            copy.start()

    def arrive(i):
        for copy in queue[i]:
            copy.wait()
        if i + ahead < len(queue):
            for copy in queue[i + ahead]:
                copy.start()

    row = lax.broadcasted_iota(jnp.int32, (rows, HD), 0)
    cos2, sin2 = cos_sin(row, turns(lax.broadcasted_iota(jnp.int32, (1, HD), 0)))
    for copy in small:
        copy.wait()
    bias_v[...] = mask_bias(rows, plen[seq * prompts + which])
    if with_dec:
        steps, slots, _ = dec_v.shape
        for t in range(steps):
            flat_v[t * slots : (t + 1) * slots, :] = dec_v[t].astype(F32)
        x_v[rows:, :] = flat_v[...].astype(BF)
    arrive(0)
    raw_kv[...] = dot(x_v[:, :half], wkv_v[:half])
    arrive(1)
    raw_kv[...] += dot(x_v[:, half:], wkv_v[half:])
    kv = pack.at[:, pl.ds(0, 2 * HD)]
    mine = pack.at[:, pl.ds(2 * HD, tiles * pair)]
    for j in range(tiles + 1):
        if j < tiles:
            arrive(2 + j)
            raw[j] = dot(x_v[...], wq_v[j])
        if j == 0:
            kv[:, :HD] = rope(norm(raw_kv[:rows, :HD], kg[...]), cos2, sin2).astype(BF)
            kv[:, HD:] = raw_kv[:rows, HD:].astype(BF)
        else:
            heads = (2 * j - 2, 2 * j - 1)
            for i, h in enumerate(heads):
                piece = raw[j - 1, :rows, i * HD : (i + 1) * HD]
                mine[:, h * HD : (h + 1) * HD] = rope(norm(piece, qg[...]), cos2, sin2).astype(BF)
            attention(heads, mine, kv, bias_v, s_v, w_v, mine)
    outs = [pltpu.make_async_copy(pack, pack_h, out_sem.at[0])]
    outs[-1].start()
    for j in range(2):
        arrive(2 + tiles + j)
    if with_dec:
        decode_attention(
            n_seq, slots, plen, adm, clen, raw.at[:, pl.ds(rows, every - rows)],
            raw_kv.at[pl.ds(rows, every - rows)], [kv, kv1], cache, qg, kg, part,
        )
        outs.append(pltpu.make_async_copy(part, part_h, out_sem.at[3]))
        outs[-1].start()
    for j in range(2):
        at = pl.ds(j * nb, nb)
        send[:, at] = dot(mine[...], wo_v[j]).astype(BF)
        outs.append(pltpu.make_async_copy(send.at[:, at], send_h.at[:, at], out_sem.at[1 + j]))
        outs[-1].start()
    for copy in outs:
        copy.wait()


def prompt_part(which, n_head, n_seq, plen, qg, kg, x, wq, wk, wv, wo, decode=()):
    prompts, rows, width = x.shape
    local = wq.shape[1]
    nb = width // n_head
    pair = 2 * HD
    tiles = local // pair
    send = (rows, 2 * nb)
    pack = (rows, pair + local)
    outs = [jax.ShapeDtypeStruct(send, BF), jax.ShapeDtypeStruct(pack, BF)]
    every = rows
    extra = []
    if decode:
        adm, clen, dec, cache, _ = decode
        dec_rows = dec.shape[0] * dec.shape[1]
        every += dec_rows
        part = (dec_rows * (local // HD) + 8, HD)
        outs.append(jax.ShapeDtypeStruct(part, F32))
        extra = [
            pltpu.VMEM(dec.shape, BF),
            pltpu.VMEM((dec_rows, width), F32),
            pltpu.VMEM(cache.shape, BF),
            pltpu.VMEM((rows, pair), BF),
            pltpu.VMEM(part, F32),
            pltpu.SMEM(adm.shape, jnp.int32),
            pltpu.SMEM(clen.shape, jnp.int32),
            pltpu.SemaphoreType.DMA((2,)),
        ]
    return pl.pallas_call(
        functools.partial(prompt_kernel, which, n_head, n_seq, bool(decode)),
        out_shape=outs,
        in_specs=[HB] * (8 + len(decode)),
        out_specs=[HB] * len(outs),
        scratch_shapes=[
            pltpu.VMEM((every, width), BF),
            pltpu.VMEM((width, pair), BF),
            pltpu.VMEM((tiles, width, pair), BF),
            pltpu.VMEM((2, local, nb), BF),
            pltpu.VMEM((tiles, every, pair), F32),
            pltpu.VMEM((every, pair), F32),
            pltpu.VMEM(send, BF),
            pltpu.VMEM(pack, BF),
            pltpu.SMEM(plen.shape, jnp.int32),
            pltpu.VMEM(qg.shape, F32),
            pltpu.VMEM(kg.shape, F32),
        ]
        + attention_scratch(rows, local // HD)
        + [
            pltpu.SemaphoreType.DMA((2,)),
            pltpu.SemaphoreType.DMA((2, 2)),
            pltpu.SemaphoreType.DMA((tiles,)),
            pltpu.SemaphoreType.DMA((2,)),
            pltpu.SemaphoreType.DMA((6,)),
            pltpu.SemaphoreType.DMA((4,)),
        ]
        + extra,
        compiler_params=pltpu.CompilerParams(vmem_limit_bytes=LIMIT_A * MIB),
        cost_estimate=BRIEF,
        name="prompt_%d" % which,
    )(plen, qg, kg, x, wq, wk, wv, wo, *decode)


def third_kernel(n_seq, pack0_h, pack1_h, wo_hbm, own0, own1, blocks, leave, wo_a, wo_b, packs, pack_sem, wo_sem):
    _, rows, _ = packs.shape
    _, local, nb = wo_a.shape
    first, second = partners()
    head, seq = lax.axis_index("head"), lax.axis_index("seq")
    wo_v = [wo_a.at[0], wo_a.at[1], wo_b.at[0], wo_b.at[1]]
    pack_copies = [
        pltpu.make_async_copy(src, packs.at[p], pack_sem.at[p])
        for p, src in enumerate((pack0_h, pack1_h))
    ]
    copies = [
        out_copy(wo_hbm, block, nb, wo_v[j], wo_sem.at[j])
        for j, block in enumerate((head, second, 3 - head, first))
    ]
    for copy in pack_copies + copies:
        copy.start()
    each = rows // n_seq
    new = lax.broadcasted_iota(jnp.int32, (rows, rows), 0)
    old = lax.broadcasted_iota(jnp.int32, (rows, rows), 1)
    move = jnp.where(old == lax.rem(new, each) * n_seq + new // each, 1.0, 0.0).astype(BF)
    both = 2 * HD
    for copy in pack_copies:
        copy.wait()
    for p in range(2):
        moved = dot(move, packs[p, :, :both]).astype(BF)
        for d in range(n_seq):
            blocks[d, p * each : (p + 1) * each] = moved[d * each : (d + 1) * each]
    half = n_seq // 2
    leave[...] = blocks[pl.ds((1 - seq // half) * half, half)]
    mine = packs[:, :, both:].reshape(2 * rows, local)
    for j in range(2):
        copies[j].wait()
        mixed = dot(mine, wo_v[j][...]).astype(BF)
        own0[:, j * nb : (j + 1) * nb] = mixed[:rows]
        own1[:, j * nb : (j + 1) * nb] = mixed[rows:]
    for copy in copies[2:]:
        copy.wait()


def third(n_head, n_seq, pack0, pack1, wo):
    rows = pack0.shape[0]
    local, width = wo.shape
    nb = width // n_head
    blocks = (n_seq, 2 * rows // n_seq, 2 * HD)
    return pl.pallas_call(
        functools.partial(third_kernel, n_seq),
        out_shape=[jax.ShapeDtypeStruct((rows, 2 * nb), BF)] * 2
        + [
            jax.ShapeDtypeStruct(blocks, BF),
            jax.ShapeDtypeStruct((n_seq // 2,) + blocks[1:], BF),
        ]
        + [jax.ShapeDtypeStruct((2, local, nb), BF)] * 2,
        in_specs=[HB] * 3,
        out_specs=[VM] * 6,
        scratch_shapes=[
            pltpu.VMEM((2,) + pack0.shape, BF),
            pltpu.SemaphoreType.DMA((2,)),
            pltpu.SemaphoreType.DMA((4,)),
        ],
        compiler_params=pltpu.CompilerParams(vmem_limit_bytes=LIMIT_B * MIB),
        cost_estimate=BRIEF,
        name="third",
    )(pack0, pack1, wo)


def joined(bit, mine, other):
    count = mine.shape[0] - 8
    swap = lax.rem(lax.axis_index("seq") // bit, 2) == 1
    one, two = mine[...], other[...]
    low = jnp.where(swap, two, one)
    high = jnp.where(swap, one, two)
    eye = unit(count)

    def column(row):
        return jnp.sum(jnp.where(eye, row, 0.0), axis=1, keepdims=True)

    row_a, row_b = low[count : count + 1, :], high[count : count + 1, :]
    best = jnp.maximum(row_a, row_b)
    scale_a, scale_b = jnp.exp2(row_a - best), jnp.exp2(row_b - best)
    total = scale_a + scale_b
    inverse = 1.0 / total
    mixed = low[:count] * column(scale_a * inverse) + high[:count] * column(scale_b * inverse)
    return mixed, best + jnp.log2(total)


def range_start(seq, size):
    return seq // size * size


def range_start(seq, size):
    return seq // size * size


def join_kernel(bit, mine, other, out):
    count = mine.shape[0] - 8
    mixed, level = joined(bit, mine, other)
    out[:count, :] = mixed
    out[count : count + 1, :] = level


def join(bit, mine, other):
    return pl.pallas_call(
        functools.partial(join_kernel, bit),
        out_shape=jax.ShapeDtypeStruct(mine.shape, F32),
        in_specs=[VM] * 2,
        out_specs=VM,
        compiler_params=pltpu.CompilerParams(vmem_limit_bytes=8 * MIB),
        cost_estimate=BRIEF,
        name="join_%d" % bit,
    )(mine, other)


def hop_kernel(bit, *refs):
    held, leave = refs[:-1], refs[-1]
    seq = lax.axis_index("seq")
    size = bit // 2
    target = range_start(seq, bit) + size * (1 - lax.rem(seq // size, 2))
    at = 0
    for array in held:
        sources, dests = array.shape[:2]
        skip = target - range_start(seq, dests)
        for k in range(sources):
            leave[at] = array[k, pl.ds(skip, size)]
            at += 1


def hop(bit, held):
    sources = sum(array.shape[0] for array in held)
    return pl.pallas_call(
        functools.partial(hop_kernel, bit),
        out_shape=jax.ShapeDtypeStruct((sources, bit // 2) + held[0].shape[2:], BF),
        in_specs=[VM] * len(held),
        out_specs=VM,
        compiler_params=pltpu.CompilerParams(vmem_limit_bytes=8 * MIB),
        cost_estimate=BRIEF,
        name="hop_%d" % bit,
    )(*held)


def pass_on_kernel(own, got, on):
    nb = on.shape[1]
    on[...] = (own[:, nb:].astype(F32) + got[:, :nb].astype(F32)).astype(BF)


def pass_on(p, own, got):
    rows, both = got.shape
    return pl.pallas_call(
        pass_on_kernel,
        out_shape=jax.ShapeDtypeStruct((rows, both // 2), BF),
        in_specs=[VM] * 2,
        out_specs=VM,
        compiler_params=pltpu.CompilerParams(vmem_limit_bytes=8 * MIB),
        cost_estimate=BRIEF,
        name="pass_on_%d" % p,
    )(own, got)


def decode_out_kernel(bit, mine, other, wo_a, wo_b, *outs):
    count = mine.shape[0] - 8
    rows = outs[0].shape[0]
    mixed, _ = joined(bit, mine, other)
    mixed = mixed.astype(BF)
    flat = jnp.concatenate([mixed[i * rows : (i + 1) * rows] for i in range(count // rows)], axis=1)
    for j, out in enumerate(outs):
        out[...] = dot(flat, (wo_a, wo_b)[j // 2][j % 2]).astype(BF)


def decode_project(bit, dec_rows, mine, other, wo_a, wo_b):
    nb = wo_a.shape[2]
    return pl.pallas_call(
        functools.partial(decode_out_kernel, bit),
        out_shape=[jax.ShapeDtypeStruct((dec_rows, nb), BF)] * 4,
        in_specs=[VM] * 4,
        out_specs=[VM] * 4,
        compiler_params=pltpu.CompilerParams(vmem_limit_bytes=LIMIT_C * MIB),
        cost_estimate=BRIEF,
        name="decode_project",
    )(mine, other, wo_a, wo_b)


def sum_parts(stage, out, sems, own, got, last):
    rows, nb = last.shape
    step = rows // 2
    copies = []
    for i in range(2):
        at = pl.ds(i * step, step)
        stage[at] = (
            own[at, :nb].astype(F32) + got[at, nb:].astype(F32) + last[at].astype(F32)
        ).astype(BF)
        copies.append(pltpu.make_async_copy(stage.at[at], out.at[at], sems.at[i]))
        copies[-1].start()
    return copies


def finish_first_kernel(p, slots, own, got, last, *refs):
    pieces, (out, dec_out, stage, sems) = refs[:-4], refs[-4:]
    copies = sum_parts(stage, out.at[p], sems, own, got, last)
    total = pieces[0][...].astype(F32)
    for piece in pieces[1:]:
        total = total + piece[...].astype(F32)
    for t in range(dec_out.shape[0]):
        dec_out[t] = total[t * slots : (t + 1) * slots].astype(BF)
    for copy in copies:
        copy.wait()


def finish_first(p, prompts, steps, slots, own, got, last, pieces):
    rows, nb = last.shape
    return pl.pallas_call(
        functools.partial(finish_first_kernel, p, slots),
        out_shape=[
            jax.ShapeDtypeStruct((prompts, rows, nb), BF),
            jax.ShapeDtypeStruct((steps, slots, nb), BF),
        ],
        in_specs=[VM] * (3 + len(pieces)),
        out_specs=[HB, VM],
        scratch_shapes=[pltpu.VMEM((rows, nb), BF), pltpu.SemaphoreType.DMA((2,))],
        compiler_params=pltpu.CompilerParams(vmem_limit_bytes=8 * MIB),
        cost_estimate=BRIEF,
        name="finish_%d" % p,
    )(own, got, last, *pieces)


def finish_last_kernel(p, bits, own, got, last, *refs):
    held, (_, out, handed, stage, sems, keep_sem) = refs[: len(bits) + 1], refs[len(bits) + 1 :]
    seq = lax.axis_index("seq")
    copies = []
    sources = [0]
    for j, array in enumerate(held):
        if j:
            sources = sources + [bits[j - 1] ^ source for source in sources]
        for k in range(array.shape[0]):
            source = seq ^ sources[len(copies)]
            copies.append(
                pltpu.make_async_copy(
                    array.at[k, seq - range_start(seq, array.shape[1])],
                    handed.at[source],
                    keep_sem.at[len(copies)],
                )
            )
            copies[-1].start()
    for copy in sum_parts(stage, out.at[p], sems, own, got, last) + copies:
        copy.wait()


def finish_last(p, bits, own, got, last, held, partial):
    rows, nb = last.shape
    n_seq = held[0].shape[1]
    return pl.pallas_call(
        functools.partial(finish_last_kernel, p, bits),
        out_shape=[
            jax.ShapeDtypeStruct(partial.shape, BF),
            jax.ShapeDtypeStruct((n_seq,) + held[0].shape[2:], BF),
        ],
        in_specs=[VM] * (3 + len(held)) + [HB],
        out_specs=[HB] * 2,
        scratch_shapes=[
            pltpu.VMEM((rows, nb), BF),
            pltpu.SemaphoreType.DMA((2,)),
            pltpu.SemaphoreType.DMA((n_seq,)),
        ],
        input_output_aliases={3 + len(held): 0},
        compiler_params=pltpu.CompilerParams(vmem_limit_bytes=8 * MIB),
        cost_estimate=BRIEF,
        name="finish_%d" % p,
    )(own, got, last, *held, partial)


def after(value, other):
    return lax.optimization_barrier((value, other))[0]


def local(
    prompts, prompt_len, admitted, cache_len, cache_kv, dec_tokens, w_query, w_key, w_value, w_out, q_gain, k_gain
):
    n_seq = lax.axis_size("seq")
    n_head = lax.axis_size("head")
    pr_dev, rows, width = prompts.shape
    steps, slots, _ = dec_tokens.shape
    dec_rows = steps * slots
    each = rows // n_seq
    qg, kg = q_gain.reshape(1, HD), k_gain.reshape(1, HD)
    def head_move(value, masks):
        pairs = [
            (h * n_seq + s, (h ^ masks[s % 2]) * n_seq + s)
            for h in range(n_head)
            for s in range(n_seq)
        ]
        return lax.ppermute(value, ("head", "seq"), pairs)

    def seq_move(value, bit):
        return lax.ppermute(value, "seq", [(i, i ^ bit) for i in range(n_seq)])

    bits = []
    while 2 ** len(bits) < n_seq:
        bits.append(2 ** len(bits))
    bits = bits[::-1]

    common = (prompt_len, qg, kg, prompts, w_query, w_key, w_value, w_out)
    send1, pack1 = prompt_part(1, n_head, n_seq, *common)
    got1 = head_move(send1, (1, 2))
    send0, pack0, part = prompt_part(
        0, n_head, n_seq, *common, decode=(admitted, cache_len, dec_tokens, cache_kv[0], pack1)
    )
    got0 = head_move(send0, (1, 2))
    other = seq_move(part, bits[0])
    own0, own1, blocks, leave, *wo = third(n_head, n_seq, pack0, pack1, w_out)
    other = after(other, leave)
    for i, bit in enumerate(bits[:-1]):
        part = join(bit, part, other)
        other = seq_move(part, bits[i + 1])
    held = [blocks[None], seq_move(leave, bits[0])[None]]
    on1 = pass_on(1, own1, lax.optimization_barrier((got1, other, held[1]))[0])
    last1 = head_move(on1, (2, 1))
    on0 = pass_on(0, own0, after(got0, on1))
    last0 = head_move(on0, (2, 1))
    leave = hop(bits[0], held)
    pieces = decode_project(bits[-1], dec_rows, part, after(after(other, on0), leave), *wo)
    pieces = [
        pieces[0],
        head_move(pieces[1], (2, 1)),
        head_move(pieces[2], (3, 3)),
        head_move(pieces[3], (1, 2)),
    ]
    held.append(after(seq_move(leave, bits[1]), pieces[0]))
    for i, bit in enumerate(bits[1:-1]):
        held.append(seq_move(hop(bit, held), bits[i + 2]))
    partial, decode_out = finish_first(1, pr_dev, steps, slots, own1, got1, last1, pieces)
    prefill_out, handed = finish_last(0, bits, own0, got0, last0, held, partial)
    return (prefill_out, handed.reshape(1, pr_dev * n_seq, each, 2 * HD), decode_out)


def solution(mesh):
    placed = (
        P("seq", None, None),
        P(),
        P(),
        P(),
        P("head", None, "seq", None),
        P(),
        P(None, "head"),
        P(None, "head"),
        P(None, "head"),
        P("head", None),
        P(),
        P(),
    )
    return jax.shard_map(
        local,
        mesh=mesh,
        in_specs=placed,
        out_specs=(P("seq", None, "head"), P("head", None, "seq", None), P(None, None, "head")),
        check_vma=False,
    )
```

```python
import functools

import jax
import jax.numpy as jnp
import numpy as np
from jax import lax
from jax.experimental import pallas as pl
from jax.experimental.pallas import tpu as pltpu
from jax.sharding import PartitionSpec as P

HD = 128
EPS = 1e-06
THETA = 1000000.0
NEG = -1e30
LOG2E = 1.4426950408889634
SCALE = HD**-0.5
C2 = SCALE * LOG2E
BF = jnp.bfloat16
F32 = jnp.float32
HB = pl.BlockSpec(memory_space=pltpu.HBM)
VM = pl.BlockSpec(memory_space=pltpu.VMEM)
BRIEF = pl.CostEstimate(flops=1, bytes_accessed=1, transcendentals=0)
MIB = 1024 * 1024
LIMIT_A = 60
LIMIT_B = 36
LIMIT_C = 16


def frequencies():
    half = HD // 2
    freq = np.float32(THETA) ** (-np.arange(half, dtype=np.float32) / np.float32(half))
    return freq.astype(np.float32)


def turns(places):
    lane = lax.broadcasted_iota(jnp.int32, places.shape, 1)
    freq = jnp.zeros(places.shape, F32)
    spot = lax.rem(lane, HD // 2)
    for i, value in enumerate(frequencies()):
        freq = jnp.where(spot == i, float(value), freq)
    return freq


def cos_sin(places, freq):
    angle = places.astype(F32) * freq
    lane = lax.broadcasted_iota(jnp.int32, places.shape, 1)
    return jnp.cos(angle), jnp.where(lane < HD // 2, -1.0, 1.0) * jnp.sin(angle)


def prompt_table(length):
    angle = np.arange(length, dtype=np.float32)[:, None] * frequencies()[None, :]
    cosine, sine = np.cos(angle), np.sin(angle)
    return np.concatenate([cosine, cosine, -sine, sine], axis=1).astype(np.float32)


def dot(a, b):
    return jnp.dot(a, b, preferred_element_type=F32)


def dot_nt(a, b):
    return lax.dot_general(a, b, (((1,), (1,)), ((), ())), preferred_element_type=F32)


def norm(values, gain):
    square = jnp.mean(values * values, axis=-1, keepdims=True)
    return values * lax.rsqrt(square + EPS) * gain


def rope(values, cos2, sin2):
    return values * cos2 + pltpu.roll(values, HD // 2, 1) * sin2


def effective_lengths(plen, adm, clen, slots):
    out = []
    for r in range(slots):
        taken = adm[r]
        out.append(jnp.where(taken >= 0, plen[jnp.maximum(taken, 0)], clen[r]))
    return out


def by_slot(index, values):
    result = jnp.full(index.shape, values[0])
    for r in range(1, len(values)):
        result = jnp.where(index == r, values[r], result)
    return result


def partners():
    head, seq = lax.axis_index("head"), lax.axis_index("seq")
    flip_x = head + 1 - 2 * lax.rem(head, 2)
    flip_y = lax.rem(head + 2, 4)
    even = lax.rem(seq, 2) == 0
    return jnp.where(even, flip_x, flip_y), jnp.where(even, flip_y, flip_x)


def out_copy(wo_hbm, block, nb, dest, sem):
    return pltpu.make_async_copy(
        wo_hbm.at[:, pl.ds(pl.multiple_of(block * nb, nb), nb)], dest, sem
    )


def mask_bias(rows, length):
    row_at = lax.broadcasted_iota(jnp.int32, (rows, rows), 0)
    col_at = lax.broadcasted_iota(jnp.int32, (rows, rows), 1)
    return jnp.where((col_at <= row_at) & (col_at < length), 0.0, NEG).astype(F32)


def attention(heads, queries, kv, bias_v, s_v, w_v, attn):
    rows = kv.shape[0]
    half = rows // 2
    quarter = rows // 4
    for h in heads:
        at = slice(h * HD, (h + 1) * HD)
        s_v[h, :half, :half] = dot_nt(queries[:half, at], kv[:half, :HD])
        s_v[h, half:, :] = dot_nt(queries[half:, at], kv[:, :HD])
    for h in heads:
        for block in range(4):
            at = slice(block * quarter, (block + 1) * quarter)
            keys = half if block < 2 else rows
            scores = s_v[h, at, :keys] + bias_v[at, :keys]
            top = jnp.max(scores, axis=-1, keepdims=True)
            expo = jnp.exp2((scores - top) * C2)
            total = jnp.sum(expo, axis=-1, keepdims=True)
            w_v[h, at, :keys] = (expo * (1.0 / total)).astype(BF)
    for h in heads:
        at = slice(h * HD, (h + 1) * HD)
        attn[:half, at] = dot(w_v[h, :half, :half], kv[:half, HD:]).astype(BF)
        attn[half:, at] = dot(w_v[h, half:, :], kv[:, HD:]).astype(BF)


def attention_scratch(rows, heads):
    return [
        pltpu.VMEM((rows, rows), F32),
        pltpu.VMEM((heads, rows, rows), F32),
        pltpu.VMEM((heads, rows, rows), BF),
    ]


def unit(count):
    return lax.broadcasted_iota(jnp.int32, (count, count), 0) == lax.broadcasted_iota(
        jnp.int32, (count, count), 1
    )


def decode_attention(n_seq, slots, plen, adm, clen, raw, raw_kv, kvs, cache, qg, kg, part):
    seq = lax.axis_index("seq")
    dec_rows = raw.shape[0]
    width = cache.shape[1]
    rows = kvs[0].shape[0]
    eff = effective_lengths(plen, adm, clen, slots)
    row = lax.broadcasted_iota(jnp.int32, (dec_rows, HD), 0)
    places = by_slot(lax.rem(row, slots), eff) + row // slots
    cos2, sin2 = cos_sin(places, turns(row))
    new_key = rope(norm(raw_kv[:, :HD], kg[...]), cos2, sin2).astype(BF)
    new_value = raw_kv[:, HD:].astype(BF)
    queries = jnp.concatenate(
        [
            rope(norm(raw[:, h * HD : (h + 1) * HD], qg[...]), cos2, sin2).astype(BF)
            for h in range(raw.shape[1] // HD)
        ],
        axis=0,
    )
    count = queries.shape[0]

    row = lax.rem(lax.broadcasted_iota(jnp.int32, (count, 1), 0), dec_rows)
    slot, step = lax.rem(row, slots), row // slots
    taken = by_slot(slot, [adm[r] for r in range(slots)])
    scores, masks, values = [], [], []
    at = lax.broadcasted_iota(jnp.int32, (1, width), 1) * n_seq + seq
    for r in range(slots):
        limit = jnp.where(adm[r] >= 0, 0, clen[r])
        masks.append((slot == r) & (at < limit))
        scores.append(dot_nt(queries, cache[r, :, :HD]))
        values.append(cache[r, :, HD:])
    spot = lax.broadcasted_iota(jnp.int32, (1, rows), 1)
    for p, kv in enumerate(kvs):
        prompt = seq * len(kvs) + p
        masks.append((taken == prompt) & (spot < plen[prompt]))
        scores.append(dot_nt(queries, kv[:, :HD]))
        values.append(kv[:, HD:])
    other = lax.broadcasted_iota(jnp.int32, (1, dec_rows), 1)
    first = jnp.where(seq == 0, 1, 0)
    masks.append(
        (lax.rem(other, slots) == slot) & (other // slots <= step) & (first + 0 * other > 0)
    )
    scores.append(dot_nt(queries, new_key))
    values.append(new_value)

    top = jnp.full((count, 1), NEG, F32)
    scores = [jnp.where(mask, score, NEG) for mask, score in zip(masks, scores)]
    for score in scores:
        top = jnp.maximum(top, jnp.max(score, axis=-1, keepdims=True))
    total = jnp.zeros((count, 1), F32)
    acc = jnp.zeros((count, HD), F32)
    for mask, score, value in zip(masks, scores, values):
        expo = jnp.where(mask, jnp.exp2((score - top) * C2), 0.0)
        total = total + jnp.sum(expo, axis=-1, keepdims=True)
        acc = acc + dot(expo.astype(BF), value)
    some = total > 0.0
    safe = jnp.where(some, total, 1.0)
    part[:count, :] = acc * (1.0 / safe)
    level = jnp.where(some, top * C2 + jnp.log2(safe), NEG)
    part[count : count + 1, :] = jnp.sum(jnp.where(unit(count), level, 0.0), axis=0, keepdims=True)


def cut_points(width):
    step = width // 8
    return [0, step, 2 * step, 4 * step, 6 * step, 8 * step]


def prompt_kernel(which, n_head, n_seq, with_dec, *refs):
    it = iter(refs)
    take = lambda count: [next(it) for _ in range(count)]
    plen_h, qg_h, kg_h, table_h, x_hbm, wq_hbm, wk_hbm, wv_hbm, wo_hbm = take(9)
    if with_dec:
        adm_h, clen_h, dec_hbm, cache_h, pack1_h = take(5)
    send_h, pack_h = take(2)
    if with_dec:
        part_h, blocks_h, leave_h = take(3)
    x_v, w_v, wo_v, raw, send, pack, plen, qg, kg, table = take(10)
    bias_v, s_v, p_v = take(3)
    x_sem, w_sem, wo_sem, small_sem, out_sem = take(5)
    if with_dec:
        dec_v, flat_v, cache, kv1, part, blocks, adm, clen, dec_sem = take(9)
    prompts, rows, width = x_hbm.shape
    local = wq_hbm.shape[1]
    nb = width // n_head
    seq = lax.axis_index("seq")
    first, _ = partners()
    diag = 3 - lax.axis_index("head")
    every = x_v.shape[0]

    cuts = cut_points(width)
    chunks = len(cuts) - 1
    queue = []
    for c in range(chunks):
        at = pl.ds(cuts[c], cuts[c + 1] - cuts[c])
        queue.append(
            [
                pltpu.make_async_copy(
                    x_hbm.at[which, :, at], x_v.at[pl.ds(0, rows), at], x_sem.at[c]
                ),
                pltpu.make_async_copy(wk_hbm.at[at], w_v.at[at, pl.ds(local, HD)], w_sem.at[0, c]),
                pltpu.make_async_copy(
                    wv_hbm.at[at], w_v.at[at, pl.ds(local + HD, HD)], w_sem.at[1, c]
                ),
                pltpu.make_async_copy(wq_hbm.at[at], w_v.at[at, pl.ds(0, local)], w_sem.at[2, c]),
            ]
        )
    o_copies = [
        out_copy(wo_hbm, block, nb, wo_v.at[j], wo_sem.at[j]) for j, block in enumerate((diag, first))
    ]
    queue += [[copy] for copy in o_copies]
    small = [(plen_h, plen), (qg_h, qg), (kg_h, kg), (table_h, table)]
    if with_dec:
        small += [(adm_h, adm), (clen_h, clen), (dec_hbm, dec_v)]
        queue[-1] = queue[-1] + [
            pltpu.make_async_copy(cache_h, cache, dec_sem.at[0]),
            pltpu.make_async_copy(pack1_h.at[:, pl.ds(0, 2 * HD)], kv1, dec_sem.at[1]),
        ]
    small = [
        pltpu.make_async_copy(src, dst, small_sem.at[i]) for i, (src, dst) in enumerate(small)
    ]
    ahead = 3
    for copy in queue[0] + small:
        copy.start()
    for group in queue[1:ahead]:
        for copy in group:
            copy.start()

    def arrive(i):
        for copy in queue[i]:
            copy.wait()
        if i + ahead < len(queue):
            for copy in queue[i + ahead]:
                copy.start()

    for copy in small:
        copy.wait()
    bias_v[...] = mask_bias(rows, plen[seq * prompts + which])
    if with_dec:
        steps, slots, _ = dec_v.shape
        for t in range(steps):
            flat_v[t * slots : (t + 1) * slots, :] = dec_v[t].astype(F32)
        x_v[rows:, :] = flat_v[...].astype(BF)
    for c in range(chunks):
        arrive(c)
        at = slice(cuts[c], cuts[c + 1])
        if c == 0:
            raw[...] = dot(x_v[:, at], w_v[at, :])
        else:
            raw[...] += dot(x_v[:, at], w_v[at, :])
    for j in range(2):
        arrive(chunks + j)

    cos2, sin2 = table[:, :HD], table[:, HD:]
    kv = pack.at[:, pl.ds(0, 2 * HD)]
    mine = pack.at[:, pl.ds(2 * HD, local)]
    kv[:, :HD] = rope(norm(raw[:rows, local : local + HD], kg[...]), cos2, sin2).astype(BF)
    kv[:, HD:] = raw[:rows, local + HD :].astype(BF)
    outs = []
    if with_dec:
        each = rows // n_seq
        new = lax.broadcasted_iota(jnp.int32, (rows, rows), 0)
        old = lax.broadcasted_iota(jnp.int32, (rows, rows), 1)
        move = jnp.where(old == lax.rem(new, each) * n_seq + new // each, 1.0, 0.0).astype(BF)
        for p, source in enumerate((kv, kv1)):
            moved = dot(move, source[...]).astype(BF)
            for d in range(n_seq):
                blocks[d, p * each : (p + 1) * each] = moved[d * each : (d + 1) * each]
        half = n_seq // 2
        away = (1 - seq // half) * half
        outs += [
            pltpu.make_async_copy(blocks, blocks_h, out_sem.at[4]),
            pltpu.make_async_copy(blocks.at[pl.ds(away, half)], leave_h, out_sem.at[5]),
        ]
        for copy in outs:
            copy.start()
    for h in range(local // HD):
        at = slice(h * HD, (h + 1) * HD)
        mine[:, at] = rope(norm(raw[:rows, at], qg[...]), cos2, sin2).astype(BF)
    attention(range(local // HD), mine, kv, bias_v, s_v, p_v, mine)
    outs.append(pltpu.make_async_copy(pack, pack_h, out_sem.at[0]))
    outs[-1].start()
    if with_dec:
        decode_attention(
            n_seq, slots, plen, adm, clen, raw.at[pl.ds(rows, every - rows), pl.ds(0, local)],
            raw.at[pl.ds(rows, every - rows), pl.ds(local, 2 * HD)], [kv, kv1], cache, qg, kg, part,
        )
        outs.append(pltpu.make_async_copy(part, part_h, out_sem.at[3]))
        outs[-1].start()
    for j in range(2):
        at = pl.ds(j * nb, nb)
        send[:, at] = dot(mine[...], wo_v[j]).astype(BF)
        outs.append(pltpu.make_async_copy(send.at[:, at], send_h.at[:, at], out_sem.at[1 + j]))
        outs[-1].start()
    for copy in outs:
        copy.wait()


def prompt_part(which, n_head, n_seq, plen, qg, kg, table, x, wq, wk, wv, wo, decode=()):
    prompts, rows, width = x.shape
    local = wq.shape[1]
    nb = width // n_head
    both = 2 * HD
    send = (rows, 2 * nb)
    pack = (rows, both + local)
    outs = [jax.ShapeDtypeStruct(send, BF), jax.ShapeDtypeStruct(pack, BF)]
    every = rows
    extra = []
    if decode:
        adm, clen, dec, cache, _ = decode
        dec_rows = dec.shape[0] * dec.shape[1]
        every += dec_rows
        part = (dec_rows * (local // HD) + 8, HD)
        blocks = (n_seq, prompts * rows // n_seq, both)
        outs += [
            jax.ShapeDtypeStruct(part, F32),
            jax.ShapeDtypeStruct(blocks, BF),
            jax.ShapeDtypeStruct((n_seq // 2,) + blocks[1:], BF),
        ]
        extra = [
            pltpu.VMEM(dec.shape, BF),
            pltpu.VMEM((dec_rows, width), F32),
            pltpu.VMEM(cache.shape, BF),
            pltpu.VMEM((rows, both), BF),
            pltpu.VMEM(part, F32),
            pltpu.VMEM(blocks, BF),
            pltpu.SMEM(adm.shape, jnp.int32),
            pltpu.SMEM(clen.shape, jnp.int32),
            pltpu.SemaphoreType.DMA((2,)),
        ]
    chunks = len(cut_points(width)) - 1
    return pl.pallas_call(
        functools.partial(prompt_kernel, which, n_head, n_seq, bool(decode)),
        out_shape=outs,
        in_specs=[HB] * (9 + len(decode)),
        out_specs=[HB] * len(outs),
        scratch_shapes=[
            pltpu.VMEM((every, width), BF),
            pltpu.VMEM((width, local + both), BF),
            pltpu.VMEM((2, local, nb), BF),
            pltpu.VMEM((every, local + both), F32),
            pltpu.VMEM(send, BF),
            pltpu.VMEM(pack, BF),
            pltpu.SMEM(plen.shape, jnp.int32),
            pltpu.VMEM(qg.shape, F32),
            pltpu.VMEM(kg.shape, F32),
            pltpu.VMEM(table.shape, F32),
        ]
        + attention_scratch(rows, local // HD)
        + [
            pltpu.SemaphoreType.DMA((chunks,)),
            pltpu.SemaphoreType.DMA((3, chunks)),
            pltpu.SemaphoreType.DMA((2,)),
            pltpu.SemaphoreType.DMA((7,)),
            pltpu.SemaphoreType.DMA((6,)),
        ]
        + extra,
        compiler_params=pltpu.CompilerParams(vmem_limit_bytes=LIMIT_A * MIB),
        cost_estimate=BRIEF,
        name="prompt_%d" % which,
    )(plen, qg, kg, table, x, wq, wk, wv, wo, *decode)


def third_kernel(pack0_h, pack1_h, wo_hbm, own0, own1, wo_a, wo_b, attns, pack_sem, wo_sem):
    _, local, nb = wo_a.shape
    rows = own0.shape[0]
    first, second = partners()
    head = lax.axis_index("head")
    wo_v = [wo_a.at[0], wo_a.at[1], wo_b.at[0], wo_b.at[1]]
    pack_copies = [
        pltpu.make_async_copy(
            src.at[:, pl.ds(2 * HD, local)], attns.at[pl.ds(p * rows, rows)], pack_sem.at[p]
        )
        for p, src in enumerate((pack0_h, pack1_h))
    ]
    copies = [
        out_copy(wo_hbm, block, nb, wo_v[j], wo_sem.at[j])
        for j, block in enumerate((head, second, 3 - head, first))
    ]
    for copy in pack_copies + copies:
        copy.start()
    for copy in pack_copies:
        copy.wait()
    for j in range(2):
        copies[j].wait()
        mixed = dot(attns[...], wo_v[j][...]).astype(BF)
        own0[:, j * nb : (j + 1) * nb] = mixed[:rows]
        own1[:, j * nb : (j + 1) * nb] = mixed[rows:]
    for copy in copies[2:]:
        copy.wait()


def third(n_head, pack0, pack1, wo):
    rows = pack0.shape[0]
    local, width = wo.shape
    nb = width // n_head
    return pl.pallas_call(
        third_kernel,
        out_shape=[jax.ShapeDtypeStruct((rows, 2 * nb), BF)] * 2
        + [jax.ShapeDtypeStruct((2, local, nb), BF)] * 2,
        in_specs=[HB] * 3,
        out_specs=[VM] * 4,
        scratch_shapes=[
            pltpu.VMEM((2 * rows, local), BF),
            pltpu.SemaphoreType.DMA((2,)),
            pltpu.SemaphoreType.DMA((4,)),
        ],
        compiler_params=pltpu.CompilerParams(vmem_limit_bytes=LIMIT_B * MIB),
        cost_estimate=BRIEF,
        name="third",
    )(pack0, pack1, wo)


def joined(bit, mine, other):
    count = mine.shape[0] - 8
    swap = lax.rem(lax.axis_index("seq") // bit, 2) == 1
    one, two = mine[...], other[...]
    low = jnp.where(swap, two, one)
    high = jnp.where(swap, one, two)
    eye = unit(count)

    def column(row):
        return jnp.sum(jnp.where(eye, row, 0.0), axis=1, keepdims=True)

    row_a, row_b = low[count : count + 1, :], high[count : count + 1, :]
    best = jnp.maximum(row_a, row_b)
    scale_a, scale_b = jnp.exp2(row_a - best), jnp.exp2(row_b - best)
    total = scale_a + scale_b
    inverse = 1.0 / total
    mixed = low[:count] * column(scale_a * inverse) + high[:count] * column(scale_b * inverse)
    return mixed, best + jnp.log2(total)


def range_start(seq, size):
    return seq // size * size


def range_start(seq, size):
    return seq // size * size


def join_kernel(bit, mine, other, out):
    count = mine.shape[0] - 8
    mixed, level = joined(bit, mine, other)
    out[:count, :] = mixed
    out[count : count + 1, :] = level


def join(bit, mine, other):
    return pl.pallas_call(
        functools.partial(join_kernel, bit),
        out_shape=jax.ShapeDtypeStruct(mine.shape, F32),
        in_specs=[VM] * 2,
        out_specs=VM,
        compiler_params=pltpu.CompilerParams(vmem_limit_bytes=8 * MIB),
        cost_estimate=BRIEF,
        name="join_%d" % bit,
    )(mine, other)


def hop_kernel(bit, *refs):
    held, leave = refs[:-1], refs[-1]
    seq = lax.axis_index("seq")
    size = bit // 2
    target = range_start(seq, bit) + size * (1 - lax.rem(seq // size, 2))
    at = 0
    for array in held:
        sources, dests = array.shape[:2]
        skip = target - range_start(seq, dests)
        for k in range(sources):
            leave[at] = array[k, pl.ds(skip, size)]
            at += 1


def hop(bit, held):
    sources = sum(array.shape[0] for array in held)
    return pl.pallas_call(
        functools.partial(hop_kernel, bit),
        out_shape=jax.ShapeDtypeStruct((sources, bit // 2) + held[0].shape[2:], BF),
        in_specs=[VM] * len(held),
        out_specs=VM,
        compiler_params=pltpu.CompilerParams(vmem_limit_bytes=8 * MIB),
        cost_estimate=BRIEF,
        name="hop_%d" % bit,
    )(*held)


def pass_on_kernel(own, got, on):
    nb = on.shape[1]
    on[...] = (own[:, nb:].astype(F32) + got[:, :nb].astype(F32)).astype(BF)


def pass_on(p, own, got):
    rows, both = got.shape
    return pl.pallas_call(
        pass_on_kernel,
        out_shape=jax.ShapeDtypeStruct((rows, both // 2), BF),
        in_specs=[VM] * 2,
        out_specs=VM,
        compiler_params=pltpu.CompilerParams(vmem_limit_bytes=8 * MIB),
        cost_estimate=BRIEF,
        name="pass_on_%d" % p,
    )(own, got)


def decode_out_kernel(bit, mine, other, wo_a, wo_b, *outs):
    count = mine.shape[0] - 8
    rows = outs[0].shape[0]
    mixed, _ = joined(bit, mine, other)
    mixed = mixed.astype(BF)
    flat = jnp.concatenate([mixed[i * rows : (i + 1) * rows] for i in range(count // rows)], axis=1)
    for j, out in enumerate(outs):
        out[...] = dot(flat, (wo_a, wo_b)[j // 2][j % 2]).astype(BF)


def decode_project(bit, dec_rows, mine, other, wo_a, wo_b):
    nb = wo_a.shape[2]
    return pl.pallas_call(
        functools.partial(decode_out_kernel, bit),
        out_shape=[jax.ShapeDtypeStruct((dec_rows, nb), BF)] * 4,
        in_specs=[VM] * 4,
        out_specs=[VM] * 4,
        compiler_params=pltpu.CompilerParams(vmem_limit_bytes=LIMIT_C * MIB),
        cost_estimate=BRIEF,
        name="decode_project",
    )(mine, other, wo_a, wo_b)


def sum_parts(stage, out, sems, own, got, last):
    rows, nb = last.shape
    step = rows // 2
    copies = []
    for i in range(2):
        at = pl.ds(i * step, step)
        stage[at] = (
            own[at, :nb].astype(F32) + got[at, nb:].astype(F32) + last[at].astype(F32)
        ).astype(BF)
        copies.append(pltpu.make_async_copy(stage.at[at], out.at[at], sems.at[i]))
        copies[-1].start()
    return copies


def finish_first_kernel(p, slots, own, got, last, *refs):
    pieces, (out, dec_out, stage, sems) = refs[:-4], refs[-4:]
    copies = sum_parts(stage, out.at[p], sems, own, got, last)
    total = pieces[0][...].astype(F32)
    for piece in pieces[1:]:
        total = total + piece[...].astype(F32)
    for t in range(dec_out.shape[0]):
        dec_out[t] = total[t * slots : (t + 1) * slots].astype(BF)
    for copy in copies:
        copy.wait()


def finish_first(p, prompts, steps, slots, own, got, last, pieces):
    rows, nb = last.shape
    return pl.pallas_call(
        functools.partial(finish_first_kernel, p, slots),
        out_shape=[
            jax.ShapeDtypeStruct((prompts, rows, nb), BF),
            jax.ShapeDtypeStruct((steps, slots, nb), BF),
        ],
        in_specs=[VM] * (3 + len(pieces)),
        out_specs=[HB, VM],
        scratch_shapes=[pltpu.VMEM((rows, nb), BF), pltpu.SemaphoreType.DMA((2,))],
        compiler_params=pltpu.CompilerParams(vmem_limit_bytes=8 * MIB),
        cost_estimate=BRIEF,
        name="finish_%d" % p,
    )(own, got, last, *pieces)


def finish_last_kernel(p, bits, own, got, last, *refs):
    held, (_, out, handed, stage, sems, keep_sem) = refs[: len(bits) + 1], refs[len(bits) + 1 :]
    seq = lax.axis_index("seq")
    copies = []
    sources = [0]
    for j, array in enumerate(held):
        if j:
            sources = sources + [bits[j - 1] ^ source for source in sources]
        for k in range(array.shape[0]):
            source = seq ^ sources[len(copies)]
            copies.append(
                pltpu.make_async_copy(
                    array.at[k, seq - range_start(seq, array.shape[1])],
                    handed.at[source],
                    keep_sem.at[len(copies)],
                )
            )
            copies[-1].start()
    for copy in sum_parts(stage, out.at[p], sems, own, got, last) + copies:
        copy.wait()


def finish_last(p, bits, own, got, last, held, partial):
    rows, nb = last.shape
    n_seq = held[0].shape[1]
    return pl.pallas_call(
        functools.partial(finish_last_kernel, p, bits),
        out_shape=[
            jax.ShapeDtypeStruct(partial.shape, BF),
            jax.ShapeDtypeStruct((n_seq,) + held[0].shape[2:], BF),
        ],
        in_specs=[VM] * (3 + len(held)) + [HB],
        out_specs=[HB] * 2,
        scratch_shapes=[
            pltpu.VMEM((rows, nb), BF),
            pltpu.SemaphoreType.DMA((2,)),
            pltpu.SemaphoreType.DMA((n_seq,)),
        ],
        input_output_aliases={3 + len(held): 0},
        compiler_params=pltpu.CompilerParams(vmem_limit_bytes=8 * MIB),
        cost_estimate=BRIEF,
        name="finish_%d" % p,
    )(own, got, last, *held, partial)


def after(value, other):
    return lax.optimization_barrier((value, other))[0]


def local(
    prompts, prompt_len, admitted, cache_len, cache_kv, dec_tokens, w_query, w_key, w_value, w_out, q_gain, k_gain
):
    n_seq = lax.axis_size("seq")
    n_head = lax.axis_size("head")
    pr_dev, rows, width = prompts.shape
    steps, slots, _ = dec_tokens.shape
    dec_rows = steps * slots
    each = rows // n_seq
    qg, kg = q_gain.reshape(1, HD), k_gain.reshape(1, HD)
    def head_move(value, masks):
        pairs = [
            (h * n_seq + s, (h ^ masks[s % 2]) * n_seq + s)
            for h in range(n_head)
            for s in range(n_seq)
        ]
        return lax.ppermute(value, ("head", "seq"), pairs)

    def seq_move(value, bit):
        return lax.ppermute(value, "seq", [(i, i ^ bit) for i in range(n_seq)])

    bits = []
    while 2 ** len(bits) < n_seq:
        bits.append(2 ** len(bits))
    bits = bits[::-1]

    table = jnp.asarray(prompt_table(rows))
    common = (prompt_len, qg, kg, table, prompts, w_query, w_key, w_value, w_out)
    send1, pack1 = prompt_part(1, n_head, n_seq, *common)
    got1 = head_move(send1, (1, 2))
    send0, pack0, part, blocks, leave = prompt_part(
        0, n_head, n_seq, *common, decode=(admitted, cache_len, dec_tokens, cache_kv[0], pack1)
    )
    got0 = head_move(send0, (1, 2))
    other = seq_move(part, bits[0])
    arrived = seq_move(leave, bits[0])
    own0, own1, *wo = third(n_head, pack0, pack1, w_out)
    other, arrived, _ = lax.optimization_barrier((other, arrived, own0))
    for i, bit in enumerate(bits[:-1]):
        part = join(bit, part, other)
        other = seq_move(part, bits[i + 1])
    held = [blocks[None], after(arrived, part)[None]]
    leave = hop(bits[0], held)
    on1 = pass_on(1, own1, after(got1, leave))
    last1 = head_move(on1, (2, 1))
    pieces = decode_project(bits[-1], dec_rows, part, after(other, on1), *wo)
    on0 = pass_on(0, own0, after(got0, pieces[0]))
    last0 = head_move(on0, (2, 1))
    pieces = [
        pieces[0],
        head_move(pieces[1], (2, 1)),
        head_move(pieces[2], (3, 3)),
        head_move(pieces[3], (1, 2)),
    ]
    held.append(lax.optimization_barrier((seq_move(leave, bits[1]), *pieces))[0])
    for i, bit in enumerate(bits[1:-1]):
        held.append(seq_move(hop(bit, held), bits[i + 2]))
    partial, decode_out = finish_first(1, pr_dev, steps, slots, own1, got1, last1, pieces)
    prefill_out, handed = finish_last(0, bits, own0, got0, last0, held, partial)
    return (prefill_out, handed.reshape(1, pr_dev * n_seq, each, 2 * HD), decode_out)


def solution(mesh):
    placed = (
        P("seq", None, None),
        P(),
        P(),
        P(),
        P("head", None, "seq", None),
        P(),
        P(None, "head"),
        P(None, "head"),
        P(None, "head"),
        P("head", None),
        P(),
        P(),
    )
    return jax.shard_map(
        local,
        mesh=mesh,
        in_specs=placed,
        out_specs=(P("seq", None, "head"), P("head", None, "seq", None), P(None, None, "head")),
        check_vma=False,
    )
```

```python
import functools

import jax
import jax.numpy as jnp
import numpy as np
from jax import lax
from jax.experimental import pallas as pl
from jax.experimental.pallas import tpu as pltpu
from jax.sharding import PartitionSpec as P

HD = 128
EPS = 1e-06
THETA = 1000000.0
NEG = -1e30
LOG2E = 1.4426950408889634
SCALE = HD**-0.5
C2 = SCALE * LOG2E
BF = jnp.bfloat16
F32 = jnp.float32
HB = pl.BlockSpec(memory_space=pltpu.HBM)
VM = pl.BlockSpec(memory_space=pltpu.VMEM)
BRIEF = pl.CostEstimate(flops=1, bytes_accessed=1, transcendentals=0)
MIB = 1024 * 1024
LIMIT_A = 60
LIMIT_B = 36
LIMIT_C = 16


def frequencies():
    half = HD // 2
    freq = np.float32(THETA) ** (-np.arange(half, dtype=np.float32) / np.float32(half))
    return freq.astype(np.float32)


def turns(places):
    lane = lax.broadcasted_iota(jnp.int32, places.shape, 1)
    freq = jnp.zeros(places.shape, F32)
    spot = lax.rem(lane, HD // 2)
    for i, value in enumerate(frequencies()):
        freq = jnp.where(spot == i, float(value), freq)
    return freq


def cos_sin(places, freq):
    angle = places.astype(F32) * freq
    lane = lax.broadcasted_iota(jnp.int32, places.shape, 1)
    return jnp.cos(angle), jnp.where(lane < HD // 2, -1.0, 1.0) * jnp.sin(angle)


def prompt_table(length):
    angle = np.arange(length, dtype=np.float32)[:, None] * frequencies()[None, :]
    cosine, sine = np.cos(angle), np.sin(angle)
    return np.concatenate([cosine, cosine, -sine, sine], axis=1).astype(np.float32)


def dot(a, b):
    return jnp.dot(a, b, preferred_element_type=F32)


def dot_nt(a, b):
    return lax.dot_general(a, b, (((1,), (1,)), ((), ())), preferred_element_type=F32)


def norm(values, gain):
    square = jnp.mean(values * values, axis=-1, keepdims=True)
    return values * lax.rsqrt(square + EPS) * gain


def rope(values, cos2, sin2):
    return values * cos2 + pltpu.roll(values, HD // 2, 1) * sin2


def effective_lengths(plen, adm, clen, slots):
    out = []
    for r in range(slots):
        taken = adm[r]
        out.append(jnp.where(taken >= 0, plen[jnp.maximum(taken, 0)], clen[r]))
    return out


def by_slot(index, values):
    result = jnp.full(index.shape, values[0])
    for r in range(1, len(values)):
        result = jnp.where(index == r, values[r], result)
    return result


def partners():
    head, seq = lax.axis_index("head"), lax.axis_index("seq")
    flip_x = head + 1 - 2 * lax.rem(head, 2)
    flip_y = lax.rem(head + 2, 4)
    even = lax.rem(seq, 2) == 0
    return jnp.where(even, flip_x, flip_y), jnp.where(even, flip_y, flip_x)


def out_copy(wo_hbm, block, nb, dest, sem):
    return pltpu.make_async_copy(
        wo_hbm.at[:, pl.ds(pl.multiple_of(block * nb, nb), nb)], dest, sem
    )


def mask_bias(rows, length):
    row_at = lax.broadcasted_iota(jnp.int32, (rows, rows), 0)
    col_at = lax.broadcasted_iota(jnp.int32, (rows, rows), 1)
    return jnp.where((col_at <= row_at) & (col_at < length), 0.0, NEG).astype(F32)


def attention(heads, queries, kv, bias_v, s_v, w_v, attn):
    rows = kv.shape[0]
    half = rows // 2
    quarter = rows // 4
    for h in heads:
        at = slice(h * HD, (h + 1) * HD)
        s_v[h, :half, :half] = dot_nt(queries[:half, at], kv[:half, :HD])
        s_v[h, half:, :] = dot_nt(queries[half:, at], kv[:, :HD])
    for h in heads:
        for block in range(4):
            at = slice(block * quarter, (block + 1) * quarter)
            keys = half if block < 2 else rows
            scores = s_v[h, at, :keys] + bias_v[at, :keys]
            top = jnp.max(scores, axis=-1, keepdims=True)
            expo = jnp.exp2((scores - top) * C2)
            total = jnp.sum(expo, axis=-1, keepdims=True)
            w_v[h, at, :keys] = (expo * (1.0 / total)).astype(BF)
    for h in heads:
        at = slice(h * HD, (h + 1) * HD)
        attn[:half, at] = dot(w_v[h, :half, :half], kv[:half, HD:]).astype(BF)
        attn[half:, at] = dot(w_v[h, half:, :], kv[:, HD:]).astype(BF)


def attention_scratch(rows, heads):
    return [
        pltpu.VMEM((rows, rows), F32),
        pltpu.VMEM((heads, rows, rows), F32),
        pltpu.VMEM((heads, rows, rows), BF),
    ]


def unit(count):
    return lax.broadcasted_iota(jnp.int32, (count, count), 0) == lax.broadcasted_iota(
        jnp.int32, (count, count), 1
    )


def decode_attention(n_seq, slots, plen, adm, clen, raw, raw_kv, kvs, cache, qg, kg, part):
    seq = lax.axis_index("seq")
    dec_rows = raw.shape[0]
    width = cache.shape[1]
    rows = kvs[0].shape[0]
    eff = effective_lengths(plen, adm, clen, slots)
    row = lax.broadcasted_iota(jnp.int32, (dec_rows, HD), 0)
    places = by_slot(lax.rem(row, slots), eff) + row // slots
    cos2, sin2 = cos_sin(places, turns(row))
    new_key = rope(norm(raw_kv[:, :HD], kg[...]), cos2, sin2).astype(BF)
    new_value = raw_kv[:, HD:].astype(BF)
    queries = jnp.concatenate(
        [
            rope(norm(raw[:, h * HD : (h + 1) * HD], qg[...]), cos2, sin2).astype(BF)
            for h in range(raw.shape[1] // HD)
        ],
        axis=0,
    )
    count = queries.shape[0]

    row = lax.rem(lax.broadcasted_iota(jnp.int32, (count, 1), 0), dec_rows)
    slot, step = lax.rem(row, slots), row // slots
    taken = by_slot(slot, [adm[r] for r in range(slots)])
    scores, masks, values = [], [], []
    at = lax.broadcasted_iota(jnp.int32, (1, width), 1) * n_seq + seq
    for r in range(slots):
        limit = jnp.where(adm[r] >= 0, 0, clen[r])
        masks.append((slot == r) & (at < limit))
        scores.append(dot_nt(queries, cache[r, :, :HD]))
        values.append(cache[r, :, HD:])
    spot = lax.broadcasted_iota(jnp.int32, (1, rows), 1)
    for p, kv in enumerate(kvs):
        prompt = seq * len(kvs) + p
        masks.append((taken == prompt) & (spot < plen[prompt]))
        scores.append(dot_nt(queries, kv[:, :HD]))
        values.append(kv[:, HD:])
    other = lax.broadcasted_iota(jnp.int32, (1, dec_rows), 1)
    first = jnp.where(seq == 0, 1, 0)
    masks.append(
        (lax.rem(other, slots) == slot) & (other // slots <= step) & (first + 0 * other > 0)
    )
    scores.append(dot_nt(queries, new_key))
    values.append(new_value)

    top = jnp.full((count, 1), NEG, F32)
    scores = [jnp.where(mask, score, NEG) for mask, score in zip(masks, scores)]
    for score in scores:
        top = jnp.maximum(top, jnp.max(score, axis=-1, keepdims=True))
    total = jnp.zeros((count, 1), F32)
    acc = jnp.zeros((count, HD), F32)
    for mask, score, value in zip(masks, scores, values):
        expo = jnp.where(mask, jnp.exp2((score - top) * C2), 0.0)
        total = total + jnp.sum(expo, axis=-1, keepdims=True)
        acc = acc + dot(expo.astype(BF), value)
    some = total > 0.0
    safe = jnp.where(some, total, 1.0)
    part[:count, :] = acc * (1.0 / safe)
    level = jnp.where(some, top * C2 + jnp.log2(safe), NEG)
    part[count : count + 1, :] = jnp.sum(jnp.where(unit(count), level, 0.0), axis=0, keepdims=True)


def prompt_kernel(which, n_head, n_seq, with_dec, *refs):
    it = iter(refs)
    take = lambda count: [next(it) for _ in range(count)]
    plen_h, qg_h, kg_h, table_h, x_hbm, wq_hbm, wk_hbm, wv_hbm, wo_hbm = take(9)
    if with_dec:
        adm_h, clen_h, dec_hbm, cache_h, pack1_h = take(5)
    send_h, pack_h = take(2)
    if with_dec:
        part_h, blocks_h, leave_h = take(3)
    x_v, wkv_v, wq_v, wo_v, raw, raw_kv, send, pack, plen, qg, kg, table = take(12)
    bias_v, s_v, p_v = take(3)
    x_sem, wkv_sem, wq_sem, wo_sem, small_sem, out_sem = take(6)
    if with_dec:
        dec_v, flat_v, cache, kv1, part, blocks, adm, clen, dec_sem = take(9)
    prompts, rows, width = x_hbm.shape
    tiles, _, pair = wq_v.shape
    local = tiles * pair
    nb = width // n_head
    seq = lax.axis_index("seq")
    first, _ = partners()
    diag = 3 - lax.axis_index("head")
    every = x_v.shape[0]
    middle = width // 2

    halves = [slice(0, middle), slice(middle, width)]
    front = []
    for c in range(2):
        at = pl.ds(c * middle, middle)
        front.append(
            [
                pltpu.make_async_copy(
                    x_hbm.at[which, :, at], x_v.at[pl.ds(0, rows), at], x_sem.at[c]
                ),
                pltpu.make_async_copy(wk_hbm.at[at], wkv_v.at[at, pl.ds(0, HD)], wkv_sem.at[0, c]),
                pltpu.make_async_copy(wv_hbm.at[at], wkv_v.at[at, pl.ds(HD, HD)], wkv_sem.at[1, c]),
            ]
        )
    q_copies = [
        pltpu.make_async_copy(wq_hbm.at[:, pl.ds(j * pair, pair)], wq_v.at[j], wq_sem.at[j])
        for j in range(tiles)
    ]
    late = [
        out_copy(wo_hbm, block, nb, wo_v.at[j], wo_sem.at[j]) for j, block in enumerate((diag, first))
    ]
    small = [(plen_h, plen), (qg_h, qg), (kg_h, kg), (table_h, table)]
    if with_dec:
        small += [(adm_h, adm), (clen_h, clen), (dec_hbm, dec_v)]
        late += [
            pltpu.make_async_copy(cache_h, cache, dec_sem.at[0]),
            pltpu.make_async_copy(pack1_h.at[:, pl.ds(0, pair)], kv1, dec_sem.at[1]),
        ]
    small = [
        pltpu.make_async_copy(src, dst, small_sem.at[i]) for i, (src, dst) in enumerate(small)
    ]
    for copy in front[0] + small + front[1] + q_copies + late:
        copy.start()
    for copy in small:
        copy.wait()
    bias_v[...] = mask_bias(rows, plen[seq * prompts + which])
    if with_dec:
        steps, slots, _ = dec_v.shape
        for t in range(steps):
            flat_v[t * slots : (t + 1) * slots, :] = dec_v[t].astype(F32)
        x_v[rows:, :] = flat_v[...].astype(BF)
    for copy in front[0]:
        copy.wait()
    raw_kv[...] = dot(x_v[:, halves[0]], wkv_v[halves[0]])
    for copy in front[1]:
        copy.wait()
    raw_kv[...] += dot(x_v[:, halves[1]], wkv_v[halves[1]])
    cos2, sin2 = table[:, :HD], table[:, HD:]
    kv = pack.at[:, pl.ds(0, pair)]
    mine = pack.at[:, pl.ds(pair, local)]
    for j in range(tiles + 1):
        if j < tiles:
            q_copies[j].wait()
            raw[:, j * pair : (j + 1) * pair] = dot(x_v[...], wq_v[j])
        if j == 0:
            kv[:, :HD] = rope(norm(raw_kv[:rows, :HD], kg[...]), cos2, sin2).astype(BF)
            kv[:, HD:] = raw_kv[:rows, HD:].astype(BF)
        else:
            heads = (2 * j - 2, 2 * j - 1)
            for h in heads:
                at = slice(h * HD, (h + 1) * HD)
                mine[:, at] = rope(norm(raw[:rows, at], qg[...]), cos2, sin2).astype(BF)
            attention(heads, mine, kv, bias_v, s_v, p_v, mine)
    for copy in late:
        copy.wait()
    outs = []
    if with_dec:
        each = rows // n_seq
        new = lax.broadcasted_iota(jnp.int32, (rows, rows), 0)
        old = lax.broadcasted_iota(jnp.int32, (rows, rows), 1)
        move = jnp.where(old == lax.rem(new, each) * n_seq + new // each, 1.0, 0.0).astype(BF)
        for p, source in enumerate((kv, kv1)):
            moved = dot(move, source[...]).astype(BF)
            for d in range(n_seq):
                blocks[d, p * each : (p + 1) * each] = moved[d * each : (d + 1) * each]
        half = n_seq // 2
        away = (1 - seq // half) * half
        outs += [
            pltpu.make_async_copy(blocks, blocks_h, out_sem.at[4]),
            pltpu.make_async_copy(blocks.at[pl.ds(away, half)], leave_h, out_sem.at[5]),
        ]
        for copy in outs:
            copy.start()
    outs.append(pltpu.make_async_copy(pack, pack_h, out_sem.at[0]))
    outs[-1].start()
    if with_dec:
        decode_attention(
            n_seq, slots, plen, adm, clen, raw.at[pl.ds(rows, every - rows)],
            raw_kv.at[pl.ds(rows, every - rows)], [kv, kv1], cache, qg, kg, part,
        )
        outs.append(pltpu.make_async_copy(part, part_h, out_sem.at[3]))
        outs[-1].start()
    for j in range(2):
        at = pl.ds(j * nb, nb)
        send[:, at] = dot(mine[...], wo_v[j]).astype(BF)
        outs.append(pltpu.make_async_copy(send.at[:, at], send_h.at[:, at], out_sem.at[1 + j]))
        outs[-1].start()
    for copy in outs:
        copy.wait()


def prompt_part(which, n_head, n_seq, plen, qg, kg, table, x, wq, wk, wv, wo, decode=()):
    prompts, rows, width = x.shape
    local = wq.shape[1]
    nb = width // n_head
    both = 2 * HD
    send = (rows, 2 * nb)
    pack = (rows, both + local)
    outs = [jax.ShapeDtypeStruct(send, BF), jax.ShapeDtypeStruct(pack, BF)]
    every = rows
    extra = []
    if decode:
        adm, clen, dec, cache, _ = decode
        dec_rows = dec.shape[0] * dec.shape[1]
        every += dec_rows
        part = (dec_rows * (local // HD) + 8, HD)
        blocks = (n_seq, prompts * rows // n_seq, both)
        outs += [
            jax.ShapeDtypeStruct(part, F32),
            jax.ShapeDtypeStruct(blocks, BF),
            jax.ShapeDtypeStruct((n_seq // 2,) + blocks[1:], BF),
        ]
        extra = [
            pltpu.VMEM(dec.shape, BF),
            pltpu.VMEM((dec_rows, width), F32),
            pltpu.VMEM(cache.shape, BF),
            pltpu.VMEM((rows, both), BF),
            pltpu.VMEM(part, F32),
            pltpu.VMEM(blocks, BF),
            pltpu.SMEM(adm.shape, jnp.int32),
            pltpu.SMEM(clen.shape, jnp.int32),
            pltpu.SemaphoreType.DMA((2,)),
        ]
    tiles = local // both
    return pl.pallas_call(
        functools.partial(prompt_kernel, which, n_head, n_seq, bool(decode)),
        out_shape=outs,
        in_specs=[HB] * (9 + len(decode)),
        out_specs=[HB] * len(outs),
        scratch_shapes=[
            pltpu.VMEM((every, width), BF),
            pltpu.VMEM((width, both), BF),
            pltpu.VMEM((tiles, width, both), BF),
            pltpu.VMEM((2, local, nb), BF),
            pltpu.VMEM((every, local), F32),
            pltpu.VMEM((every, both), F32),
            pltpu.VMEM(send, BF),
            pltpu.VMEM(pack, BF),
            pltpu.SMEM(plen.shape, jnp.int32),
            pltpu.VMEM(qg.shape, F32),
            pltpu.VMEM(kg.shape, F32),
            pltpu.VMEM(table.shape, F32),
        ]
        + attention_scratch(rows, local // HD)
        + [
            pltpu.SemaphoreType.DMA((2,)),
            pltpu.SemaphoreType.DMA((2, 2)),
            pltpu.SemaphoreType.DMA((tiles,)),
            pltpu.SemaphoreType.DMA((2,)),
            pltpu.SemaphoreType.DMA((7,)),
            pltpu.SemaphoreType.DMA((6,)),
        ]
        + extra,
        compiler_params=pltpu.CompilerParams(vmem_limit_bytes=LIMIT_A * MIB),
        cost_estimate=BRIEF,
        name="prompt_%d" % which,
    )(plen, qg, kg, table, x, wq, wk, wv, wo, *decode)


def third_kernel(pack0_h, pack1_h, wo_hbm, own0, own1, wo_a, wo_b, attns, pack_sem, wo_sem):
    _, local, nb = wo_a.shape
    rows = own0.shape[0]
    first, second = partners()
    head = lax.axis_index("head")
    wo_v = [wo_a.at[0], wo_a.at[1], wo_b.at[0], wo_b.at[1]]
    pack_copies = [
        pltpu.make_async_copy(
            src.at[:, pl.ds(2 * HD, local)], attns.at[pl.ds(p * rows, rows)], pack_sem.at[p]
        )
        for p, src in enumerate((pack0_h, pack1_h))
    ]
    copies = [
        out_copy(wo_hbm, block, nb, wo_v[j], wo_sem.at[j])
        for j, block in enumerate((head, second, 3 - head, first))
    ]
    for copy in pack_copies + copies:
        copy.start()
    for copy in pack_copies:
        copy.wait()
    for j in range(2):
        copies[j].wait()
        mixed = dot(attns[...], wo_v[j][...]).astype(BF)
        own0[:, j * nb : (j + 1) * nb] = mixed[:rows]
        own1[:, j * nb : (j + 1) * nb] = mixed[rows:]
    for copy in copies[2:]:
        copy.wait()


def third(n_head, pack0, pack1, wo):
    rows = pack0.shape[0]
    local, width = wo.shape
    nb = width // n_head
    return pl.pallas_call(
        third_kernel,
        out_shape=[jax.ShapeDtypeStruct((rows, 2 * nb), BF)] * 2
        + [jax.ShapeDtypeStruct((2, local, nb), BF)] * 2,
        in_specs=[HB] * 3,
        out_specs=[VM] * 4,
        scratch_shapes=[
            pltpu.VMEM((2 * rows, local), BF),
            pltpu.SemaphoreType.DMA((2,)),
            pltpu.SemaphoreType.DMA((4,)),
        ],
        compiler_params=pltpu.CompilerParams(vmem_limit_bytes=LIMIT_B * MIB),
        cost_estimate=BRIEF,
        name="third",
    )(pack0, pack1, wo)


def joined(bit, mine, other):
    count = mine.shape[0] - 8
    swap = lax.rem(lax.axis_index("seq") // bit, 2) == 1
    one, two = mine[...], other[...]
    low = jnp.where(swap, two, one)
    high = jnp.where(swap, one, two)
    eye = unit(count)

    def column(row):
        return jnp.sum(jnp.where(eye, row, 0.0), axis=1, keepdims=True)

    row_a, row_b = low[count : count + 1, :], high[count : count + 1, :]
    best = jnp.maximum(row_a, row_b)
    scale_a, scale_b = jnp.exp2(row_a - best), jnp.exp2(row_b - best)
    total = scale_a + scale_b
    inverse = 1.0 / total
    mixed = low[:count] * column(scale_a * inverse) + high[:count] * column(scale_b * inverse)
    return mixed, best + jnp.log2(total)


def range_start(seq, size):
    return seq // size * size


def range_start(seq, size):
    return seq // size * size


def join_kernel(bit, mine, other, out):
    count = mine.shape[0] - 8
    mixed, level = joined(bit, mine, other)
    out[:count, :] = mixed
    out[count : count + 1, :] = level


def join(bit, mine, other):
    return pl.pallas_call(
        functools.partial(join_kernel, bit),
        out_shape=jax.ShapeDtypeStruct(mine.shape, F32),
        in_specs=[VM] * 2,
        out_specs=VM,
        compiler_params=pltpu.CompilerParams(vmem_limit_bytes=8 * MIB),
        cost_estimate=BRIEF,
        name="join_%d" % bit,
    )(mine, other)


def hop_kernel(bit, *refs):
    held, leave = refs[:-1], refs[-1]
    seq = lax.axis_index("seq")
    size = bit // 2
    target = range_start(seq, bit) + size * (1 - lax.rem(seq // size, 2))
    at = 0
    for array in held:
        sources, dests = array.shape[:2]
        skip = target - range_start(seq, dests)
        for k in range(sources):
            leave[at] = array[k, pl.ds(skip, size)]
            at += 1


def hop(bit, held):
    sources = sum(array.shape[0] for array in held)
    return pl.pallas_call(
        functools.partial(hop_kernel, bit),
        out_shape=jax.ShapeDtypeStruct((sources, bit // 2) + held[0].shape[2:], BF),
        in_specs=[VM] * len(held),
        out_specs=VM,
        compiler_params=pltpu.CompilerParams(vmem_limit_bytes=8 * MIB),
        cost_estimate=BRIEF,
        name="hop_%d" % bit,
    )(*held)


def pass_on_kernel(own, got, on):
    nb = on.shape[1]
    on[...] = (own[:, nb:].astype(F32) + got[:, :nb].astype(F32)).astype(BF)


def pass_on(p, own, got):
    rows, both = got.shape
    return pl.pallas_call(
        pass_on_kernel,
        out_shape=jax.ShapeDtypeStruct((rows, both // 2), BF),
        in_specs=[VM] * 2,
        out_specs=VM,
        compiler_params=pltpu.CompilerParams(vmem_limit_bytes=8 * MIB),
        cost_estimate=BRIEF,
        name="pass_on_%d" % p,
    )(own, got)


def decode_out_kernel(bit, mine, other, wo_a, wo_b, *outs):
    count = mine.shape[0] - 8
    rows = outs[0].shape[0]
    mixed, _ = joined(bit, mine, other)
    mixed = mixed.astype(BF)
    flat = jnp.concatenate([mixed[i * rows : (i + 1) * rows] for i in range(count // rows)], axis=1)
    for j, out in enumerate(outs):
        out[...] = dot(flat, (wo_a, wo_b)[j // 2][j % 2]).astype(BF)


def decode_project(bit, dec_rows, mine, other, wo_a, wo_b):
    nb = wo_a.shape[2]
    return pl.pallas_call(
        functools.partial(decode_out_kernel, bit),
        out_shape=[jax.ShapeDtypeStruct((dec_rows, nb), BF)] * 4,
        in_specs=[VM] * 4,
        out_specs=[VM] * 4,
        compiler_params=pltpu.CompilerParams(vmem_limit_bytes=LIMIT_C * MIB),
        cost_estimate=BRIEF,
        name="decode_project",
    )(mine, other, wo_a, wo_b)


def sum_parts(stage, out, sems, own, got, last):
    rows, nb = last.shape
    step = rows // 2
    copies = []
    for i in range(2):
        at = pl.ds(i * step, step)
        stage[at] = (
            own[at, :nb].astype(F32) + got[at, nb:].astype(F32) + last[at].astype(F32)
        ).astype(BF)
        copies.append(pltpu.make_async_copy(stage.at[at], out.at[at], sems.at[i]))
        copies[-1].start()
    return copies


def finish_first_kernel(p, slots, own, got, last, *refs):
    pieces, (out, dec_out, stage, sems) = refs[:-4], refs[-4:]
    copies = sum_parts(stage, out.at[p], sems, own, got, last)
    total = pieces[0][...].astype(F32)
    for piece in pieces[1:]:
        total = total + piece[...].astype(F32)
    for t in range(dec_out.shape[0]):
        dec_out[t] = total[t * slots : (t + 1) * slots].astype(BF)
    for copy in copies:
        copy.wait()


def finish_first(p, prompts, steps, slots, own, got, last, pieces):
    rows, nb = last.shape
    return pl.pallas_call(
        functools.partial(finish_first_kernel, p, slots),
        out_shape=[
            jax.ShapeDtypeStruct((prompts, rows, nb), BF),
            jax.ShapeDtypeStruct((steps, slots, nb), BF),
        ],
        in_specs=[VM] * (3 + len(pieces)),
        out_specs=[HB, VM],
        scratch_shapes=[pltpu.VMEM((rows, nb), BF), pltpu.SemaphoreType.DMA((2,))],
        compiler_params=pltpu.CompilerParams(vmem_limit_bytes=8 * MIB),
        cost_estimate=BRIEF,
        name="finish_%d" % p,
    )(own, got, last, *pieces)


def finish_last_kernel(p, bits, own, got, last, *refs):
    held, (_, out, handed, stage, sems, keep_sem) = refs[: len(bits) + 1], refs[len(bits) + 1 :]
    seq = lax.axis_index("seq")
    copies = []
    sources = [0]
    for j, array in enumerate(held):
        if j:
            sources = sources + [bits[j - 1] ^ source for source in sources]
        for k in range(array.shape[0]):
            source = seq ^ sources[len(copies)]
            copies.append(
                pltpu.make_async_copy(
                    array.at[k, seq - range_start(seq, array.shape[1])],
                    handed.at[source],
                    keep_sem.at[len(copies)],
                )
            )
            copies[-1].start()
    for copy in sum_parts(stage, out.at[p], sems, own, got, last) + copies:
        copy.wait()


def finish_last(p, bits, own, got, last, held, partial):
    rows, nb = last.shape
    n_seq = held[0].shape[1]
    return pl.pallas_call(
        functools.partial(finish_last_kernel, p, bits),
        out_shape=[
            jax.ShapeDtypeStruct(partial.shape, BF),
            jax.ShapeDtypeStruct((n_seq,) + held[0].shape[2:], BF),
        ],
        in_specs=[VM] * (3 + len(held)) + [HB],
        out_specs=[HB] * 2,
        scratch_shapes=[
            pltpu.VMEM((rows, nb), BF),
            pltpu.SemaphoreType.DMA((2,)),
            pltpu.SemaphoreType.DMA((n_seq,)),
        ],
        input_output_aliases={3 + len(held): 0},
        compiler_params=pltpu.CompilerParams(vmem_limit_bytes=8 * MIB),
        cost_estimate=BRIEF,
        name="finish_%d" % p,
    )(own, got, last, *held, partial)


def after(value, other):
    return lax.optimization_barrier((value, other))[0]


def local(
    prompts, prompt_len, admitted, cache_len, cache_kv, dec_tokens, w_query, w_key, w_value, w_out, q_gain, k_gain
):
    n_seq = lax.axis_size("seq")
    n_head = lax.axis_size("head")
    pr_dev, rows, width = prompts.shape
    steps, slots, _ = dec_tokens.shape
    dec_rows = steps * slots
    each = rows // n_seq
    qg, kg = q_gain.reshape(1, HD), k_gain.reshape(1, HD)
    def head_move(value, masks):
        pairs = [
            (h * n_seq + s, (h ^ masks[s % 2]) * n_seq + s)
            for h in range(n_head)
            for s in range(n_seq)
        ]
        return lax.ppermute(value, ("head", "seq"), pairs)

    def seq_move(value, bit):
        return lax.ppermute(value, "seq", [(i, i ^ bit) for i in range(n_seq)])

    bits = []
    while 2 ** len(bits) < n_seq:
        bits.append(2 ** len(bits))
    bits = bits[::-1]

    table = jnp.asarray(prompt_table(rows))
    common = (prompt_len, qg, kg, table, prompts, w_query, w_key, w_value, w_out)
    send1, pack1 = prompt_part(1, n_head, n_seq, *common)
    got1 = head_move(send1, (1, 2))
    send0, pack0, part, blocks, leave = prompt_part(
        0, n_head, n_seq, *common, decode=(admitted, cache_len, dec_tokens, cache_kv[0], pack1)
    )
    got0 = head_move(send0, (1, 2))
    other = seq_move(part, bits[0])
    arrived = seq_move(leave, bits[0])
    own0, own1, *wo = third(n_head, pack0, pack1, w_out)
    other = after(other, own0)
    on1 = None
    for i, bit in enumerate(bits[:-1]):
        part = join(bit, part, other)
        other = seq_move(part, bits[i + 1])
        if on1 is None:
            on1 = pass_on(1, own1, after(got1, part))
            last1 = head_move(on1, (2, 1))
            other = after(other, on1)
    held = [blocks[None], after(arrived, part)[None]]
    leave = hop(bits[0], held)
    held.append(seq_move(leave, bits[1]))
    pieces = decode_project(bits[-1], dec_rows, part, after(other, leave), *wo)
    on0 = pass_on(0, own0, after(got0, pieces[0]))
    last0 = head_move(on0, (2, 1))
    pieces = [
        pieces[0],
        head_move(pieces[1], (2, 1)),
        head_move(pieces[2], (3, 3)),
        head_move(pieces[3], (1, 2)),
    ]
    held[-1] = lax.optimization_barrier((held[-1], *pieces))[0]
    for i, bit in enumerate(bits[1:-1]):
        held.append(seq_move(hop(bit, held), bits[i + 2]))
    partial, decode_out = finish_first(1, pr_dev, steps, slots, own1, got1, last1, pieces)
    prefill_out, handed = finish_last(0, bits, own0, got0, last0, held, partial)
    return (prefill_out, handed.reshape(1, pr_dev * n_seq, each, 2 * HD), decode_out)


def solution(mesh):
    placed = (
        P("seq", None, None),
        P(),
        P(),
        P(),
        P("head", None, "seq", None),
        P(),
        P(None, "head"),
        P(None, "head"),
        P(None, "head"),
        P("head", None),
        P(),
        P(),
    )
    return jax.shard_map(
        local,
        mesh=mesh,
        in_specs=placed,
        out_specs=(P("seq", None, "head"), P("head", None, "seq", None), P(None, None, "head")),
        check_vma=False,
    )
```

```python
import functools

import jax
import jax.numpy as jnp
import numpy as np
from jax import lax
from jax.experimental import pallas as pl
from jax.experimental.pallas import tpu as pltpu
from jax.sharding import PartitionSpec as P

HD = 128
EPS = 1e-06
THETA = 1000000.0
NEG = -1e30
LOG2E = 1.4426950408889634
SCALE = HD**-0.5
C2 = SCALE * LOG2E
BF = jnp.bfloat16
F32 = jnp.float32
HB = pl.BlockSpec(memory_space=pltpu.HBM)
VM = pl.BlockSpec(memory_space=pltpu.VMEM)
BRIEF = pl.CostEstimate(flops=1, bytes_accessed=1, transcendentals=0)
MIB = 1024 * 1024
LIMIT_A = 60
LIMIT_B = 50
LIMIT_C = 50


def frequencies():
    half = HD // 2
    freq = np.float32(THETA) ** (-np.arange(half, dtype=np.float32) / np.float32(half))
    return freq.astype(np.float32)


def turns(places):
    lane = lax.broadcasted_iota(jnp.int32, places.shape, 1)
    freq = jnp.zeros(places.shape, F32)
    spot = lax.rem(lane, HD // 2)
    for i, value in enumerate(frequencies()):
        freq = jnp.where(spot == i, float(value), freq)
    return freq


def cos_sin(places, freq):
    angle = places.astype(F32) * freq
    lane = lax.broadcasted_iota(jnp.int32, places.shape, 1)
    return jnp.cos(angle), jnp.where(lane < HD // 2, -1.0, 1.0) * jnp.sin(angle)


def prompt_table(length):
    angle = np.arange(length, dtype=np.float32)[:, None] * frequencies()[None, :]
    cosine, sine = np.cos(angle), np.sin(angle)
    return np.concatenate([cosine, cosine, -sine, sine], axis=1).astype(np.float32)


def dot(a, b):
    return jnp.dot(a, b, preferred_element_type=F32)


def dot_nt(a, b):
    return lax.dot_general(a, b, (((1,), (1,)), ((), ())), preferred_element_type=F32)


def norm(values, gain):
    square = jnp.mean(values * values, axis=-1, keepdims=True)
    return values * lax.rsqrt(square + EPS) * gain


def rope(values, cos2, sin2):
    return values * cos2 + pltpu.roll(values, HD // 2, 1) * sin2


def effective_lengths(plen, adm, clen, slots):
    out = []
    for r in range(slots):
        taken = adm[r]
        out.append(jnp.where(taken >= 0, plen[jnp.maximum(taken, 0)], clen[r]))
    return out


def by_slot(index, values):
    result = jnp.full(index.shape, values[0])
    for r in range(1, len(values)):
        result = jnp.where(index == r, values[r], result)
    return result


def partners():
    head, seq = lax.axis_index("head"), lax.axis_index("seq")
    flip_x = head + 1 - 2 * lax.rem(head, 2)
    flip_y = lax.rem(head + 2, 4)
    even = lax.rem(seq, 2) == 0
    return jnp.where(even, flip_x, flip_y), jnp.where(even, flip_y, flip_x)


def out_copy(wo_hbm, block, nb, dest, sem):
    return pltpu.make_async_copy(
        wo_hbm.at[:, pl.ds(pl.multiple_of(block * nb, nb), nb)], dest, sem
    )


def mask_bias(rows, length):
    row_at = lax.broadcasted_iota(jnp.int32, (rows, rows), 0)
    col_at = lax.broadcasted_iota(jnp.int32, (rows, rows), 1)
    return jnp.where((col_at <= row_at) & (col_at < length), 0.0, NEG).astype(F32)


def attention(heads, queries, kv, bias_v, s_v, w_v, attn):
    rows = kv.shape[0]
    half = rows // 2
    quarter = rows // 4
    for h in heads:
        at = slice(h * HD, (h + 1) * HD)
        s_v[h, :half, :half] = dot_nt(queries[:half, at], kv[:half, :HD])
        s_v[h, half:, :] = dot_nt(queries[half:, at], kv[:, :HD])
    for h in heads:
        for block in range(4):
            at = slice(block * quarter, (block + 1) * quarter)
            keys = half if block < 2 else rows
            scores = s_v[h, at, :keys] + bias_v[at, :keys]
            top = jnp.max(scores, axis=-1, keepdims=True)
            expo = jnp.exp2((scores - top) * C2)
            total = jnp.sum(expo, axis=-1, keepdims=True)
            w_v[h, at, :keys] = (expo * (1.0 / total)).astype(BF)
    for h in heads:
        at = slice(h * HD, (h + 1) * HD)
        attn[:half, at] = dot(w_v[h, :half, :half], kv[:half, HD:]).astype(BF)
        attn[half:, at] = dot(w_v[h, half:, :], kv[:, HD:]).astype(BF)


def attention_scratch(rows, heads):
    return [
        pltpu.VMEM((rows, rows), F32),
        pltpu.VMEM((heads, rows, rows), F32),
        pltpu.VMEM((heads, rows, rows), BF),
    ]


def unit(count):
    return lax.broadcasted_iota(jnp.int32, (count, count), 0) == lax.broadcasted_iota(
        jnp.int32, (count, count), 1
    )


def decode_attention(n_seq, slots, plen, adm, clen, raw, raw_kv, kvs, cache, qg, kg, part):
    seq = lax.axis_index("seq")
    dec_rows = raw.shape[0]
    width = cache.shape[1]
    rows = kvs[0].shape[0]
    eff = effective_lengths(plen, adm, clen, slots)
    row = lax.broadcasted_iota(jnp.int32, (dec_rows, HD), 0)
    places = by_slot(lax.rem(row, slots), eff) + row // slots
    cos2, sin2 = cos_sin(places, turns(row))
    new_key = rope(norm(raw_kv[:, :HD], kg[...]), cos2, sin2).astype(BF)
    new_value = raw_kv[:, HD:].astype(BF)
    queries = jnp.concatenate(
        [
            rope(norm(raw[:, h * HD : (h + 1) * HD], qg[...]), cos2, sin2).astype(BF)
            for h in range(raw.shape[1] // HD)
        ],
        axis=0,
    )
    count = queries.shape[0]

    row = lax.rem(lax.broadcasted_iota(jnp.int32, (count, 1), 0), dec_rows)
    slot, step = lax.rem(row, slots), row // slots
    taken = by_slot(slot, [adm[r] for r in range(slots)])
    scores, masks, values = [], [], []
    at = lax.broadcasted_iota(jnp.int32, (1, width), 1) * n_seq + seq
    for r in range(slots):
        limit = jnp.where(adm[r] >= 0, 0, clen[r])
        masks.append((slot == r) & (at < limit))
        scores.append(dot_nt(queries, cache[r, :, :HD]))
        values.append(cache[r, :, HD:])
    spot = lax.broadcasted_iota(jnp.int32, (1, rows), 1)
    for p, kv in enumerate(kvs):
        prompt = seq * len(kvs) + p
        masks.append((taken == prompt) & (spot < plen[prompt]))
        scores.append(dot_nt(queries, kv[:, :HD]))
        values.append(kv[:, HD:])
    other = lax.broadcasted_iota(jnp.int32, (1, dec_rows), 1)
    first = jnp.where(seq == 0, 1, 0)
    masks.append(
        (lax.rem(other, slots) == slot) & (other // slots <= step) & (first + 0 * other > 0)
    )
    scores.append(dot_nt(queries, new_key))
    values.append(new_value)

    top = jnp.full((count, 1), NEG, F32)
    scores = [jnp.where(mask, score, NEG) for mask, score in zip(masks, scores)]
    for score in scores:
        top = jnp.maximum(top, jnp.max(score, axis=-1, keepdims=True))
    total = jnp.zeros((count, 1), F32)
    acc = jnp.zeros((count, HD), F32)
    for mask, score, value in zip(masks, scores, values):
        expo = jnp.where(mask, jnp.exp2((score - top) * C2), 0.0)
        total = total + jnp.sum(expo, axis=-1, keepdims=True)
        acc = acc + dot(expo.astype(BF), value)
    some = total > 0.0
    safe = jnp.where(some, total, 1.0)
    part[:count, :] = acc * (1.0 / safe)
    level = jnp.where(some, top * C2 + jnp.log2(safe), NEG)
    part[count : count + 1, :] = jnp.sum(jnp.where(unit(count), level, 0.0), axis=0, keepdims=True)


def project_kernel(n_head, *refs):
    plen_h, qg_h, kg_h, table_h, x_hbm, dec_hbm, wq_hbm, wk_hbm, wv_hbm, wo_hbm = refs[:10]
    send_h, pack_h, new_h = refs[10:13]
    x_v, dec_v, flat_v, wkv_v, wq_v, wo_v, raw, raw_kv, send, pack = refs[13:23]
    plen, qg, kg, table = refs[23:27]
    bias_v, s_v, w_v = refs[27:30]
    x_sem, dec_sem, wkv_sem, wq_sem, wo_sem, small_sem, out_sem = refs[30:]
    prompts, rows, width = x_hbm.shape
    steps, slots, _ = dec_hbm.shape
    dec_rows = steps * slots
    local = wq_v.shape[1]
    nb = width // n_head
    lead = prompts - 1
    seq = lax.axis_index("seq")
    first, _ = partners()
    diag = 3 - lax.axis_index("head")
    front = rows + dec_rows

    cuts = cut_points(width)
    queue = []
    for c in range(len(cuts) - 1):
        at = pl.ds(cuts[c], cuts[c + 1] - cuts[c])
        queue.append(
            [
                pltpu.make_async_copy(
                    x_hbm.at[lead, :, at], x_v.at[pl.ds(0, rows), at], x_sem.at[0, c]
                ),
                pltpu.make_async_copy(
                    x_hbm.at[0, :, at], x_v.at[pl.ds(front, rows), at], x_sem.at[1, c]
                ),
                pltpu.make_async_copy(wk_hbm.at[at], wkv_v.at[at, pl.ds(0, HD)], wkv_sem.at[0, c]),
                pltpu.make_async_copy(wv_hbm.at[at], wkv_v.at[at, pl.ds(HD, HD)], wkv_sem.at[1, c]),
                pltpu.make_async_copy(wq_hbm.at[at], wq_v.at[at], wq_sem.at[c]),
            ]
        )
    small = [
        pltpu.make_async_copy(src, dst, small_sem.at[i])
        for i, (src, dst) in enumerate(
            [(plen_h, plen), (qg_h, qg), (kg_h, kg), (table_h, table)]
        )
    ]
    dec_copy = pltpu.make_async_copy(dec_hbm, dec_v, dec_sem)
    o_copies = [
        out_copy(wo_hbm, block, nb, wo_v.at[j], wo_sem.at[j]) for j, block in enumerate((diag, first))
    ]
    ahead = 3
    queue += [[copy] for copy in o_copies]
    for copy in [dec_copy] + queue[0] + small:
        copy.start()
    for group in queue[1:ahead]:
        for copy in group:
            copy.start()
    for copy in small:
        copy.wait()
    bias_v[...] = mask_bias(rows, plen[seq * prompts + lead])
    dec_copy.wait()
    for t in range(steps):
        flat_v[t * slots : (t + 1) * slots, :] = dec_v[t].astype(F32)
    x_v[rows:front, :] = flat_v[...].astype(BF)
    for c in range(len(cuts) - 1):
        for copy in queue[c]:
            copy.wait()
        if c + ahead < len(queue):
            for copy in queue[c + ahead]:
                copy.start()
        at = slice(cuts[c], cuts[c + 1])
        kv_part = dot(x_v[:, at], wkv_v[at, :])
        q_part = dot(x_v[:front, at], wq_v[at, :])
        if c == 0:
            raw_kv[...] = kv_part
            raw[...] = q_part
        else:
            raw_kv[...] += kv_part
            raw[...] += q_part
    cos2, sin2 = table[:, :HD], table[:, HD:]
    both = 2 * HD
    kvs = [pack.at[:, pl.ds(p * both, both)] for p in range(prompts)]
    for p, start in ((lead, 0), (0, front)):
        at = slice(start, start + rows)
        kvs[p][:, :HD] = rope(norm(raw_kv[at, :HD], kg[...]), cos2, sin2).astype(BF)
        kvs[p][:, HD:] = raw_kv[at, HD:].astype(BF)
    outs = [
        pltpu.make_async_copy(raw.at[pl.ds(rows, dec_rows)], new_h.at[:, pl.ds(0, local)], out_sem.at[0]),
        pltpu.make_async_copy(
            raw_kv.at[pl.ds(rows, dec_rows)], new_h.at[:, pl.ds(local, both)], out_sem.at[1]
        ),
    ]
    for copy in outs:
        copy.start()
    for copy in o_copies:
        copy.wait()
    base = prompts * both
    mine = pack.at[:, pl.ds(base, local)]
    pair = 2 * HD
    for j in range(local // pair):
        later = dot(x_v[front:, :], wq_v[:, j * pair : (j + 1) * pair])
        for h in (2 * j, 2 * j + 1):
            piece = raw[:rows, h * HD : (h + 1) * HD]
            mine[:, h * HD : (h + 1) * HD] = rope(norm(piece, qg[...]), cos2, sin2).astype(BF)
        attention((2 * j, 2 * j + 1), mine, kvs[lead], bias_v, s_v, w_v, mine)
        for i in range(2):
            col = base + local + (2 * j + i) * HD
            piece = later[:, i * HD : (i + 1) * HD]
            pack[:, col : col + HD] = rope(norm(piece, qg[...]), cos2, sin2).astype(BF)
    outs.append(pltpu.make_async_copy(pack, pack_h, out_sem.at[2]))
    outs[-1].start()
    for j in range(2):
        at = pl.ds(j * nb, nb)
        send[:, at] = dot(mine[...], wo_v[j]).astype(BF)
        outs.append(pltpu.make_async_copy(send.at[:, at], send_h.at[:, at], out_sem.at[3 + j]))
        outs[-1].start()
    for copy in outs:
        copy.wait()


def cut_points(width):
    step = width // 8
    return [0, step, 2 * step, 4 * step, 6 * step, 8 * step]


def project(n_head, plen, qg, kg, table, x, dec, wq, wk, wv, wo):
    prompts, rows, width = x.shape
    dec_rows = dec.shape[0] * dec.shape[1]
    local = wq.shape[1]
    nb = width // n_head
    every = prompts * rows + dec_rows
    send = (rows, 2 * nb)
    pack = (rows, 2 * prompts * HD + prompts * local)
    chunks = len(cut_points(width)) - 1
    return pl.pallas_call(
        functools.partial(project_kernel, n_head),
        out_shape=[
            jax.ShapeDtypeStruct(send, BF),
            jax.ShapeDtypeStruct(pack, BF),
            jax.ShapeDtypeStruct((dec_rows, local + 2 * HD), F32),
        ],
        in_specs=[HB] * 10,
        out_specs=[HB] * 3,
        scratch_shapes=[
            pltpu.VMEM((every, width), BF),
            pltpu.VMEM(dec.shape, BF),
            pltpu.VMEM((dec_rows, width), F32),
            pltpu.VMEM((width, 2 * HD), BF),
            pltpu.VMEM((width, local), BF),
            pltpu.VMEM((2, local, nb), BF),
            pltpu.VMEM((rows + dec_rows, local), F32),
            pltpu.VMEM((every, 2 * HD), F32),
            pltpu.VMEM(send, BF),
            pltpu.VMEM(pack, BF),
            pltpu.SMEM(plen.shape, jnp.int32),
            pltpu.VMEM(qg.shape, F32),
            pltpu.VMEM(kg.shape, F32),
            pltpu.VMEM(table.shape, F32),
        ]
        + attention_scratch(rows, local // HD)
        + [
            pltpu.SemaphoreType.DMA((2, chunks)),
            pltpu.SemaphoreType.DMA,
            pltpu.SemaphoreType.DMA((2, chunks)),
            pltpu.SemaphoreType.DMA((chunks,)),
            pltpu.SemaphoreType.DMA((2,)),
            pltpu.SemaphoreType.DMA((4,)),
            pltpu.SemaphoreType.DMA((5,)),
        ],
        compiler_params=pltpu.CompilerParams(vmem_limit_bytes=LIMIT_A * MIB),
        cost_estimate=BRIEF,
        name="project",
    )(plen, qg, kg, table, x, dec, wq, wk, wv, wo)


def second_kernel(n_seq, prompts, *refs):
    plen_h, adm_h, clen_h, qg_h, kg_h, pack_h, new_h, cache_h, wo_hbm = refs[:9]
    send, own0, own1, part, blocks, leave = refs[9:15]
    pack, attn, new, cache, wo_v, plen, adm, clen, qg, kg = refs[15:25]
    bias_v, s_v, w_v = refs[25:28]
    pack_sem, small_sem, wo_sem, cache_sem = refs[28:]
    rows = pack.shape[0]
    _, local, nb = wo_v.shape
    seq = lax.axis_index("seq")
    first, second = partners()
    head = lax.axis_index("head")
    pack_copy = pltpu.make_async_copy(pack_h, pack, pack_sem)
    cache_copy = pltpu.make_async_copy(cache_h, cache, cache_sem)
    small = [
        pltpu.make_async_copy(src, dst, small_sem.at[i])
        for i, (src, dst) in enumerate(
            [(plen_h, plen), (adm_h, adm), (clen_h, clen), (qg_h, qg), (kg_h, kg), (new_h, new)]
        )
    ]
    copies = [
        out_copy(wo_hbm, block, nb, wo_v.at[j], wo_sem.at[j])
        for j, block in enumerate((head, second, 3 - head, first))
    ]
    for copy in small + [pack_copy] + copies[:2] + [cache_copy] + copies[2:]:
        copy.start()
    for copy in small:
        copy.wait()
    bias_v[...] = mask_bias(rows, plen[seq * prompts])
    pack_copy.wait()
    both = 2 * HD
    base = prompts * both
    kvs = [pack.at[:, pl.ds(p * both, both)] for p in range(prompts)]
    other = pack.at[:, pl.ds(base, local)]
    queries = pack.at[:, pl.ds(base + local, local)]
    hb = nb // 2

    each = rows // n_seq
    to_row = lax.broadcasted_iota(jnp.int32, (rows, rows), 0)
    from_row = lax.broadcasted_iota(jnp.int32, (rows, rows), 1)
    move = jnp.where(from_row == lax.rem(to_row, each) * n_seq + to_row // each, 1.0, 0.0).astype(BF)
    for p, kv in enumerate(kvs):
        moved = dot(move, kv[...]).astype(BF)
        for d in range(n_seq):
            blocks[d, p * each : (p + 1) * each] = moved[d * each : (d + 1) * each]
    half = n_seq // 2
    leave[...] = blocks[pl.ds((1 - seq // half) * half, half)]
    for j in range(local // both):
        if j in (1, 2):
            copies[j - 1].wait()
            for i in range(2):
                at = slice(i * hb, (i + 1) * hb)
                to = slice((j - 1) * nb + i * hb, (j - 1) * nb + (i + 1) * hb)
                own1[:, to] = dot(other[...], wo_v[j - 1, :, at]).astype(BF)
        attention((2 * j, 2 * j + 1), queries, kvs[0], bias_v, s_v, w_v, attn)
    cache_copy.wait()
    for copy in copies[2:]:
        copy.wait()
    for j in range(2):
        send[:, j * nb : (j + 1) * nb] = dot(attn[...], wo_v[2 + j]).astype(BF)
    decode_attention(
        n_seq, cache.shape[0], plen, adm, clen, new.at[:, pl.ds(0, local)],
        new.at[:, pl.ds(local, both)], kvs, cache, qg, kg, part,
    )
    for j in range(2):
        own0[:, j * nb : (j + 1) * nb] = dot(attn[...], wo_v[j]).astype(BF)


def second(n_head, n_seq, prompts, plen, adm, clen, qg, kg, pack, new, cache, wo):
    rows = pack.shape[0]
    local, width = wo.shape
    nb = width // n_head
    blocks = (n_seq, prompts * rows // n_seq, 2 * HD)
    return pl.pallas_call(
        functools.partial(second_kernel, n_seq, prompts),
        out_shape=[jax.ShapeDtypeStruct((rows, 2 * nb), BF)] * 3
        + [
            jax.ShapeDtypeStruct((new.shape[0] * (local // HD) + 8, HD), F32),
            jax.ShapeDtypeStruct(blocks, BF),
            jax.ShapeDtypeStruct((n_seq // 2,) + blocks[1:], BF),
        ],
        in_specs=[HB] * 9,
        out_specs=[VM] * 6,
        scratch_shapes=[
            pltpu.VMEM(pack.shape, BF),
            pltpu.VMEM((rows, local), BF),
            pltpu.VMEM(new.shape, F32),
            pltpu.VMEM(cache.shape, BF),
            pltpu.VMEM((4, local, nb), BF),
            pltpu.SMEM(plen.shape, jnp.int32),
            pltpu.SMEM(adm.shape, jnp.int32),
            pltpu.SMEM(clen.shape, jnp.int32),
            pltpu.VMEM(qg.shape, F32),
            pltpu.VMEM(kg.shape, F32),
        ]
        + attention_scratch(rows, local // HD)
        + [
            pltpu.SemaphoreType.DMA,
            pltpu.SemaphoreType.DMA((6,)),
            pltpu.SemaphoreType.DMA((4,)),
            pltpu.SemaphoreType.DMA,
        ],
        compiler_params=pltpu.CompilerParams(vmem_limit_bytes=LIMIT_B * MIB),
        cost_estimate=BRIEF,
        name="second",
    )(plen, adm, clen, qg, kg, pack, new, cache, wo)


def joined(bit, mine, other):
    count = mine.shape[0] - 8
    swap = lax.rem(lax.axis_index("seq") // bit, 2) == 1
    one, two = mine[...], other[...]
    low = jnp.where(swap, two, one)
    high = jnp.where(swap, one, two)
    eye = unit(count)

    def column(row):
        return jnp.sum(jnp.where(eye, row, 0.0), axis=1, keepdims=True)

    row_a, row_b = low[count : count + 1, :], high[count : count + 1, :]
    best = jnp.maximum(row_a, row_b)
    scale_a, scale_b = jnp.exp2(row_a - best), jnp.exp2(row_b - best)
    total = scale_a + scale_b
    inverse = 1.0 / total
    mixed = low[:count] * column(scale_a * inverse) + high[:count] * column(scale_b * inverse)
    return mixed, best + jnp.log2(total)


def range_start(seq, size):
    return seq // size * size


def range_start(seq, size):
    return seq // size * size


def join_kernel(bit, mine, other, out):
    count = mine.shape[0] - 8
    mixed, level = joined(bit, mine, other)
    out[:count, :] = mixed
    out[count : count + 1, :] = level


def join(bit, mine, other):
    return pl.pallas_call(
        functools.partial(join_kernel, bit),
        out_shape=jax.ShapeDtypeStruct(mine.shape, F32),
        in_specs=[VM] * 2,
        out_specs=VM,
        compiler_params=pltpu.CompilerParams(vmem_limit_bytes=8 * MIB),
        cost_estimate=BRIEF,
        name="join_%d" % bit,
    )(mine, other)


def hop_kernel(bit, *refs):
    held, leave = refs[:-1], refs[-1]
    seq = lax.axis_index("seq")
    size = bit // 2
    target = range_start(seq, bit) + size * (1 - lax.rem(seq // size, 2))
    at = 0
    for array in held:
        sources, dests = array.shape[:2]
        skip = target - range_start(seq, dests)
        for k in range(sources):
            leave[at] = array[k, pl.ds(skip, size)]
            at += 1


def hop(bit, held):
    sources = sum(array.shape[0] for array in held)
    return pl.pallas_call(
        functools.partial(hop_kernel, bit),
        out_shape=jax.ShapeDtypeStruct((sources, bit // 2) + held[0].shape[2:], BF),
        in_specs=[VM] * len(held),
        out_specs=VM,
        compiler_params=pltpu.CompilerParams(vmem_limit_bytes=8 * MIB),
        cost_estimate=BRIEF,
        name="hop_%d" % bit,
    )(*held)


def pass_on_kernel(own, got, on):
    nb = on.shape[1]
    on[...] = (own[:, nb:].astype(F32) + got[:, :nb].astype(F32)).astype(BF)


def pass_on(p, own, got):
    rows, both = got.shape
    return pl.pallas_call(
        pass_on_kernel,
        out_shape=jax.ShapeDtypeStruct((rows, both // 2), BF),
        in_specs=[VM] * 2,
        out_specs=VM,
        compiler_params=pltpu.CompilerParams(vmem_limit_bytes=8 * MIB),
        cost_estimate=BRIEF,
        name="pass_on_%d" % p,
    )(own, got)


def decode_out_kernel(bit, mine, other, wo_hbm, *refs):
    outs, (wo_v, sems) = refs[:4], refs[4:]
    count = mine.shape[0] - 8
    rows, nb = outs[0].shape
    first, second = partners()
    head = lax.axis_index("head")
    copies = [
        out_copy(wo_hbm, block, nb, wo_v.at[j], sems.at[j])
        for j, block in enumerate((head, second, 3 - head, first))
    ]
    for copy in copies:
        copy.start()
    mixed, _ = joined(bit, mine, other)
    mixed = mixed.astype(BF)
    flat = jnp.concatenate([mixed[i * rows : (i + 1) * rows] for i in range(count // rows)], axis=1)
    for j, out in enumerate(outs):
        copies[j].wait()
        out[...] = dot(flat, wo_v[j]).astype(BF)


def decode_project(bit, n_head, dec_rows, mine, other, wo):
    local, width = wo.shape
    nb = width // n_head
    return pl.pallas_call(
        functools.partial(decode_out_kernel, bit),
        out_shape=[jax.ShapeDtypeStruct((dec_rows, nb), BF)] * 4,
        in_specs=[VM, VM, HB],
        out_specs=[VM] * 4,
        scratch_shapes=[pltpu.VMEM((4, local, nb), BF), pltpu.SemaphoreType.DMA((4,))],
        compiler_params=pltpu.CompilerParams(vmem_limit_bytes=LIMIT_C * MIB),
        cost_estimate=BRIEF,
        name="decode_project",
    )(mine, other, wo)


def sum_parts(stage, out, sems, own, got, last):
    rows, nb = last.shape
    step = rows // 2
    copies = []
    for i in range(2):
        at = pl.ds(i * step, step)
        stage[at] = (
            own[at, :nb].astype(F32) + got[at, nb:].astype(F32) + last[at].astype(F32)
        ).astype(BF)
        copies.append(pltpu.make_async_copy(stage.at[at], out.at[at], sems.at[i]))
        copies[-1].start()
    return copies


def finish_first_kernel(p, bits, own, got, last, *refs):
    held, (out, handed, stage, sems, keep_sem) = refs[: len(bits) + 1], refs[len(bits) + 1 :]
    seq = lax.axis_index("seq")
    copies = []
    sources = [0]
    for j, array in enumerate(held):
        if j:
            sources = sources + [bits[j - 1] ^ source for source in sources]
        for k in range(array.shape[0]):
            source = seq ^ sources[len(copies)]
            copies.append(
                pltpu.make_async_copy(
                    array.at[k, seq - range_start(seq, array.shape[1])],
                    handed.at[source],
                    keep_sem.at[len(copies)],
                )
            )
            copies[-1].start()
    for copy in sum_parts(stage, out.at[p], sems, own, got, last) + copies:
        copy.wait()


def finish_first(p, prompts, bits, own, got, last, held):
    rows, nb = last.shape
    n_seq = held[0].shape[1]
    return pl.pallas_call(
        functools.partial(finish_first_kernel, p, bits),
        out_shape=[
            jax.ShapeDtypeStruct((prompts, rows, nb), BF),
            jax.ShapeDtypeStruct((n_seq,) + held[0].shape[2:], BF),
        ],
        in_specs=[VM] * (3 + len(held)),
        out_specs=[HB] * 2,
        scratch_shapes=[
            pltpu.VMEM((rows, nb), BF),
            pltpu.SemaphoreType.DMA((2,)),
            pltpu.SemaphoreType.DMA((n_seq,)),
        ],
        compiler_params=pltpu.CompilerParams(vmem_limit_bytes=8 * MIB),
        cost_estimate=BRIEF,
        name="finish_%d" % p,
    )(own, got, last, *held)


def finish_last_kernel(p, slots, own, got, last, *refs):
    pieces, (_, out, dec_out, stage, sems) = refs[:-5], refs[-5:]
    copies = sum_parts(stage, out.at[p], sems, own, got, last)
    total = pieces[0][...].astype(F32)
    for piece in pieces[1:]:
        total = total + piece[...].astype(F32)
    for t in range(dec_out.shape[0]):
        dec_out[t] = total[t * slots : (t + 1) * slots].astype(BF)
    for copy in copies:
        copy.wait()


def finish_last(p, steps, slots, own, got, last, pieces, partial):
    rows, nb = last.shape
    return pl.pallas_call(
        functools.partial(finish_last_kernel, p, slots),
        out_shape=[
            jax.ShapeDtypeStruct(partial.shape, BF),
            jax.ShapeDtypeStruct((steps, slots, nb), BF),
        ],
        in_specs=[VM] * (3 + len(pieces)) + [HB],
        out_specs=[HB, VM],
        scratch_shapes=[pltpu.VMEM((rows, nb), BF), pltpu.SemaphoreType.DMA((2,))],
        input_output_aliases={3 + len(pieces): 0},
        compiler_params=pltpu.CompilerParams(vmem_limit_bytes=8 * MIB),
        cost_estimate=BRIEF,
        name="finish_%d" % p,
    )(own, got, last, *pieces, partial)


def after(value, other):
    return lax.optimization_barrier((value, other))[0]


def local(
    prompts, prompt_len, admitted, cache_len, cache_kv, dec_tokens, w_query, w_key, w_value, w_out, q_gain, k_gain
):
    n_seq = lax.axis_size("seq")
    n_head = lax.axis_size("head")
    pr_dev, rows, width = prompts.shape
    steps, slots, _ = dec_tokens.shape
    dec_rows = steps * slots
    each = rows // n_seq
    qg, kg = q_gain.reshape(1, HD), k_gain.reshape(1, HD)
    def head_move(value, masks):
        pairs = [
            (h * n_seq + s, (h ^ masks[s % 2]) * n_seq + s)
            for h in range(n_head)
            for s in range(n_seq)
        ]
        return lax.ppermute(value, ("head", "seq"), pairs)

    def seq_move(value, bit):
        return lax.ppermute(value, "seq", [(i, i ^ bit) for i in range(n_seq)])

    bits = []
    while 2 ** len(bits) < n_seq:
        bits.append(2 ** len(bits))
    bits = bits[::-1]

    table = jnp.asarray(prompt_table(rows))
    send1, pack, new = project(
        n_head, prompt_len, qg, kg, table, prompts, dec_tokens, w_query, w_key, w_value, w_out
    )
    got1 = head_move(send1, (1, 2))
    send0, own0, own1, part, blocks, leave = second(
        n_head, n_seq, pr_dev, prompt_len, admitted, cache_len, qg, kg, pack, new, cache_kv[0], w_out
    )
    got0 = head_move(send0, (1, 2))
    other = seq_move(part, bits[0])
    arrived = seq_move(leave, bits[0])
    for i, bit in enumerate(bits[:-1]):
        part = join(bit, part, other)
        other = seq_move(part, bits[i + 1])
    on1 = pass_on(1, own1, after(got1, part))
    last1 = head_move(on1, (2, 1))
    held = [blocks[None], after(arrived, part)[None]]
    leave = hop(bits[0], held)
    held.append(seq_move(leave, bits[1]))
    got0, other = lax.optimization_barrier((got0, other, on1, leave))[:2]
    on0 = pass_on(0, own0, got0)
    last0 = head_move(on0, (2, 1))
    for i, bit in enumerate(bits[1:-1]):
        leave = hop(bit, held)
        held.append(seq_move(leave, bits[i + 2]))
    other = lax.optimization_barrier((other, on0, leave))[0]
    pieces = decode_project(bits[-1], n_head, dec_rows, part, other, w_out)
    pieces = [
        pieces[0],
        head_move(pieces[1], (2, 1)),
        head_move(pieces[2], (3, 3)),
        head_move(pieces[3], (1, 2)),
    ]
    partial, handed = finish_first(1, pr_dev, bits, own1, got1, last1, held)
    prefill_out, decode_out = finish_last(0, steps, slots, own0, got0, last0, pieces, partial)
    return (prefill_out, handed.reshape(1, pr_dev * n_seq, each, 2 * HD), decode_out)


def solution(mesh):
    placed = (
        P("seq", None, None),
        P(),
        P(),
        P(),
        P("head", None, "seq", None),
        P(),
        P(None, "head"),
        P(None, "head"),
        P(None, "head"),
        P("head", None),
        P(),
        P(),
    )
    return jax.shard_map(
        local,
        mesh=mesh,
        in_specs=placed,
        out_specs=(P("seq", None, "head"), P("head", None, "seq", None), P(None, None, "head")),
        check_vma=False,
    )
```

```python
import functools

import jax
import jax.numpy as jnp
import numpy as np
from jax import lax
from jax.experimental import pallas as pl
from jax.experimental.pallas import tpu as pltpu
from jax.sharding import PartitionSpec as P

HD = 128
EPS = 1e-06
THETA = 1000000.0
NEG = -1e30
LOG2E = 1.4426950408889634
SCALE = HD**-0.5
C2 = SCALE * LOG2E
BF = jnp.bfloat16
F32 = jnp.float32
HB = pl.BlockSpec(memory_space=pltpu.HBM)
VM = pl.BlockSpec(memory_space=pltpu.VMEM)
BRIEF = pl.CostEstimate(flops=1, bytes_accessed=1, transcendentals=0)
MIB = 1024 * 1024
LIMIT_A = 60
LIMIT_B = 50
LIMIT_C = 42


def frequencies():
    half = HD // 2
    freq = np.float32(THETA) ** (-np.arange(half, dtype=np.float32) / np.float32(half))
    return freq.astype(np.float32)


def turns(places):
    lane = lax.broadcasted_iota(jnp.int32, places.shape, 1)
    freq = jnp.zeros(places.shape, F32)
    spot = lax.rem(lane, HD // 2)
    for i, value in enumerate(frequencies()):
        freq = jnp.where(spot == i, float(value), freq)
    return freq


def cos_sin(places, freq):
    angle = places.astype(F32) * freq
    lane = lax.broadcasted_iota(jnp.int32, places.shape, 1)
    return jnp.cos(angle), jnp.where(lane < HD // 2, -1.0, 1.0) * jnp.sin(angle)


def prompt_table(length):
    angle = np.arange(length, dtype=np.float32)[:, None] * frequencies()[None, :]
    cosine, sine = np.cos(angle), np.sin(angle)
    return np.concatenate([cosine, cosine, -sine, sine], axis=1).astype(np.float32)


def dot(a, b):
    return jnp.dot(a, b, preferred_element_type=F32)


def dot_nt(a, b):
    return lax.dot_general(a, b, (((1,), (1,)), ((), ())), preferred_element_type=F32)


def norm(values, gain):
    square = jnp.mean(values * values, axis=-1, keepdims=True)
    return values * lax.rsqrt(square + EPS) * gain


def rope(values, cos2, sin2):
    return values * cos2 + pltpu.roll(values, HD // 2, 1) * sin2


def effective_lengths(plen, adm, clen, slots):
    out = []
    for r in range(slots):
        taken = adm[r]
        out.append(jnp.where(taken >= 0, plen[jnp.maximum(taken, 0)], clen[r]))
    return out


def by_slot(index, values):
    result = jnp.full(index.shape, values[0])
    for r in range(1, len(values)):
        result = jnp.where(index == r, values[r], result)
    return result


def partners():
    head, seq = lax.axis_index("head"), lax.axis_index("seq")
    flip_x = head + 1 - 2 * lax.rem(head, 2)
    flip_y = lax.rem(head + 2, 4)
    even = lax.rem(seq, 2) == 0
    return jnp.where(even, flip_x, flip_y), jnp.where(even, flip_y, flip_x)


def out_copy(wo_hbm, block, nb, dest, sem):
    return pltpu.make_async_copy(
        wo_hbm.at[:, pl.ds(pl.multiple_of(block * nb, nb), nb)], dest, sem
    )


def mask_bias(rows, length):
    row_at = lax.broadcasted_iota(jnp.int32, (rows, rows), 0)
    col_at = lax.broadcasted_iota(jnp.int32, (rows, rows), 1)
    return jnp.where((col_at <= row_at) & (col_at < length), 0.0, NEG).astype(F32)


def attention(heads, queries, kv, bias_v, s_v, w_v, attn):
    rows = kv.shape[0]
    half = rows // 2
    quarter = rows // 4
    for h in heads:
        at = slice(h * HD, (h + 1) * HD)
        s_v[h, :half, :half] = dot_nt(queries[:half, at], kv[:half, :HD])
        s_v[h, half:, :] = dot_nt(queries[half:, at], kv[:, :HD])
    for h in heads:
        for block in range(4):
            at = slice(block * quarter, (block + 1) * quarter)
            keys = half if block < 2 else rows
            scores = s_v[h, at, :keys] + bias_v[at, :keys]
            top = jnp.max(scores, axis=-1, keepdims=True)
            expo = jnp.exp2((scores - top) * C2)
            total = jnp.sum(expo, axis=-1, keepdims=True)
            w_v[h, at, :keys] = (expo * (1.0 / total)).astype(BF)
    for h in heads:
        at = slice(h * HD, (h + 1) * HD)
        attn[:half, at] = dot(w_v[h, :half, :half], kv[:half, HD:]).astype(BF)
        attn[half:, at] = dot(w_v[h, half:, :], kv[:, HD:]).astype(BF)


def attention_scratch(rows, heads):
    return [
        pltpu.VMEM((rows, rows), F32),
        pltpu.VMEM((heads, rows, rows), F32),
        pltpu.VMEM((heads, rows, rows), BF),
    ]


def unit(count):
    return lax.broadcasted_iota(jnp.int32, (count, count), 0) == lax.broadcasted_iota(
        jnp.int32, (count, count), 1
    )


def decode_places(plen, adm, clen, slots, dec_rows):
    eff = effective_lengths(plen, adm, clen, slots)
    row = lax.broadcasted_iota(jnp.int32, (dec_rows, HD), 0)
    return by_slot(lax.rem(row, slots), eff) + row // slots


def decode_attention(n_seq, slots, plen, adm, clen, rotated, new, kvs, cache, part):
    seq = lax.axis_index("seq")
    dec_rows = rotated.shape[0]
    width = cache.shape[1]
    rows = kvs[0].shape[0]
    new_key, new_value = new[:, :HD], new[:, HD:]
    queries = jnp.concatenate(
        [rotated[:, h * HD : (h + 1) * HD] for h in range(rotated.shape[1] // HD)], axis=0
    )
    count = queries.shape[0]

    row = lax.rem(lax.broadcasted_iota(jnp.int32, (count, 1), 0), dec_rows)
    slot, step = lax.rem(row, slots), row // slots
    taken = by_slot(slot, [adm[r] for r in range(slots)])
    scores, masks, values = [], [], []
    at = lax.broadcasted_iota(jnp.int32, (1, width), 1) * n_seq + seq
    for r in range(slots):
        limit = jnp.where(adm[r] >= 0, 0, clen[r])
        masks.append((slot == r) & (at < limit))
        scores.append(dot_nt(queries, cache[r, :, :HD]))
        values.append(cache[r, :, HD:])
    spot = lax.broadcasted_iota(jnp.int32, (1, rows), 1)
    for p, kv in enumerate(kvs):
        prompt = seq * len(kvs) + p
        masks.append((taken == prompt) & (spot < plen[prompt]))
        scores.append(dot_nt(queries, kv[:, :HD]))
        values.append(kv[:, HD:])
    other = lax.broadcasted_iota(jnp.int32, (1, dec_rows), 1)
    first = jnp.where(seq == 0, 1, 0)
    masks.append(
        (lax.rem(other, slots) == slot) & (other // slots <= step) & (first + 0 * other > 0)
    )
    scores.append(dot_nt(queries, new_key))
    values.append(new_value)

    top = jnp.full((count, 1), NEG, F32)
    scores = [jnp.where(mask, score, NEG) for mask, score in zip(masks, scores)]
    for score in scores:
        top = jnp.maximum(top, jnp.max(score, axis=-1, keepdims=True))
    total = jnp.zeros((count, 1), F32)
    acc = jnp.zeros((count, HD), F32)
    for mask, score, value in zip(masks, scores, values):
        expo = jnp.where(mask, jnp.exp2((score - top) * C2), 0.0)
        total = total + jnp.sum(expo, axis=-1, keepdims=True)
        acc = acc + dot(expo.astype(BF), value)
    some = total > 0.0
    safe = jnp.where(some, total, 1.0)
    part[:count, :] = acc * (1.0 / safe)
    level = jnp.where(some, top * C2 + jnp.log2(safe), NEG)
    part[count : count + 1, :] = jnp.sum(jnp.where(unit(count), level, 0.0), axis=0, keepdims=True)


def project_kernel(n_head, n_seq, *refs):
    plen_h, adm_h, clen_h, qg_h, kg_h, table_h, x_hbm, dec_hbm, wq_hbm, wk_hbm, wv_hbm, wo_hbm = refs[:12]
    send_h, pack_h, blocks_h, leave_h = refs[12:16]
    x_v, dec_v, flat_v, wkv_v, wq_v, wo_v, raw, raw_kv, send, pack, blocks = refs[16:27]
    plen, adm, clen, qg, kg, table = refs[27:33]
    bias_v, s_v, w_v = refs[33:36]
    x_sem, dec_sem, wkv_sem, wq_sem, wo_sem, small_sem, out_sem = refs[36:]
    prompts, rows, width = x_hbm.shape
    steps, slots, _ = dec_hbm.shape
    dec_rows = steps * slots
    local = wq_v.shape[1]
    nb = width // n_head
    lead = prompts - 1
    seq = lax.axis_index("seq")
    first, _ = partners()
    diag = 3 - lax.axis_index("head")
    front = rows + dec_rows

    cuts = cut_points(width)
    queue = []
    for c in range(len(cuts) - 1):
        at = pl.ds(cuts[c], cuts[c + 1] - cuts[c])
        queue.append(
            [
                pltpu.make_async_copy(
                    x_hbm.at[lead, :, at], x_v.at[pl.ds(0, rows), at], x_sem.at[0, c]
                ),
                pltpu.make_async_copy(
                    x_hbm.at[0, :, at], x_v.at[pl.ds(front, rows), at], x_sem.at[1, c]
                ),
                pltpu.make_async_copy(wk_hbm.at[at], wkv_v.at[at, pl.ds(0, HD)], wkv_sem.at[0, c]),
                pltpu.make_async_copy(wv_hbm.at[at], wkv_v.at[at, pl.ds(HD, HD)], wkv_sem.at[1, c]),
                pltpu.make_async_copy(wq_hbm.at[at], wq_v.at[at], wq_sem.at[c]),
            ]
        )
    small = [
        pltpu.make_async_copy(src, dst, small_sem.at[i])
        for i, (src, dst) in enumerate(
            [(plen_h, plen), (qg_h, qg), (kg_h, kg), (table_h, table), (adm_h, adm), (clen_h, clen)]
        )
    ]
    dec_copy = pltpu.make_async_copy(dec_hbm, dec_v, dec_sem)
    o_copies = [
        out_copy(wo_hbm, block, nb, wo_v.at[j], wo_sem.at[j]) for j, block in enumerate((diag, first))
    ]
    ahead = 3
    queue += [[copy] for copy in o_copies]
    for copy in [dec_copy] + queue[0] + small:
        copy.start()
    for group in queue[1:ahead]:
        for copy in group:
            copy.start()
    for copy in small:
        copy.wait()
    bias_v[...] = mask_bias(rows, plen[seq * prompts + lead])
    dec_copy.wait()
    for t in range(steps):
        flat_v[t * slots : (t + 1) * slots, :] = dec_v[t].astype(F32)
    x_v[rows:front, :] = flat_v[...].astype(BF)
    for c in range(len(cuts) - 1):
        for copy in queue[c]:
            copy.wait()
        if c + ahead < len(queue):
            for copy in queue[c + ahead]:
                copy.start()
        at = slice(cuts[c], cuts[c + 1])
        kv_part = dot(x_v[:, at], wkv_v[at, :])
        q_part = dot(x_v[:front, at], wq_v[at, :])
        if c == 0:
            raw_kv[...] = kv_part
            raw[...] = q_part
        else:
            raw_kv[...] += kv_part
            raw[...] += q_part
    cos2, sin2 = table[:, :HD], table[:, HD:]
    both = 2 * HD
    base = prompts * both
    whole = pl.ds(0, rows)
    kvs = [pack.at[whole, pl.ds(p * both, both)] for p in range(prompts)]
    for p, start in ((lead, 0), (0, front)):
        at = slice(start, start + rows)
        kvs[p][:, :HD] = rope(norm(raw_kv[at, :HD], kg[...]), cos2, sin2).astype(BF)
        kvs[p][:, HD:] = raw_kv[at, HD:].astype(BF)
    each = rows // n_seq
    to_row = lax.broadcasted_iota(jnp.int32, (rows, rows), 0)
    from_row = lax.broadcasted_iota(jnp.int32, (rows, rows), 1)
    move = jnp.where(from_row == lax.rem(to_row, each) * n_seq + to_row // each, 1.0, 0.0).astype(BF)
    for p, kv in enumerate(kvs):
        moved = dot(move, kv[...]).astype(BF)
        for d in range(n_seq):
            blocks[d, p * each : (p + 1) * each] = moved[d * each : (d + 1) * each]
    half = n_seq // 2
    away = (1 - seq // half) * half
    outs = [
        pltpu.make_async_copy(blocks, blocks_h, out_sem.at[0]),
        pltpu.make_async_copy(blocks.at[pl.ds(away, half)], leave_h, out_sem.at[1]),
    ]
    for copy in outs:
        copy.start()
    places = decode_places(plen, adm, clen, slots, dec_rows)
    dcos2, dsin2 = cos_sin(places, turns(places))
    new_at = slice(rows, front)
    pack[new_at, :] = jnp.zeros((dec_rows, pack.shape[1]), BF)
    pack[new_at, :HD] = rope(norm(raw_kv[new_at, :HD], kg[...]), dcos2, dsin2).astype(BF)
    pack[new_at, HD:both] = raw_kv[new_at, HD:].astype(BF)
    for h in range(local // HD):
        piece = raw[new_at, h * HD : (h + 1) * HD]
        col = base + h * HD
        pack[new_at, col : col + HD] = rope(norm(piece, qg[...]), dcos2, dsin2).astype(BF)
    for copy in o_copies:
        copy.wait()
    mine = pack.at[whole, pl.ds(base, local)]
    pair = 2 * HD
    for j in range(local // pair):
        later = dot(x_v[front:, :], wq_v[:, j * pair : (j + 1) * pair])
        for h in (2 * j, 2 * j + 1):
            piece = raw[:rows, h * HD : (h + 1) * HD]
            mine[:, h * HD : (h + 1) * HD] = rope(norm(piece, qg[...]), cos2, sin2).astype(BF)
        attention((2 * j, 2 * j + 1), mine, kvs[lead], bias_v, s_v, w_v, mine)
        for i in range(2):
            col = base + local + (2 * j + i) * HD
            piece = later[:, i * HD : (i + 1) * HD]
            pack[:rows, col : col + HD] = rope(norm(piece, qg[...]), cos2, sin2).astype(BF)
    outs.append(pltpu.make_async_copy(pack, pack_h, out_sem.at[2]))
    outs[-1].start()
    for j in range(2):
        at = pl.ds(j * nb, nb)
        send[:, at] = dot(mine[...], wo_v[j]).astype(BF)
        outs.append(pltpu.make_async_copy(send.at[:, at], send_h.at[:, at], out_sem.at[3 + j]))
        outs[-1].start()
    for copy in outs:
        copy.wait()


def cut_points(width):
    step = width // 8
    return [0, step, 2 * step, 4 * step, 6 * step, 8 * step]


def project(n_head, n_seq, plen, adm, clen, qg, kg, table, x, dec, wq, wk, wv, wo):
    prompts, rows, width = x.shape
    dec_rows = dec.shape[0] * dec.shape[1]
    local = wq.shape[1]
    nb = width // n_head
    every = prompts * rows + dec_rows
    send = (rows, 2 * nb)
    pack = (rows + dec_rows, 2 * prompts * HD + prompts * local)
    blocks = (n_seq, prompts * rows // n_seq, 2 * HD)
    chunks = len(cut_points(width)) - 1
    return pl.pallas_call(
        functools.partial(project_kernel, n_head, n_seq),
        out_shape=[
            jax.ShapeDtypeStruct(send, BF),
            jax.ShapeDtypeStruct(pack, BF),
            jax.ShapeDtypeStruct(blocks, BF),
            jax.ShapeDtypeStruct((n_seq // 2,) + blocks[1:], BF),
        ],
        in_specs=[HB] * 12,
        out_specs=[HB] * 4,
        scratch_shapes=[
            pltpu.VMEM((every, width), BF),
            pltpu.VMEM(dec.shape, BF),
            pltpu.VMEM((dec_rows, width), F32),
            pltpu.VMEM((width, 2 * HD), BF),
            pltpu.VMEM((width, local), BF),
            pltpu.VMEM((2, local, nb), BF),
            pltpu.VMEM((rows + dec_rows, local), F32),
            pltpu.VMEM((every, 2 * HD), F32),
            pltpu.VMEM(send, BF),
            pltpu.VMEM(pack, BF),
            pltpu.VMEM(blocks, BF),
            pltpu.SMEM(plen.shape, jnp.int32),
            pltpu.SMEM(adm.shape, jnp.int32),
            pltpu.SMEM(clen.shape, jnp.int32),
            pltpu.VMEM(qg.shape, F32),
            pltpu.VMEM(kg.shape, F32),
            pltpu.VMEM(table.shape, F32),
        ]
        + attention_scratch(rows, local // HD)
        + [
            pltpu.SemaphoreType.DMA((2, chunks)),
            pltpu.SemaphoreType.DMA,
            pltpu.SemaphoreType.DMA((2, chunks)),
            pltpu.SemaphoreType.DMA((chunks,)),
            pltpu.SemaphoreType.DMA((2,)),
            pltpu.SemaphoreType.DMA((6,)),
            pltpu.SemaphoreType.DMA((5,)),
        ],
        compiler_params=pltpu.CompilerParams(vmem_limit_bytes=LIMIT_A * MIB),
        cost_estimate=BRIEF,
        name="project",
    )(plen, adm, clen, qg, kg, table, x, dec, wq, wk, wv, wo)


def second_kernel(n_seq, prompts, *refs):
    plen_h, adm_h, clen_h, pack_h, cache_h, wo_hbm = refs[:6]
    send, attn, own1, part = refs[6:10]
    pack, cache, wo_v, plen, adm, clen = refs[10:16]
    bias_v, s_v, w_v = refs[16:19]
    pack_sem, small_sem, wo_sem, cache_sem = refs[19:]
    rows = attn.shape[0]
    dec_rows = pack.shape[0] - rows
    _, local, nb = wo_v.shape
    seq = lax.axis_index("seq")
    first, second = partners()
    head = lax.axis_index("head")
    pack_copy = pltpu.make_async_copy(pack_h, pack, pack_sem)
    cache_copy = pltpu.make_async_copy(cache_h, cache, cache_sem)
    small = [
        pltpu.make_async_copy(src, dst, small_sem.at[i])
        for i, (src, dst) in enumerate([(plen_h, plen), (adm_h, adm), (clen_h, clen)])
    ]
    copies = [
        out_copy(wo_hbm, block, nb, wo_v.at[j], wo_sem.at[j])
        for j, block in enumerate((head, second, 3 - head, first))
    ]
    for copy in small + [pack_copy] + copies[:2] + [cache_copy] + copies[2:]:
        copy.start()
    for copy in small:
        copy.wait()
    bias_v[...] = mask_bias(rows, plen[seq * prompts])
    pack_copy.wait()
    both = 2 * HD
    base = prompts * both
    whole = pl.ds(0, rows)
    kvs = [pack.at[whole, pl.ds(p * both, both)] for p in range(prompts)]
    other = pack.at[whole, pl.ds(base, local)]
    queries = pack.at[whole, pl.ds(base + local, local)]
    hb = nb // 2

    for j in range(local // both):
        if j in (1, 2):
            copies[j - 1].wait()
            for i in range(2):
                at = slice(i * hb, (i + 1) * hb)
                to = slice((j - 1) * nb + i * hb, (j - 1) * nb + (i + 1) * hb)
                own1[:, to] = dot(other[...], wo_v[j - 1, :, at]).astype(BF)
        attention((2 * j, 2 * j + 1), queries, kvs[0], bias_v, s_v, w_v, attn)
    cache_copy.wait()
    for copy in copies[2:]:
        copy.wait()
    for j in range(2):
        send[:, j * nb : (j + 1) * nb] = dot(attn[...], wo_v[2 + j]).astype(BF)
    decode_attention(
        n_seq, cache.shape[0], plen, adm, clen, pack.at[pl.ds(rows, dec_rows), pl.ds(base, local)],
        pack.at[pl.ds(rows, dec_rows), pl.ds(0, both)], kvs, cache, part,
    )


def second(n_head, n_seq, prompts, rows, plen, adm, clen, pack, cache, wo):
    local, width = wo.shape
    nb = width // n_head
    dec_rows = pack.shape[0] - rows
    return pl.pallas_call(
        functools.partial(second_kernel, n_seq, prompts),
        out_shape=[
            jax.ShapeDtypeStruct((rows, 2 * nb), BF),
            jax.ShapeDtypeStruct((rows, local), BF),
            jax.ShapeDtypeStruct((rows, 2 * nb), BF),
            jax.ShapeDtypeStruct((dec_rows * (local // HD) + 8, HD), F32),
        ],
        in_specs=[HB] * 6,
        out_specs=[VM] * 4,
        scratch_shapes=[
            pltpu.VMEM(pack.shape, BF),
            pltpu.VMEM(cache.shape, BF),
            pltpu.VMEM((4, local, nb), BF),
            pltpu.SMEM(plen.shape, jnp.int32),
            pltpu.SMEM(adm.shape, jnp.int32),
            pltpu.SMEM(clen.shape, jnp.int32),
        ]
        + attention_scratch(rows, local // HD)
        + [
            pltpu.SemaphoreType.DMA,
            pltpu.SemaphoreType.DMA((3,)),
            pltpu.SemaphoreType.DMA((4,)),
            pltpu.SemaphoreType.DMA,
        ],
        compiler_params=pltpu.CompilerParams(vmem_limit_bytes=LIMIT_B * MIB),
        cost_estimate=BRIEF,
        name="second",
    )(plen, adm, clen, pack, cache, wo)


def third_kernel(attn, wo_hbm, own, wo_a, wo_b, wo_sem):
    nb = wo_a.shape[2]
    first, second = partners()
    head = lax.axis_index("head")
    wo_v = [wo_a.at[0], wo_a.at[1], wo_b.at[0], wo_b.at[1]]
    copies = [
        out_copy(wo_hbm, block, nb, wo_v[j], wo_sem.at[j])
        for j, block in enumerate((head, second, 3 - head, first))
    ]
    for copy in copies:
        copy.start()
    for j in range(2):
        copies[j].wait()
        own[:, j * nb : (j + 1) * nb] = dot(attn[...], wo_v[j][...]).astype(BF)
    for copy in copies[2:]:
        copy.wait()


def third(n_head, attn, wo):
    rows = attn.shape[0]
    local, width = wo.shape
    nb = width // n_head
    return pl.pallas_call(
        third_kernel,
        out_shape=[jax.ShapeDtypeStruct((rows, 2 * nb), BF)]
        + [jax.ShapeDtypeStruct((2, local, nb), BF)] * 2,
        in_specs=[VM, HB],
        out_specs=[VM] * 3,
        scratch_shapes=[pltpu.SemaphoreType.DMA((4,))],
        compiler_params=pltpu.CompilerParams(vmem_limit_bytes=LIMIT_C * MIB),
        cost_estimate=BRIEF,
        name="third",
    )(attn, wo)


def joined(bit, mine, other):
    count = mine.shape[0] - 8
    swap = lax.rem(lax.axis_index("seq") // bit, 2) == 1
    one, two = mine[...], other[...]
    low = jnp.where(swap, two, one)
    high = jnp.where(swap, one, two)
    eye = unit(count)

    def column(row):
        return jnp.sum(jnp.where(eye, row, 0.0), axis=1, keepdims=True)

    row_a, row_b = low[count : count + 1, :], high[count : count + 1, :]
    best = jnp.maximum(row_a, row_b)
    scale_a, scale_b = jnp.exp2(row_a - best), jnp.exp2(row_b - best)
    total = scale_a + scale_b
    inverse = 1.0 / total
    mixed = low[:count] * column(scale_a * inverse) + high[:count] * column(scale_b * inverse)
    return mixed, best + jnp.log2(total)


def range_start(seq, size):
    return seq // size * size


def range_start(seq, size):
    return seq // size * size


def join_kernel(bit, mine, other, out):
    count = mine.shape[0] - 8
    mixed, level = joined(bit, mine, other)
    out[:count, :] = mixed
    out[count : count + 1, :] = level


def join(bit, mine, other):
    return pl.pallas_call(
        functools.partial(join_kernel, bit),
        out_shape=jax.ShapeDtypeStruct(mine.shape, F32),
        in_specs=[VM] * 2,
        out_specs=VM,
        compiler_params=pltpu.CompilerParams(vmem_limit_bytes=8 * MIB),
        cost_estimate=BRIEF,
        name="join_%d" % bit,
    )(mine, other)


def hop_kernel(bit, *refs):
    held, leave = refs[:-1], refs[-1]
    seq = lax.axis_index("seq")
    size = bit // 2
    target = range_start(seq, bit) + size * (1 - lax.rem(seq // size, 2))
    at = 0
    for array in held:
        sources, dests = array.shape[:2]
        skip = target - range_start(seq, dests)
        for k in range(sources):
            leave[at] = array[k, pl.ds(skip, size)]
            at += 1


def hop(bit, held):
    sources = sum(array.shape[0] for array in held)
    return pl.pallas_call(
        functools.partial(hop_kernel, bit),
        out_shape=jax.ShapeDtypeStruct((sources, bit // 2) + held[0].shape[2:], BF),
        in_specs=[VM] * len(held),
        out_specs=VM,
        compiler_params=pltpu.CompilerParams(vmem_limit_bytes=8 * MIB),
        cost_estimate=BRIEF,
        name="hop_%d" % bit,
    )(*held)


def pass_on_kernel(own, got, on):
    nb = on.shape[1]
    on[...] = (own[:, nb:].astype(F32) + got[:, :nb].astype(F32)).astype(BF)


def pass_on(p, own, got):
    rows, both = got.shape
    return pl.pallas_call(
        pass_on_kernel,
        out_shape=jax.ShapeDtypeStruct((rows, both // 2), BF),
        in_specs=[VM] * 2,
        out_specs=VM,
        compiler_params=pltpu.CompilerParams(vmem_limit_bytes=8 * MIB),
        cost_estimate=BRIEF,
        name="pass_on_%d" % p,
    )(own, got)


def decode_out_kernel(bit, mine, other, wo_a, wo_b, *outs):
    count = mine.shape[0] - 8
    rows = outs[0].shape[0]
    mixed, _ = joined(bit, mine, other)
    mixed = mixed.astype(BF)
    flat = jnp.concatenate([mixed[i * rows : (i + 1) * rows] for i in range(count // rows)], axis=1)
    for j, out in enumerate(outs):
        out[...] = dot(flat, (wo_a, wo_b)[j // 2][j % 2]).astype(BF)


def decode_project(bit, dec_rows, mine, other, wo_a, wo_b):
    nb = wo_a.shape[2]
    return pl.pallas_call(
        functools.partial(decode_out_kernel, bit),
        out_shape=[jax.ShapeDtypeStruct((dec_rows, nb), BF)] * 4,
        in_specs=[VM] * 4,
        out_specs=[VM] * 4,
        compiler_params=pltpu.CompilerParams(vmem_limit_bytes=16 * MIB),
        cost_estimate=BRIEF,
        name="decode_project",
    )(mine, other, wo_a, wo_b)


def sum_parts(stage, out, sems, own, got, last):
    rows, nb = last.shape
    step = rows // 2
    copies = []
    for i in range(2):
        at = pl.ds(i * step, step)
        stage[at] = (
            own[at, :nb].astype(F32) + got[at, nb:].astype(F32) + last[at].astype(F32)
        ).astype(BF)
        copies.append(pltpu.make_async_copy(stage.at[at], out.at[at], sems.at[i]))
        copies[-1].start()
    return copies


def finish_first_kernel(p, bits, own, got, last, *refs):
    held, (out, handed, stage, sems, keep_sem) = refs[: len(bits) + 1], refs[len(bits) + 1 :]
    seq = lax.axis_index("seq")
    copies = []
    sources = [0]
    for j, array in enumerate(held):
        if j:
            sources = sources + [bits[j - 1] ^ source for source in sources]
        for k in range(array.shape[0]):
            source = seq ^ sources[len(copies)]
            copies.append(
                pltpu.make_async_copy(
                    array.at[k, seq - range_start(seq, array.shape[1])],
                    handed.at[source],
                    keep_sem.at[len(copies)],
                )
            )
            copies[-1].start()
    for copy in sum_parts(stage, out.at[p], sems, own, got, last) + copies:
        copy.wait()


def finish_first(p, prompts, bits, own, got, last, held):
    rows, nb = last.shape
    n_seq = held[0].shape[1]
    return pl.pallas_call(
        functools.partial(finish_first_kernel, p, bits),
        out_shape=[
            jax.ShapeDtypeStruct((prompts, rows, nb), BF),
            jax.ShapeDtypeStruct((n_seq,) + held[0].shape[2:], BF),
        ],
        in_specs=[VM] * (3 + len(held)),
        out_specs=[HB] * 2,
        scratch_shapes=[
            pltpu.VMEM((rows, nb), BF),
            pltpu.SemaphoreType.DMA((2,)),
            pltpu.SemaphoreType.DMA((n_seq,)),
        ],
        compiler_params=pltpu.CompilerParams(vmem_limit_bytes=8 * MIB),
        cost_estimate=BRIEF,
        name="finish_%d" % p,
    )(own, got, last, *held)


def finish_last_kernel(p, slots, own, got, last, *refs):
    pieces, (_, out, dec_out, stage, sems) = refs[:-5], refs[-5:]
    copies = sum_parts(stage, out.at[p], sems, own, got, last)
    total = pieces[0][...].astype(F32)
    for piece in pieces[1:]:
        total = total + piece[...].astype(F32)
    for t in range(dec_out.shape[0]):
        dec_out[t] = total[t * slots : (t + 1) * slots].astype(BF)
    for copy in copies:
        copy.wait()


def finish_last(p, steps, slots, own, got, last, pieces, partial):
    rows, nb = last.shape
    return pl.pallas_call(
        functools.partial(finish_last_kernel, p, slots),
        out_shape=[
            jax.ShapeDtypeStruct(partial.shape, BF),
            jax.ShapeDtypeStruct((steps, slots, nb), BF),
        ],
        in_specs=[VM] * (3 + len(pieces)) + [HB],
        out_specs=[HB, VM],
        scratch_shapes=[pltpu.VMEM((rows, nb), BF), pltpu.SemaphoreType.DMA((2,))],
        input_output_aliases={3 + len(pieces): 0},
        compiler_params=pltpu.CompilerParams(vmem_limit_bytes=8 * MIB),
        cost_estimate=BRIEF,
        name="finish_%d" % p,
    )(own, got, last, *pieces, partial)


def after(value, other):
    return lax.optimization_barrier((value, other))[0]


def local(
    prompts, prompt_len, admitted, cache_len, cache_kv, dec_tokens, w_query, w_key, w_value, w_out, q_gain, k_gain
):
    n_seq = lax.axis_size("seq")
    n_head = lax.axis_size("head")
    pr_dev, rows, width = prompts.shape
    steps, slots, _ = dec_tokens.shape
    dec_rows = steps * slots
    each = rows // n_seq
    qg, kg = q_gain.reshape(1, HD), k_gain.reshape(1, HD)
    def head_move(value, masks):
        pairs = [
            (h * n_seq + s, (h ^ masks[s % 2]) * n_seq + s)
            for h in range(n_head)
            for s in range(n_seq)
        ]
        return lax.ppermute(value, ("head", "seq"), pairs)

    def seq_move(value, bit):
        return lax.ppermute(value, "seq", [(i, i ^ bit) for i in range(n_seq)])

    bits = []
    while 2 ** len(bits) < n_seq:
        bits.append(2 ** len(bits))
    bits = bits[::-1]

    table = jnp.asarray(prompt_table(rows))
    scalars = (prompt_len, admitted, cache_len)
    send1, pack, blocks, leave = project(
        n_head, n_seq, *scalars, qg, kg, table, prompts, dec_tokens, w_query, w_key, w_value, w_out
    )
    got1 = head_move(send1, (1, 2))
    arrived = seq_move(leave, bits[0])
    send0, attn0, own1, part = second(
        n_head, n_seq, pr_dev, rows, *scalars, pack, cache_kv[0], w_out
    )
    send0, arrived = lax.optimization_barrier((send0, arrived))
    got0 = head_move(send0, (1, 2))
    other = seq_move(part, bits[0])
    own0, *wo = third(n_head, attn0, w_out)
    other, got1 = lax.optimization_barrier((other, got1, own0))[:2]
    for i, bit in enumerate(bits[:-1]):
        part = join(bit, part, other)
        other = seq_move(part, bits[i + 1])
    held = [blocks[None], after(arrived, part)[None]]
    leave = hop(bits[0], held)
    held.append(seq_move(leave, bits[1]))
    on1 = pass_on(1, own1, after(got1, part))
    last1 = head_move(on1, (2, 1))
    got0, other, held[-1] = lax.optimization_barrier((got0, other, held[-1], on1))[:3]
    on0 = pass_on(0, own0, got0)
    last0 = head_move(on0, (2, 1))
    held[-1] = after(held[-1], on0)
    for i, bit in enumerate(bits[1:-1]):
        leave = hop(bit, held)
        held.append(seq_move(leave, bits[i + 2]))
    other = lax.optimization_barrier((other, on0, leave))[0]
    pieces = decode_project(bits[-1], dec_rows, part, other, *wo)
    pieces = [
        pieces[0],
        head_move(pieces[1], (2, 1)),
        head_move(pieces[2], (3, 3)),
        head_move(pieces[3], (1, 2)),
    ]
    partial, handed = finish_first(1, pr_dev, bits, own1, got1, last1, held)
    prefill_out, decode_out = finish_last(0, steps, slots, own0, got0, last0, pieces, partial)
    return (prefill_out, handed.reshape(1, pr_dev * n_seq, each, 2 * HD), decode_out)


def solution(mesh):
    placed = (
        P("seq", None, None),
        P(),
        P(),
        P(),
        P("head", None, "seq", None),
        P(),
        P(None, "head"),
        P(None, "head"),
        P(None, "head"),
        P("head", None),
        P(),
        P(),
    )
    return jax.shard_map(
        local,
        mesh=mesh,
        in_specs=placed,
        out_specs=(P("seq", None, "head"), P("head", None, "seq", None), P(None, None, "head")),
        check_vma=False,
    )
```

```python
import functools

import jax
import jax.numpy as jnp
import numpy as np
from jax import lax
from jax.experimental import pallas as pl
from jax.experimental.pallas import tpu as pltpu
from jax.sharding import PartitionSpec as P

HD = 128
EPS = 1e-06
THETA = 1000000.0
NEG = -1e30
LOG2E = 1.4426950408889634
SCALE = HD**-0.5
C2 = SCALE * LOG2E
BF = jnp.bfloat16
F32 = jnp.float32
HB = pl.BlockSpec(memory_space=pltpu.HBM)
VM = pl.BlockSpec(memory_space=pltpu.VMEM)
BRIEF = pl.CostEstimate(flops=1, bytes_accessed=1, transcendentals=0)
MIB = 1024 * 1024
LIMIT_A = 60
LIMIT_B = 50
LIMIT_C = 42


def frequencies():
    half = HD // 2
    freq = np.float32(THETA) ** (-np.arange(half, dtype=np.float32) / np.float32(half))
    return freq.astype(np.float32)


def turns(places):
    lane = lax.broadcasted_iota(jnp.int32, places.shape, 1)
    freq = jnp.zeros(places.shape, F32)
    spot = lax.rem(lane, HD // 2)
    for i, value in enumerate(frequencies()):
        freq = jnp.where(spot == i, float(value), freq)
    return freq


def cos_sin(places, freq):
    angle = places.astype(F32) * freq
    lane = lax.broadcasted_iota(jnp.int32, places.shape, 1)
    return jnp.cos(angle), jnp.where(lane < HD // 2, -1.0, 1.0) * jnp.sin(angle)


def prompt_table(length):
    angle = np.arange(length, dtype=np.float32)[:, None] * frequencies()[None, :]
    cosine, sine = np.cos(angle), np.sin(angle)
    return np.concatenate([cosine, cosine, -sine, sine], axis=1).astype(np.float32)


def dot(a, b):
    return jnp.dot(a, b, preferred_element_type=F32)


def dot_nt(a, b):
    return lax.dot_general(a, b, (((1,), (1,)), ((), ())), preferred_element_type=F32)


def norm(values, gain):
    square = jnp.mean(values * values, axis=-1, keepdims=True)
    return values * lax.rsqrt(square + EPS) * gain


def rope(values, cos2, sin2):
    return values * cos2 + pltpu.roll(values, HD // 2, 1) * sin2


def effective_lengths(plen, adm, clen, slots):
    out = []
    for r in range(slots):
        taken = adm[r]
        out.append(jnp.where(taken >= 0, plen[jnp.maximum(taken, 0)], clen[r]))
    return out


def by_slot(index, values):
    result = jnp.full(index.shape, values[0])
    for r in range(1, len(values)):
        result = jnp.where(index == r, values[r], result)
    return result


def partners():
    head, seq = lax.axis_index("head"), lax.axis_index("seq")
    flip_x = head + 1 - 2 * lax.rem(head, 2)
    flip_y = lax.rem(head + 2, 4)
    even = lax.rem(seq, 2) == 0
    return jnp.where(even, flip_x, flip_y), jnp.where(even, flip_y, flip_x)


def out_copy(wo_hbm, block, nb, dest, sem):
    return pltpu.make_async_copy(
        wo_hbm.at[:, pl.ds(pl.multiple_of(block * nb, nb), nb)], dest, sem
    )


def mask_bias(rows, length):
    row_at = lax.broadcasted_iota(jnp.int32, (rows, rows), 0)
    col_at = lax.broadcasted_iota(jnp.int32, (rows, rows), 1)
    return jnp.where((col_at <= row_at) & (col_at < length), 0.0, NEG).astype(F32)


def attention(heads, queries, kv, bias_v, s_v, w_v, attn, skip=0):
    rows = kv.shape[0]
    half = rows // 2
    quarter = rows // 4
    for h in heads:
        at = slice((h - skip) * HD, (h - skip + 1) * HD)
        s_v[h, :half, :half] = dot_nt(queries[:half, at], kv[:half, :HD])
        s_v[h, half:, :] = dot_nt(queries[half:, at], kv[:, :HD])
    for h in heads:
        for block in range(4):
            at = slice(block * quarter, (block + 1) * quarter)
            keys = half if block < 2 else rows
            scores = s_v[h, at, :keys] + bias_v[at, :keys]
            top = jnp.max(scores, axis=-1, keepdims=True)
            expo = jnp.exp2((scores - top) * C2)
            total = jnp.sum(expo, axis=-1, keepdims=True)
            w_v[h, at, :keys] = (expo * (1.0 / total)).astype(BF)
    for h in heads:
        at = slice(h * HD, (h + 1) * HD)
        attn[:half, at] = dot(w_v[h, :half, :half], kv[:half, HD:]).astype(BF)
        attn[half:, at] = dot(w_v[h, half:, :], kv[:, HD:]).astype(BF)


def attention_scratch(rows, heads):
    return [
        pltpu.VMEM((rows, rows), F32),
        pltpu.VMEM((heads, rows, rows), F32),
        pltpu.VMEM((heads, rows, rows), BF),
    ]


def unit(count):
    return lax.broadcasted_iota(jnp.int32, (count, count), 0) == lax.broadcasted_iota(
        jnp.int32, (count, count), 1
    )


def decode_places(plen, adm, clen, slots, dec_rows):
    eff = effective_lengths(plen, adm, clen, slots)
    row = lax.broadcasted_iota(jnp.int32, (dec_rows, HD), 0)
    return by_slot(lax.rem(row, slots), eff) + row // slots


def decode_attention(n_seq, slots, plen, adm, clen, rotated, new, kvs, cache, part):
    seq = lax.axis_index("seq")
    dec_rows = rotated.shape[0]
    width = cache.shape[1]
    rows = kvs[0].shape[0]
    new_key, new_value = new[:, :HD], new[:, HD:]
    queries = jnp.concatenate(
        [rotated[:, h * HD : (h + 1) * HD] for h in range(rotated.shape[1] // HD)], axis=0
    )
    count = queries.shape[0]

    row = lax.rem(lax.broadcasted_iota(jnp.int32, (count, 1), 0), dec_rows)
    slot, step = lax.rem(row, slots), row // slots
    taken = by_slot(slot, [adm[r] for r in range(slots)])
    scores, masks, values = [], [], []
    at = lax.broadcasted_iota(jnp.int32, (1, width), 1) * n_seq + seq
    for r in range(slots):
        limit = jnp.where(adm[r] >= 0, 0, clen[r])
        masks.append((slot == r) & (at < limit))
        scores.append(dot_nt(queries, cache[r, :, :HD]))
        values.append(cache[r, :, HD:])
    spot = lax.broadcasted_iota(jnp.int32, (1, rows), 1)
    for p, kv in enumerate(kvs):
        prompt = seq * len(kvs) + p
        masks.append((taken == prompt) & (spot < plen[prompt]))
        scores.append(dot_nt(queries, kv[:, :HD]))
        values.append(kv[:, HD:])
    other = lax.broadcasted_iota(jnp.int32, (1, dec_rows), 1)
    first = jnp.where(seq == 0, 1, 0)
    masks.append(
        (lax.rem(other, slots) == slot) & (other // slots <= step) & (first + 0 * other > 0)
    )
    scores.append(dot_nt(queries, new_key))
    values.append(new_value)

    top = jnp.full((count, 1), NEG, F32)
    scores = [jnp.where(mask, score, NEG) for mask, score in zip(masks, scores)]
    for score in scores:
        top = jnp.maximum(top, jnp.max(score, axis=-1, keepdims=True))
    total = jnp.zeros((count, 1), F32)
    acc = jnp.zeros((count, HD), F32)
    for mask, score, value in zip(masks, scores, values):
        expo = jnp.where(mask, jnp.exp2((score - top) * C2), 0.0)
        total = total + jnp.sum(expo, axis=-1, keepdims=True)
        acc = acc + dot(expo.astype(BF), value)
    some = total > 0.0
    safe = jnp.where(some, total, 1.0)
    part[:count, :] = acc * (1.0 / safe)
    level = jnp.where(some, top * C2 + jnp.log2(safe), NEG)
    part[count : count + 1, :] = jnp.sum(jnp.where(unit(count), level, 0.0), axis=0, keepdims=True)


def project_kernel(n_head, n_seq, *refs):
    plen_h, adm_h, clen_h, qg_h, kg_h, table_h, x_hbm, dec_hbm, wq_hbm, wk_hbm, wv_hbm, wo_hbm = refs[:12]
    send_h, pack_h, blocks_h, leave_h = refs[12:16]
    x_v, dec_v, flat_v, wkv_v, wq_v, wo_v, raw, raw_kv, send, pack, blocks = refs[16:27]
    plen, adm, clen, qg, kg, table = refs[27:33]
    bias_v, s_v, w_v = refs[33:36]
    x_sem, dec_sem, wkv_sem, wq_sem, wo_sem, small_sem, out_sem = refs[36:]
    prompts, rows, width = x_hbm.shape
    steps, slots, _ = dec_hbm.shape
    dec_rows = steps * slots
    local = wq_v.shape[1]
    nb = width // n_head
    lead = prompts - 1
    seq = lax.axis_index("seq")
    first, _ = partners()
    diag = 3 - lax.axis_index("head")
    front = rows + dec_rows

    cuts = cut_points(width)
    queue = []
    for c in range(len(cuts) - 1):
        at = pl.ds(cuts[c], cuts[c + 1] - cuts[c])
        queue.append(
            [
                pltpu.make_async_copy(
                    x_hbm.at[lead, :, at], x_v.at[pl.ds(0, rows), at], x_sem.at[0, c]
                ),
                pltpu.make_async_copy(
                    x_hbm.at[0, :, at], x_v.at[pl.ds(front, rows), at], x_sem.at[1, c]
                ),
                pltpu.make_async_copy(wk_hbm.at[at], wkv_v.at[at, pl.ds(0, HD)], wkv_sem.at[0, c]),
                pltpu.make_async_copy(wv_hbm.at[at], wkv_v.at[at, pl.ds(HD, HD)], wkv_sem.at[1, c]),
                pltpu.make_async_copy(wq_hbm.at[at], wq_v.at[at], wq_sem.at[c]),
            ]
        )
    small = [
        pltpu.make_async_copy(src, dst, small_sem.at[i])
        for i, (src, dst) in enumerate(
            [(plen_h, plen), (qg_h, qg), (kg_h, kg), (table_h, table), (adm_h, adm), (clen_h, clen)]
        )
    ]
    dec_copy = pltpu.make_async_copy(dec_hbm, dec_v, dec_sem)
    o_copies = [
        out_copy(wo_hbm, block, nb, wo_v.at[j], wo_sem.at[j]) for j, block in enumerate((diag, first))
    ]
    ahead = 4
    queue += [[copy] for copy in o_copies]
    for copy in [dec_copy] + queue[0] + small:
        copy.start()
    for group in queue[1:ahead]:
        for copy in group:
            copy.start()
    for copy in small:
        copy.wait()
    bias_v[...] = mask_bias(rows, plen[seq * prompts + lead])
    dec_copy.wait()
    for t in range(steps):
        flat_v[t * slots : (t + 1) * slots, :] = dec_v[t].astype(F32)
    x_v[rows:front, :] = flat_v[...].astype(BF)
    for c in range(len(cuts) - 1):
        for copy in queue[c]:
            copy.wait()
        if c + ahead < len(queue):
            for copy in queue[c + ahead]:
                copy.start()
        at = slice(cuts[c], cuts[c + 1])
        kv_part = dot(x_v[:, at], wkv_v[at, :])
        q_part = dot(x_v[:front, at], wq_v[at, :])
        if c == 0:
            raw_kv[...] = kv_part
            raw[...] = q_part
        else:
            raw_kv[...] += kv_part
            raw[...] += q_part
    cos2, sin2 = table[:, :HD], table[:, HD:]
    both = 2 * HD
    base = prompts * both
    whole = pl.ds(0, rows)
    kvs = [pack.at[whole, pl.ds(p * both, both)] for p in range(prompts)]
    for p, start in ((lead, 0), (0, front)):
        at = slice(start, start + rows)
        kvs[p][:, :HD] = rope(norm(raw_kv[at, :HD], kg[...]), cos2, sin2).astype(BF)
        kvs[p][:, HD:] = raw_kv[at, HD:].astype(BF)
    each = rows // n_seq
    to_row = lax.broadcasted_iota(jnp.int32, (rows, rows), 0)
    from_row = lax.broadcasted_iota(jnp.int32, (rows, rows), 1)
    move = jnp.where(from_row == lax.rem(to_row, each) * n_seq + to_row // each, 1.0, 0.0).astype(BF)
    for p, kv in enumerate(kvs):
        moved = dot(move, kv[...]).astype(BF)
        for d in range(n_seq):
            blocks[d, p * each : (p + 1) * each] = moved[d * each : (d + 1) * each]
    half = n_seq // 2
    away = (1 - seq // half) * half
    outs = [
        pltpu.make_async_copy(blocks, blocks_h, out_sem.at[0]),
        pltpu.make_async_copy(blocks.at[pl.ds(away, half)], leave_h, out_sem.at[1]),
    ]
    for copy in outs:
        copy.start()
    places = decode_places(plen, adm, clen, slots, dec_rows)
    dcos2, dsin2 = cos_sin(places, turns(places))
    new_at = slice(rows, front)
    pack[new_at, :] = jnp.zeros((dec_rows, pack.shape[1]), BF)
    pack[new_at, :HD] = rope(norm(raw_kv[new_at, :HD], kg[...]), dcos2, dsin2).astype(BF)
    pack[new_at, HD:both] = raw_kv[new_at, HD:].astype(BF)
    for h in range(local // HD):
        piece = raw[new_at, h * HD : (h + 1) * HD]
        col = base + h * HD
        pack[new_at, col : col + HD] = rope(norm(piece, qg[...]), dcos2, dsin2).astype(BF)
    for copy in o_copies:
        copy.wait()
    mine = pack.at[whole, pl.ds(base, local)]
    pair = 2 * HD
    for j in range(local // pair):
        later = None
        if j % 2 == 0:
            later = dot(x_v[front:, :], wq_v[:, j // 2 * pair : (j // 2 + 1) * pair])
        for h in (2 * j, 2 * j + 1):
            piece = raw[:rows, h * HD : (h + 1) * HD]
            mine[:, h * HD : (h + 1) * HD] = rope(norm(piece, qg[...]), cos2, sin2).astype(BF)
        attention((2 * j, 2 * j + 1), mine, kvs[lead], bias_v, s_v, w_v, mine)
        if later is not None:
            for i in range(2):
                col = base + local + (j + i) * HD
                piece = later[:, i * HD : (i + 1) * HD]
                pack[:rows, col : col + HD] = rope(norm(piece, qg[...]), cos2, sin2).astype(BF)
    outs.append(pltpu.make_async_copy(pack, pack_h, out_sem.at[2]))
    outs[-1].start()
    hb = nb // 2
    for j in range(4):
        at = pl.ds(j * hb, hb)
        send[:, at] = dot(mine[...], wo_v[j // 2, :, (j % 2) * hb : (j % 2 + 1) * hb]).astype(BF)
        outs.append(pltpu.make_async_copy(send.at[:, at], send_h.at[:, at], out_sem.at[3 + j]))
        outs[-1].start()
    for copy in outs:
        copy.wait()


def cut_points(width):
    step = width // 16
    return [step * i for i in (0, 1, 2, 4, 8, 12, 16)]


def project(n_head, n_seq, plen, adm, clen, qg, kg, table, x, dec, wq, wk, wv, wo):
    prompts, rows, width = x.shape
    dec_rows = dec.shape[0] * dec.shape[1]
    local = wq.shape[1]
    nb = width // n_head
    every = prompts * rows + dec_rows
    send = (rows, 2 * nb)
    pack = (rows + dec_rows, 2 * prompts * HD + local + local // 2)
    blocks = (n_seq, prompts * rows // n_seq, 2 * HD)
    chunks = len(cut_points(width)) - 1
    return pl.pallas_call(
        functools.partial(project_kernel, n_head, n_seq),
        out_shape=[
            jax.ShapeDtypeStruct(send, BF),
            jax.ShapeDtypeStruct(pack, BF),
            jax.ShapeDtypeStruct(blocks, BF),
            jax.ShapeDtypeStruct((n_seq // 2,) + blocks[1:], BF),
        ],
        in_specs=[HB] * 12,
        out_specs=[HB] * 4,
        scratch_shapes=[
            pltpu.VMEM((every, width), BF),
            pltpu.VMEM(dec.shape, BF),
            pltpu.VMEM((dec_rows, width), F32),
            pltpu.VMEM((width, 2 * HD), BF),
            pltpu.VMEM((width, local), BF),
            pltpu.VMEM((2, local, nb), BF),
            pltpu.VMEM((rows + dec_rows, local), F32),
            pltpu.VMEM((every, 2 * HD), F32),
            pltpu.VMEM(send, BF),
            pltpu.VMEM(pack, BF),
            pltpu.VMEM(blocks, BF),
            pltpu.SMEM(plen.shape, jnp.int32),
            pltpu.SMEM(adm.shape, jnp.int32),
            pltpu.SMEM(clen.shape, jnp.int32),
            pltpu.VMEM(qg.shape, F32),
            pltpu.VMEM(kg.shape, F32),
            pltpu.VMEM(table.shape, F32),
        ]
        + attention_scratch(rows, local // HD)
        + [
            pltpu.SemaphoreType.DMA((2, chunks)),
            pltpu.SemaphoreType.DMA,
            pltpu.SemaphoreType.DMA((2, chunks)),
            pltpu.SemaphoreType.DMA((chunks,)),
            pltpu.SemaphoreType.DMA((2,)),
            pltpu.SemaphoreType.DMA((6,)),
            pltpu.SemaphoreType.DMA((7,)),
        ],
        compiler_params=pltpu.CompilerParams(vmem_limit_bytes=LIMIT_A * MIB),
        cost_estimate=BRIEF,
        name="project",
    )(plen, adm, clen, qg, kg, table, x, dec, wq, wk, wv, wo)


def second_kernel(n_seq, prompts, *refs):
    plen_h, adm_h, clen_h, qg_h, table_h, pack_h, x_hbm, wq_hbm, cache_h, wo_hbm = refs[:10]
    send, attn, own1, part = refs[10:14]
    pack, x_v, wq_v, q_v, cache, wo_v, plen, adm, clen, qg, table = refs[14:25]
    bias_v, s_v, w_v = refs[25:28]
    pack_sem, small_sem, wo_sem, cache_sem, more_sem = refs[28:]
    rows = attn.shape[0]
    dec_rows = pack.shape[0] - rows
    _, local, nb = wo_v.shape
    seq = lax.axis_index("seq")
    first, second = partners()
    head = lax.axis_index("head")
    pack_copy = pltpu.make_async_copy(pack_h, pack, pack_sem)
    cache_copy = pltpu.make_async_copy(cache_h, cache, cache_sem)
    small = [
        pltpu.make_async_copy(src, dst, small_sem.at[i])
        for i, (src, dst) in enumerate(
            [(plen_h, plen), (adm_h, adm), (clen_h, clen), (qg_h, qg), (table_h, table)]
        )
    ]
    copies = [
        out_copy(wo_hbm, block, nb, wo_v.at[j], wo_sem.at[j])
        for j, block in enumerate((head, second, 3 - head, first))
    ]
    more = [
        pltpu.make_async_copy(x_hbm.at[0], x_v, more_sem.at[0]),
        pltpu.make_async_copy(wq_hbm.at[:, pl.ds(local // 2, local // 2)], wq_v, more_sem.at[1]),
    ]
    for copy in small + [pack_copy] + more + copies[:1]:
        copy.start()
    for copy in small:
        copy.wait()
    bias_v[...] = mask_bias(rows, plen[seq * prompts])
    pack_copy.wait()
    both = 2 * HD
    base = prompts * both
    whole = pl.ds(0, rows)
    kvs = [pack.at[whole, pl.ds(p * both, both)] for p in range(prompts)]
    other = pack.at[whole, pl.ds(base, local)]
    queries = pack.at[whole, pl.ds(base + local, local // 2)]
    hb = nb // 2

    cos2, sin2 = table[:, :HD], table[:, HD:]
    pairs = local // both
    middle = pairs // 2
    for j in range(pairs):
        if j == 1:
            for copy in more:
                copy.wait()
            for copy in copies[1:2] + [cache_copy] + copies[2:]:
                copy.start()
        if j in (1, 2):
            at = slice((j - 1) * both, j * both)
            later = dot(x_v[...], wq_v[:, at])
            for i in range(2):
                piece = later[:, i * HD : (i + 1) * HD]
                col = (j - 1) * both + i * HD
                q_v[:, col : col + HD] = rope(norm(piece, qg[...]), cos2, sin2).astype(BF)
        if j in (2, 3):
            copies[j - 2].wait()
            for i in range(2):
                at = slice(i * hb, (i + 1) * hb)
                to = slice((j - 2) * nb + i * hb, (j - 2) * nb + (i + 1) * hb)
                own1[:, to] = dot(other[...], wo_v[j - 2, :, at]).astype(BF)
        heads = (2 * j, 2 * j + 1)
        if j < middle:
            attention(heads, queries, kvs[0], bias_v, s_v, w_v, attn)
        else:
            attention(heads, q_v, kvs[0], bias_v, s_v, w_v, attn, 2 * middle)
    cache_copy.wait()
    for copy in copies[2:]:
        copy.wait()
    for j in range(2):
        send[:, j * nb : (j + 1) * nb] = dot(attn[...], wo_v[2 + j]).astype(BF)
    decode_attention(
        n_seq, cache.shape[0], plen, adm, clen, pack.at[pl.ds(rows, dec_rows), pl.ds(base, local)],
        pack.at[pl.ds(rows, dec_rows), pl.ds(0, both)], kvs, cache, part,
    )


def second(n_head, n_seq, plen, adm, clen, qg, table, pack, x, wq, cache, wo):
    prompts, rows, _ = x.shape
    local, width = wo.shape
    nb = width // n_head
    dec_rows = pack.shape[0] - rows
    return pl.pallas_call(
        functools.partial(second_kernel, n_seq, prompts),
        out_shape=[
            jax.ShapeDtypeStruct((rows, 2 * nb), BF),
            jax.ShapeDtypeStruct((rows, local), BF),
            jax.ShapeDtypeStruct((rows, 2 * nb), BF),
            jax.ShapeDtypeStruct((dec_rows * (local // HD) + 8, HD), F32),
        ],
        in_specs=[HB] * 10,
        out_specs=[VM] * 4,
        scratch_shapes=[
            pltpu.VMEM(pack.shape, BF),
            pltpu.VMEM((rows, width), BF),
            pltpu.VMEM((width, local // 2), BF),
            pltpu.VMEM((rows, local // 2), BF),
            pltpu.VMEM(cache.shape, BF),
            pltpu.VMEM((4, local, nb), BF),
            pltpu.SMEM(plen.shape, jnp.int32),
            pltpu.SMEM(adm.shape, jnp.int32),
            pltpu.SMEM(clen.shape, jnp.int32),
            pltpu.VMEM(qg.shape, F32),
            pltpu.VMEM(table.shape, F32),
        ]
        + attention_scratch(rows, local // HD)
        + [
            pltpu.SemaphoreType.DMA,
            pltpu.SemaphoreType.DMA((5,)),
            pltpu.SemaphoreType.DMA((4,)),
            pltpu.SemaphoreType.DMA,
            pltpu.SemaphoreType.DMA((2,)),
        ],
        compiler_params=pltpu.CompilerParams(vmem_limit_bytes=LIMIT_B * MIB),
        cost_estimate=BRIEF,
        name="second",
    )(plen, adm, clen, qg, table, pack, x, wq, cache, wo)


def third_kernel(attn, wo_hbm, own, wo_a, wo_b, wo_sem):
    nb = wo_a.shape[2]
    first, second = partners()
    head = lax.axis_index("head")
    wo_v = [wo_a.at[0], wo_a.at[1], wo_b.at[0], wo_b.at[1]]
    copies = [
        out_copy(wo_hbm, block, nb, wo_v[j], wo_sem.at[j])
        for j, block in enumerate((head, second, 3 - head, first))
    ]
    for copy in copies:
        copy.start()
    for j in range(2):
        copies[j].wait()
        own[:, j * nb : (j + 1) * nb] = dot(attn[...], wo_v[j][...]).astype(BF)
    for copy in copies[2:]:
        copy.wait()


def third(n_head, attn, wo):
    rows = attn.shape[0]
    local, width = wo.shape
    nb = width // n_head
    return pl.pallas_call(
        third_kernel,
        out_shape=[jax.ShapeDtypeStruct((rows, 2 * nb), BF)]
        + [jax.ShapeDtypeStruct((2, local, nb), BF)] * 2,
        in_specs=[VM, HB],
        out_specs=[VM] * 3,
        scratch_shapes=[pltpu.SemaphoreType.DMA((4,))],
        compiler_params=pltpu.CompilerParams(vmem_limit_bytes=LIMIT_C * MIB),
        cost_estimate=BRIEF,
        name="third",
    )(attn, wo)


def joined(bit, mine, other):
    count = mine.shape[0] - 8
    swap = lax.rem(lax.axis_index("seq") // bit, 2) == 1
    one, two = mine[...], other[...]
    low = jnp.where(swap, two, one)
    high = jnp.where(swap, one, two)
    eye = unit(count)

    def column(row):
        return jnp.sum(jnp.where(eye, row, 0.0), axis=1, keepdims=True)

    row_a, row_b = low[count : count + 1, :], high[count : count + 1, :]
    best = jnp.maximum(row_a, row_b)
    scale_a, scale_b = jnp.exp2(row_a - best), jnp.exp2(row_b - best)
    total = scale_a + scale_b
    inverse = 1.0 / total
    mixed = low[:count] * column(scale_a * inverse) + high[:count] * column(scale_b * inverse)
    return mixed, best + jnp.log2(total)


def range_start(seq, size):
    return seq // size * size


def range_start(seq, size):
    return seq // size * size


def join_kernel(bit, mine, other, out):
    count = mine.shape[0] - 8
    mixed, level = joined(bit, mine, other)
    out[:count, :] = mixed
    out[count : count + 1, :] = level


def join(bit, mine, other):
    return pl.pallas_call(
        functools.partial(join_kernel, bit),
        out_shape=jax.ShapeDtypeStruct(mine.shape, F32),
        in_specs=[VM] * 2,
        out_specs=VM,
        compiler_params=pltpu.CompilerParams(vmem_limit_bytes=8 * MIB),
        cost_estimate=BRIEF,
        name="join_%d" % bit,
    )(mine, other)


def hop_kernel(bit, *refs):
    held, leave = refs[:-1], refs[-1]
    seq = lax.axis_index("seq")
    size = bit // 2
    target = range_start(seq, bit) + size * (1 - lax.rem(seq // size, 2))
    at = 0
    for array in held:
        sources, dests = array.shape[:2]
        skip = target - range_start(seq, dests)
        for k in range(sources):
            leave[at] = array[k, pl.ds(skip, size)]
            at += 1


def hop(bit, held):
    sources = sum(array.shape[0] for array in held)
    return pl.pallas_call(
        functools.partial(hop_kernel, bit),
        out_shape=jax.ShapeDtypeStruct((sources, bit // 2) + held[0].shape[2:], BF),
        in_specs=[VM] * len(held),
        out_specs=VM,
        compiler_params=pltpu.CompilerParams(vmem_limit_bytes=8 * MIB),
        cost_estimate=BRIEF,
        name="hop_%d" % bit,
    )(*held)


def pass_on_kernel(own, got, on):
    nb = on.shape[1]
    on[...] = (own[:, nb:].astype(F32) + got[:, :nb].astype(F32)).astype(BF)


def pass_on(p, own, got):
    rows, both = got.shape
    return pl.pallas_call(
        pass_on_kernel,
        out_shape=jax.ShapeDtypeStruct((rows, both // 2), BF),
        in_specs=[VM] * 2,
        out_specs=VM,
        compiler_params=pltpu.CompilerParams(vmem_limit_bytes=8 * MIB),
        cost_estimate=BRIEF,
        name="pass_on_%d" % p,
    )(own, got)


def decode_out_kernel(bit, mine, other, wo_a, wo_b, *outs):
    count = mine.shape[0] - 8
    rows = outs[0].shape[0]
    mixed, _ = joined(bit, mine, other)
    mixed = mixed.astype(BF)
    flat = jnp.concatenate([mixed[i * rows : (i + 1) * rows] for i in range(count // rows)], axis=1)
    for j, out in enumerate(outs):
        out[...] = dot(flat, (wo_a, wo_b)[j // 2][j % 2]).astype(BF)


def decode_project(bit, dec_rows, mine, other, wo_a, wo_b):
    nb = wo_a.shape[2]
    return pl.pallas_call(
        functools.partial(decode_out_kernel, bit),
        out_shape=[jax.ShapeDtypeStruct((dec_rows, nb), BF)] * 4,
        in_specs=[VM] * 4,
        out_specs=[VM] * 4,
        compiler_params=pltpu.CompilerParams(vmem_limit_bytes=16 * MIB),
        cost_estimate=BRIEF,
        name="decode_project",
    )(mine, other, wo_a, wo_b)


def sum_parts(stage, out, sems, own, got, last):
    rows, nb = last.shape
    step = rows // 2
    copies = []
    for i in range(2):
        at = pl.ds(i * step, step)
        stage[at] = (
            own[at, :nb].astype(F32) + got[at, nb:].astype(F32) + last[at].astype(F32)
        ).astype(BF)
        copies.append(pltpu.make_async_copy(stage.at[at], out.at[at], sems.at[i]))
        copies[-1].start()
    return copies


def finish_first_kernel(p, bits, own, got, last, *refs):
    held, (out, handed, stage, sems, keep_sem) = refs[: len(bits) + 1], refs[len(bits) + 1 :]
    seq = lax.axis_index("seq")
    copies = []
    sources = [0]
    for j, array in enumerate(held):
        if j:
            sources = sources + [bits[j - 1] ^ source for source in sources]
        for k in range(array.shape[0]):
            source = seq ^ sources[len(copies)]
            copies.append(
                pltpu.make_async_copy(
                    array.at[k, seq - range_start(seq, array.shape[1])],
                    handed.at[source],
                    keep_sem.at[len(copies)],
                )
            )
            copies[-1].start()
    for copy in sum_parts(stage, out.at[p], sems, own, got, last) + copies:
        copy.wait()


def finish_first(p, prompts, bits, own, got, last, held):
    rows, nb = last.shape
    n_seq = held[0].shape[1]
    return pl.pallas_call(
        functools.partial(finish_first_kernel, p, bits),
        out_shape=[
            jax.ShapeDtypeStruct((prompts, rows, nb), BF),
            jax.ShapeDtypeStruct((n_seq,) + held[0].shape[2:], BF),
        ],
        in_specs=[VM] * (3 + len(held)),
        out_specs=[HB] * 2,
        scratch_shapes=[
            pltpu.VMEM((rows, nb), BF),
            pltpu.SemaphoreType.DMA((2,)),
            pltpu.SemaphoreType.DMA((n_seq,)),
        ],
        compiler_params=pltpu.CompilerParams(vmem_limit_bytes=8 * MIB),
        cost_estimate=BRIEF,
        name="finish_%d" % p,
    )(own, got, last, *held)


def finish_last_kernel(p, own, got, last, _, out, stage, sems):
    for copy in sum_parts(stage, out.at[p], sems, own, got, last):
        copy.wait()


def finish_last(p, own, got, last, partial):
    rows, nb = last.shape
    return pl.pallas_call(
        functools.partial(finish_last_kernel, p),
        out_shape=jax.ShapeDtypeStruct(partial.shape, BF),
        in_specs=[VM] * 3 + [HB],
        out_specs=HB,
        scratch_shapes=[pltpu.VMEM((rows, nb), BF), pltpu.SemaphoreType.DMA((2,))],
        input_output_aliases={3: 0},
        compiler_params=pltpu.CompilerParams(vmem_limit_bytes=8 * MIB),
        cost_estimate=BRIEF,
        name="finish_%d" % p,
    )(own, got, last, partial)


def decode_sum_kernel(slots, *refs):
    pieces, out = refs[:-1], refs[-1]
    total = pieces[0][...].astype(F32)
    for piece in pieces[1:]:
        total = total + piece[...].astype(F32)
    for t in range(out.shape[0]):
        out[t] = total[t * slots : (t + 1) * slots].astype(BF)


def decode_sum(steps, slots, pieces):
    return pl.pallas_call(
        functools.partial(decode_sum_kernel, slots),
        out_shape=jax.ShapeDtypeStruct((steps, slots, pieces[0].shape[1]), BF),
        in_specs=[VM] * len(pieces),
        out_specs=VM,
        compiler_params=pltpu.CompilerParams(vmem_limit_bytes=8 * MIB),
        cost_estimate=BRIEF,
        name="decode_sum",
    )(*pieces)


def after(value, other):
    return lax.optimization_barrier((value, other))[0]


def local(
    prompts, prompt_len, admitted, cache_len, cache_kv, dec_tokens, w_query, w_key, w_value, w_out, q_gain, k_gain
):
    n_seq = lax.axis_size("seq")
    n_head = lax.axis_size("head")
    pr_dev, rows, width = prompts.shape
    steps, slots, _ = dec_tokens.shape
    dec_rows = steps * slots
    each = rows // n_seq
    qg, kg = q_gain.reshape(1, HD), k_gain.reshape(1, HD)
    def head_move(value, masks):
        pairs = [
            (h * n_seq + s, (h ^ masks[s % 2]) * n_seq + s)
            for h in range(n_head)
            for s in range(n_seq)
        ]
        return lax.ppermute(value, ("head", "seq"), pairs)

    def seq_move(value, bit):
        return lax.ppermute(value, "seq", [(i, i ^ bit) for i in range(n_seq)])

    bits = []
    while 2 ** len(bits) < n_seq:
        bits.append(2 ** len(bits))
    bits = bits[::-1]

    table = jnp.asarray(prompt_table(rows))
    scalars = (prompt_len, admitted, cache_len)
    send1, pack, blocks, leave = project(
        n_head, n_seq, *scalars, qg, kg, table, prompts, dec_tokens, w_query, w_key, w_value, w_out
    )
    got1 = head_move(send1, (1, 2))
    arrived = seq_move(leave, bits[0])
    send0, attn0, own1, part = second(
        n_head, n_seq, *scalars, qg, table, pack, prompts, w_query, cache_kv[0], w_out
    )
    send0, arrived = lax.optimization_barrier((send0, arrived))
    got0 = head_move(send0, (1, 2))
    other = seq_move(part, bits[0])
    own0, *wo = third(n_head, attn0, w_out)
    other, got1 = lax.optimization_barrier((other, got1, own0))[:2]
    for i, bit in enumerate(bits[:-1]):
        part = join(bit, part, other)
        other = seq_move(part, bits[i + 1])
    held = [blocks[None], after(arrived, part)[None]]
    leave = hop(bits[0], held)
    held.append(seq_move(leave, bits[1]))
    on1 = pass_on(1, own1, after(got1, part))
    last1 = head_move(on1, (2, 1))
    got0, other, held[-1] = lax.optimization_barrier((got0, other, held[-1], on1))[:3]
    on0 = pass_on(0, own0, got0)
    last0 = head_move(on0, (2, 1))
    held[-1] = after(held[-1], on0)
    for i, bit in enumerate(bits[1:-1]):
        leave = hop(bit, held)
        held.append(seq_move(leave, bits[i + 2]))
    other = lax.optimization_barrier((other, on0, leave))[0]
    pieces = decode_project(bits[-1], dec_rows, part, other, *wo)
    pieces = [
        pieces[0],
        head_move(pieces[1], (2, 1)),
        head_move(pieces[2], (3, 3)),
        head_move(pieces[3], (1, 2)),
    ]
    partial, handed = finish_first(1, pr_dev, bits, own1, got1, last1, held)
    prefill_out = finish_last(0, own0, got0, last0, partial)
    pieces[1] = after(pieces[1], prefill_out)
    decode_out = decode_sum(steps, slots, pieces)
    return (prefill_out, handed.reshape(1, pr_dev * n_seq, each, 2 * HD), decode_out)


def solution(mesh):
    placed = (
        P("seq", None, None),
        P(),
        P(),
        P(),
        P("head", None, "seq", None),
        P(),
        P(None, "head"),
        P(None, "head"),
        P(None, "head"),
        P("head", None),
        P(),
        P(),
    )
    return jax.shard_map(
        local,
        mesh=mesh,
        in_specs=placed,
        out_specs=(P("seq", None, "head"), P("head", None, "seq", None), P(None, None, "head")),
        check_vma=False,
    )
```

```python
import functools

import jax
import jax.numpy as jnp
import numpy as np
from jax import lax
from jax.experimental import pallas as pl
from jax.experimental.pallas import tpu as pltpu
from jax.sharding import PartitionSpec as P

HD = 128
EPS = 1e-06
THETA = 1000000.0
NEG = -1e30
LOG2E = 1.4426950408889634
SCALE = HD**-0.5
C2 = SCALE * LOG2E
BF = jnp.bfloat16
F32 = jnp.float32
HB = pl.BlockSpec(memory_space=pltpu.HBM)
VM = pl.BlockSpec(memory_space=pltpu.VMEM)
BRIEF = pl.CostEstimate(flops=1, bytes_accessed=1, transcendentals=0)
MIB = 1024 * 1024
LIMIT_A = 60
LIMIT_B = 50
LIMIT_C = 42


def frequencies():
    half = HD // 2
    freq = np.float32(THETA) ** (-np.arange(half, dtype=np.float32) / np.float32(half))
    return freq.astype(np.float32)


def turns(places):
    lane = lax.broadcasted_iota(jnp.int32, places.shape, 1)
    freq = jnp.zeros(places.shape, F32)
    spot = lax.rem(lane, HD // 2)
    for i, value in enumerate(frequencies()):
        freq = jnp.where(spot == i, float(value), freq)
    return freq


def cos_sin(places, freq):
    angle = places.astype(F32) * freq
    lane = lax.broadcasted_iota(jnp.int32, places.shape, 1)
    return jnp.cos(angle), jnp.where(lane < HD // 2, -1.0, 1.0) * jnp.sin(angle)


def prompt_table(length):
    angle = np.arange(length, dtype=np.float32)[:, None] * frequencies()[None, :]
    cosine, sine = np.cos(angle), np.sin(angle)
    return np.concatenate([cosine, cosine, -sine, sine], axis=1).astype(np.float32)


def dot(a, b):
    return jnp.dot(a, b, preferred_element_type=F32)


def dot_nt(a, b):
    return lax.dot_general(a, b, (((1,), (1,)), ((), ())), preferred_element_type=F32)


def norm(values, gain):
    square = jnp.mean(values * values, axis=-1, keepdims=True)
    return values * lax.rsqrt(square + EPS) * gain


def rope(values, cos2, sin2):
    return values * cos2 + pltpu.roll(values, HD // 2, 1) * sin2


def effective_lengths(plen, adm, clen, slots):
    out = []
    for r in range(slots):
        taken = adm[r]
        out.append(jnp.where(taken >= 0, plen[jnp.maximum(taken, 0)], clen[r]))
    return out


def by_slot(index, values):
    result = jnp.full(index.shape, values[0])
    for r in range(1, len(values)):
        result = jnp.where(index == r, values[r], result)
    return result


def partners():
    head, seq = lax.axis_index("head"), lax.axis_index("seq")
    flip_x = head + 1 - 2 * lax.rem(head, 2)
    flip_y = lax.rem(head + 2, 4)
    even = lax.rem(seq, 2) == 0
    return jnp.where(even, flip_x, flip_y), jnp.where(even, flip_y, flip_x)


def out_copy(wo_hbm, block, nb, dest, sem):
    return pltpu.make_async_copy(
        wo_hbm.at[:, pl.ds(pl.multiple_of(block * nb, nb), nb)], dest, sem
    )


def mask_bias(rows, length):
    row_at = lax.broadcasted_iota(jnp.int32, (rows, rows), 0)
    col_at = lax.broadcasted_iota(jnp.int32, (rows, rows), 1)
    return jnp.where((col_at <= row_at) & (col_at < length), 0.0, NEG).astype(F32)


def attention(heads, queries, kv, bias_v, s_v, w_v, attn, skip=0):
    rows = kv.shape[0]
    half = rows // 2
    quarter = rows // 4
    for h in heads:
        at = slice((h - skip) * HD, (h - skip + 1) * HD)
        s_v[h, :half, :half] = dot_nt(queries[:half, at], kv[:half, :HD])
        s_v[h, half:, :] = dot_nt(queries[half:, at], kv[:, :HD])
    for h in heads:
        for block in range(4):
            at = slice(block * quarter, (block + 1) * quarter)
            keys = half if block < 2 else rows
            scores = s_v[h, at, :keys] + bias_v[at, :keys]
            top = jnp.max(scores, axis=-1, keepdims=True)
            expo = jnp.exp2((scores - top) * C2)
            total = jnp.sum(expo, axis=-1, keepdims=True)
            w_v[h, at, :keys] = (expo * (1.0 / total)).astype(BF)
    for h in heads:
        at = slice(h * HD, (h + 1) * HD)
        attn[:half, at] = dot(w_v[h, :half, :half], kv[:half, HD:]).astype(BF)
        attn[half:, at] = dot(w_v[h, half:, :], kv[:, HD:]).astype(BF)


def attention_scratch(rows, heads):
    return [
        pltpu.VMEM((rows, rows), F32),
        pltpu.VMEM((heads, rows, rows), F32),
        pltpu.VMEM((heads, rows, rows), BF),
    ]


def unit(count):
    return lax.broadcasted_iota(jnp.int32, (count, count), 0) == lax.broadcasted_iota(
        jnp.int32, (count, count), 1
    )


def decode_places(plen, adm, clen, slots, dec_rows):
    eff = effective_lengths(plen, adm, clen, slots)
    row = lax.broadcasted_iota(jnp.int32, (dec_rows, HD), 0)
    return by_slot(lax.rem(row, slots), eff) + row // slots


def decode_attention(n_seq, slots, plen, adm, clen, rotated, new, kvs, cache, part):
    seq = lax.axis_index("seq")
    dec_rows = rotated.shape[0]
    width = cache.shape[1]
    rows = kvs[0].shape[0]
    new_key, new_value = new[:, :HD], new[:, HD:]
    queries = jnp.concatenate(
        [rotated[:, h * HD : (h + 1) * HD] for h in range(rotated.shape[1] // HD)], axis=0
    )
    count = queries.shape[0]

    row = lax.rem(lax.broadcasted_iota(jnp.int32, (count, 1), 0), dec_rows)
    slot, step = lax.rem(row, slots), row // slots
    taken = by_slot(slot, [adm[r] for r in range(slots)])
    scores, masks, values = [], [], []
    at = lax.broadcasted_iota(jnp.int32, (1, width), 1) * n_seq + seq
    for r in range(slots):
        limit = jnp.where(adm[r] >= 0, 0, clen[r])
        masks.append((slot == r) & (at < limit))
        scores.append(dot_nt(queries, cache[r, :, :HD]))
        values.append(cache[r, :, HD:])
    spot = lax.broadcasted_iota(jnp.int32, (1, rows), 1)
    for p, kv in enumerate(kvs):
        prompt = seq * len(kvs) + p
        masks.append((taken == prompt) & (spot < plen[prompt]))
        scores.append(dot_nt(queries, kv[:, :HD]))
        values.append(kv[:, HD:])
    other = lax.broadcasted_iota(jnp.int32, (1, dec_rows), 1)
    first = jnp.where(seq == 0, 1, 0)
    masks.append(
        (lax.rem(other, slots) == slot) & (other // slots <= step) & (first + 0 * other > 0)
    )
    scores.append(dot_nt(queries, new_key))
    values.append(new_value)

    top = jnp.full((count, 1), NEG, F32)
    scores = [jnp.where(mask, score, NEG) for mask, score in zip(masks, scores)]
    for score in scores:
        top = jnp.maximum(top, jnp.max(score, axis=-1, keepdims=True))
    total = jnp.zeros((count, 1), F32)
    acc = jnp.zeros((count, HD), F32)
    for mask, score, value in zip(masks, scores, values):
        expo = jnp.where(mask, jnp.exp2((score - top) * C2), 0.0)
        total = total + jnp.sum(expo, axis=-1, keepdims=True)
        acc = acc + dot(expo.astype(BF), value)
    some = total > 0.0
    safe = jnp.where(some, total, 1.0)
    part[:count, :] = acc * (1.0 / safe)
    level = jnp.where(some, top * C2 + jnp.log2(safe), NEG)
    part[count : count + 1, :] = jnp.sum(jnp.where(unit(count), level, 0.0), axis=0, keepdims=True)


def project_kernel(n_head, n_seq, *refs):
    plen_h, adm_h, clen_h, qg_h, kg_h, table_h, x_hbm, dec_hbm, wq_hbm, wk_hbm, wv_hbm, wo_hbm = refs[:12]
    pass_h, keep_h, pack_h, blocks_h, leave_h = refs[12:17]
    x_v, dec_v, flat_v, wkv_v, wq_v, wo_v, raw, raw_kv, send, pack, blocks = refs[17:28]
    plen, adm, clen, qg, kg, table = refs[28:34]
    bias_v, s_v, w_v = refs[34:37]
    x_sem, dec_sem, wkv_sem, wq_sem, wo_sem, small_sem, out_sem = refs[37:]
    prompts, rows, width = x_hbm.shape
    steps, slots, _ = dec_hbm.shape
    dec_rows = steps * slots
    local = wq_v.shape[1]
    nb = width // n_head
    lead = prompts - 1
    seq = lax.axis_index("seq")
    first, _ = partners()
    diag = 3 - lax.axis_index("head")
    front = rows + dec_rows

    cuts = cut_points(width)
    queue = []
    for c in range(len(cuts) - 1):
        at = pl.ds(cuts[c], cuts[c + 1] - cuts[c])
        queue.append(
            [
                pltpu.make_async_copy(
                    x_hbm.at[lead, :, at], x_v.at[pl.ds(0, rows), at], x_sem.at[0, c]
                ),
                pltpu.make_async_copy(
                    x_hbm.at[0, :, at], x_v.at[pl.ds(front, rows), at], x_sem.at[1, c]
                ),
                pltpu.make_async_copy(wk_hbm.at[at], wkv_v.at[at, pl.ds(0, HD)], wkv_sem.at[0, c]),
                pltpu.make_async_copy(wv_hbm.at[at], wkv_v.at[at, pl.ds(HD, HD)], wkv_sem.at[1, c]),
                pltpu.make_async_copy(wq_hbm.at[at], wq_v.at[at], wq_sem.at[c]),
            ]
        )
    small = [
        pltpu.make_async_copy(src, dst, small_sem.at[i])
        for i, (src, dst) in enumerate(
            [(plen_h, plen), (qg_h, qg), (kg_h, kg), (table_h, table), (adm_h, adm), (clen_h, clen)]
        )
    ]
    dec_copy = pltpu.make_async_copy(dec_hbm, dec_v, dec_sem)
    o_copies = [
        out_copy(wo_hbm, block, nb, wo_v.at[j], wo_sem.at[j]) for j, block in enumerate((diag, first))
    ]
    ahead = 4
    queue += [[copy] for copy in o_copies]
    for copy in [dec_copy] + queue[0] + small:
        copy.start()
    for group in queue[1:ahead]:
        for copy in group:
            copy.start()
    for copy in small:
        copy.wait()
    bias_v[...] = mask_bias(rows, plen[seq * prompts + lead])
    dec_copy.wait()
    for t in range(steps):
        flat_v[t * slots : (t + 1) * slots, :] = dec_v[t].astype(F32)
    x_v[rows:front, :] = flat_v[...].astype(BF)
    for c in range(len(cuts) - 1):
        for copy in queue[c]:
            copy.wait()
        if c + ahead < len(queue):
            for copy in queue[c + ahead]:
                copy.start()
        at = slice(cuts[c], cuts[c + 1])
        kv_part = dot(x_v[:, at], wkv_v[at, :])
        q_part = dot(x_v[:front, at], wq_v[at, :])
        if c == 0:
            raw_kv[...] = kv_part
            raw[...] = q_part
        else:
            raw_kv[...] += kv_part
            raw[...] += q_part
    cos2, sin2 = table[:, :HD], table[:, HD:]
    both = 2 * HD
    base = prompts * both
    whole = pl.ds(0, rows)
    kvs = [pack.at[whole, pl.ds(p * both, both)] for p in range(prompts)]
    for p, start in ((lead, 0), (0, front)):
        at = slice(start, start + rows)
        kvs[p][:, :HD] = rope(norm(raw_kv[at, :HD], kg[...]), cos2, sin2).astype(BF)
        kvs[p][:, HD:] = raw_kv[at, HD:].astype(BF)
    each = rows // n_seq
    to_row = lax.broadcasted_iota(jnp.int32, (rows, rows), 0)
    from_row = lax.broadcasted_iota(jnp.int32, (rows, rows), 1)
    move = jnp.where(from_row == lax.rem(to_row, each) * n_seq + to_row // each, 1.0, 0.0).astype(BF)
    for p, kv in enumerate(kvs):
        moved = dot(move, kv[...]).astype(BF)
        for d in range(n_seq):
            blocks[d, p * each : (p + 1) * each] = moved[d * each : (d + 1) * each]
    half = n_seq // 2
    away = (1 - seq // half) * half
    outs = [
        pltpu.make_async_copy(blocks, blocks_h, out_sem.at[0]),
        pltpu.make_async_copy(blocks.at[pl.ds(away, half)], leave_h, out_sem.at[1]),
    ]
    for copy in outs:
        copy.start()
    places = decode_places(plen, adm, clen, slots, dec_rows)
    dcos2, dsin2 = cos_sin(places, turns(places))
    new_at = slice(rows, front)
    pack[new_at, :] = jnp.zeros((dec_rows, pack.shape[1]), BF)
    pack[new_at, :HD] = rope(norm(raw_kv[new_at, :HD], kg[...]), dcos2, dsin2).astype(BF)
    pack[new_at, HD:both] = raw_kv[new_at, HD:].astype(BF)
    for h in range(local // HD):
        piece = raw[new_at, h * HD : (h + 1) * HD]
        col = base + h * HD
        pack[new_at, col : col + HD] = rope(norm(piece, qg[...]), dcos2, dsin2).astype(BF)
    for copy in o_copies:
        copy.wait()
    mine = pack.at[whole, pl.ds(base, local)]
    pair = 2 * HD
    for j in range(local // pair):
        later = dot(x_v[front:, :], wq_v[:, j * pair : (j + 1) * pair])
        for h in (2 * j, 2 * j + 1):
            piece = raw[:rows, h * HD : (h + 1) * HD]
            mine[:, h * HD : (h + 1) * HD] = rope(norm(piece, qg[...]), cos2, sin2).astype(BF)
        attention((2 * j, 2 * j + 1), mine, kvs[lead], bias_v, s_v, w_v, mine)
        for i in range(2):
            col = base + local + (2 * j + i) * HD
            piece = later[:, i * HD : (i + 1) * HD]
            pack[:rows, col : col + HD] = rope(norm(piece, qg[...]), cos2, sin2).astype(BF)
    outs.append(pltpu.make_async_copy(pack, pack_h, out_sem.at[2]))
    outs[-1].start()
    hb = nb // 2
    for j in range(4):
        at = pl.ds(j % 2 * hb, hb)
        send[j // 2, :, at] = dot(mine[...], wo_v[j // 2, :, at]).astype(BF)
        target = (pass_h, keep_h)[j // 2]
        outs.append(
            pltpu.make_async_copy(send.at[j // 2, :, at], target.at[:, at], out_sem.at[3 + j])
        )
        outs[-1].start()
    for copy in outs:
        copy.wait()


def cut_points(width):
    step = width // 16
    return [step * i for i in (0, 1, 2, 4, 8, 12, 16)]


def project(n_head, n_seq, plen, adm, clen, qg, kg, table, x, dec, wq, wk, wv, wo):
    prompts, rows, width = x.shape
    dec_rows = dec.shape[0] * dec.shape[1]
    local = wq.shape[1]
    nb = width // n_head
    every = prompts * rows + dec_rows
    send = (rows, nb)
    pack = (rows + dec_rows, 2 * prompts * HD + prompts * local)
    blocks = (n_seq, prompts * rows // n_seq, 2 * HD)
    chunks = len(cut_points(width)) - 1
    return pl.pallas_call(
        functools.partial(project_kernel, n_head, n_seq),
        out_shape=[
            jax.ShapeDtypeStruct(send, BF),
            jax.ShapeDtypeStruct(send, BF),
            jax.ShapeDtypeStruct(pack, BF),
            jax.ShapeDtypeStruct(blocks, BF),
            jax.ShapeDtypeStruct((n_seq // 2,) + blocks[1:], BF),
        ],
        in_specs=[HB] * 12,
        out_specs=[HB] * 5,
        scratch_shapes=[
            pltpu.VMEM((every, width), BF),
            pltpu.VMEM(dec.shape, BF),
            pltpu.VMEM((dec_rows, width), F32),
            pltpu.VMEM((width, 2 * HD), BF),
            pltpu.VMEM((width, local), BF),
            pltpu.VMEM((2, local, nb), BF),
            pltpu.VMEM((rows + dec_rows, local), F32),
            pltpu.VMEM((every, 2 * HD), F32),
            pltpu.VMEM((2,) + send, BF),
            pltpu.VMEM(pack, BF),
            pltpu.VMEM(blocks, BF),
            pltpu.SMEM(plen.shape, jnp.int32),
            pltpu.SMEM(adm.shape, jnp.int32),
            pltpu.SMEM(clen.shape, jnp.int32),
            pltpu.VMEM(qg.shape, F32),
            pltpu.VMEM(kg.shape, F32),
            pltpu.VMEM(table.shape, F32),
        ]
        + attention_scratch(rows, local // HD)
        + [
            pltpu.SemaphoreType.DMA((2, chunks)),
            pltpu.SemaphoreType.DMA,
            pltpu.SemaphoreType.DMA((2, chunks)),
            pltpu.SemaphoreType.DMA((chunks,)),
            pltpu.SemaphoreType.DMA((2,)),
            pltpu.SemaphoreType.DMA((6,)),
            pltpu.SemaphoreType.DMA((7,)),
        ],
        compiler_params=pltpu.CompilerParams(vmem_limit_bytes=LIMIT_A * MIB),
        cost_estimate=BRIEF,
        name="project",
    )(plen, adm, clen, qg, kg, table, x, dec, wq, wk, wv, wo)


def second_kernel(n_seq, prompts, *refs):
    plen_h, adm_h, clen_h, pack_h, cache_h, wo_hbm = refs[:6]
    pass_v, keep_v, attn, own1, part = refs[6:11]
    pack, cache, wo_v, plen, adm, clen = refs[11:17]
    bias_v, s_v, w_v = refs[17:20]
    pack_sem, small_sem, wo_sem, cache_sem = refs[20:]
    rows = attn.shape[0]
    dec_rows = pack.shape[0] - rows
    _, local, nb = wo_v.shape
    seq = lax.axis_index("seq")
    first, second = partners()
    head = lax.axis_index("head")
    pack_copy = pltpu.make_async_copy(pack_h, pack, pack_sem)
    cache_copy = pltpu.make_async_copy(cache_h, cache, cache_sem)
    small = [
        pltpu.make_async_copy(src, dst, small_sem.at[i])
        for i, (src, dst) in enumerate([(plen_h, plen), (adm_h, adm), (clen_h, clen)])
    ]
    copies = [
        out_copy(wo_hbm, block, nb, wo_v.at[j], wo_sem.at[j])
        for j, block in enumerate((head, second, 3 - head, first))
    ]
    for copy in small + [pack_copy] + copies[:2] + [cache_copy] + copies[2:]:
        copy.start()
    for copy in small:
        copy.wait()
    bias_v[...] = mask_bias(rows, plen[seq * prompts])
    pack_copy.wait()
    both = 2 * HD
    base = prompts * both
    whole = pl.ds(0, rows)
    kvs = [pack.at[whole, pl.ds(p * both, both)] for p in range(prompts)]
    other = pack.at[whole, pl.ds(base, local)]
    queries = pack.at[whole, pl.ds(base + local, local)]
    hb = nb // 2

    for j in range(local // both):
        if j in (1, 2):
            copies[j - 1].wait()
            for i in range(2):
                at = slice(i * hb, (i + 1) * hb)
                to = slice((j - 1) * nb + i * hb, (j - 1) * nb + (i + 1) * hb)
                own1[:, to] = dot(other[...], wo_v[j - 1, :, at]).astype(BF)
        attention((2 * j, 2 * j + 1), queries, kvs[0], bias_v, s_v, w_v, attn)
    cache_copy.wait()
    for copy in copies[2:]:
        copy.wait()
    for j, send in enumerate((pass_v, keep_v)):
        send[...] = dot(attn[...], wo_v[2 + j]).astype(BF)
    decode_attention(
        n_seq, cache.shape[0], plen, adm, clen, pack.at[pl.ds(rows, dec_rows), pl.ds(base, local)],
        pack.at[pl.ds(rows, dec_rows), pl.ds(0, both)], kvs, cache, part,
    )


def second(n_head, n_seq, prompts, rows, plen, adm, clen, pack, cache, wo):
    local, width = wo.shape
    nb = width // n_head
    dec_rows = pack.shape[0] - rows
    return pl.pallas_call(
        functools.partial(second_kernel, n_seq, prompts),
        out_shape=[
            jax.ShapeDtypeStruct((rows, nb), BF),
            jax.ShapeDtypeStruct((rows, nb), BF),
            jax.ShapeDtypeStruct((rows, local), BF),
            jax.ShapeDtypeStruct((rows, 2 * nb), BF),
            jax.ShapeDtypeStruct((dec_rows * (local // HD) + 8, HD), F32),
        ],
        in_specs=[HB] * 6,
        out_specs=[VM] * 5,
        scratch_shapes=[
            pltpu.VMEM(pack.shape, BF),
            pltpu.VMEM(cache.shape, BF),
            pltpu.VMEM((4, local, nb), BF),
            pltpu.SMEM(plen.shape, jnp.int32),
            pltpu.SMEM(adm.shape, jnp.int32),
            pltpu.SMEM(clen.shape, jnp.int32),
        ]
        + attention_scratch(rows, local // HD)
        + [
            pltpu.SemaphoreType.DMA,
            pltpu.SemaphoreType.DMA((3,)),
            pltpu.SemaphoreType.DMA((4,)),
            pltpu.SemaphoreType.DMA,
        ],
        compiler_params=pltpu.CompilerParams(vmem_limit_bytes=LIMIT_B * MIB),
        cost_estimate=BRIEF,
        name="second",
    )(plen, adm, clen, pack, cache, wo)


def third_kernel(attn, wo_hbm, own, wo_a, wo_b, wo_sem):
    nb = wo_a.shape[2]
    first, second = partners()
    head = lax.axis_index("head")
    wo_v = [wo_a.at[0], wo_a.at[1], wo_b.at[0], wo_b.at[1]]
    copies = [
        out_copy(wo_hbm, block, nb, wo_v[j], wo_sem.at[j])
        for j, block in enumerate((head, second, 3 - head, first))
    ]
    for copy in copies:
        copy.start()
    for j in range(2):
        copies[j].wait()
        own[:, j * nb : (j + 1) * nb] = dot(attn[...], wo_v[j][...]).astype(BF)
    for copy in copies[2:]:
        copy.wait()


def third(n_head, attn, wo):
    rows = attn.shape[0]
    local, width = wo.shape
    nb = width // n_head
    return pl.pallas_call(
        third_kernel,
        out_shape=[jax.ShapeDtypeStruct((rows, 2 * nb), BF)]
        + [jax.ShapeDtypeStruct((2, local, nb), BF)] * 2,
        in_specs=[VM, HB],
        out_specs=[VM] * 3,
        scratch_shapes=[pltpu.SemaphoreType.DMA((4,))],
        compiler_params=pltpu.CompilerParams(vmem_limit_bytes=LIMIT_C * MIB),
        cost_estimate=BRIEF,
        name="third",
    )(attn, wo)


def joined(bit, mine, other):
    count = mine.shape[0] - 8
    swap = lax.rem(lax.axis_index("seq") // bit, 2) == 1
    one, two = mine[...], other[...]
    low = jnp.where(swap, two, one)
    high = jnp.where(swap, one, two)
    eye = unit(count)

    def column(row):
        return jnp.sum(jnp.where(eye, row, 0.0), axis=1, keepdims=True)

    row_a, row_b = low[count : count + 1, :], high[count : count + 1, :]
    best = jnp.maximum(row_a, row_b)
    scale_a, scale_b = jnp.exp2(row_a - best), jnp.exp2(row_b - best)
    total = scale_a + scale_b
    inverse = 1.0 / total
    mixed = low[:count] * column(scale_a * inverse) + high[:count] * column(scale_b * inverse)
    return mixed, best + jnp.log2(total)


def range_start(seq, size):
    return seq // size * size


def range_start(seq, size):
    return seq // size * size


def join_kernel(bit, mine, other, out):
    count = mine.shape[0] - 8
    mixed, level = joined(bit, mine, other)
    out[:count, :] = mixed
    out[count : count + 1, :] = level


def join(bit, mine, other):
    return pl.pallas_call(
        functools.partial(join_kernel, bit),
        out_shape=jax.ShapeDtypeStruct(mine.shape, F32),
        in_specs=[VM] * 2,
        out_specs=VM,
        compiler_params=pltpu.CompilerParams(vmem_limit_bytes=8 * MIB),
        cost_estimate=BRIEF,
        name="join_%d" % bit,
    )(mine, other)


def hop_kernel(bit, *refs):
    held, leave = refs[:-1], refs[-1]
    seq = lax.axis_index("seq")
    size = bit // 2
    target = range_start(seq, bit) + size * (1 - lax.rem(seq // size, 2))
    at = 0
    for array in held:
        sources, dests = array.shape[:2]
        skip = target - range_start(seq, dests)
        for k in range(sources):
            leave[at] = array[k, pl.ds(skip, size)]
            at += 1


def hop(bit, held):
    sources = sum(array.shape[0] for array in held)
    return pl.pallas_call(
        functools.partial(hop_kernel, bit),
        out_shape=jax.ShapeDtypeStruct((sources, bit // 2) + held[0].shape[2:], BF),
        in_specs=[VM] * len(held),
        out_specs=VM,
        compiler_params=pltpu.CompilerParams(vmem_limit_bytes=8 * MIB),
        cost_estimate=BRIEF,
        name="hop_%d" % bit,
    )(*held)


def pass_on_kernel(own, got, on):
    nb = on.shape[1]
    on[...] = (own[:, nb:].astype(F32) + got[...].astype(F32)).astype(BF)


def pass_on(p, own, got):
    return pl.pallas_call(
        pass_on_kernel,
        out_shape=jax.ShapeDtypeStruct(got.shape, BF),
        in_specs=[VM] * 2,
        out_specs=VM,
        compiler_params=pltpu.CompilerParams(vmem_limit_bytes=8 * MIB),
        cost_estimate=BRIEF,
        name="pass_on_%d" % p,
    )(own, got)


def decode_out_kernel(bit, mine, other, wo_a, wo_b, *outs):
    count = mine.shape[0] - 8
    rows = outs[0].shape[0]
    mixed, _ = joined(bit, mine, other)
    mixed = mixed.astype(BF)
    flat = jnp.concatenate([mixed[i * rows : (i + 1) * rows] for i in range(count // rows)], axis=1)
    for j, out in enumerate(outs):
        out[...] = dot(flat, (wo_a, wo_b)[j // 2][j % 2]).astype(BF)


def decode_project(bit, dec_rows, mine, other, wo_a, wo_b):
    nb = wo_a.shape[2]
    return pl.pallas_call(
        functools.partial(decode_out_kernel, bit),
        out_shape=[jax.ShapeDtypeStruct((dec_rows, nb), BF)] * 4,
        in_specs=[VM] * 4,
        out_specs=[VM] * 4,
        compiler_params=pltpu.CompilerParams(vmem_limit_bytes=16 * MIB),
        cost_estimate=BRIEF,
        name="decode_project",
    )(mine, other, wo_a, wo_b)


def sum_parts(stage, out, sems, own, got, last):
    rows, nb = last.shape
    step = rows // 2
    copies = []
    for i in range(2):
        at = pl.ds(i * step, step)
        stage[at] = (
            own[at, :nb].astype(F32) + got[at].astype(F32) + last[at].astype(F32)
        ).astype(BF)
        copies.append(pltpu.make_async_copy(stage.at[at], out.at[at], sems.at[i]))
        copies[-1].start()
    return copies


def finish_first_kernel(p, bits, own, got, last, *refs):
    held, (out, handed, stage, sems, keep_sem) = refs[: len(bits) + 1], refs[len(bits) + 1 :]
    seq = lax.axis_index("seq")
    copies = []
    sources = [0]
    for j, array in enumerate(held):
        if j:
            sources = sources + [bits[j - 1] ^ source for source in sources]
        for k in range(array.shape[0]):
            source = seq ^ sources[len(copies)]
            copies.append(
                pltpu.make_async_copy(
                    array.at[k, seq - range_start(seq, array.shape[1])],
                    handed.at[source],
                    keep_sem.at[len(copies)],
                )
            )
            copies[-1].start()
    for copy in sum_parts(stage, out.at[p], sems, own, got, last) + copies:
        copy.wait()


def finish_first(p, prompts, bits, own, got, last, held):
    rows, nb = last.shape
    n_seq = held[0].shape[1]
    return pl.pallas_call(
        functools.partial(finish_first_kernel, p, bits),
        out_shape=[
            jax.ShapeDtypeStruct((prompts, rows, nb), BF),
            jax.ShapeDtypeStruct((n_seq,) + held[0].shape[2:], BF),
        ],
        in_specs=[VM] * (3 + len(held)),
        out_specs=[HB] * 2,
        scratch_shapes=[
            pltpu.VMEM((rows, nb), BF),
            pltpu.SemaphoreType.DMA((2,)),
            pltpu.SemaphoreType.DMA((n_seq,)),
        ],
        compiler_params=pltpu.CompilerParams(vmem_limit_bytes=8 * MIB),
        cost_estimate=BRIEF,
        name="finish_%d" % p,
    )(own, got, last, *held)


def finish_last_kernel(p, own, got, last, _, out, stage, sems):
    for copy in sum_parts(stage, out.at[p], sems, own, got, last):
        copy.wait()


def finish_last(p, own, got, last, partial):
    rows, nb = last.shape
    return pl.pallas_call(
        functools.partial(finish_last_kernel, p),
        out_shape=jax.ShapeDtypeStruct(partial.shape, BF),
        in_specs=[VM] * 3 + [HB],
        out_specs=HB,
        scratch_shapes=[pltpu.VMEM((rows, nb), BF), pltpu.SemaphoreType.DMA((2,))],
        input_output_aliases={3: 0},
        compiler_params=pltpu.CompilerParams(vmem_limit_bytes=8 * MIB),
        cost_estimate=BRIEF,
        name="finish_%d" % p,
    )(own, got, last, partial)


def decode_sum_kernel(slots, *refs):
    pieces, out = refs[:-1], refs[-1]
    total = pieces[0][...].astype(F32)
    for piece in pieces[1:]:
        total = total + piece[...].astype(F32)
    for t in range(out.shape[0]):
        out[t] = total[t * slots : (t + 1) * slots].astype(BF)


def decode_sum(steps, slots, pieces):
    return pl.pallas_call(
        functools.partial(decode_sum_kernel, slots),
        out_shape=jax.ShapeDtypeStruct((steps, slots, pieces[0].shape[1]), BF),
        in_specs=[VM] * len(pieces),
        out_specs=VM,
        compiler_params=pltpu.CompilerParams(vmem_limit_bytes=8 * MIB),
        cost_estimate=BRIEF,
        name="decode_sum",
    )(*pieces)


def after(value, other):
    return lax.optimization_barrier((value, other))[0]


def local(
    prompts, prompt_len, admitted, cache_len, cache_kv, dec_tokens, w_query, w_key, w_value, w_out, q_gain, k_gain
):
    n_seq = lax.axis_size("seq")
    n_head = lax.axis_size("head")
    pr_dev, rows, width = prompts.shape
    steps, slots, _ = dec_tokens.shape
    dec_rows = steps * slots
    each = rows // n_seq
    qg, kg = q_gain.reshape(1, HD), k_gain.reshape(1, HD)
    def head_move(value, masks):
        pairs = [
            (h * n_seq + s, (h ^ masks[s % 2]) * n_seq + s)
            for h in range(n_head)
            for s in range(n_seq)
        ]
        return lax.ppermute(value, ("head", "seq"), pairs)

    def seq_move(value, bit):
        return lax.ppermute(value, "seq", [(i, i ^ bit) for i in range(n_seq)])

    bits = []
    while 2 ** len(bits) < n_seq:
        bits.append(2 ** len(bits))
    bits = bits[::-1]

    table = jnp.asarray(prompt_table(rows))
    scalars = (prompt_len, admitted, cache_len)
    pass1, keep1, pack, blocks, leave = project(
        n_head, n_seq, *scalars, qg, kg, table, prompts, dec_tokens, w_query, w_key, w_value, w_out
    )
    pass1 = head_move(pass1, (1, 2))
    keep1 = head_move(keep1, (1, 2))
    arrived = seq_move(leave, bits[0])
    pass0, keep0, attn0, own1, part = second(
        n_head, n_seq, pr_dev, rows, *scalars, pack, cache_kv[0], w_out
    )
    pass0, keep0, arrived = lax.optimization_barrier((pass0, keep0, arrived))
    pass0 = head_move(pass0, (1, 2))
    keep0 = head_move(keep0, (1, 2))
    other = seq_move(part, bits[0])
    own0, *wo = third(n_head, attn0, w_out)
    other, pass1, keep1 = lax.optimization_barrier((other, pass1, keep1, own0))[:3]
    for i, bit in enumerate(bits[:-1]):
        part = join(bit, part, other)
        other = seq_move(part, bits[i + 1])
    held = [blocks[None], after(arrived, part)[None]]
    leave = hop(bits[0], held)
    held.append(seq_move(leave, bits[1]))
    on1 = pass_on(1, own1, after(pass1, part))
    last1 = head_move(on1, (2, 1))
    pass0, keep0, other, held[-1] = lax.optimization_barrier((pass0, keep0, other, held[-1], on1))[:4]
    on0 = pass_on(0, own0, pass0)
    last0 = head_move(on0, (2, 1))
    held[-1] = after(held[-1], on0)
    for i, bit in enumerate(bits[1:-1]):
        leave = hop(bit, held)
        held.append(seq_move(leave, bits[i + 2]))
    other = lax.optimization_barrier((other, on0, leave))[0]
    pieces = decode_project(bits[-1], dec_rows, part, other, *wo)
    pieces = [
        pieces[0],
        head_move(pieces[1], (2, 1)),
        head_move(pieces[2], (3, 3)),
        head_move(pieces[3], (1, 2)),
    ]
    partial, handed = finish_first(1, pr_dev, bits, own1, keep1, last1, held)
    prefill_out = finish_last(0, own0, keep0, last0, partial)
    pieces[1] = after(pieces[1], prefill_out)
    decode_out = decode_sum(steps, slots, pieces)
    return (prefill_out, handed.reshape(1, pr_dev * n_seq, each, 2 * HD), decode_out)


def solution(mesh):
    placed = (
        P("seq", None, None),
        P(),
        P(),
        P(),
        P("head", None, "seq", None),
        P(),
        P(None, "head"),
        P(None, "head"),
        P(None, "head"),
        P("head", None),
        P(),
        P(),
    )
    return jax.shard_map(
        local,
        mesh=mesh,
        in_specs=placed,
        out_specs=(P("seq", None, "head"), P("head", None, "seq", None), P(None, None, "head")),
        check_vma=False,
    )
```

```python
import functools

import jax
import jax.numpy as jnp
import numpy as np
from jax import lax
from jax.experimental import pallas as pl
from jax.experimental.pallas import tpu as pltpu
from jax.sharding import PartitionSpec as P

HD = 128
EPS = 1e-06
THETA = 1000000.0
NEG = -1e30
LOG2E = 1.4426950408889634
SCALE = HD**-0.5
C2 = SCALE * LOG2E
BF = jnp.bfloat16
F32 = jnp.float32
HB = pl.BlockSpec(memory_space=pltpu.HBM)
VM = pl.BlockSpec(memory_space=pltpu.VMEM)
BRIEF = pl.CostEstimate(flops=1, bytes_accessed=1, transcendentals=0)
MIB = 1024 * 1024
LIMIT_A = 60
LIMIT_B = 50
LIMIT_C = 42


def frequencies():
    half = HD // 2
    freq = np.float32(THETA) ** (-np.arange(half, dtype=np.float32) / np.float32(half))
    return freq.astype(np.float32)


def turns(places):
    lane = lax.broadcasted_iota(jnp.int32, places.shape, 1)
    freq = jnp.zeros(places.shape, F32)
    spot = lax.rem(lane, HD // 2)
    for i, value in enumerate(frequencies()):
        freq = jnp.where(spot == i, float(value), freq)
    return freq


def cos_sin(places, freq):
    angle = places.astype(F32) * freq
    lane = lax.broadcasted_iota(jnp.int32, places.shape, 1)
    return jnp.cos(angle), jnp.where(lane < HD // 2, -1.0, 1.0) * jnp.sin(angle)


def prompt_table(length):
    angle = np.arange(length, dtype=np.float32)[:, None] * frequencies()[None, :]
    cosine, sine = np.cos(angle), np.sin(angle)
    return np.concatenate([cosine, cosine, -sine, sine], axis=1).astype(np.float32)


def dot(a, b):
    return jnp.dot(a, b, preferred_element_type=F32)


def dot_nt(a, b):
    return lax.dot_general(a, b, (((1,), (1,)), ((), ())), preferred_element_type=F32)


def norm(values, gain):
    square = jnp.mean(values * values, axis=-1, keepdims=True)
    return values * lax.rsqrt(square + EPS) * gain


def norm_rows(values, gain):
    ones = jnp.ones((HD, HD), BF)
    square = values * values
    high = square.astype(BF)
    low = (square - high.astype(F32)).astype(BF)
    total = dot(high, ones) + dot(low, ones)
    return values * lax.rsqrt(total * (1.0 / HD) + EPS) * gain


def rope(values, cos2, sin2):
    return values * cos2 + pltpu.roll(values, HD // 2, 1) * sin2


def effective_lengths(plen, adm, clen, slots):
    out = []
    for r in range(slots):
        taken = adm[r]
        out.append(jnp.where(taken >= 0, plen[jnp.maximum(taken, 0)], clen[r]))
    return out


def by_slot(index, values):
    result = jnp.full(index.shape, values[0])
    for r in range(1, len(values)):
        result = jnp.where(index == r, values[r], result)
    return result


def partners():
    head, seq = lax.axis_index("head"), lax.axis_index("seq")
    flip_x = head + 1 - 2 * lax.rem(head, 2)
    flip_y = lax.rem(head + 2, 4)
    even = lax.rem(seq, 2) == 0
    return jnp.where(even, flip_x, flip_y), jnp.where(even, flip_y, flip_x)


def out_copy(wo_hbm, block, nb, dest, sem):
    return pltpu.make_async_copy(
        wo_hbm.at[:, pl.ds(pl.multiple_of(block * nb, nb), nb)], dest, sem
    )


def mask_bias(rows, length):
    row_at = lax.broadcasted_iota(jnp.int32, (rows, rows), 0)
    col_at = lax.broadcasted_iota(jnp.int32, (rows, rows), 1)
    return jnp.where((col_at <= row_at) & (col_at < length), 0.0, NEG).astype(F32)


def attention(heads, queries, kv, values, bias_v, s_v, w_v, attn):
    rows = kv.shape[0]
    half = rows // 2
    quarter = rows // 4
    for h in heads:
        at = slice(h * HD, (h + 1) * HD)
        s_v[h, :half, :half] = dot_nt(queries[:half, at], kv[:half, :HD])
        s_v[h, half:, :] = dot_nt(queries[half:, at], kv[:, :HD])
    for h in heads:
        for block in range(4):
            at = slice(block * quarter, (block + 1) * quarter)
            keys = half if block < 2 else rows
            scores = s_v[h, at, :keys] + bias_v[at, :keys]
            top = jnp.max(scores, axis=-1, keepdims=True)
            w_v[h, at, :keys] = jnp.exp2((scores - top) * C2).astype(BF)
    for h in heads:
        at = slice(h * HD, (h + 1) * HD)
        for part, keys in ((slice(0, half), half), (slice(half, rows), rows)):
            mixed = dot(w_v[h, part, :keys], values[:keys])
            attn[part, at] = (mixed[:, :HD] / mixed[:, HD:]).astype(BF)


def attention_scratch(rows, heads):
    return [
        pltpu.VMEM((rows, rows), F32),
        pltpu.VMEM((heads, rows, rows), F32),
        pltpu.VMEM((heads, rows, rows), BF),
        pltpu.VMEM((rows, 2 * HD), BF),
    ]


def unit(count):
    return lax.broadcasted_iota(jnp.int32, (count, count), 0) == lax.broadcasted_iota(
        jnp.int32, (count, count), 1
    )


def decode_places(plen, adm, clen, slots, dec_rows):
    eff = effective_lengths(plen, adm, clen, slots)
    row = lax.broadcasted_iota(jnp.int32, (dec_rows, HD), 0)
    return by_slot(lax.rem(row, slots), eff) + row // slots


def decode_attention(n_seq, slots, plen, adm, clen, rotated, new, kvs, cache, part):
    seq = lax.axis_index("seq")
    dec_rows = rotated.shape[0]
    width = cache.shape[1]
    rows = kvs[0].shape[0]
    new_key, new_value = new[:, :HD], new[:, HD:]
    queries = jnp.concatenate(
        [rotated[:, h * HD : (h + 1) * HD] for h in range(rotated.shape[1] // HD)], axis=0
    )
    count = queries.shape[0]

    row = lax.rem(lax.broadcasted_iota(jnp.int32, (count, 1), 0), dec_rows)
    slot, step = lax.rem(row, slots), row // slots
    taken = by_slot(slot, [adm[r] for r in range(slots)])
    scores, masks, values = [], [], []
    at = lax.broadcasted_iota(jnp.int32, (1, width), 1) * n_seq + seq
    for r in range(slots):
        limit = jnp.where(adm[r] >= 0, 0, clen[r])
        masks.append((slot == r) & (at < limit))
        scores.append(dot_nt(queries, cache[r, :, :HD]))
        values.append(cache[r, :, HD:])
    spot = lax.broadcasted_iota(jnp.int32, (1, rows), 1)
    for p, kv in enumerate(kvs):
        prompt = seq * len(kvs) + p
        masks.append((taken == prompt) & (spot < plen[prompt]))
        scores.append(dot_nt(queries, kv[:, :HD]))
        values.append(kv[:, HD:])
    other = lax.broadcasted_iota(jnp.int32, (1, dec_rows), 1)
    first = jnp.where(seq == 0, 1, 0)
    masks.append(
        (lax.rem(other, slots) == slot) & (other // slots <= step) & (first + 0 * other > 0)
    )
    scores.append(dot_nt(queries, new_key))
    values.append(new_value)

    top = jnp.full((count, 1), NEG, F32)
    scores = [jnp.where(mask, score, NEG) for mask, score in zip(masks, scores)]
    for score in scores:
        top = jnp.maximum(top, jnp.max(score, axis=-1, keepdims=True))
    total = jnp.zeros((count, 1), F32)
    acc = jnp.zeros((count, HD), F32)
    for mask, score, value in zip(masks, scores, values):
        expo = jnp.where(mask, jnp.exp2((score - top) * C2), 0.0)
        total = total + jnp.sum(expo, axis=-1, keepdims=True)
        acc = acc + dot(expo.astype(BF), value)
    some = total > 0.0
    safe = jnp.where(some, total, 1.0)
    part[:count, :] = acc * (1.0 / safe)
    level = jnp.where(some, top * C2 + jnp.log2(safe), NEG)
    part[count : count + 1, :] = jnp.sum(jnp.where(unit(count), level, 0.0), axis=0, keepdims=True)


def project_kernel(n_head, n_seq, *refs):
    plen_h, adm_h, clen_h, qg_h, kg_h, table_h, x_hbm, dec_hbm, wq_hbm, wk_hbm, wv_hbm, wo_hbm = refs[:12]
    send_h, pack_h, blocks_h, leave_h = refs[12:16]
    x_v, dec_v, flat_v, wkv_v, wq_v, wo_v, raw, raw_kv, send, pack, blocks = refs[16:27]
    plen, adm, clen, qg, kg, table = refs[27:33]
    bias_v, s_v, w_v, values = refs[33:37]
    x_sem, dec_sem, wkv_sem, wq_sem, wo_sem, small_sem, out_sem = refs[37:]
    prompts, rows, width = x_hbm.shape
    steps, slots, _ = dec_hbm.shape
    dec_rows = steps * slots
    local = wq_v.shape[1]
    nb = width // n_head
    lead = prompts - 1
    seq = lax.axis_index("seq")
    first, _ = partners()
    diag = 3 - lax.axis_index("head")
    front = rows + dec_rows

    cuts = cut_points(width)
    queue = []
    for c in range(len(cuts) - 1):
        at = pl.ds(cuts[c], cuts[c + 1] - cuts[c])
        queue.append(
            [
                pltpu.make_async_copy(
                    x_hbm.at[lead, :, at], x_v.at[pl.ds(0, rows), at], x_sem.at[0, c]
                ),
                pltpu.make_async_copy(
                    x_hbm.at[0, :, at], x_v.at[pl.ds(front, rows), at], x_sem.at[1, c]
                ),
                pltpu.make_async_copy(wk_hbm.at[at], wkv_v.at[at, pl.ds(0, HD)], wkv_sem.at[0, c]),
                pltpu.make_async_copy(wv_hbm.at[at], wkv_v.at[at, pl.ds(HD, HD)], wkv_sem.at[1, c]),
                pltpu.make_async_copy(wq_hbm.at[at], wq_v.at[at], wq_sem.at[c]),
            ]
        )
    small = [
        pltpu.make_async_copy(src, dst, small_sem.at[i])
        for i, (src, dst) in enumerate(
            [(plen_h, plen), (qg_h, qg), (kg_h, kg), (table_h, table), (adm_h, adm), (clen_h, clen)]
        )
    ]
    dec_copy = pltpu.make_async_copy(dec_hbm, dec_v, dec_sem)
    o_copies = [
        out_copy(wo_hbm, block, nb, wo_v.at[j], wo_sem.at[j]) for j, block in enumerate((diag, first))
    ]
    ahead = 3
    queue += [[copy] for copy in o_copies]
    for copy in [dec_copy] + queue[0] + small:
        copy.start()
    for group in queue[1:ahead]:
        for copy in group:
            copy.start()
    for copy in small:
        copy.wait()
    bias_v[...] = mask_bias(rows, plen[seq * prompts + lead])
    dec_copy.wait()
    for t in range(steps):
        flat_v[t * slots : (t + 1) * slots, :] = dec_v[t].astype(F32)
    x_v[rows:front, :] = flat_v[...].astype(BF)
    for c in range(len(cuts) - 1):
        for copy in queue[c]:
            copy.wait()
        if c + ahead < len(queue):
            for copy in queue[c + ahead]:
                copy.start()
        at = slice(cuts[c], cuts[c + 1])
        kv_part = dot(x_v[:, at], wkv_v[at, :])
        q_part = dot(x_v[:front, at], wq_v[at, :])
        if c == 0:
            raw_kv[...] = kv_part
            raw[...] = q_part
        else:
            raw_kv[...] += kv_part
            raw[...] += q_part
    cos2, sin2 = table[:, :HD], table[:, HD:]
    both = 2 * HD
    base = prompts * both
    whole = pl.ds(0, rows)
    kvs = [pack.at[whole, pl.ds(p * both, both)] for p in range(prompts)]
    for p, start in ((lead, 0), (0, front)):
        at = slice(start, start + rows)
        kvs[p][:, :HD] = rope(norm_rows(raw_kv[at, :HD], kg[...]), cos2, sin2).astype(BF)
        kvs[p][:, HD:] = raw_kv[at, HD:].astype(BF)
    values[:, :HD] = kvs[lead][:, HD:]
    values[:, HD:] = jnp.ones((rows, HD), BF)
    each = rows // n_seq
    to_row = lax.broadcasted_iota(jnp.int32, (rows, rows), 0)
    from_row = lax.broadcasted_iota(jnp.int32, (rows, rows), 1)
    move = jnp.where(from_row == lax.rem(to_row, each) * n_seq + to_row // each, 1.0, 0.0).astype(BF)
    for p, kv in enumerate(kvs):
        moved = dot(move, kv[...]).astype(BF)
        for d in range(n_seq):
            blocks[d, p * each : (p + 1) * each] = moved[d * each : (d + 1) * each]
    half = n_seq // 2
    away = (1 - seq // half) * half
    outs = [
        pltpu.make_async_copy(blocks, blocks_h, out_sem.at[0]),
        pltpu.make_async_copy(blocks.at[pl.ds(away, half)], leave_h, out_sem.at[1]),
    ]
    for copy in outs:
        copy.start()
    places = decode_places(plen, adm, clen, slots, dec_rows)
    dcos2, dsin2 = cos_sin(places, turns(places))
    new_at = slice(rows, front)
    pack[new_at, :] = jnp.zeros((dec_rows, pack.shape[1]), BF)
    pack[new_at, :HD] = rope(norm(raw_kv[new_at, :HD], kg[...]), dcos2, dsin2).astype(BF)
    pack[new_at, HD:both] = raw_kv[new_at, HD:].astype(BF)
    for h in range(local // HD):
        piece = raw[new_at, h * HD : (h + 1) * HD]
        col = base + h * HD
        pack[new_at, col : col + HD] = rope(norm(piece, qg[...]), dcos2, dsin2).astype(BF)
    for copy in o_copies:
        copy.wait()
    mine = pack.at[whole, pl.ds(base, local)]
    pair = 2 * HD
    for j in range(local // pair):
        later = dot(x_v[front:, :], wq_v[:, j * pair : (j + 1) * pair])
        for h in (2 * j, 2 * j + 1):
            piece = raw[:rows, h * HD : (h + 1) * HD]
            mine[:, h * HD : (h + 1) * HD] = rope(norm_rows(piece, qg[...]), cos2, sin2).astype(BF)
        attention((2 * j, 2 * j + 1), mine, kvs[lead], values, bias_v, s_v, w_v, mine)
        for i in range(2):
            col = base + local + (2 * j + i) * HD
            piece = later[:, i * HD : (i + 1) * HD]
            pack[:rows, col : col + HD] = rope(norm_rows(piece, qg[...]), cos2, sin2).astype(BF)
    outs.append(pltpu.make_async_copy(pack, pack_h, out_sem.at[2]))
    outs[-1].start()
    for j in range(2):
        at = pl.ds(j * nb, nb)
        send[:, at] = dot(mine[...], wo_v[j]).astype(BF)
        outs.append(pltpu.make_async_copy(send.at[:, at], send_h.at[:, at], out_sem.at[3 + j]))
        outs[-1].start()
    for copy in outs:
        copy.wait()


def cut_points(width):
    step = width // 8
    return [0, step, 2 * step, 4 * step, 6 * step, 8 * step]


def project(n_head, n_seq, plen, adm, clen, qg, kg, table, x, dec, wq, wk, wv, wo):
    prompts, rows, width = x.shape
    dec_rows = dec.shape[0] * dec.shape[1]
    local = wq.shape[1]
    nb = width // n_head
    every = prompts * rows + dec_rows
    send = (rows, 2 * nb)
    pack = (rows + dec_rows, 2 * prompts * HD + prompts * local)
    blocks = (n_seq, prompts * rows // n_seq, 2 * HD)
    chunks = len(cut_points(width)) - 1
    return pl.pallas_call(
        functools.partial(project_kernel, n_head, n_seq),
        out_shape=[
            jax.ShapeDtypeStruct(send, BF),
            jax.ShapeDtypeStruct(pack, BF),
            jax.ShapeDtypeStruct(blocks, BF),
            jax.ShapeDtypeStruct((n_seq // 2,) + blocks[1:], BF),
        ],
        in_specs=[HB] * 12,
        out_specs=[HB] * 4,
        scratch_shapes=[
            pltpu.VMEM((every, width), BF),
            pltpu.VMEM(dec.shape, BF),
            pltpu.VMEM((dec_rows, width), F32),
            pltpu.VMEM((width, 2 * HD), BF),
            pltpu.VMEM((width, local), BF),
            pltpu.VMEM((2, local, nb), BF),
            pltpu.VMEM((rows + dec_rows, local), F32),
            pltpu.VMEM((every, 2 * HD), F32),
            pltpu.VMEM(send, BF),
            pltpu.VMEM(pack, BF),
            pltpu.VMEM(blocks, BF),
            pltpu.SMEM(plen.shape, jnp.int32),
            pltpu.SMEM(adm.shape, jnp.int32),
            pltpu.SMEM(clen.shape, jnp.int32),
            pltpu.VMEM(qg.shape, F32),
            pltpu.VMEM(kg.shape, F32),
            pltpu.VMEM(table.shape, F32),
        ]
        + attention_scratch(rows, local // HD)
        + [
            pltpu.SemaphoreType.DMA((2, chunks)),
            pltpu.SemaphoreType.DMA,
            pltpu.SemaphoreType.DMA((2, chunks)),
            pltpu.SemaphoreType.DMA((chunks,)),
            pltpu.SemaphoreType.DMA((2,)),
            pltpu.SemaphoreType.DMA((6,)),
            pltpu.SemaphoreType.DMA((5,)),
        ],
        compiler_params=pltpu.CompilerParams(vmem_limit_bytes=LIMIT_A * MIB),
        cost_estimate=BRIEF,
        name="project",
    )(plen, adm, clen, qg, kg, table, x, dec, wq, wk, wv, wo)


def second_kernel(n_seq, prompts, *refs):
    plen_h, adm_h, clen_h, pack_h, cache_h, wo_hbm = refs[:6]
    send, attn, own1, part = refs[6:10]
    pack, cache, wo_v, plen, adm, clen = refs[10:16]
    bias_v, s_v, w_v, values = refs[16:20]
    pack_sem, small_sem, wo_sem, cache_sem = refs[20:]
    rows = attn.shape[0]
    dec_rows = pack.shape[0] - rows
    _, local, nb = wo_v.shape
    seq = lax.axis_index("seq")
    first, second = partners()
    head = lax.axis_index("head")
    pack_copy = pltpu.make_async_copy(pack_h, pack, pack_sem)
    cache_copy = pltpu.make_async_copy(cache_h, cache, cache_sem)
    small = [
        pltpu.make_async_copy(src, dst, small_sem.at[i])
        for i, (src, dst) in enumerate([(plen_h, plen), (adm_h, adm), (clen_h, clen)])
    ]
    copies = [
        out_copy(wo_hbm, block, nb, wo_v.at[j], wo_sem.at[j])
        for j, block in enumerate((head, second, 3 - head, first))
    ]
    for copy in small + [pack_copy] + copies[:2] + [cache_copy] + copies[2:]:
        copy.start()
    for copy in small:
        copy.wait()
    bias_v[...] = mask_bias(rows, plen[seq * prompts])
    pack_copy.wait()
    both = 2 * HD
    base = prompts * both
    whole = pl.ds(0, rows)
    kvs = [pack.at[whole, pl.ds(p * both, both)] for p in range(prompts)]
    other = pack.at[whole, pl.ds(base, local)]
    queries = pack.at[whole, pl.ds(base + local, local)]
    hb = nb // 2
    values[:, :HD] = kvs[0][:, HD:]
    values[:, HD:] = jnp.ones((rows, HD), BF)
    for j in range(local // both):
        if j in (1, 2):
            copies[j - 1].wait()
            for i in range(2):
                at = slice(i * hb, (i + 1) * hb)
                to = slice((j - 1) * nb + i * hb, (j - 1) * nb + (i + 1) * hb)
                own1[:, to] = dot(other[...], wo_v[j - 1, :, at]).astype(BF)
        attention((2 * j, 2 * j + 1), queries, kvs[0], values, bias_v, s_v, w_v, attn)
    cache_copy.wait()
    for copy in copies[2:]:
        copy.wait()
    for j in range(2):
        send[:, j * nb : (j + 1) * nb] = dot(attn[...], wo_v[2 + j]).astype(BF)
    decode_attention(
        n_seq, cache.shape[0], plen, adm, clen, pack.at[pl.ds(rows, dec_rows), pl.ds(base, local)],
        pack.at[pl.ds(rows, dec_rows), pl.ds(0, both)], kvs, cache, part,
    )


def second(n_head, n_seq, prompts, rows, plen, adm, clen, pack, cache, wo):
    local, width = wo.shape
    nb = width // n_head
    dec_rows = pack.shape[0] - rows
    return pl.pallas_call(
        functools.partial(second_kernel, n_seq, prompts),
        out_shape=[
            jax.ShapeDtypeStruct((rows, 2 * nb), BF),
            jax.ShapeDtypeStruct((rows, local), BF),
            jax.ShapeDtypeStruct((rows, 2 * nb), BF),
            jax.ShapeDtypeStruct((dec_rows * (local // HD) + 8, HD), F32),
        ],
        in_specs=[HB] * 6,
        out_specs=[VM] * 4,
        scratch_shapes=[
            pltpu.VMEM(pack.shape, BF),
            pltpu.VMEM(cache.shape, BF),
            pltpu.VMEM((4, local, nb), BF),
            pltpu.SMEM(plen.shape, jnp.int32),
            pltpu.SMEM(adm.shape, jnp.int32),
            pltpu.SMEM(clen.shape, jnp.int32),
        ]
        + attention_scratch(rows, local // HD)
        + [
            pltpu.SemaphoreType.DMA,
            pltpu.SemaphoreType.DMA((3,)),
            pltpu.SemaphoreType.DMA((4,)),
            pltpu.SemaphoreType.DMA,
        ],
        compiler_params=pltpu.CompilerParams(vmem_limit_bytes=LIMIT_B * MIB),
        cost_estimate=BRIEF,
        name="second",
    )(plen, adm, clen, pack, cache, wo)


def third_kernel(attn, wo_hbm, own, wo_a, wo_b, wo_sem):
    nb = wo_a.shape[2]
    first, second = partners()
    head = lax.axis_index("head")
    wo_v = [wo_a.at[0], wo_a.at[1], wo_b.at[0], wo_b.at[1]]
    copies = [
        out_copy(wo_hbm, block, nb, wo_v[j], wo_sem.at[j])
        for j, block in enumerate((head, second, 3 - head, first))
    ]
    for copy in copies:
        copy.start()
    for j in range(2):
        copies[j].wait()
        own[:, j * nb : (j + 1) * nb] = dot(attn[...], wo_v[j][...]).astype(BF)
    for copy in copies[2:]:
        copy.wait()


def third(n_head, attn, wo):
    rows = attn.shape[0]
    local, width = wo.shape
    nb = width // n_head
    return pl.pallas_call(
        third_kernel,
        out_shape=[jax.ShapeDtypeStruct((rows, 2 * nb), BF)]
        + [jax.ShapeDtypeStruct((2, local, nb), BF)] * 2,
        in_specs=[VM, HB],
        out_specs=[VM] * 3,
        scratch_shapes=[pltpu.SemaphoreType.DMA((4,))],
        compiler_params=pltpu.CompilerParams(vmem_limit_bytes=LIMIT_C * MIB),
        cost_estimate=BRIEF,
        name="third",
    )(attn, wo)


def joined(bit, mine, other):
    count = mine.shape[0] - 8
    swap = lax.rem(lax.axis_index("seq") // bit, 2) == 1
    one, two = mine[...], other[...]
    low = jnp.where(swap, two, one)
    high = jnp.where(swap, one, two)
    eye = unit(count)

    def column(row):
        return jnp.sum(jnp.where(eye, row, 0.0), axis=1, keepdims=True)

    row_a, row_b = low[count : count + 1, :], high[count : count + 1, :]
    best = jnp.maximum(row_a, row_b)
    scale_a, scale_b = jnp.exp2(row_a - best), jnp.exp2(row_b - best)
    total = scale_a + scale_b
    inverse = 1.0 / total
    mixed = low[:count] * column(scale_a * inverse) + high[:count] * column(scale_b * inverse)
    return mixed, best + jnp.log2(total)


def range_start(seq, size):
    return seq // size * size


def range_start(seq, size):
    return seq // size * size


def join_kernel(bit, mine, other, out):
    count = mine.shape[0] - 8
    mixed, level = joined(bit, mine, other)
    out[:count, :] = mixed
    out[count : count + 1, :] = level


def join(bit, mine, other):
    return pl.pallas_call(
        functools.partial(join_kernel, bit),
        out_shape=jax.ShapeDtypeStruct(mine.shape, F32),
        in_specs=[VM] * 2,
        out_specs=VM,
        compiler_params=pltpu.CompilerParams(vmem_limit_bytes=8 * MIB),
        cost_estimate=BRIEF,
        name="join_%d" % bit,
    )(mine, other)


def hop_kernel(bit, *refs):
    held, leave = refs[:-1], refs[-1]
    seq = lax.axis_index("seq")
    size = bit // 2
    target = range_start(seq, bit) + size * (1 - lax.rem(seq // size, 2))
    at = 0
    for array in held:
        sources, dests = array.shape[:2]
        skip = target - range_start(seq, dests)
        for k in range(sources):
            leave[at] = array[k, pl.ds(skip, size)]
            at += 1


def hop(bit, held):
    sources = sum(array.shape[0] for array in held)
    return pl.pallas_call(
        functools.partial(hop_kernel, bit),
        out_shape=jax.ShapeDtypeStruct((sources, bit // 2) + held[0].shape[2:], BF),
        in_specs=[VM] * len(held),
        out_specs=VM,
        compiler_params=pltpu.CompilerParams(vmem_limit_bytes=8 * MIB),
        cost_estimate=BRIEF,
        name="hop_%d" % bit,
    )(*held)


def pass_on_kernel(own, got, on):
    nb = on.shape[1]
    on[...] = (own[:, nb:].astype(F32) + got[:, :nb].astype(F32)).astype(BF)


def pass_on(p, own, got):
    rows, both = got.shape
    return pl.pallas_call(
        pass_on_kernel,
        out_shape=jax.ShapeDtypeStruct((rows, both // 2), BF),
        in_specs=[VM] * 2,
        out_specs=VM,
        compiler_params=pltpu.CompilerParams(vmem_limit_bytes=8 * MIB),
        cost_estimate=BRIEF,
        name="pass_on_%d" % p,
    )(own, got)


def decode_out_kernel(bit, mine, other, wo_a, wo_b, *outs):
    count = mine.shape[0] - 8
    rows = outs[0].shape[0]
    mixed, _ = joined(bit, mine, other)
    mixed = mixed.astype(BF)
    flat = jnp.concatenate([mixed[i * rows : (i + 1) * rows] for i in range(count // rows)], axis=1)
    for j, out in enumerate(outs):
        out[...] = dot(flat, (wo_a, wo_b)[j // 2][j % 2]).astype(BF)


def decode_project(bit, dec_rows, mine, other, wo_a, wo_b):
    nb = wo_a.shape[2]
    return pl.pallas_call(
        functools.partial(decode_out_kernel, bit),
        out_shape=[jax.ShapeDtypeStruct((dec_rows, nb), BF)] * 4,
        in_specs=[VM] * 4,
        out_specs=[VM] * 4,
        compiler_params=pltpu.CompilerParams(vmem_limit_bytes=16 * MIB),
        cost_estimate=BRIEF,
        name="decode_project",
    )(mine, other, wo_a, wo_b)


def sum_parts(stage, out, sems, own, got, last):
    rows, nb = last.shape
    step = rows // 2
    copies = []
    for i in range(2):
        at = pl.ds(i * step, step)
        stage[at] = (
            own[at, :nb].astype(F32) + got[at, nb:].astype(F32) + last[at].astype(F32)
        ).astype(BF)
        copies.append(pltpu.make_async_copy(stage.at[at], out.at[at], sems.at[i]))
        copies[-1].start()
    return copies


def finish_first_kernel(p, bits, own, got, last, *refs):
    held, (out, handed, stage, sems, keep_sem) = refs[: len(bits) + 1], refs[len(bits) + 1 :]
    seq = lax.axis_index("seq")
    copies = []
    sources = [0]
    for j, array in enumerate(held):
        if j:
            sources = sources + [bits[j - 1] ^ source for source in sources]
        for k in range(array.shape[0]):
            source = seq ^ sources[len(copies)]
            copies.append(
                pltpu.make_async_copy(
                    array.at[k, seq - range_start(seq, array.shape[1])],
                    handed.at[source],
                    keep_sem.at[len(copies)],
                )
            )
            copies[-1].start()
    for copy in sum_parts(stage, out.at[p], sems, own, got, last) + copies:
        copy.wait()


def finish_first(p, prompts, bits, own, got, last, held):
    rows, nb = last.shape
    n_seq = held[0].shape[1]
    return pl.pallas_call(
        functools.partial(finish_first_kernel, p, bits),
        out_shape=[
            jax.ShapeDtypeStruct((prompts, rows, nb), BF),
            jax.ShapeDtypeStruct((n_seq,) + held[0].shape[2:], BF),
        ],
        in_specs=[VM] * (3 + len(held)),
        out_specs=[HB] * 2,
        scratch_shapes=[
            pltpu.VMEM((rows, nb), BF),
            pltpu.SemaphoreType.DMA((2,)),
            pltpu.SemaphoreType.DMA((n_seq,)),
        ],
        compiler_params=pltpu.CompilerParams(vmem_limit_bytes=8 * MIB),
        cost_estimate=BRIEF,
        name="finish_%d" % p,
    )(own, got, last, *held)


def finish_last_kernel(p, slots, own, got, last, *refs):
    pieces, (_, out, dec_out, stage, sems) = refs[:-5], refs[-5:]
    copies = sum_parts(stage, out.at[p], sems, own, got, last)
    total = pieces[0][...].astype(F32)
    for piece in pieces[1:]:
        total = total + piece[...].astype(F32)
    for t in range(dec_out.shape[0]):
        dec_out[t] = total[t * slots : (t + 1) * slots].astype(BF)
    for copy in copies:
        copy.wait()


def finish_last(p, steps, slots, own, got, last, pieces, partial):
    rows, nb = last.shape
    return pl.pallas_call(
        functools.partial(finish_last_kernel, p, slots),
        out_shape=[
            jax.ShapeDtypeStruct(partial.shape, BF),
            jax.ShapeDtypeStruct((steps, slots, nb), BF),
        ],
        in_specs=[VM] * (3 + len(pieces)) + [HB],
        out_specs=[HB, VM],
        scratch_shapes=[pltpu.VMEM((rows, nb), BF), pltpu.SemaphoreType.DMA((2,))],
        input_output_aliases={3 + len(pieces): 0},
        compiler_params=pltpu.CompilerParams(vmem_limit_bytes=8 * MIB),
        cost_estimate=BRIEF,
        name="finish_%d" % p,
    )(own, got, last, *pieces, partial)


def after(value, other):
    return lax.optimization_barrier((value, other))[0]


def local(
    prompts, prompt_len, admitted, cache_len, cache_kv, dec_tokens, w_query, w_key, w_value, w_out, q_gain, k_gain
):
    n_seq = lax.axis_size("seq")
    n_head = lax.axis_size("head")
    pr_dev, rows, width = prompts.shape
    steps, slots, _ = dec_tokens.shape
    dec_rows = steps * slots
    each = rows // n_seq
    qg, kg = q_gain.reshape(1, HD), k_gain.reshape(1, HD)
    def head_move(value, masks):
        pairs = [
            (h * n_seq + s, (h ^ masks[s % 2]) * n_seq + s)
            for h in range(n_head)
            for s in range(n_seq)
        ]
        return lax.ppermute(value, ("head", "seq"), pairs)

    def seq_move(value, bit):
        return lax.ppermute(value, "seq", [(i, i ^ bit) for i in range(n_seq)])

    bits = []
    while 2 ** len(bits) < n_seq:
        bits.append(2 ** len(bits))
    bits = bits[::-1]

    table = jnp.asarray(prompt_table(rows))
    scalars = (prompt_len, admitted, cache_len)
    send1, pack, blocks, leave = project(
        n_head, n_seq, *scalars, qg, kg, table, prompts, dec_tokens, w_query, w_key, w_value, w_out
    )
    got1 = head_move(send1, (1, 2))
    arrived = seq_move(leave, bits[0])
    send0, attn0, own1, part = second(
        n_head, n_seq, pr_dev, rows, *scalars, pack, cache_kv[0], w_out
    )
    send0, arrived = lax.optimization_barrier((send0, arrived))
    got0 = head_move(send0, (1, 2))
    other = seq_move(part, bits[0])
    own0, *wo = third(n_head, attn0, w_out)
    other, got1 = lax.optimization_barrier((other, got1, own0))[:2]
    for i, bit in enumerate(bits[:-1]):
        part = join(bit, part, other)
        other = seq_move(part, bits[i + 1])
    held = [blocks[None], after(arrived, part)[None]]
    leave = hop(bits[0], held)
    held.append(seq_move(leave, bits[1]))
    on1 = pass_on(1, own1, after(got1, part))
    last1 = head_move(on1, (2, 1))
    got0, other, held[-1] = lax.optimization_barrier((got0, other, held[-1], on1))[:3]
    on0 = pass_on(0, own0, got0)
    last0 = head_move(on0, (2, 1))
    held[-1] = after(held[-1], on0)
    for i, bit in enumerate(bits[1:-1]):
        leave = hop(bit, held)
        held.append(seq_move(leave, bits[i + 2]))
    other = lax.optimization_barrier((other, on0, leave))[0]
    pieces = decode_project(bits[-1], dec_rows, part, other, *wo)
    pieces = [
        pieces[0],
        head_move(pieces[1], (2, 1)),
        head_move(pieces[2], (3, 3)),
        head_move(pieces[3], (1, 2)),
    ]
    partial, handed = finish_first(1, pr_dev, bits, own1, got1, last1, held)
    prefill_out, decode_out = finish_last(0, steps, slots, own0, got0, last0, pieces, partial)
    return (prefill_out, handed.reshape(1, pr_dev * n_seq, each, 2 * HD), decode_out)


def solution(mesh):
    placed = (
        P("seq", None, None),
        P(),
        P(),
        P(),
        P("head", None, "seq", None),
        P(),
        P(None, "head"),
        P(None, "head"),
        P(None, "head"),
        P("head", None),
        P(),
        P(),
    )
    return jax.shard_map(
        local,
        mesh=mesh,
        in_specs=placed,
        out_specs=(P("seq", None, "head"), P("head", None, "seq", None), P(None, None, "head")),
        check_vma=False,
    )
```

```python
import functools

import jax
import jax.numpy as jnp
import numpy as np
from jax import lax
from jax.experimental import pallas as pl
from jax.experimental.pallas import tpu as pltpu
from jax.sharding import PartitionSpec as P

HD = 128
EPS = 1e-06
THETA = 1000000.0
NEG = -1e30
LOG2E = 1.4426950408889634
SCALE = HD**-0.5
C2 = SCALE * LOG2E
BF = jnp.bfloat16
F32 = jnp.float32
HB = pl.BlockSpec(memory_space=pltpu.HBM)
VM = pl.BlockSpec(memory_space=pltpu.VMEM)
BRIEF = pl.CostEstimate(flops=1, bytes_accessed=1, transcendentals=0)
MIB = 1024 * 1024
LIMIT_A = 60
LIMIT_B = 50
LIMIT_C = 42


def frequencies():
    half = HD // 2
    freq = np.float32(THETA) ** (-np.arange(half, dtype=np.float32) / np.float32(half))
    return freq.astype(np.float32)


def turns(places):
    lane = lax.broadcasted_iota(jnp.int32, places.shape, 1)
    freq = jnp.zeros(places.shape, F32)
    spot = lax.rem(lane, HD // 2)
    for i, value in enumerate(frequencies()):
        freq = jnp.where(spot == i, float(value), freq)
    return freq


def cos_sin(places, freq):
    angle = places.astype(F32) * freq
    lane = lax.broadcasted_iota(jnp.int32, places.shape, 1)
    return jnp.cos(angle), jnp.where(lane < HD // 2, -1.0, 1.0) * jnp.sin(angle)


def prompt_table(length):
    angle = np.arange(length, dtype=np.float32)[:, None] * frequencies()[None, :]
    cosine, sine = np.cos(angle), np.sin(angle)
    return np.concatenate([cosine, cosine, -sine, sine], axis=1).astype(np.float32)


def dot(a, b):
    return jnp.dot(a, b, preferred_element_type=F32)


def dot_nt(a, b):
    return lax.dot_general(a, b, (((1,), (1,)), ((), ())), preferred_element_type=F32)


def norm(values, gain):
    square = jnp.mean(values * values, axis=-1, keepdims=True)
    return values * lax.rsqrt(square + EPS) * gain


def rope(values, cos2, sin2):
    return values * cos2 + pltpu.roll(values, HD // 2, 1) * sin2


def effective_lengths(plen, adm, clen, slots):
    out = []
    for r in range(slots):
        taken = adm[r]
        out.append(jnp.where(taken >= 0, plen[jnp.maximum(taken, 0)], clen[r]))
    return out


def by_slot(index, values):
    result = jnp.full(index.shape, values[0])
    for r in range(1, len(values)):
        result = jnp.where(index == r, values[r], result)
    return result


def partners():
    head, seq = lax.axis_index("head"), lax.axis_index("seq")
    flip_x = head + 1 - 2 * lax.rem(head, 2)
    flip_y = lax.rem(head + 2, 4)
    even = lax.rem(seq, 2) == 0
    return jnp.where(even, flip_x, flip_y), jnp.where(even, flip_y, flip_x)


def out_copy(wo_hbm, block, nb, dest, sem):
    return pltpu.make_async_copy(
        wo_hbm.at[:, pl.ds(pl.multiple_of(block * nb, nb), nb)], dest, sem
    )


def mask_bias(rows, length):
    row_at = lax.broadcasted_iota(jnp.int32, (rows, rows), 0)
    col_at = lax.broadcasted_iota(jnp.int32, (rows, rows), 1)
    return jnp.where((col_at <= row_at) & (col_at < length), 0.0, NEG).astype(F32)


def attention(heads, q_v, kv, values, bias_v, s_v, w_v, attn):
    rows = kv.shape[0]
    half = rows // 2
    quarter = rows // 4
    low, count = heads[0], len(heads)
    group = pl.ds(low, count)
    parts = ((pl.ds(0, half), half), (pl.ds(half, half), rows))
    for part, keys in parts:
        queries = q_v[group, part].reshape(count * half, HD)
        scores = dot_nt(queries, kv[:keys, :HD])
        s_v[group, part, :keys] = scores.reshape(count, half, keys)
    for h in heads:
        for block in range(4):
            at = slice(block * quarter, (block + 1) * quarter)
            keys = half if block < 2 else rows
            scores = s_v[h, at, :keys] + bias_v[at, :keys]
            top = jnp.max(scores, axis=-1, keepdims=True)
            w_v[h, at, :keys] = jnp.exp2((scores - top) * C2).astype(BF)
    for part, keys in parts:
        weights = w_v[group, part, :keys].reshape(count * half, keys)
        mixed = dot(weights, values[:keys])
        mixed = (mixed[:, :HD] / mixed[:, HD:]).astype(BF)
        for i, h in enumerate(heads):
            attn[part, h * HD : (h + 1) * HD] = mixed[i * half : (i + 1) * half]


def attention_scratch(rows, heads):
    return [
        pltpu.VMEM((rows, rows), F32),
        pltpu.VMEM((heads, rows, rows), F32),
        pltpu.VMEM((heads, rows, rows), BF),
        pltpu.VMEM((rows, 2 * HD), BF),
        pltpu.VMEM((heads, rows, HD), BF),
    ]


def unit(count):
    return lax.broadcasted_iota(jnp.int32, (count, count), 0) == lax.broadcasted_iota(
        jnp.int32, (count, count), 1
    )


def decode_places(plen, adm, clen, slots, dec_rows):
    eff = effective_lengths(plen, adm, clen, slots)
    row = lax.broadcasted_iota(jnp.int32, (dec_rows, HD), 0)
    return by_slot(lax.rem(row, slots), eff) + row // slots


def decode_attention(n_seq, slots, plen, adm, clen, rotated, new, kvs, cache, part):
    seq = lax.axis_index("seq")
    dec_rows = rotated.shape[0]
    width = cache.shape[1]
    rows = kvs[0].shape[0]
    new_key, new_value = new[:, :HD], new[:, HD:]
    queries = jnp.concatenate(
        [rotated[:, h * HD : (h + 1) * HD] for h in range(rotated.shape[1] // HD)], axis=0
    )
    count = queries.shape[0]

    row = lax.rem(lax.broadcasted_iota(jnp.int32, (count, 1), 0), dec_rows)
    slot, step = lax.rem(row, slots), row // slots
    taken = by_slot(slot, [adm[r] for r in range(slots)])
    scores, masks, values = [], [], []
    at = lax.broadcasted_iota(jnp.int32, (1, width), 1) * n_seq + seq
    for r in range(slots):
        limit = jnp.where(adm[r] >= 0, 0, clen[r])
        masks.append((slot == r) & (at < limit))
        scores.append(dot_nt(queries, cache[r, :, :HD]))
        values.append(cache[r, :, HD:])
    spot = lax.broadcasted_iota(jnp.int32, (1, rows), 1)
    for p, kv in enumerate(kvs):
        prompt = seq * len(kvs) + p
        masks.append((taken == prompt) & (spot < plen[prompt]))
        scores.append(dot_nt(queries, kv[:, :HD]))
        values.append(kv[:, HD:])
    other = lax.broadcasted_iota(jnp.int32, (1, dec_rows), 1)
    first = jnp.where(seq == 0, 1, 0)
    masks.append(
        (lax.rem(other, slots) == slot) & (other // slots <= step) & (first + 0 * other > 0)
    )
    scores.append(dot_nt(queries, new_key))
    values.append(new_value)

    top = jnp.full((count, 1), NEG, F32)
    scores = [jnp.where(mask, score, NEG) for mask, score in zip(masks, scores)]
    for score in scores:
        top = jnp.maximum(top, jnp.max(score, axis=-1, keepdims=True))
    total = jnp.zeros((count, 1), F32)
    acc = jnp.zeros((count, HD), F32)
    for mask, score, value in zip(masks, scores, values):
        expo = jnp.where(mask, jnp.exp2((score - top) * C2), 0.0)
        total = total + jnp.sum(expo, axis=-1, keepdims=True)
        acc = acc + dot(expo.astype(BF), value)
    some = total > 0.0
    safe = jnp.where(some, total, 1.0)
    part[:count, :] = acc * (1.0 / safe)
    level = jnp.where(some, top * C2 + jnp.log2(safe), NEG)
    part[count : count + 1, :] = jnp.sum(jnp.where(unit(count), level, 0.0), axis=0, keepdims=True)


def project_kernel(n_head, n_seq, *refs):
    plen_h, adm_h, clen_h, qg_h, kg_h, table_h, x_hbm, dec_hbm, wq_hbm, wk_hbm, wv_hbm, wo_hbm = refs[:12]
    send_h, pack_h, blocks_h, leave_h = refs[12:16]
    x_v, dec_v, flat_v, wkv_v, wq_v, wo_v, raw, raw_kv, send, pack, blocks = refs[16:27]
    plen, adm, clen, qg, kg, table = refs[27:33]
    bias_v, s_v, w_v, values, q_v = refs[33:38]
    x_sem, dec_sem, wkv_sem, wq_sem, wo_sem, small_sem, out_sem = refs[38:]
    prompts, rows, width = x_hbm.shape
    steps, slots, _ = dec_hbm.shape
    dec_rows = steps * slots
    local = wq_v.shape[1]
    nb = width // n_head
    lead = prompts - 1
    seq = lax.axis_index("seq")
    first, _ = partners()
    diag = 3 - lax.axis_index("head")
    front = rows + dec_rows

    cuts = cut_points(width)
    queue = []
    for c in range(len(cuts) - 1):
        at = pl.ds(cuts[c], cuts[c + 1] - cuts[c])
        queue.append(
            [
                pltpu.make_async_copy(
                    x_hbm.at[lead, :, at], x_v.at[pl.ds(0, rows), at], x_sem.at[0, c]
                ),
                pltpu.make_async_copy(
                    x_hbm.at[0, :, at], x_v.at[pl.ds(front, rows), at], x_sem.at[1, c]
                ),
                pltpu.make_async_copy(wk_hbm.at[at], wkv_v.at[at, pl.ds(0, HD)], wkv_sem.at[0, c]),
                pltpu.make_async_copy(wv_hbm.at[at], wkv_v.at[at, pl.ds(HD, HD)], wkv_sem.at[1, c]),
                pltpu.make_async_copy(wq_hbm.at[at], wq_v.at[at], wq_sem.at[c]),
            ]
        )
    small = [
        pltpu.make_async_copy(src, dst, small_sem.at[i])
        for i, (src, dst) in enumerate(
            [(plen_h, plen), (qg_h, qg), (kg_h, kg), (table_h, table), (adm_h, adm), (clen_h, clen)]
        )
    ]
    dec_copy = pltpu.make_async_copy(dec_hbm, dec_v, dec_sem)
    o_copies = [
        out_copy(wo_hbm, block, nb, wo_v.at[j], wo_sem.at[j]) for j, block in enumerate((diag, first))
    ]
    ahead = 3
    queue += [[copy] for copy in o_copies]
    for copy in [dec_copy] + queue[0] + small:
        copy.start()
    for group in queue[1:ahead]:
        for copy in group:
            copy.start()
    for copy in small:
        copy.wait()
    bias_v[...] = mask_bias(rows, plen[seq * prompts + lead])
    dec_copy.wait()
    for t in range(steps):
        flat_v[t * slots : (t + 1) * slots, :] = dec_v[t].astype(F32)
    x_v[rows:front, :] = flat_v[...].astype(BF)
    for c in range(len(cuts) - 1):
        for copy in queue[c]:
            copy.wait()
        if c + ahead < len(queue):
            for copy in queue[c + ahead]:
                copy.start()
        at = slice(cuts[c], cuts[c + 1])
        kv_part = dot(x_v[:, at], wkv_v[at, :])
        q_part = dot(x_v[:front, at], wq_v[at, :])
        if c == 0:
            raw_kv[...] = kv_part
            raw[...] = q_part
        else:
            raw_kv[...] += kv_part
            raw[...] += q_part
    cos2, sin2 = table[:, :HD], table[:, HD:]
    both = 2 * HD
    base = prompts * both
    whole = pl.ds(0, rows)
    kvs = [pack.at[whole, pl.ds(p * both, both)] for p in range(prompts)]
    for p, start in ((lead, 0), (0, front)):
        at = slice(start, start + rows)
        kvs[p][:, :HD] = rope(norm(raw_kv[at, :HD], kg[...]), cos2, sin2).astype(BF)
        kvs[p][:, HD:] = raw_kv[at, HD:].astype(BF)
    values[:, :HD] = kvs[lead][:, HD:]
    values[:, HD:] = jnp.ones((rows, HD), BF)
    each = rows // n_seq
    to_row = lax.broadcasted_iota(jnp.int32, (rows, rows), 0)
    from_row = lax.broadcasted_iota(jnp.int32, (rows, rows), 1)
    move = jnp.where(from_row == lax.rem(to_row, each) * n_seq + to_row // each, 1.0, 0.0).astype(BF)
    for p, kv in enumerate(kvs):
        moved = dot(move, kv[...]).astype(BF)
        for d in range(n_seq):
            blocks[d, p * each : (p + 1) * each] = moved[d * each : (d + 1) * each]
    half = n_seq // 2
    away = (1 - seq // half) * half
    outs = [
        pltpu.make_async_copy(blocks, blocks_h, out_sem.at[0]),
        pltpu.make_async_copy(blocks.at[pl.ds(away, half)], leave_h, out_sem.at[1]),
    ]
    for copy in outs:
        copy.start()
    places = decode_places(plen, adm, clen, slots, dec_rows)
    dcos2, dsin2 = cos_sin(places, turns(places))
    new_at = slice(rows, front)
    pack[new_at, :] = jnp.zeros((dec_rows, pack.shape[1]), BF)
    pack[new_at, :HD] = rope(norm(raw_kv[new_at, :HD], kg[...]), dcos2, dsin2).astype(BF)
    pack[new_at, HD:both] = raw_kv[new_at, HD:].astype(BF)
    for h in range(local // HD):
        piece = raw[new_at, h * HD : (h + 1) * HD]
        col = base + h * HD
        pack[new_at, col : col + HD] = rope(norm(piece, qg[...]), dcos2, dsin2).astype(BF)
    for copy in o_copies:
        copy.wait()
    mine = pack.at[whole, pl.ds(base, local)]
    wide = 4 * HD
    for j in range(local // wide):
        later = dot(x_v[front:, :], wq_v[:, j * wide : (j + 1) * wide])
        heads = range(4 * j, 4 * j + 4)
        for h in heads:
            piece = raw[:rows, h * HD : (h + 1) * HD]
            q_v[h] = rope(norm(piece, qg[...]), cos2, sin2).astype(BF)
        attention(heads, q_v, kvs[lead], values, bias_v, s_v, w_v, mine)
        for i, h in enumerate(heads):
            col = base + local + h * HD
            piece = later[:, i * HD : (i + 1) * HD]
            pack[:rows, col : col + HD] = rope(norm(piece, qg[...]), cos2, sin2).astype(BF)
    outs.append(pltpu.make_async_copy(pack, pack_h, out_sem.at[2]))
    outs[-1].start()
    for j in range(2):
        at = pl.ds(j * nb, nb)
        send[:, at] = dot(mine[...], wo_v[j]).astype(BF)
        outs.append(pltpu.make_async_copy(send.at[:, at], send_h.at[:, at], out_sem.at[3 + j]))
        outs[-1].start()
    for copy in outs:
        copy.wait()


def cut_points(width):
    step = width // 8
    return [0, step, 2 * step, 4 * step, 6 * step, 8 * step]


def project(n_head, n_seq, plen, adm, clen, qg, kg, table, x, dec, wq, wk, wv, wo):
    prompts, rows, width = x.shape
    dec_rows = dec.shape[0] * dec.shape[1]
    local = wq.shape[1]
    nb = width // n_head
    every = prompts * rows + dec_rows
    send = (rows, 2 * nb)
    pack = (rows + dec_rows, 2 * prompts * HD + prompts * local)
    blocks = (n_seq, prompts * rows // n_seq, 2 * HD)
    chunks = len(cut_points(width)) - 1
    return pl.pallas_call(
        functools.partial(project_kernel, n_head, n_seq),
        out_shape=[
            jax.ShapeDtypeStruct(send, BF),
            jax.ShapeDtypeStruct(pack, BF),
            jax.ShapeDtypeStruct(blocks, BF),
            jax.ShapeDtypeStruct((n_seq // 2,) + blocks[1:], BF),
        ],
        in_specs=[HB] * 12,
        out_specs=[HB] * 4,
        scratch_shapes=[
            pltpu.VMEM((every, width), BF),
            pltpu.VMEM(dec.shape, BF),
            pltpu.VMEM((dec_rows, width), F32),
            pltpu.VMEM((width, 2 * HD), BF),
            pltpu.VMEM((width, local), BF),
            pltpu.VMEM((2, local, nb), BF),
            pltpu.VMEM((rows + dec_rows, local), F32),
            pltpu.VMEM((every, 2 * HD), F32),
            pltpu.VMEM(send, BF),
            pltpu.VMEM(pack, BF),
            pltpu.VMEM(blocks, BF),
            pltpu.SMEM(plen.shape, jnp.int32),
            pltpu.SMEM(adm.shape, jnp.int32),
            pltpu.SMEM(clen.shape, jnp.int32),
            pltpu.VMEM(qg.shape, F32),
            pltpu.VMEM(kg.shape, F32),
            pltpu.VMEM(table.shape, F32),
        ]
        + attention_scratch(rows, local // HD)
        + [
            pltpu.SemaphoreType.DMA((2, chunks)),
            pltpu.SemaphoreType.DMA,
            pltpu.SemaphoreType.DMA((2, chunks)),
            pltpu.SemaphoreType.DMA((chunks,)),
            pltpu.SemaphoreType.DMA((2,)),
            pltpu.SemaphoreType.DMA((6,)),
            pltpu.SemaphoreType.DMA((5,)),
        ],
        compiler_params=pltpu.CompilerParams(vmem_limit_bytes=LIMIT_A * MIB),
        cost_estimate=BRIEF,
        name="project",
    )(plen, adm, clen, qg, kg, table, x, dec, wq, wk, wv, wo)


def second_kernel(n_seq, prompts, *refs):
    plen_h, adm_h, clen_h, pack_h, cache_h, wo_hbm = refs[:6]
    send, attn, own1, part = refs[6:10]
    pack, cache, wo_v, plen, adm, clen = refs[10:16]
    bias_v, s_v, w_v, values, q_v = refs[16:21]
    pack_sem, small_sem, wo_sem, cache_sem = refs[21:]
    rows = attn.shape[0]
    dec_rows = pack.shape[0] - rows
    _, local, nb = wo_v.shape
    seq = lax.axis_index("seq")
    first, second = partners()
    head = lax.axis_index("head")
    pack_copy = pltpu.make_async_copy(pack_h, pack, pack_sem)
    cache_copy = pltpu.make_async_copy(cache_h, cache, cache_sem)
    small = [
        pltpu.make_async_copy(src, dst, small_sem.at[i])
        for i, (src, dst) in enumerate([(plen_h, plen), (adm_h, adm), (clen_h, clen)])
    ]
    copies = [
        out_copy(wo_hbm, block, nb, wo_v.at[j], wo_sem.at[j])
        for j, block in enumerate((head, second, 3 - head, first))
    ]
    for copy in small + [pack_copy] + copies[:2] + [cache_copy] + copies[2:]:
        copy.start()
    for copy in small:
        copy.wait()
    bias_v[...] = mask_bias(rows, plen[seq * prompts])
    pack_copy.wait()
    both = 2 * HD
    base = prompts * both
    whole = pl.ds(0, rows)
    kvs = [pack.at[whole, pl.ds(p * both, both)] for p in range(prompts)]
    other = pack.at[whole, pl.ds(base, local)]
    queries = pack.at[whole, pl.ds(base + local, local)]
    values[:, :HD] = kvs[0][:, HD:]
    values[:, HD:] = jnp.ones((rows, HD), BF)
    for h in range(local // HD):
        q_v[h] = queries[:, h * HD : (h + 1) * HD]
    for j in range(local // (4 * HD)):
        if j == 1:
            for i in range(2):
                copies[i].wait()
                own1[:, i * nb : (i + 1) * nb] = dot(other[...], wo_v[i]).astype(BF)
        attention(range(4 * j, 4 * j + 4), q_v, kvs[0], values, bias_v, s_v, w_v, attn)
    cache_copy.wait()
    for copy in copies[2:]:
        copy.wait()
    for j in range(2):
        send[:, j * nb : (j + 1) * nb] = dot(attn[...], wo_v[2 + j]).astype(BF)
    decode_attention(
        n_seq, cache.shape[0], plen, adm, clen, pack.at[pl.ds(rows, dec_rows), pl.ds(base, local)],
        pack.at[pl.ds(rows, dec_rows), pl.ds(0, both)], kvs, cache, part,
    )


def second(n_head, n_seq, prompts, rows, plen, adm, clen, pack, cache, wo):
    local, width = wo.shape
    nb = width // n_head
    dec_rows = pack.shape[0] - rows
    return pl.pallas_call(
        functools.partial(second_kernel, n_seq, prompts),
        out_shape=[
            jax.ShapeDtypeStruct((rows, 2 * nb), BF),
            jax.ShapeDtypeStruct((rows, local), BF),
            jax.ShapeDtypeStruct((rows, 2 * nb), BF),
            jax.ShapeDtypeStruct((dec_rows * (local // HD) + 8, HD), F32),
        ],
        in_specs=[HB] * 6,
        out_specs=[VM] * 4,
        scratch_shapes=[
            pltpu.VMEM(pack.shape, BF),
            pltpu.VMEM(cache.shape, BF),
            pltpu.VMEM((4, local, nb), BF),
            pltpu.SMEM(plen.shape, jnp.int32),
            pltpu.SMEM(adm.shape, jnp.int32),
            pltpu.SMEM(clen.shape, jnp.int32),
        ]
        + attention_scratch(rows, local // HD)
        + [
            pltpu.SemaphoreType.DMA,
            pltpu.SemaphoreType.DMA((3,)),
            pltpu.SemaphoreType.DMA((4,)),
            pltpu.SemaphoreType.DMA,
        ],
        compiler_params=pltpu.CompilerParams(vmem_limit_bytes=LIMIT_B * MIB),
        cost_estimate=BRIEF,
        name="second",
    )(plen, adm, clen, pack, cache, wo)


def third_kernel(attn, wo_hbm, own, wo_a, wo_b, wo_sem):
    nb = wo_a.shape[2]
    first, second = partners()
    head = lax.axis_index("head")
    wo_v = [wo_a.at[0], wo_a.at[1], wo_b.at[0], wo_b.at[1]]
    copies = [
        out_copy(wo_hbm, block, nb, wo_v[j], wo_sem.at[j])
        for j, block in enumerate((head, second, 3 - head, first))
    ]
    for copy in copies:
        copy.start()
    for j in range(2):
        copies[j].wait()
        own[:, j * nb : (j + 1) * nb] = dot(attn[...], wo_v[j][...]).astype(BF)
    for copy in copies[2:]:
        copy.wait()


def third(n_head, attn, wo):
    rows = attn.shape[0]
    local, width = wo.shape
    nb = width // n_head
    return pl.pallas_call(
        third_kernel,
        out_shape=[jax.ShapeDtypeStruct((rows, 2 * nb), BF)]
        + [jax.ShapeDtypeStruct((2, local, nb), BF)] * 2,
        in_specs=[VM, HB],
        out_specs=[VM] * 3,
        scratch_shapes=[pltpu.SemaphoreType.DMA((4,))],
        compiler_params=pltpu.CompilerParams(vmem_limit_bytes=LIMIT_C * MIB),
        cost_estimate=BRIEF,
        name="third",
    )(attn, wo)


def joined(bit, mine, other):
    count = mine.shape[0] - 8
    swap = lax.rem(lax.axis_index("seq") // bit, 2) == 1
    one, two = mine[...], other[...]
    low = jnp.where(swap, two, one)
    high = jnp.where(swap, one, two)
    eye = unit(count)

    def column(row):
        return jnp.sum(jnp.where(eye, row, 0.0), axis=1, keepdims=True)

    row_a, row_b = low[count : count + 1, :], high[count : count + 1, :]
    best = jnp.maximum(row_a, row_b)
    scale_a, scale_b = jnp.exp2(row_a - best), jnp.exp2(row_b - best)
    total = scale_a + scale_b
    inverse = 1.0 / total
    mixed = low[:count] * column(scale_a * inverse) + high[:count] * column(scale_b * inverse)
    return mixed, best + jnp.log2(total)


def range_start(seq, size):
    return seq // size * size


def range_start(seq, size):
    return seq // size * size


def join_kernel(bit, mine, other, out):
    count = mine.shape[0] - 8
    mixed, level = joined(bit, mine, other)
    out[:count, :] = mixed
    out[count : count + 1, :] = level


def join(bit, mine, other):
    return pl.pallas_call(
        functools.partial(join_kernel, bit),
        out_shape=jax.ShapeDtypeStruct(mine.shape, F32),
        in_specs=[VM] * 2,
        out_specs=VM,
        compiler_params=pltpu.CompilerParams(vmem_limit_bytes=8 * MIB),
        cost_estimate=BRIEF,
        name="join_%d" % bit,
    )(mine, other)


def hop_kernel(bit, *refs):
    held, leave = refs[:-1], refs[-1]
    seq = lax.axis_index("seq")
    size = bit // 2
    target = range_start(seq, bit) + size * (1 - lax.rem(seq // size, 2))
    at = 0
    for array in held:
        sources, dests = array.shape[:2]
        skip = target - range_start(seq, dests)
        for k in range(sources):
            leave[at] = array[k, pl.ds(skip, size)]
            at += 1


def hop(bit, held):
    sources = sum(array.shape[0] for array in held)
    return pl.pallas_call(
        functools.partial(hop_kernel, bit),
        out_shape=jax.ShapeDtypeStruct((sources, bit // 2) + held[0].shape[2:], BF),
        in_specs=[VM] * len(held),
        out_specs=VM,
        compiler_params=pltpu.CompilerParams(vmem_limit_bytes=8 * MIB),
        cost_estimate=BRIEF,
        name="hop_%d" % bit,
    )(*held)


def pass_on_kernel(own, got, on):
    nb = on.shape[1]
    on[...] = (own[:, nb:].astype(F32) + got[:, :nb].astype(F32)).astype(BF)


def pass_on(p, own, got):
    rows, both = got.shape
    return pl.pallas_call(
        pass_on_kernel,
        out_shape=jax.ShapeDtypeStruct((rows, both // 2), BF),
        in_specs=[VM] * 2,
        out_specs=VM,
        compiler_params=pltpu.CompilerParams(vmem_limit_bytes=8 * MIB),
        cost_estimate=BRIEF,
        name="pass_on_%d" % p,
    )(own, got)


def decode_out_kernel(bit, mine, other, wo_a, wo_b, *outs):
    count = mine.shape[0] - 8
    rows = outs[0].shape[0]
    mixed, _ = joined(bit, mine, other)
    mixed = mixed.astype(BF)
    flat = jnp.concatenate([mixed[i * rows : (i + 1) * rows] for i in range(count // rows)], axis=1)
    for j, out in enumerate(outs):
        out[...] = dot(flat, (wo_a, wo_b)[j // 2][j % 2]).astype(BF)


def decode_project(bit, dec_rows, mine, other, wo_a, wo_b):
    nb = wo_a.shape[2]
    return pl.pallas_call(
        functools.partial(decode_out_kernel, bit),
        out_shape=[jax.ShapeDtypeStruct((dec_rows, nb), BF)] * 4,
        in_specs=[VM] * 4,
        out_specs=[VM] * 4,
        compiler_params=pltpu.CompilerParams(vmem_limit_bytes=16 * MIB),
        cost_estimate=BRIEF,
        name="decode_project",
    )(mine, other, wo_a, wo_b)


def sum_parts(stage, out, sems, own, got, last):
    rows, nb = last.shape
    step = rows // 2
    copies = []
    for i in range(2):
        at = pl.ds(i * step, step)
        stage[at] = (
            own[at, :nb].astype(F32) + got[at, nb:].astype(F32) + last[at].astype(F32)
        ).astype(BF)
        copies.append(pltpu.make_async_copy(stage.at[at], out.at[at], sems.at[i]))
        copies[-1].start()
    return copies


def finish_first_kernel(p, bits, own, got, last, *refs):
    held, (out, handed, stage, sems, keep_sem) = refs[: len(bits) + 1], refs[len(bits) + 1 :]
    seq = lax.axis_index("seq")
    copies = []
    sources = [0]
    for j, array in enumerate(held):
        if j:
            sources = sources + [bits[j - 1] ^ source for source in sources]
        for k in range(array.shape[0]):
            source = seq ^ sources[len(copies)]
            copies.append(
                pltpu.make_async_copy(
                    array.at[k, seq - range_start(seq, array.shape[1])],
                    handed.at[source],
                    keep_sem.at[len(copies)],
                )
            )
            copies[-1].start()
    for copy in sum_parts(stage, out.at[p], sems, own, got, last) + copies:
        copy.wait()


def finish_first(p, prompts, bits, own, got, last, held):
    rows, nb = last.shape
    n_seq = held[0].shape[1]
    return pl.pallas_call(
        functools.partial(finish_first_kernel, p, bits),
        out_shape=[
            jax.ShapeDtypeStruct((prompts, rows, nb), BF),
            jax.ShapeDtypeStruct((n_seq,) + held[0].shape[2:], BF),
        ],
        in_specs=[VM] * (3 + len(held)),
        out_specs=[HB] * 2,
        scratch_shapes=[
            pltpu.VMEM((rows, nb), BF),
            pltpu.SemaphoreType.DMA((2,)),
            pltpu.SemaphoreType.DMA((n_seq,)),
        ],
        compiler_params=pltpu.CompilerParams(vmem_limit_bytes=8 * MIB),
        cost_estimate=BRIEF,
        name="finish_%d" % p,
    )(own, got, last, *held)


def finish_last_kernel(p, slots, own, got, last, *refs):
    pieces, (_, out, dec_out, stage, sems) = refs[:-5], refs[-5:]
    copies = sum_parts(stage, out.at[p], sems, own, got, last)
    total = pieces[0][...].astype(F32)
    for piece in pieces[1:]:
        total = total + piece[...].astype(F32)
    for t in range(dec_out.shape[0]):
        dec_out[t] = total[t * slots : (t + 1) * slots].astype(BF)
    for copy in copies:
        copy.wait()


def finish_last(p, steps, slots, own, got, last, pieces, partial):
    rows, nb = last.shape
    return pl.pallas_call(
        functools.partial(finish_last_kernel, p, slots),
        out_shape=[
            jax.ShapeDtypeStruct(partial.shape, BF),
            jax.ShapeDtypeStruct((steps, slots, nb), BF),
        ],
        in_specs=[VM] * (3 + len(pieces)) + [HB],
        out_specs=[HB, VM],
        scratch_shapes=[pltpu.VMEM((rows, nb), BF), pltpu.SemaphoreType.DMA((2,))],
        input_output_aliases={3 + len(pieces): 0},
        compiler_params=pltpu.CompilerParams(vmem_limit_bytes=8 * MIB),
        cost_estimate=BRIEF,
        name="finish_%d" % p,
    )(own, got, last, *pieces, partial)


def after(value, other):
    return lax.optimization_barrier((value, other))[0]


def local(
    prompts, prompt_len, admitted, cache_len, cache_kv, dec_tokens, w_query, w_key, w_value, w_out, q_gain, k_gain
):
    n_seq = lax.axis_size("seq")
    n_head = lax.axis_size("head")
    pr_dev, rows, width = prompts.shape
    steps, slots, _ = dec_tokens.shape
    dec_rows = steps * slots
    each = rows // n_seq
    qg, kg = q_gain.reshape(1, HD), k_gain.reshape(1, HD)
    def head_move(value, masks):
        pairs = [
            (h * n_seq + s, (h ^ masks[s % 2]) * n_seq + s)
            for h in range(n_head)
            for s in range(n_seq)
        ]
        return lax.ppermute(value, ("head", "seq"), pairs)

    def seq_move(value, bit):
        return lax.ppermute(value, "seq", [(i, i ^ bit) for i in range(n_seq)])

    bits = []
    while 2 ** len(bits) < n_seq:
        bits.append(2 ** len(bits))
    bits = bits[::-1]

    table = jnp.asarray(prompt_table(rows))
    scalars = (prompt_len, admitted, cache_len)
    send1, pack, blocks, leave = project(
        n_head, n_seq, *scalars, qg, kg, table, prompts, dec_tokens, w_query, w_key, w_value, w_out
    )
    got1 = head_move(send1, (1, 2))
    arrived = seq_move(leave, bits[0])
    send0, attn0, own1, part = second(
        n_head, n_seq, pr_dev, rows, *scalars, pack, cache_kv[0], w_out
    )
    send0, arrived = lax.optimization_barrier((send0, arrived))
    got0 = head_move(send0, (1, 2))
    other = seq_move(part, bits[0])
    own0, *wo = third(n_head, attn0, w_out)
    other, got1 = lax.optimization_barrier((other, got1, own0))[:2]
    for i, bit in enumerate(bits[:-1]):
        part = join(bit, part, other)
        other = seq_move(part, bits[i + 1])
    held = [blocks[None], after(arrived, part)[None]]
    leave = hop(bits[0], held)
    held.append(seq_move(leave, bits[1]))
    on1 = pass_on(1, own1, after(got1, part))
    last1 = head_move(on1, (2, 1))
    got0, other, held[-1] = lax.optimization_barrier((got0, other, held[-1], on1))[:3]
    on0 = pass_on(0, own0, got0)
    last0 = head_move(on0, (2, 1))
    held[-1] = after(held[-1], on0)
    for i, bit in enumerate(bits[1:-1]):
        leave = hop(bit, held)
        held.append(seq_move(leave, bits[i + 2]))
    other = lax.optimization_barrier((other, on0, leave))[0]
    pieces = decode_project(bits[-1], dec_rows, part, other, *wo)
    pieces = [
        pieces[0],
        head_move(pieces[1], (2, 1)),
        head_move(pieces[2], (3, 3)),
        head_move(pieces[3], (1, 2)),
    ]
    partial, handed = finish_first(1, pr_dev, bits, own1, got1, last1, held)
    prefill_out, decode_out = finish_last(0, steps, slots, own0, got0, last0, pieces, partial)
    return (prefill_out, handed.reshape(1, pr_dev * n_seq, each, 2 * HD), decode_out)


def solution(mesh):
    placed = (
        P("seq", None, None),
        P(),
        P(),
        P(),
        P("head", None, "seq", None),
        P(),
        P(None, "head"),
        P(None, "head"),
        P(None, "head"),
        P("head", None),
        P(),
        P(),
    )
    return jax.shard_map(
        local,
        mesh=mesh,
        in_specs=placed,
        out_specs=(P("seq", None, "head"), P("head", None, "seq", None), P(None, None, "head")),
        check_vma=False,
    )
```

```python
import functools

import jax
import jax.numpy as jnp
import numpy as np
from jax import lax
from jax.experimental import pallas as pl
from jax.experimental.pallas import tpu as pltpu
from jax.sharding import PartitionSpec as P

HD = 128
EPS = 1e-06
THETA = 1000000.0
NEG = -1e30
LOG2E = 1.4426950408889634
SCALE = HD**-0.5
C2 = SCALE * LOG2E
BF = jnp.bfloat16
F32 = jnp.float32
HB = pl.BlockSpec(memory_space=pltpu.HBM)
VM = pl.BlockSpec(memory_space=pltpu.VMEM)
BRIEF = pl.CostEstimate(flops=1, bytes_accessed=1, transcendentals=0)
MIB = 1024 * 1024
LIMIT_A = 60
LIMIT_B = 50
LIMIT_C = 42


def frequencies():
    half = HD // 2
    freq = np.float32(THETA) ** (-np.arange(half, dtype=np.float32) / np.float32(half))
    return freq.astype(np.float32)


def turns(places):
    lane = lax.broadcasted_iota(jnp.int32, places.shape, 1)
    freq = jnp.zeros(places.shape, F32)
    spot = lax.rem(lane, HD // 2)
    for i, value in enumerate(frequencies()):
        freq = jnp.where(spot == i, float(value), freq)
    return freq


def cos_sin(places, freq):
    angle = places.astype(F32) * freq
    lane = lax.broadcasted_iota(jnp.int32, places.shape, 1)
    return jnp.cos(angle), jnp.where(lane < HD // 2, -1.0, 1.0) * jnp.sin(angle)


def prompt_table(length):
    angle = np.arange(length, dtype=np.float32)[:, None] * frequencies()[None, :]
    cosine, sine = np.cos(angle), np.sin(angle)
    return np.concatenate([cosine, cosine, -sine, sine], axis=1).astype(np.float32)


def dot(a, b):
    return jnp.dot(a, b, preferred_element_type=F32)


def dot_nt(a, b):
    return lax.dot_general(a, b, (((1,), (1,)), ((), ())), preferred_element_type=F32)


def norm(values, gain):
    square = jnp.mean(values * values, axis=-1, keepdims=True)
    return values * lax.rsqrt(square + EPS) * gain


def rope(values, cos2, sin2):
    return values * cos2 + pltpu.roll(values, HD // 2, 1) * sin2


def effective_lengths(plen, adm, clen, slots):
    out = []
    for r in range(slots):
        taken = adm[r]
        out.append(jnp.where(taken >= 0, plen[jnp.maximum(taken, 0)], clen[r]))
    return out


def by_slot(index, values):
    result = jnp.full(index.shape, values[0])
    for r in range(1, len(values)):
        result = jnp.where(index == r, values[r], result)
    return result


def partners():
    head, seq = lax.axis_index("head"), lax.axis_index("seq")
    flip_x = head + 1 - 2 * lax.rem(head, 2)
    flip_y = lax.rem(head + 2, 4)
    even = lax.rem(seq, 2) == 0
    return jnp.where(even, flip_x, flip_y), jnp.where(even, flip_y, flip_x)


def out_copy(wo_hbm, block, nb, dest, sem):
    return pltpu.make_async_copy(
        wo_hbm.at[:, pl.ds(pl.multiple_of(block * nb, nb), nb)], dest, sem
    )


def mask_bias(rows, length):
    row_at = lax.broadcasted_iota(jnp.int32, (rows, rows), 0)
    col_at = lax.broadcasted_iota(jnp.int32, (rows, rows), 1)
    return jnp.where((col_at <= row_at) & (col_at < length), 0.0, NEG).astype(F32)


def attention(heads, q_v, kv, values, bias_v, s_v, w_v, attn):
    rows = kv.shape[0]
    half = rows // 2
    quarter = rows // 4
    low, count = heads[0], len(heads)
    group = pl.ds(low, count)
    parts = ((pl.ds(0, half), half), (pl.ds(half, half), rows))
    for part, keys in parts:
        queries = q_v[group, part].reshape(count * half, HD)
        scores = dot_nt(queries, kv[:keys, :HD])
        s_v[group, part, :keys] = scores.reshape(count, half, keys)
    for h in heads:
        for block in range(4):
            at = slice(block * quarter, (block + 1) * quarter)
            keys = half if block < 2 else rows
            scores = s_v[h, at, :keys] + bias_v[at, :keys]
            top = jnp.max(scores, axis=-1, keepdims=True)
            w_v[h, at, :keys] = jnp.exp2((scores - top) * C2).astype(BF)
    for part, keys in parts:
        weights = w_v[group, part, :keys].reshape(count * half, keys)
        mixed = dot(weights, values[:keys])
        mixed = (mixed[:, :HD] / mixed[:, HD:]).astype(BF)
        for i, h in enumerate(heads):
            attn[part, h * HD : (h + 1) * HD] = mixed[i * half : (i + 1) * half]


def attention_scratch(rows, heads):
    return [
        pltpu.VMEM((rows, rows), F32),
        pltpu.VMEM((heads, rows, rows), F32),
        pltpu.VMEM((heads, rows, rows), BF),
        pltpu.VMEM((rows, 2 * HD), BF),
        pltpu.VMEM((heads, rows, HD), BF),
    ]


def unit(count):
    return lax.broadcasted_iota(jnp.int32, (count, count), 0) == lax.broadcasted_iota(
        jnp.int32, (count, count), 1
    )


def decode_places(plen, adm, clen, slots, dec_rows):
    eff = effective_lengths(plen, adm, clen, slots)
    row = lax.broadcasted_iota(jnp.int32, (dec_rows, HD), 0)
    return by_slot(lax.rem(row, slots), eff) + row // slots


def decode_attention(n_seq, slots, plen, adm, clen, rotated, new, kvs, cache, part):
    seq = lax.axis_index("seq")
    dec_rows = rotated.shape[0]
    width = cache.shape[1]
    rows = kvs[0].shape[0]
    new_key, new_value = new[:, :HD], new[:, HD:]
    queries = jnp.concatenate(
        [rotated[:, h * HD : (h + 1) * HD] for h in range(rotated.shape[1] // HD)], axis=0
    )
    count = queries.shape[0]

    row = lax.rem(lax.broadcasted_iota(jnp.int32, (count, 1), 0), dec_rows)
    slot, step = lax.rem(row, slots), row // slots
    taken = by_slot(slot, [adm[r] for r in range(slots)])
    scores, masks, values = [], [], []
    at = lax.broadcasted_iota(jnp.int32, (1, width), 1) * n_seq + seq
    for r in range(slots):
        limit = jnp.where(adm[r] >= 0, 0, clen[r])
        masks.append((slot == r) & (at < limit))
        scores.append(dot_nt(queries, cache[r, :, :HD]))
        values.append(cache[r, :, HD:])
    spot = lax.broadcasted_iota(jnp.int32, (1, rows), 1)
    for p, kv in enumerate(kvs):
        prompt = seq * len(kvs) + p
        masks.append((taken == prompt) & (spot < plen[prompt]))
        scores.append(dot_nt(queries, kv[:, :HD]))
        values.append(kv[:, HD:])
    other = lax.broadcasted_iota(jnp.int32, (1, dec_rows), 1)
    first = jnp.where(seq == 0, 1, 0)
    masks.append(
        (lax.rem(other, slots) == slot) & (other // slots <= step) & (first + 0 * other > 0)
    )
    scores.append(dot_nt(queries, new_key))
    values.append(new_value)

    top = jnp.full((count, 1), NEG, F32)
    scores = [jnp.where(mask, score, NEG) for mask, score in zip(masks, scores)]
    for score in scores:
        top = jnp.maximum(top, jnp.max(score, axis=-1, keepdims=True))
    total = jnp.zeros((count, 1), F32)
    acc = jnp.zeros((count, HD), F32)
    for mask, score, value in zip(masks, scores, values):
        expo = jnp.where(mask, jnp.exp2((score - top) * C2), 0.0)
        total = total + jnp.sum(expo, axis=-1, keepdims=True)
        acc = acc + dot(expo.astype(BF), value)
    some = total > 0.0
    safe = jnp.where(some, total, 1.0)
    part[:count, :] = acc * (1.0 / safe)
    level = jnp.where(some, top * C2 + jnp.log2(safe), NEG)
    part[count : count + 1, :] = jnp.sum(jnp.where(unit(count), level, 0.0), axis=0, keepdims=True)


def project_kernel(n_head, n_seq, *refs):
    plen_h, adm_h, clen_h, qg_h, kg_h, table_h, x_hbm, dec_hbm, wq_hbm, wk_hbm, wv_hbm, wo_hbm = refs[:12]
    send_h, pack_h, blocks_h, leave_h = refs[12:16]
    x_v, dec_v, flat_v, wkv_v, wq_v, wo_v, raw, raw_kv, send, pack, blocks = refs[16:27]
    plen, adm, clen, qg, kg, table = refs[27:33]
    bias_v, s_v, w_v, values, q_v = refs[33:38]
    x_sem, dec_sem, wkv_sem, wq_sem, wo_sem, small_sem, out_sem = refs[38:]
    prompts, rows, width = x_hbm.shape
    steps, slots, _ = dec_hbm.shape
    dec_rows = steps * slots
    local = wq_v.shape[1]
    nb = width // n_head
    lead = prompts - 1
    seq = lax.axis_index("seq")
    first, _ = partners()
    diag = 3 - lax.axis_index("head")
    front = rows + dec_rows

    cuts = cut_points(width)
    queue = []
    for c in range(len(cuts) - 1):
        at = pl.ds(cuts[c], cuts[c + 1] - cuts[c])
        queue.append(
            [
                pltpu.make_async_copy(
                    x_hbm.at[lead, :, at], x_v.at[pl.ds(0, rows), at], x_sem.at[0, c]
                ),
                pltpu.make_async_copy(wk_hbm.at[at], wkv_v.at[at, pl.ds(0, HD)], wkv_sem.at[0, c]),
                pltpu.make_async_copy(wv_hbm.at[at], wkv_v.at[at, pl.ds(HD, HD)], wkv_sem.at[1, c]),
                pltpu.make_async_copy(wq_hbm.at[at], wq_v.at[at], wq_sem.at[c]),
            ]
        )
    small = [
        pltpu.make_async_copy(src, dst, small_sem.at[i])
        for i, (src, dst) in enumerate(
            [(plen_h, plen), (qg_h, qg), (kg_h, kg), (table_h, table), (adm_h, adm), (clen_h, clen)]
        )
    ]
    dec_copy = pltpu.make_async_copy(dec_hbm, dec_v, dec_sem)
    o_copies = [
        out_copy(wo_hbm, block, nb, wo_v.at[j], wo_sem.at[j]) for j, block in enumerate((diag, first))
    ]
    x0_copy = pltpu.make_async_copy(x_hbm.at[0], x_v.at[pl.ds(front, rows)], x_sem.at[1, 0])
    ahead = 3
    queue += [[x0_copy]] + [[copy] for copy in o_copies]
    for copy in [dec_copy] + queue[0] + small:
        copy.start()
    for group in queue[1:ahead]:
        for copy in group:
            copy.start()
    for copy in small:
        copy.wait()
    bias_v[...] = mask_bias(rows, plen[seq * prompts + lead])
    dec_copy.wait()
    for t in range(steps):
        flat_v[t * slots : (t + 1) * slots, :] = dec_v[t].astype(F32)
    x_v[rows:front, :] = flat_v[...].astype(BF)
    for c in range(len(cuts) - 1):
        for copy in queue[c]:
            copy.wait()
        if c + ahead < len(queue):
            for copy in queue[c + ahead]:
                copy.start()
        at = slice(cuts[c], cuts[c + 1])
        kv_part = dot(x_v[:front, at], wkv_v[at, :])
        q_part = dot(x_v[:front, at], wq_v[at, :])
        if c == 0:
            raw_kv[...] = kv_part
            raw[...] = q_part
        else:
            raw_kv[...] += kv_part
            raw[...] += q_part
    cos2, sin2 = table[:, :HD], table[:, HD:]
    both = 2 * HD
    base = prompts * both
    whole = pl.ds(0, rows)
    kvs = [pack.at[whole, pl.ds(p * both, both)] for p in range(prompts)]
    kvs[lead][:, :HD] = rope(norm(raw_kv[:rows, :HD], kg[...]), cos2, sin2).astype(BF)
    kvs[lead][:, HD:] = raw_kv[:rows, HD:].astype(BF)
    values[:, :HD] = kvs[lead][:, HD:]
    values[:, HD:] = jnp.ones((rows, HD), BF)
    places = decode_places(plen, adm, clen, slots, dec_rows)
    dcos2, dsin2 = cos_sin(places, turns(places))
    new_at = slice(rows, front)
    pack[new_at, :] = jnp.zeros((dec_rows, pack.shape[1]), BF)
    pack[new_at, :HD] = rope(norm(raw_kv[new_at, :HD], kg[...]), dcos2, dsin2).astype(BF)
    pack[new_at, HD:both] = raw_kv[new_at, HD:].astype(BF)
    for h in range(local // HD):
        col = base + h * HD
        at = slice(h * HD, (h + 1) * HD)
        pack[new_at, col : col + HD] = rope(norm(raw[new_at, at], qg[...]), dcos2, dsin2).astype(BF)
        q_v[h] = rope(norm(raw[:rows, at], qg[...]), cos2, sin2).astype(BF)
    x0_copy.wait()
    mine = pack.at[whole, pl.ds(base, local)]
    wide = 4 * HD
    for j in range(local // wide):
        later = dot(x_v[front:, :], wq_v[:, j * wide : (j + 1) * wide])
        if j == 0:
            kv0 = dot(x_v[front:, :], wkv_v[...])
        heads = range(4 * j, 4 * j + 4)
        attention(heads, q_v, kvs[lead], values, bias_v, s_v, w_v, mine)
        for i, h in enumerate(heads):
            col = base + local + h * HD
            piece = later[:, i * HD : (i + 1) * HD]
            pack[:rows, col : col + HD] = rope(norm(piece, qg[...]), cos2, sin2).astype(BF)
        if j == 0:
            kvs[0][:, :HD] = rope(norm(kv0[:, :HD], kg[...]), cos2, sin2).astype(BF)
            kvs[0][:, HD:] = kv0[:, HD:].astype(BF)
    each = rows // n_seq
    to_row = lax.broadcasted_iota(jnp.int32, (rows, rows), 0)
    from_row = lax.broadcasted_iota(jnp.int32, (rows, rows), 1)
    move = jnp.where(from_row == lax.rem(to_row, each) * n_seq + to_row // each, 1.0, 0.0).astype(BF)
    for p, kv in enumerate(kvs):
        moved = dot(move, kv[...]).astype(BF)
        for d in range(n_seq):
            blocks[d, p * each : (p + 1) * each] = moved[d * each : (d + 1) * each]
    half = n_seq // 2
    away = (1 - seq // half) * half
    outs = [
        pltpu.make_async_copy(blocks, blocks_h, out_sem.at[0]),
        pltpu.make_async_copy(blocks.at[pl.ds(away, half)], leave_h, out_sem.at[1]),
    ]
    for copy in outs:
        copy.start()
    for copy in o_copies:
        copy.wait()
    outs.append(pltpu.make_async_copy(pack, pack_h, out_sem.at[2]))
    outs[-1].start()
    for j in range(2):
        at = pl.ds(j * nb, nb)
        send[:, at] = dot(mine[...], wo_v[j]).astype(BF)
        outs.append(pltpu.make_async_copy(send.at[:, at], send_h.at[:, at], out_sem.at[3 + j]))
        outs[-1].start()
    for copy in outs:
        copy.wait()


def cut_points(width):
    step = width // 8
    return [0, step, 2 * step, 4 * step, 6 * step, 8 * step]


def project(n_head, n_seq, plen, adm, clen, qg, kg, table, x, dec, wq, wk, wv, wo):
    prompts, rows, width = x.shape
    dec_rows = dec.shape[0] * dec.shape[1]
    local = wq.shape[1]
    nb = width // n_head
    every = prompts * rows + dec_rows
    send = (rows, 2 * nb)
    pack = (rows + dec_rows, 2 * prompts * HD + prompts * local)
    blocks = (n_seq, prompts * rows // n_seq, 2 * HD)
    chunks = len(cut_points(width)) - 1
    return pl.pallas_call(
        functools.partial(project_kernel, n_head, n_seq),
        out_shape=[
            jax.ShapeDtypeStruct(send, BF),
            jax.ShapeDtypeStruct(pack, BF),
            jax.ShapeDtypeStruct(blocks, BF),
            jax.ShapeDtypeStruct((n_seq // 2,) + blocks[1:], BF),
        ],
        in_specs=[HB] * 12,
        out_specs=[HB] * 4,
        scratch_shapes=[
            pltpu.VMEM((every, width), BF),
            pltpu.VMEM(dec.shape, BF),
            pltpu.VMEM((dec_rows, width), F32),
            pltpu.VMEM((width, 2 * HD), BF),
            pltpu.VMEM((width, local), BF),
            pltpu.VMEM((2, local, nb), BF),
            pltpu.VMEM((rows + dec_rows, local), F32),
            pltpu.VMEM((rows + dec_rows, 2 * HD), F32),
            pltpu.VMEM(send, BF),
            pltpu.VMEM(pack, BF),
            pltpu.VMEM(blocks, BF),
            pltpu.SMEM(plen.shape, jnp.int32),
            pltpu.SMEM(adm.shape, jnp.int32),
            pltpu.SMEM(clen.shape, jnp.int32),
            pltpu.VMEM(qg.shape, F32),
            pltpu.VMEM(kg.shape, F32),
            pltpu.VMEM(table.shape, F32),
        ]
        + attention_scratch(rows, local // HD)
        + [
            pltpu.SemaphoreType.DMA((2, chunks)),
            pltpu.SemaphoreType.DMA,
            pltpu.SemaphoreType.DMA((2, chunks)),
            pltpu.SemaphoreType.DMA((chunks,)),
            pltpu.SemaphoreType.DMA((2,)),
            pltpu.SemaphoreType.DMA((6,)),
            pltpu.SemaphoreType.DMA((5,)),
        ],
        compiler_params=pltpu.CompilerParams(vmem_limit_bytes=LIMIT_A * MIB),
        cost_estimate=BRIEF,
        name="project",
    )(plen, adm, clen, qg, kg, table, x, dec, wq, wk, wv, wo)


def second_kernel(n_seq, prompts, *refs):
    plen_h, adm_h, clen_h, pack_h, cache_h, wo_hbm = refs[:6]
    send, attn, own1, part = refs[6:10]
    pack, cache, wo_v, plen, adm, clen = refs[10:16]
    bias_v, s_v, w_v, values, q_v = refs[16:21]
    pack_sem, small_sem, wo_sem, cache_sem = refs[21:]
    rows = attn.shape[0]
    dec_rows = pack.shape[0] - rows
    _, local, nb = wo_v.shape
    seq = lax.axis_index("seq")
    first, second = partners()
    head = lax.axis_index("head")
    pack_copy = pltpu.make_async_copy(pack_h, pack, pack_sem)
    cache_copy = pltpu.make_async_copy(cache_h, cache, cache_sem)
    small = [
        pltpu.make_async_copy(src, dst, small_sem.at[i])
        for i, (src, dst) in enumerate([(plen_h, plen), (adm_h, adm), (clen_h, clen)])
    ]
    copies = [
        out_copy(wo_hbm, block, nb, wo_v.at[j], wo_sem.at[j])
        for j, block in enumerate((head, second, 3 - head, first))
    ]
    for copy in small + [pack_copy] + copies[:2] + [cache_copy] + copies[2:]:
        copy.start()
    for copy in small:
        copy.wait()
    bias_v[...] = mask_bias(rows, plen[seq * prompts])
    pack_copy.wait()
    both = 2 * HD
    base = prompts * both
    whole = pl.ds(0, rows)
    kvs = [pack.at[whole, pl.ds(p * both, both)] for p in range(prompts)]
    other = pack.at[whole, pl.ds(base, local)]
    queries = pack.at[whole, pl.ds(base + local, local)]
    values[:, :HD] = kvs[0][:, HD:]
    values[:, HD:] = jnp.ones((rows, HD), BF)
    for h in range(local // HD):
        q_v[h] = queries[:, h * HD : (h + 1) * HD]
    for j in range(local // (4 * HD)):
        if j == 1:
            for i in range(2):
                copies[i].wait()
                own1[:, i * nb : (i + 1) * nb] = dot(other[...], wo_v[i]).astype(BF)
        attention(range(4 * j, 4 * j + 4), q_v, kvs[0], values, bias_v, s_v, w_v, attn)
    cache_copy.wait()
    for copy in copies[2:]:
        copy.wait()
    for j in range(2):
        send[:, j * nb : (j + 1) * nb] = dot(attn[...], wo_v[2 + j]).astype(BF)
    decode_attention(
        n_seq, cache.shape[0], plen, adm, clen, pack.at[pl.ds(rows, dec_rows), pl.ds(base, local)],
        pack.at[pl.ds(rows, dec_rows), pl.ds(0, both)], kvs, cache, part,
    )


def second(n_head, n_seq, prompts, rows, plen, adm, clen, pack, cache, wo):
    local, width = wo.shape
    nb = width // n_head
    dec_rows = pack.shape[0] - rows
    return pl.pallas_call(
        functools.partial(second_kernel, n_seq, prompts),
        out_shape=[
            jax.ShapeDtypeStruct((rows, 2 * nb), BF),
            jax.ShapeDtypeStruct((rows, local), BF),
            jax.ShapeDtypeStruct((rows, 2 * nb), BF),
            jax.ShapeDtypeStruct((dec_rows * (local // HD) + 8, HD), F32),
        ],
        in_specs=[HB] * 6,
        out_specs=[VM] * 4,
        scratch_shapes=[
            pltpu.VMEM(pack.shape, BF),
            pltpu.VMEM(cache.shape, BF),
            pltpu.VMEM((4, local, nb), BF),
            pltpu.SMEM(plen.shape, jnp.int32),
            pltpu.SMEM(adm.shape, jnp.int32),
            pltpu.SMEM(clen.shape, jnp.int32),
        ]
        + attention_scratch(rows, local // HD)
        + [
            pltpu.SemaphoreType.DMA,
            pltpu.SemaphoreType.DMA((3,)),
            pltpu.SemaphoreType.DMA((4,)),
            pltpu.SemaphoreType.DMA,
        ],
        compiler_params=pltpu.CompilerParams(vmem_limit_bytes=LIMIT_B * MIB),
        cost_estimate=BRIEF,
        name="second",
    )(plen, adm, clen, pack, cache, wo)


def third_kernel(attn, wo_hbm, own, wo_a, wo_b, wo_sem):
    nb = wo_a.shape[2]
    first, second = partners()
    head = lax.axis_index("head")
    wo_v = [wo_a.at[0], wo_a.at[1], wo_b.at[0], wo_b.at[1]]
    copies = [
        out_copy(wo_hbm, block, nb, wo_v[j], wo_sem.at[j])
        for j, block in enumerate((head, second, 3 - head, first))
    ]
    for copy in copies:
        copy.start()
    for j in range(2):
        copies[j].wait()
        own[:, j * nb : (j + 1) * nb] = dot(attn[...], wo_v[j][...]).astype(BF)
    for copy in copies[2:]:
        copy.wait()


def third(n_head, attn, wo):
    rows = attn.shape[0]
    local, width = wo.shape
    nb = width // n_head
    return pl.pallas_call(
        third_kernel,
        out_shape=[jax.ShapeDtypeStruct((rows, 2 * nb), BF)]
        + [jax.ShapeDtypeStruct((2, local, nb), BF)] * 2,
        in_specs=[VM, HB],
        out_specs=[VM] * 3,
        scratch_shapes=[pltpu.SemaphoreType.DMA((4,))],
        compiler_params=pltpu.CompilerParams(vmem_limit_bytes=LIMIT_C * MIB),
        cost_estimate=BRIEF,
        name="third",
    )(attn, wo)


def joined(bit, mine, other):
    count = mine.shape[0] - 8
    swap = lax.rem(lax.axis_index("seq") // bit, 2) == 1
    one, two = mine[...], other[...]
    low = jnp.where(swap, two, one)
    high = jnp.where(swap, one, two)
    eye = unit(count)

    def column(row):
        return jnp.sum(jnp.where(eye, row, 0.0), axis=1, keepdims=True)

    row_a, row_b = low[count : count + 1, :], high[count : count + 1, :]
    best = jnp.maximum(row_a, row_b)
    scale_a, scale_b = jnp.exp2(row_a - best), jnp.exp2(row_b - best)
    total = scale_a + scale_b
    inverse = 1.0 / total
    mixed = low[:count] * column(scale_a * inverse) + high[:count] * column(scale_b * inverse)
    return mixed, best + jnp.log2(total)


def range_start(seq, size):
    return seq // size * size


def range_start(seq, size):
    return seq // size * size


def join_kernel(bit, mine, other, out):
    count = mine.shape[0] - 8
    mixed, level = joined(bit, mine, other)
    out[:count, :] = mixed
    out[count : count + 1, :] = level


def join(bit, mine, other):
    return pl.pallas_call(
        functools.partial(join_kernel, bit),
        out_shape=jax.ShapeDtypeStruct(mine.shape, F32),
        in_specs=[VM] * 2,
        out_specs=VM,
        compiler_params=pltpu.CompilerParams(vmem_limit_bytes=8 * MIB),
        cost_estimate=BRIEF,
        name="join_%d" % bit,
    )(mine, other)


def hop_kernel(bit, *refs):
    held, leave = refs[:-1], refs[-1]
    seq = lax.axis_index("seq")
    size = bit // 2
    target = range_start(seq, bit) + size * (1 - lax.rem(seq // size, 2))
    at = 0
    for array in held:
        sources, dests = array.shape[:2]
        skip = target - range_start(seq, dests)
        for k in range(sources):
            leave[at] = array[k, pl.ds(skip, size)]
            at += 1


def hop(bit, held):
    sources = sum(array.shape[0] for array in held)
    return pl.pallas_call(
        functools.partial(hop_kernel, bit),
        out_shape=jax.ShapeDtypeStruct((sources, bit // 2) + held[0].shape[2:], BF),
        in_specs=[VM] * len(held),
        out_specs=VM,
        compiler_params=pltpu.CompilerParams(vmem_limit_bytes=8 * MIB),
        cost_estimate=BRIEF,
        name="hop_%d" % bit,
    )(*held)


def pass_on_kernel(own, got, on):
    nb = on.shape[1]
    on[...] = (own[:, nb:].astype(F32) + got[:, :nb].astype(F32)).astype(BF)


def pass_on(p, own, got):
    rows, both = got.shape
    return pl.pallas_call(
        pass_on_kernel,
        out_shape=jax.ShapeDtypeStruct((rows, both // 2), BF),
        in_specs=[VM] * 2,
        out_specs=VM,
        compiler_params=pltpu.CompilerParams(vmem_limit_bytes=8 * MIB),
        cost_estimate=BRIEF,
        name="pass_on_%d" % p,
    )(own, got)


def decode_out_kernel(bit, mine, other, wo_a, wo_b, *outs):
    count = mine.shape[0] - 8
    rows = outs[0].shape[0]
    mixed, _ = joined(bit, mine, other)
    mixed = mixed.astype(BF)
    flat = jnp.concatenate([mixed[i * rows : (i + 1) * rows] for i in range(count // rows)], axis=1)
    for j, out in enumerate(outs):
        out[...] = dot(flat, (wo_a, wo_b)[j // 2][j % 2]).astype(BF)


def decode_project(bit, dec_rows, mine, other, wo_a, wo_b):
    nb = wo_a.shape[2]
    return pl.pallas_call(
        functools.partial(decode_out_kernel, bit),
        out_shape=[jax.ShapeDtypeStruct((dec_rows, nb), BF)] * 4,
        in_specs=[VM] * 4,
        out_specs=[VM] * 4,
        compiler_params=pltpu.CompilerParams(vmem_limit_bytes=16 * MIB),
        cost_estimate=BRIEF,
        name="decode_project",
    )(mine, other, wo_a, wo_b)


def sum_parts(stage, out, sems, own, got, last):
    rows, nb = last.shape
    step = rows // 2
    copies = []
    for i in range(2):
        at = pl.ds(i * step, step)
        stage[at] = (
            own[at, :nb].astype(F32) + got[at, nb:].astype(F32) + last[at].astype(F32)
        ).astype(BF)
        copies.append(pltpu.make_async_copy(stage.at[at], out.at[at], sems.at[i]))
        copies[-1].start()
    return copies


def finish_first_kernel(p, bits, own, got, last, *refs):
    held, (out, handed, stage, sems, keep_sem) = refs[: len(bits) + 1], refs[len(bits) + 1 :]
    seq = lax.axis_index("seq")
    copies = []
    sources = [0]
    for j, array in enumerate(held):
        if j:
            sources = sources + [bits[j - 1] ^ source for source in sources]
        for k in range(array.shape[0]):
            source = seq ^ sources[len(copies)]
            copies.append(
                pltpu.make_async_copy(
                    array.at[k, seq - range_start(seq, array.shape[1])],
                    handed.at[source],
                    keep_sem.at[len(copies)],
                )
            )
            copies[-1].start()
    for copy in sum_parts(stage, out.at[p], sems, own, got, last) + copies:
        copy.wait()


def finish_first(p, prompts, bits, own, got, last, held):
    rows, nb = last.shape
    n_seq = held[0].shape[1]
    return pl.pallas_call(
        functools.partial(finish_first_kernel, p, bits),
        out_shape=[
            jax.ShapeDtypeStruct((prompts, rows, nb), BF),
            jax.ShapeDtypeStruct((n_seq,) + held[0].shape[2:], BF),
        ],
        in_specs=[VM] * (3 + len(held)),
        out_specs=[HB] * 2,
        scratch_shapes=[
            pltpu.VMEM((rows, nb), BF),
            pltpu.SemaphoreType.DMA((2,)),
            pltpu.SemaphoreType.DMA((n_seq,)),
        ],
        compiler_params=pltpu.CompilerParams(vmem_limit_bytes=8 * MIB),
        cost_estimate=BRIEF,
        name="finish_%d" % p,
    )(own, got, last, *held)


def finish_last_kernel(p, slots, own, got, last, *refs):
    pieces, (_, out, dec_out, stage, sems) = refs[:-5], refs[-5:]
    copies = sum_parts(stage, out.at[p], sems, own, got, last)
    total = pieces[0][...].astype(F32)
    for piece in pieces[1:]:
        total = total + piece[...].astype(F32)
    for t in range(dec_out.shape[0]):
        dec_out[t] = total[t * slots : (t + 1) * slots].astype(BF)
    for copy in copies:
        copy.wait()


def finish_last(p, steps, slots, own, got, last, pieces, partial):
    rows, nb = last.shape
    return pl.pallas_call(
        functools.partial(finish_last_kernel, p, slots),
        out_shape=[
            jax.ShapeDtypeStruct(partial.shape, BF),
            jax.ShapeDtypeStruct((steps, slots, nb), BF),
        ],
        in_specs=[VM] * (3 + len(pieces)) + [HB],
        out_specs=[HB, VM],
        scratch_shapes=[pltpu.VMEM((rows, nb), BF), pltpu.SemaphoreType.DMA((2,))],
        input_output_aliases={3 + len(pieces): 0},
        compiler_params=pltpu.CompilerParams(vmem_limit_bytes=8 * MIB),
        cost_estimate=BRIEF,
        name="finish_%d" % p,
    )(own, got, last, *pieces, partial)


def after(value, other):
    return lax.optimization_barrier((value, other))[0]


def local(
    prompts, prompt_len, admitted, cache_len, cache_kv, dec_tokens, w_query, w_key, w_value, w_out, q_gain, k_gain
):
    n_seq = lax.axis_size("seq")
    n_head = lax.axis_size("head")
    pr_dev, rows, width = prompts.shape
    steps, slots, _ = dec_tokens.shape
    dec_rows = steps * slots
    each = rows // n_seq
    qg, kg = q_gain.reshape(1, HD), k_gain.reshape(1, HD)
    def head_move(value, masks):
        pairs = [
            (h * n_seq + s, (h ^ masks[s % 2]) * n_seq + s)
            for h in range(n_head)
            for s in range(n_seq)
        ]
        return lax.ppermute(value, ("head", "seq"), pairs)

    def seq_move(value, bit):
        return lax.ppermute(value, "seq", [(i, i ^ bit) for i in range(n_seq)])

    bits = []
    while 2 ** len(bits) < n_seq:
        bits.append(2 ** len(bits))
    bits = bits[::-1]

    table = jnp.asarray(prompt_table(rows))
    scalars = (prompt_len, admitted, cache_len)
    send1, pack, blocks, leave = project(
        n_head, n_seq, *scalars, qg, kg, table, prompts, dec_tokens, w_query, w_key, w_value, w_out
    )
    got1 = head_move(send1, (1, 2))
    arrived = seq_move(leave, bits[0])
    send0, attn0, own1, part = second(
        n_head, n_seq, pr_dev, rows, *scalars, pack, cache_kv[0], w_out
    )
    send0, arrived = lax.optimization_barrier((send0, arrived))
    got0 = head_move(send0, (1, 2))
    other = seq_move(part, bits[0])
    own0, *wo = third(n_head, attn0, w_out)
    other, got1 = lax.optimization_barrier((other, got1, own0))[:2]
    for i, bit in enumerate(bits[:-1]):
        part = join(bit, part, other)
        other = seq_move(part, bits[i + 1])
    held = [blocks[None], after(arrived, part)[None]]
    leave = hop(bits[0], held)
    held.append(seq_move(leave, bits[1]))
    on1 = pass_on(1, own1, after(got1, part))
    last1 = head_move(on1, (2, 1))
    got0, other, held[-1] = lax.optimization_barrier((got0, other, held[-1], on1))[:3]
    on0 = pass_on(0, own0, got0)
    last0 = head_move(on0, (2, 1))
    held[-1] = after(held[-1], on0)
    for i, bit in enumerate(bits[1:-1]):
        leave = hop(bit, held)
        held.append(seq_move(leave, bits[i + 2]))
    other = lax.optimization_barrier((other, on0, leave))[0]
    pieces = decode_project(bits[-1], dec_rows, part, other, *wo)
    pieces = [
        pieces[0],
        head_move(pieces[1], (2, 1)),
        head_move(pieces[2], (3, 3)),
        head_move(pieces[3], (1, 2)),
    ]
    partial, handed = finish_first(1, pr_dev, bits, own1, got1, last1, held)
    prefill_out, decode_out = finish_last(0, steps, slots, own0, got0, last0, pieces, partial)
    return (prefill_out, handed.reshape(1, pr_dev * n_seq, each, 2 * HD), decode_out)


def solution(mesh):
    placed = (
        P("seq", None, None),
        P(),
        P(),
        P(),
        P("head", None, "seq", None),
        P(),
        P(None, "head"),
        P(None, "head"),
        P(None, "head"),
        P("head", None),
        P(),
        P(),
    )
    return jax.shard_map(
        local,
        mesh=mesh,
        in_specs=placed,
        out_specs=(P("seq", None, "head"), P("head", None, "seq", None), P(None, None, "head")),
        check_vma=False,
    )
```

```python
import functools

import jax
import jax.numpy as jnp
import numpy as np
from jax import lax
from jax.experimental import pallas as pl
from jax.experimental.pallas import tpu as pltpu
from jax.sharding import PartitionSpec as P

HD = 128
EPS = 1e-06
THETA = 1000000.0
NEG = -1e30
LOG2E = 1.4426950408889634
SCALE = HD**-0.5
C2 = SCALE * LOG2E
BF = jnp.bfloat16
F32 = jnp.float32
HB = pl.BlockSpec(memory_space=pltpu.HBM)
VM = pl.BlockSpec(memory_space=pltpu.VMEM)
BRIEF = pl.CostEstimate(flops=1, bytes_accessed=1, transcendentals=0)
MIB = 1024 * 1024
LIMIT_A = 60
LIMIT_B = 50
LIMIT_C = 42


def frequencies():
    half = HD // 2
    freq = np.float32(THETA) ** (-np.arange(half, dtype=np.float32) / np.float32(half))
    return freq.astype(np.float32)


def turns(places):
    lane = lax.broadcasted_iota(jnp.int32, places.shape, 1)
    freq = jnp.zeros(places.shape, F32)
    spot = lax.rem(lane, HD // 2)
    for i, value in enumerate(frequencies()):
        freq = jnp.where(spot == i, float(value), freq)
    return freq


def cos_sin(places, freq):
    angle = places.astype(F32) * freq
    lane = lax.broadcasted_iota(jnp.int32, places.shape, 1)
    return jnp.cos(angle), jnp.where(lane < HD // 2, -1.0, 1.0) * jnp.sin(angle)


def prompt_table(length):
    angle = np.arange(length, dtype=np.float32)[:, None] * frequencies()[None, :]
    cosine, sine = np.cos(angle), np.sin(angle)
    return np.concatenate([cosine, cosine, -sine, sine], axis=1).astype(np.float32)


def dot(a, b):
    return jnp.dot(a, b, preferred_element_type=F32)


def dot_nt(a, b):
    return lax.dot_general(a, b, (((1,), (1,)), ((), ())), preferred_element_type=F32)


def norm(values, gain):
    square = jnp.mean(values * values, axis=-1, keepdims=True)
    return values * lax.rsqrt(square + EPS) * gain


def rope(values, cos2, sin2):
    return values * cos2 + pltpu.roll(values, HD // 2, 1) * sin2


def effective_lengths(plen, adm, clen, slots):
    out = []
    for r in range(slots):
        taken = adm[r]
        out.append(jnp.where(taken >= 0, plen[jnp.maximum(taken, 0)], clen[r]))
    return out


def by_slot(index, values):
    result = jnp.full(index.shape, values[0])
    for r in range(1, len(values)):
        result = jnp.where(index == r, values[r], result)
    return result


def partners():
    head, seq = lax.axis_index("head"), lax.axis_index("seq")
    flip_x = head + 1 - 2 * lax.rem(head, 2)
    flip_y = lax.rem(head + 2, 4)
    even = lax.rem(seq, 2) == 0
    return jnp.where(even, flip_x, flip_y), jnp.where(even, flip_y, flip_x)


def out_copy(wo_hbm, block, nb, dest, sem):
    return pltpu.make_async_copy(
        wo_hbm.at[:, pl.ds(pl.multiple_of(block * nb, nb), nb)], dest, sem
    )


def mask_bias(rows, length):
    row_at = lax.broadcasted_iota(jnp.int32, (rows, rows), 0)
    col_at = lax.broadcasted_iota(jnp.int32, (rows, rows), 1)
    return jnp.where((col_at <= row_at) & (col_at < length), 0.0, NEG).astype(F32)


def attention(heads, q_v, kv, values, bias_v, s_v, w_v, attn):
    rows = kv.shape[0]
    half = rows // 2
    quarter = rows // 4
    low, count = heads[0], len(heads)
    group = pl.ds(low, count)
    parts = ((pl.ds(0, half), half), (pl.ds(half, half), rows))
    for part, keys in parts:
        queries = q_v[group, part].reshape(count * half, HD)
        scores = dot_nt(queries, kv[:keys, :HD])
        s_v[group, part, :keys] = scores.reshape(count, half, keys)
    for h in heads:
        for block in range(4):
            at = slice(block * quarter, (block + 1) * quarter)
            keys = half if block < 2 else rows
            scores = s_v[h, at, :keys] + bias_v[at, :keys]
            top = jnp.max(scores, axis=-1, keepdims=True)
            w_v[h, at, :keys] = jnp.exp2((scores - top) * C2).astype(BF)
    for part, keys in parts:
        weights = w_v[group, part, :keys].reshape(count * half, keys)
        mixed = dot(weights, values[:keys])
        mixed = (mixed[:, :HD] / mixed[:, HD:]).astype(BF)
        for i, h in enumerate(heads):
            attn[part, h * HD : (h + 1) * HD] = mixed[i * half : (i + 1) * half]


def attention_scratch(rows, heads):
    return [
        pltpu.VMEM((rows, rows), F32),
        pltpu.VMEM((heads, rows, rows), F32),
        pltpu.VMEM((heads, rows, rows), BF),
        pltpu.VMEM((rows, 2 * HD), BF),
        pltpu.VMEM((heads, rows, HD), BF),
    ]


def unit(count):
    return lax.broadcasted_iota(jnp.int32, (count, count), 0) == lax.broadcasted_iota(
        jnp.int32, (count, count), 1
    )


def decode_places(plen, adm, clen, slots, dec_rows):
    eff = effective_lengths(plen, adm, clen, slots)
    row = lax.broadcasted_iota(jnp.int32, (dec_rows, HD), 0)
    return by_slot(lax.rem(row, slots), eff) + row // slots


def decode_attention(n_seq, slots, plen, adm, clen, rotated, new, kvs, cache, part):
    seq = lax.axis_index("seq")
    dec_rows = rotated.shape[0]
    width = cache.shape[1]
    rows = kvs[0].shape[0]
    new_key, new_value = new[:, :HD], new[:, HD:]
    queries = jnp.concatenate(
        [rotated[:, h * HD : (h + 1) * HD] for h in range(rotated.shape[1] // HD)], axis=0
    )
    count = queries.shape[0]

    row = lax.rem(lax.broadcasted_iota(jnp.int32, (count, 1), 0), dec_rows)
    slot, step = lax.rem(row, slots), row // slots
    taken = by_slot(slot, [adm[r] for r in range(slots)])
    scores, masks, values = [], [], []
    at = lax.broadcasted_iota(jnp.int32, (1, width), 1) * n_seq + seq
    for r in range(slots):
        limit = jnp.where(adm[r] >= 0, 0, clen[r])
        masks.append((slot == r) & (at < limit))
        scores.append(dot_nt(queries, cache[r, :, :HD]))
        values.append(cache[r, :, HD:])
    spot = lax.broadcasted_iota(jnp.int32, (1, rows), 1)
    for p, kv in enumerate(kvs):
        prompt = seq * len(kvs) + p
        masks.append((taken == prompt) & (spot < plen[prompt]))
        scores.append(dot_nt(queries, kv[:, :HD]))
        values.append(kv[:, HD:])
    other = lax.broadcasted_iota(jnp.int32, (1, dec_rows), 1)
    first = jnp.where(seq == 0, 1, 0)
    masks.append(
        (lax.rem(other, slots) == slot) & (other // slots <= step) & (first + 0 * other > 0)
    )
    scores.append(dot_nt(queries, new_key))
    values.append(new_value)

    top = jnp.full((count, 1), NEG, F32)
    scores = [jnp.where(mask, score, NEG) for mask, score in zip(masks, scores)]
    for score in scores:
        top = jnp.maximum(top, jnp.max(score, axis=-1, keepdims=True))
    total = jnp.zeros((count, 1), F32)
    acc = jnp.zeros((count, HD), F32)
    for mask, score, value in zip(masks, scores, values):
        expo = jnp.where(mask, jnp.exp2((score - top) * C2), 0.0)
        total = total + jnp.sum(expo, axis=-1, keepdims=True)
        acc = acc + dot(expo.astype(BF), value)
    some = total > 0.0
    safe = jnp.where(some, total, 1.0)
    part[:count, :] = acc * (1.0 / safe)
    level = jnp.where(some, top * C2 + jnp.log2(safe), NEG)
    part[count : count + 1, :] = jnp.sum(jnp.where(unit(count), level, 0.0), axis=0, keepdims=True)


def project_kernel(n_head, n_seq, *refs):
    plen_h, adm_h, clen_h, qg_h, kg_h, table_h, x_hbm, dec_hbm, wq_hbm, wk_hbm, wv_hbm, wo_hbm = refs[:12]
    send_h, pack_h, blocks_h, leave_h = refs[12:16]
    x_v, dec_v, flat_v, wkv_v, wq_v, wo_v, raw, raw_kv, send, pack, blocks = refs[16:27]
    plen, adm, clen, qg, kg, table = refs[27:33]
    bias_v, s_v, w_v, values, q_v = refs[33:38]
    x_sem, dec_sem, wkv_sem, wq_sem, wo_sem, small_sem, out_sem = refs[38:]
    prompts, rows, width = x_hbm.shape
    steps, slots, _ = dec_hbm.shape
    dec_rows = steps * slots
    local = wq_v.shape[1]
    nb = width // n_head
    lead = prompts - 1
    seq = lax.axis_index("seq")
    first, _ = partners()
    diag = 3 - lax.axis_index("head")
    front = rows + dec_rows

    cuts = cut_points(width)
    queue = []
    for c in range(len(cuts) - 1):
        at = pl.ds(cuts[c], cuts[c + 1] - cuts[c])
        queue.append(
            [
                pltpu.make_async_copy(
                    x_hbm.at[lead, :, at], x_v.at[pl.ds(0, rows), at], x_sem.at[0, c]
                ),
                pltpu.make_async_copy(
                    x_hbm.at[0, :, at], x_v.at[pl.ds(front, rows), at], x_sem.at[1, c]
                ),
                pltpu.make_async_copy(wk_hbm.at[at], wkv_v.at[at, pl.ds(0, HD)], wkv_sem.at[0, c]),
                pltpu.make_async_copy(wv_hbm.at[at], wkv_v.at[at, pl.ds(HD, HD)], wkv_sem.at[1, c]),
                pltpu.make_async_copy(wq_hbm.at[at], wq_v.at[at], wq_sem.at[c]),
            ]
        )
    small = [
        pltpu.make_async_copy(src, dst, small_sem.at[i])
        for i, (src, dst) in enumerate(
            [(plen_h, plen), (qg_h, qg), (kg_h, kg), (table_h, table), (adm_h, adm), (clen_h, clen)]
        )
    ]
    dec_copy = pltpu.make_async_copy(dec_hbm, dec_v, dec_sem)
    o_copies = [
        out_copy(wo_hbm, block, nb, wo_v.at[j], wo_sem.at[j]) for j, block in enumerate((diag, first))
    ]
    ahead = 3
    for copy in [dec_copy] + queue[0] + small:
        copy.start()
    for group in queue[1:ahead]:
        for copy in group:
            copy.start()
    for copy in small:
        copy.wait()
    bias_v[...] = mask_bias(rows, plen[seq * prompts + lead])
    dec_copy.wait()
    for t in range(steps):
        flat_v[t * slots : (t + 1) * slots, :] = dec_v[t].astype(F32)
    x_v[rows:front, :] = flat_v[...].astype(BF)
    for c in range(len(cuts) - 1):
        for copy in queue[c]:
            copy.wait()
        if c + ahead < len(queue):
            for copy in queue[c + ahead]:
                copy.start()
        at = slice(cuts[c], cuts[c + 1])
        kv_part = dot(x_v[:, at], wkv_v[at, :])
        q_part = dot(x_v[:front, at], wq_v[at, :])
        if c == 0:
            raw_kv[...] = kv_part
            raw[...] = q_part
        else:
            raw_kv[...] += kv_part
            raw[...] += q_part
    for copy in o_copies:
        copy.start()
    cos2, sin2 = table[:, :HD], table[:, HD:]
    both = 2 * HD
    base = prompts * both
    whole = pl.ds(0, rows)
    kvs = [pack.at[whole, pl.ds(p * both, both)] for p in range(prompts)]
    for p, start in ((lead, 0), (0, front)):
        at = slice(start, start + rows)
        kvs[p][:, :HD] = rope(norm(raw_kv[at, :HD], kg[...]), cos2, sin2).astype(BF)
        kvs[p][:, HD:] = raw_kv[at, HD:].astype(BF)
    values[:, :HD] = kvs[lead][:, HD:]
    values[:, HD:] = jnp.ones((rows, HD), BF)
    each = rows // n_seq
    to_row = lax.broadcasted_iota(jnp.int32, (rows, rows), 0)
    from_row = lax.broadcasted_iota(jnp.int32, (rows, rows), 1)
    move = jnp.where(from_row == lax.rem(to_row, each) * n_seq + to_row // each, 1.0, 0.0).astype(BF)
    for p, kv in enumerate(kvs):
        moved = dot(move, kv[...]).astype(BF)
        for d in range(n_seq):
            blocks[d, p * each : (p + 1) * each] = moved[d * each : (d + 1) * each]
    half = n_seq // 2
    away = (1 - seq // half) * half
    outs = [
        pltpu.make_async_copy(blocks, blocks_h, out_sem.at[0]),
        pltpu.make_async_copy(blocks.at[pl.ds(away, half)], leave_h, out_sem.at[1]),
    ]
    for copy in outs:
        copy.start()
    places = decode_places(plen, adm, clen, slots, dec_rows)
    dcos2, dsin2 = cos_sin(places, turns(places))
    new_at = slice(rows, front)
    pack[new_at, :] = jnp.zeros((dec_rows, pack.shape[1]), BF)
    pack[new_at, :HD] = rope(norm(raw_kv[new_at, :HD], kg[...]), dcos2, dsin2).astype(BF)
    pack[new_at, HD:both] = raw_kv[new_at, HD:].astype(BF)
    for h in range(local // HD):
        piece = raw[new_at, h * HD : (h + 1) * HD]
        col = base + h * HD
        pack[new_at, col : col + HD] = rope(norm(piece, qg[...]), dcos2, dsin2).astype(BF)
    for copy in o_copies:
        copy.wait()
    mine = pack.at[whole, pl.ds(base, local)]
    wide = 4 * HD
    for j in range(local // wide):
        later = dot(x_v[front:, :], wq_v[:, j * wide : (j + 1) * wide])
        heads = range(4 * j, 4 * j + 4)
        for h in heads:
            piece = raw[:rows, h * HD : (h + 1) * HD]
            q_v[h] = rope(norm(piece, qg[...]), cos2, sin2).astype(BF)
        attention(heads, q_v, kvs[lead], values, bias_v, s_v, w_v, mine)
        for i, h in enumerate(heads):
            col = base + local + h * HD
            piece = later[:, i * HD : (i + 1) * HD]
            pack[:rows, col : col + HD] = rope(norm(piece, qg[...]), cos2, sin2).astype(BF)
    outs.append(pltpu.make_async_copy(pack, pack_h, out_sem.at[2]))
    outs[-1].start()
    for j in range(2):
        at = pl.ds(j * nb, nb)
        send[:, at] = dot(mine[...], wo_v[j]).astype(BF)
        outs.append(pltpu.make_async_copy(send.at[:, at], send_h.at[:, at], out_sem.at[3 + j]))
        outs[-1].start()
    for copy in outs:
        copy.wait()


def cut_points(width):
    step = width // 16
    return [step * i for i in (0, 2, 6, 10, 13, 15, 16)]


def project(n_head, n_seq, plen, adm, clen, qg, kg, table, x, dec, wq, wk, wv, wo):
    prompts, rows, width = x.shape
    dec_rows = dec.shape[0] * dec.shape[1]
    local = wq.shape[1]
    nb = width // n_head
    every = prompts * rows + dec_rows
    send = (rows, 2 * nb)
    pack = (rows + dec_rows, 2 * prompts * HD + prompts * local)
    blocks = (n_seq, prompts * rows // n_seq, 2 * HD)
    chunks = len(cut_points(width)) - 1
    return pl.pallas_call(
        functools.partial(project_kernel, n_head, n_seq),
        out_shape=[
            jax.ShapeDtypeStruct(send, BF),
            jax.ShapeDtypeStruct(pack, BF),
            jax.ShapeDtypeStruct(blocks, BF),
            jax.ShapeDtypeStruct((n_seq // 2,) + blocks[1:], BF),
        ],
        in_specs=[HB] * 12,
        out_specs=[HB] * 4,
        scratch_shapes=[
            pltpu.VMEM((every, width), BF),
            pltpu.VMEM(dec.shape, BF),
            pltpu.VMEM((dec_rows, width), F32),
            pltpu.VMEM((width, 2 * HD), BF),
            pltpu.VMEM((width, local), BF),
            pltpu.VMEM((2, local, nb), BF),
            pltpu.VMEM((rows + dec_rows, local), F32),
            pltpu.VMEM((every, 2 * HD), F32),
            pltpu.VMEM(send, BF),
            pltpu.VMEM(pack, BF),
            pltpu.VMEM(blocks, BF),
            pltpu.SMEM(plen.shape, jnp.int32),
            pltpu.SMEM(adm.shape, jnp.int32),
            pltpu.SMEM(clen.shape, jnp.int32),
            pltpu.VMEM(qg.shape, F32),
            pltpu.VMEM(kg.shape, F32),
            pltpu.VMEM(table.shape, F32),
        ]
        + attention_scratch(rows, local // HD)
        + [
            pltpu.SemaphoreType.DMA((2, chunks)),
            pltpu.SemaphoreType.DMA,
            pltpu.SemaphoreType.DMA((2, chunks)),
            pltpu.SemaphoreType.DMA((chunks,)),
            pltpu.SemaphoreType.DMA((2,)),
            pltpu.SemaphoreType.DMA((6,)),
            pltpu.SemaphoreType.DMA((5,)),
        ],
        compiler_params=pltpu.CompilerParams(vmem_limit_bytes=LIMIT_A * MIB),
        cost_estimate=BRIEF,
        name="project",
    )(plen, adm, clen, qg, kg, table, x, dec, wq, wk, wv, wo)


def second_kernel(n_seq, prompts, *refs):
    plen_h, adm_h, clen_h, pack_h, cache_h, wo_hbm = refs[:6]
    send, attn, own1, part = refs[6:10]
    pack, cache, wo_v, plen, adm, clen = refs[10:16]
    bias_v, s_v, w_v, values, q_v = refs[16:21]
    pack_sem, small_sem, wo_sem, cache_sem = refs[21:]
    rows = attn.shape[0]
    dec_rows = pack.shape[0] - rows
    _, local, nb = wo_v.shape
    seq = lax.axis_index("seq")
    first, second = partners()
    head = lax.axis_index("head")
    pack_copy = pltpu.make_async_copy(pack_h, pack, pack_sem)
    cache_copy = pltpu.make_async_copy(cache_h, cache, cache_sem)
    small = [
        pltpu.make_async_copy(src, dst, small_sem.at[i])
        for i, (src, dst) in enumerate([(plen_h, plen), (adm_h, adm), (clen_h, clen)])
    ]
    copies = [
        out_copy(wo_hbm, block, nb, wo_v.at[j], wo_sem.at[j])
        for j, block in enumerate((head, second, 3 - head, first))
    ]
    for copy in small + [pack_copy] + copies[:2] + [cache_copy] + copies[2:]:
        copy.start()
    for copy in small:
        copy.wait()
    bias_v[...] = mask_bias(rows, plen[seq * prompts])
    pack_copy.wait()
    both = 2 * HD
    base = prompts * both
    whole = pl.ds(0, rows)
    kvs = [pack.at[whole, pl.ds(p * both, both)] for p in range(prompts)]
    other = pack.at[whole, pl.ds(base, local)]
    queries = pack.at[whole, pl.ds(base + local, local)]
    values[:, :HD] = kvs[0][:, HD:]
    values[:, HD:] = jnp.ones((rows, HD), BF)
    for h in range(local // HD):
        q_v[h] = queries[:, h * HD : (h + 1) * HD]
    for j in range(local // (4 * HD)):
        if j == 1:
            for i in range(2):
                copies[i].wait()
                own1[:, i * nb : (i + 1) * nb] = dot(other[...], wo_v[i]).astype(BF)
        attention(range(4 * j, 4 * j + 4), q_v, kvs[0], values, bias_v, s_v, w_v, attn)
    cache_copy.wait()
    for copy in copies[2:]:
        copy.wait()
    for j in range(2):
        send[:, j * nb : (j + 1) * nb] = dot(attn[...], wo_v[2 + j]).astype(BF)
    decode_attention(
        n_seq, cache.shape[0], plen, adm, clen, pack.at[pl.ds(rows, dec_rows), pl.ds(base, local)],
        pack.at[pl.ds(rows, dec_rows), pl.ds(0, both)], kvs, cache, part,
    )


def second(n_head, n_seq, prompts, rows, plen, adm, clen, pack, cache, wo):
    local, width = wo.shape
    nb = width // n_head
    dec_rows = pack.shape[0] - rows
    return pl.pallas_call(
        functools.partial(second_kernel, n_seq, prompts),
        out_shape=[
            jax.ShapeDtypeStruct((rows, 2 * nb), BF),
            jax.ShapeDtypeStruct((rows, local), BF),
            jax.ShapeDtypeStruct((rows, 2 * nb), BF),
            jax.ShapeDtypeStruct((dec_rows * (local // HD) + 8, HD), F32),
        ],
        in_specs=[HB] * 6,
        out_specs=[VM] * 4,
        scratch_shapes=[
            pltpu.VMEM(pack.shape, BF),
            pltpu.VMEM(cache.shape, BF),
            pltpu.VMEM((4, local, nb), BF),
            pltpu.SMEM(plen.shape, jnp.int32),
            pltpu.SMEM(adm.shape, jnp.int32),
            pltpu.SMEM(clen.shape, jnp.int32),
        ]
        + attention_scratch(rows, local // HD)
        + [
            pltpu.SemaphoreType.DMA,
            pltpu.SemaphoreType.DMA((3,)),
            pltpu.SemaphoreType.DMA((4,)),
            pltpu.SemaphoreType.DMA,
        ],
        compiler_params=pltpu.CompilerParams(vmem_limit_bytes=LIMIT_B * MIB),
        cost_estimate=BRIEF,
        name="second",
    )(plen, adm, clen, pack, cache, wo)


def third_kernel(attn, wo_hbm, own, wo_a, wo_b, wo_sem):
    nb = wo_a.shape[2]
    first, second = partners()
    head = lax.axis_index("head")
    wo_v = [wo_a.at[0], wo_a.at[1], wo_b.at[0], wo_b.at[1]]
    copies = [
        out_copy(wo_hbm, block, nb, wo_v[j], wo_sem.at[j])
        for j, block in enumerate((head, second, 3 - head, first))
    ]
    for copy in copies:
        copy.start()
    for j in range(2):
        copies[j].wait()
        own[:, j * nb : (j + 1) * nb] = dot(attn[...], wo_v[j][...]).astype(BF)
    for copy in copies[2:]:
        copy.wait()


def third(n_head, attn, wo):
    rows = attn.shape[0]
    local, width = wo.shape
    nb = width // n_head
    return pl.pallas_call(
        third_kernel,
        out_shape=[jax.ShapeDtypeStruct((rows, 2 * nb), BF)]
        + [jax.ShapeDtypeStruct((2, local, nb), BF)] * 2,
        in_specs=[VM, HB],
        out_specs=[VM] * 3,
        scratch_shapes=[pltpu.SemaphoreType.DMA((4,))],
        compiler_params=pltpu.CompilerParams(vmem_limit_bytes=LIMIT_C * MIB),
        cost_estimate=BRIEF,
        name="third",
    )(attn, wo)


def joined(bit, mine, other):
    count = mine.shape[0] - 8
    swap = lax.rem(lax.axis_index("seq") // bit, 2) == 1
    one, two = mine[...], other[...]
    low = jnp.where(swap, two, one)
    high = jnp.where(swap, one, two)
    eye = unit(count)

    def column(row):
        return jnp.sum(jnp.where(eye, row, 0.0), axis=1, keepdims=True)

    row_a, row_b = low[count : count + 1, :], high[count : count + 1, :]
    best = jnp.maximum(row_a, row_b)
    scale_a, scale_b = jnp.exp2(row_a - best), jnp.exp2(row_b - best)
    total = scale_a + scale_b
    inverse = 1.0 / total
    mixed = low[:count] * column(scale_a * inverse) + high[:count] * column(scale_b * inverse)
    return mixed, best + jnp.log2(total)


def range_start(seq, size):
    return seq // size * size


def range_start(seq, size):
    return seq // size * size


def join_kernel(bit, mine, other, out):
    count = mine.shape[0] - 8
    mixed, level = joined(bit, mine, other)
    out[:count, :] = mixed
    out[count : count + 1, :] = level


def join(bit, mine, other):
    return pl.pallas_call(
        functools.partial(join_kernel, bit),
        out_shape=jax.ShapeDtypeStruct(mine.shape, F32),
        in_specs=[VM] * 2,
        out_specs=VM,
        compiler_params=pltpu.CompilerParams(vmem_limit_bytes=8 * MIB),
        cost_estimate=BRIEF,
        name="join_%d" % bit,
    )(mine, other)


def hop_kernel(bit, *refs):
    held, leave = refs[:-1], refs[-1]
    seq = lax.axis_index("seq")
    size = bit // 2
    target = range_start(seq, bit) + size * (1 - lax.rem(seq // size, 2))
    at = 0
    for array in held:
        sources, dests = array.shape[:2]
        skip = target - range_start(seq, dests)
        for k in range(sources):
            leave[at] = array[k, pl.ds(skip, size)]
            at += 1


def hop(bit, held):
    sources = sum(array.shape[0] for array in held)
    return pl.pallas_call(
        functools.partial(hop_kernel, bit),
        out_shape=jax.ShapeDtypeStruct((sources, bit // 2) + held[0].shape[2:], BF),
        in_specs=[VM] * len(held),
        out_specs=VM,
        compiler_params=pltpu.CompilerParams(vmem_limit_bytes=8 * MIB),
        cost_estimate=BRIEF,
        name="hop_%d" % bit,
    )(*held)


def pass_on_kernel(own, got, on):
    nb = on.shape[1]
    on[...] = (own[:, nb:].astype(F32) + got[:, :nb].astype(F32)).astype(BF)


def pass_on(p, own, got):
    rows, both = got.shape
    return pl.pallas_call(
        pass_on_kernel,
        out_shape=jax.ShapeDtypeStruct((rows, both // 2), BF),
        in_specs=[VM] * 2,
        out_specs=VM,
        compiler_params=pltpu.CompilerParams(vmem_limit_bytes=8 * MIB),
        cost_estimate=BRIEF,
        name="pass_on_%d" % p,
    )(own, got)


def decode_out_kernel(bit, mine, other, wo_a, wo_b, *outs):
    count = mine.shape[0] - 8
    rows = outs[0].shape[0]
    mixed, _ = joined(bit, mine, other)
    mixed = mixed.astype(BF)
    flat = jnp.concatenate([mixed[i * rows : (i + 1) * rows] for i in range(count // rows)], axis=1)
    for j, out in enumerate(outs):
        out[...] = dot(flat, (wo_a, wo_b)[j // 2][j % 2]).astype(BF)


def decode_project(bit, dec_rows, mine, other, wo_a, wo_b):
    nb = wo_a.shape[2]
    return pl.pallas_call(
        functools.partial(decode_out_kernel, bit),
        out_shape=[jax.ShapeDtypeStruct((dec_rows, nb), BF)] * 4,
        in_specs=[VM] * 4,
        out_specs=[VM] * 4,
        compiler_params=pltpu.CompilerParams(vmem_limit_bytes=16 * MIB),
        cost_estimate=BRIEF,
        name="decode_project",
    )(mine, other, wo_a, wo_b)


def sum_parts(stage, out, sems, own, got, last):
    rows, nb = last.shape
    step = rows // 4
    copies = []
    for i in range(4):
        at = pl.ds(i * step, step)
        stage[at] = (
            own[at, :nb].astype(F32) + got[at, nb:].astype(F32) + last[at].astype(F32)
        ).astype(BF)
        copies.append(pltpu.make_async_copy(stage.at[at], out.at[at], sems.at[i]))
        copies[-1].start()
    return copies


def finish_first_kernel(p, bits, own, got, last, *refs):
    held, (out, handed, stage, sems, keep_sem) = refs[: len(bits) + 1], refs[len(bits) + 1 :]
    seq = lax.axis_index("seq")
    copies = []
    sources = [0]
    for j, array in enumerate(held):
        if j:
            sources = sources + [bits[j - 1] ^ source for source in sources]
        for k in range(array.shape[0]):
            source = seq ^ sources[len(copies)]
            copies.append(
                pltpu.make_async_copy(
                    array.at[k, seq - range_start(seq, array.shape[1])],
                    handed.at[source],
                    keep_sem.at[len(copies)],
                )
            )
            copies[-1].start()
    for copy in sum_parts(stage, out.at[p], sems, own, got, last) + copies:
        copy.wait()


def finish_first(p, prompts, bits, own, got, last, held):
    rows, nb = last.shape
    n_seq = held[0].shape[1]
    return pl.pallas_call(
        functools.partial(finish_first_kernel, p, bits),
        out_shape=[
            jax.ShapeDtypeStruct((prompts, rows, nb), BF),
            jax.ShapeDtypeStruct((n_seq,) + held[0].shape[2:], BF),
        ],
        in_specs=[VM] * (3 + len(held)),
        out_specs=[HB] * 2,
        scratch_shapes=[
            pltpu.VMEM((rows, nb), BF),
            pltpu.SemaphoreType.DMA((4,)),
            pltpu.SemaphoreType.DMA((n_seq,)),
        ],
        compiler_params=pltpu.CompilerParams(vmem_limit_bytes=8 * MIB),
        cost_estimate=BRIEF,
        name="finish_%d" % p,
    )(own, got, last, *held)


def finish_last_kernel(p, own, got, last, _, out, stage, sems):
    for copy in sum_parts(stage, out.at[p], sems, own, got, last):
        copy.wait()


def finish_last(p, own, got, last, partial):
    rows, nb = last.shape
    return pl.pallas_call(
        functools.partial(finish_last_kernel, p),
        out_shape=jax.ShapeDtypeStruct(partial.shape, BF),
        in_specs=[VM] * 3 + [HB],
        out_specs=HB,
        scratch_shapes=[pltpu.VMEM((rows, nb), BF), pltpu.SemaphoreType.DMA((4,))],
        input_output_aliases={3: 0},
        compiler_params=pltpu.CompilerParams(vmem_limit_bytes=8 * MIB),
        cost_estimate=BRIEF,
        name="finish_%d" % p,
    )(own, got, last, partial)


def decode_sum_kernel(slots, *refs):
    pieces, out = refs[:-1], refs[-1]
    total = pieces[0][...].astype(F32)
    for piece in pieces[1:]:
        total = total + piece[...].astype(F32)
    for t in range(out.shape[0]):
        out[t] = total[t * slots : (t + 1) * slots].astype(BF)


def decode_sum(steps, slots, pieces):
    return pl.pallas_call(
        functools.partial(decode_sum_kernel, slots),
        out_shape=jax.ShapeDtypeStruct((steps, slots, pieces[0].shape[1]), BF),
        in_specs=[VM] * len(pieces),
        out_specs=VM,
        compiler_params=pltpu.CompilerParams(vmem_limit_bytes=8 * MIB),
        cost_estimate=BRIEF,
        name="decode_sum",
    )(*pieces)


def after(value, other):
    return lax.optimization_barrier((value, other))[0]


def local(
    prompts, prompt_len, admitted, cache_len, cache_kv, dec_tokens, w_query, w_key, w_value, w_out, q_gain, k_gain
):
    n_seq = lax.axis_size("seq")
    n_head = lax.axis_size("head")
    pr_dev, rows, width = prompts.shape
    steps, slots, _ = dec_tokens.shape
    dec_rows = steps * slots
    each = rows // n_seq
    qg, kg = q_gain.reshape(1, HD), k_gain.reshape(1, HD)
    def head_move(value, masks):
        pairs = [
            (h * n_seq + s, (h ^ masks[s % 2]) * n_seq + s)
            for h in range(n_head)
            for s in range(n_seq)
        ]
        return lax.ppermute(value, ("head", "seq"), pairs)

    def seq_move(value, bit):
        return lax.ppermute(value, "seq", [(i, i ^ bit) for i in range(n_seq)])

    bits = []
    while 2 ** len(bits) < n_seq:
        bits.append(2 ** len(bits))
    bits = bits[::-1]

    table = jnp.asarray(prompt_table(rows))
    scalars = (prompt_len, admitted, cache_len)
    send1, pack, blocks, leave = project(
        n_head, n_seq, *scalars, qg, kg, table, prompts, dec_tokens, w_query, w_key, w_value, w_out
    )
    got1 = head_move(send1, (1, 2))
    arrived = seq_move(leave, bits[0])
    send0, attn0, own1, part = second(
        n_head, n_seq, pr_dev, rows, *scalars, pack, cache_kv[0], w_out
    )
    send0, arrived = lax.optimization_barrier((send0, arrived))
    got0 = head_move(send0, (1, 2))
    other = seq_move(part, bits[0])
    own0, *wo = third(n_head, attn0, w_out)
    other, got1 = lax.optimization_barrier((other, got1, own0))[:2]
    for i, bit in enumerate(bits[:-1]):
        part = join(bit, part, other)
        other = seq_move(part, bits[i + 1])
    held = [blocks[None], after(arrived, part)[None]]
    leave = hop(bits[0], held)
    held.append(seq_move(leave, bits[1]))
    on1 = pass_on(1, own1, after(got1, part))
    last1 = head_move(on1, (2, 1))
    got0, other, held[-1] = lax.optimization_barrier((got0, other, held[-1], on1))[:3]
    on0 = pass_on(0, own0, got0)
    last0 = head_move(on0, (2, 1))
    held[-1] = after(held[-1], on0)
    for i, bit in enumerate(bits[1:-1]):
        leave = hop(bit, held)
        held.append(seq_move(leave, bits[i + 2]))
    other = lax.optimization_barrier((other, on0, leave))[0]
    pieces = decode_project(bits[-1], dec_rows, part, other, *wo)
    pieces = [
        pieces[0],
        head_move(pieces[1], (2, 1)),
        head_move(pieces[2], (3, 3)),
        head_move(pieces[3], (1, 2)),
    ]
    partial, handed = finish_first(1, pr_dev, bits, own1, got1, last1, held)
    pieces = list(lax.optimization_barrier((*pieces, partial))[:-1])
    decode_out = decode_sum(steps, slots, pieces)
    prefill_out = finish_last(0, own0, got0, after(last0, decode_out), partial)
    return (prefill_out, handed.reshape(1, pr_dev * n_seq, each, 2 * HD), decode_out)


def solution(mesh):
    placed = (
        P("seq", None, None),
        P(),
        P(),
        P(),
        P("head", None, "seq", None),
        P(),
        P(None, "head"),
        P(None, "head"),
        P(None, "head"),
        P("head", None),
        P(),
        P(),
    )
    return jax.shard_map(
        local,
        mesh=mesh,
        in_specs=placed,
        out_specs=(P("seq", None, "head"), P("head", None, "seq", None), P(None, None, "head")),
        check_vma=False,
    )
```

```python
import functools

import jax
import jax.numpy as jnp
import numpy as np
from jax import lax
from jax.experimental import pallas as pl
from jax.experimental.pallas import tpu as pltpu
from jax.sharding import PartitionSpec as P

HD = 128
EPS = 1e-06
THETA = 1000000.0
NEG = -1e30
LOG2E = 1.4426950408889634
SCALE = HD**-0.5
C2 = SCALE * LOG2E
BF = jnp.bfloat16
F32 = jnp.float32
HB = pl.BlockSpec(memory_space=pltpu.HBM)
VM = pl.BlockSpec(memory_space=pltpu.VMEM)
BRIEF = pl.CostEstimate(flops=1, bytes_accessed=1, transcendentals=0)
MIB = 1024 * 1024
LIMIT_A = 60
LIMIT_B = 50
LIMIT_C = 42


def frequencies():
    half = HD // 2
    freq = np.float32(THETA) ** (-np.arange(half, dtype=np.float32) / np.float32(half))
    return freq.astype(np.float32)


def turns(places):
    lane = lax.broadcasted_iota(jnp.int32, places.shape, 1)
    freq = jnp.zeros(places.shape, F32)
    spot = lax.rem(lane, HD // 2)
    for i, value in enumerate(frequencies()):
        freq = jnp.where(spot == i, float(value), freq)
    return freq


def cos_sin(places, freq):
    angle = places.astype(F32) * freq
    lane = lax.broadcasted_iota(jnp.int32, places.shape, 1)
    return jnp.cos(angle), jnp.where(lane < HD // 2, -1.0, 1.0) * jnp.sin(angle)


def prompt_table(length):
    angle = np.arange(length, dtype=np.float32)[:, None] * frequencies()[None, :]
    cosine, sine = np.cos(angle), np.sin(angle)
    return np.concatenate([cosine, cosine, -sine, sine], axis=1).astype(np.float32)


def dot(a, b):
    return jnp.dot(a, b, preferred_element_type=F32)


def dot_nt(a, b):
    return lax.dot_general(a, b, (((1,), (1,)), ((), ())), preferred_element_type=F32)


def norm(values, gain):
    square = jnp.mean(values * values, axis=-1, keepdims=True)
    return values * lax.rsqrt(square + EPS) * gain


def rope(values, cos2, sin2):
    return values * cos2 + pltpu.roll(values, HD // 2, 1) * sin2


def effective_lengths(plen, adm, clen, slots):
    out = []
    for r in range(slots):
        taken = adm[r]
        out.append(jnp.where(taken >= 0, plen[jnp.maximum(taken, 0)], clen[r]))
    return out


def by_slot(index, values):
    result = jnp.full(index.shape, values[0])
    for r in range(1, len(values)):
        result = jnp.where(index == r, values[r], result)
    return result


def partners():
    head, seq = lax.axis_index("head"), lax.axis_index("seq")
    flip_x = head + 1 - 2 * lax.rem(head, 2)
    flip_y = lax.rem(head + 2, 4)
    even = lax.rem(seq, 2) == 0
    return jnp.where(even, flip_x, flip_y), jnp.where(even, flip_y, flip_x)


def out_copy(wo_hbm, block, nb, dest, sem):
    return pltpu.make_async_copy(
        wo_hbm.at[:, pl.ds(pl.multiple_of(block * nb, nb), nb)], dest, sem
    )


def mask_bias(rows, length):
    row_at = lax.broadcasted_iota(jnp.int32, (rows, rows), 0)
    col_at = lax.broadcasted_iota(jnp.int32, (rows, rows), 1)
    return jnp.where((col_at <= row_at) & (col_at < length), 0.0, NEG).astype(F32)


def attention(heads, q_v, kv, values, bias_v, s_v, w_v, attn):
    rows = kv.shape[0]
    half = rows // 2
    quarter = rows // 4
    low, count = heads[0], len(heads)
    group = pl.ds(low, count)
    parts = ((pl.ds(0, half), half), (pl.ds(half, half), rows))
    for part, keys in parts:
        queries = q_v[group, part].reshape(count * half, HD)
        scores = dot_nt(queries, kv[:keys, :HD])
        s_v[group, part, :keys] = scores.reshape(count, half, keys)
    for h in heads:
        for block in range(4):
            at = slice(block * quarter, (block + 1) * quarter)
            keys = half if block < 2 else rows
            scores = s_v[h, at, :keys] + bias_v[at, :keys]
            top = jnp.max(scores, axis=-1, keepdims=True)
            w_v[h, at, :keys] = jnp.exp2((scores - top) * C2).astype(BF)
    for part, keys in parts:
        weights = w_v[group, part, :keys].reshape(count * half, keys)
        mixed = dot(weights, values[:keys])
        mixed = (mixed[:, :HD] / mixed[:, HD:]).astype(BF)
        for i, h in enumerate(heads):
            attn[part, h * HD : (h + 1) * HD] = mixed[i * half : (i + 1) * half]


def attention_scratch(rows, heads):
    return [
        pltpu.VMEM((rows, rows), F32),
        pltpu.VMEM((heads, rows, rows), F32),
        pltpu.VMEM((heads, rows, rows), BF),
        pltpu.VMEM((rows, 2 * HD), BF),
        pltpu.VMEM((heads, rows, HD), BF),
    ]


def unit(count):
    return lax.broadcasted_iota(jnp.int32, (count, count), 0) == lax.broadcasted_iota(
        jnp.int32, (count, count), 1
    )


def decode_places(plen, adm, clen, slots, dec_rows):
    eff = effective_lengths(plen, adm, clen, slots)
    row = lax.broadcasted_iota(jnp.int32, (dec_rows, HD), 0)
    return by_slot(lax.rem(row, slots), eff) + row // slots


def decode_attention(n_seq, slots, plen, adm, clen, rotated, new, kvs, cache, part):
    seq = lax.axis_index("seq")
    dec_rows = rotated.shape[0]
    width = cache.shape[1]
    rows = kvs[0].shape[0]
    new_key, new_value = new[:, :HD], new[:, HD:]
    queries = jnp.concatenate(
        [rotated[:, h * HD : (h + 1) * HD] for h in range(rotated.shape[1] // HD)], axis=0
    )
    count = queries.shape[0]

    row = lax.rem(lax.broadcasted_iota(jnp.int32, (count, 1), 0), dec_rows)
    slot, step = lax.rem(row, slots), row // slots
    taken = by_slot(slot, [adm[r] for r in range(slots)])
    scores, masks, values = [], [], []
    at = lax.broadcasted_iota(jnp.int32, (1, width), 1) * n_seq + seq
    for r in range(slots):
        limit = jnp.where(adm[r] >= 0, 0, clen[r])
        masks.append((slot == r) & (at < limit))
        scores.append(dot_nt(queries, cache[r, :, :HD]))
        values.append(cache[r, :, HD:])
    spot = lax.broadcasted_iota(jnp.int32, (1, rows), 1)
    for p, kv in enumerate(kvs):
        prompt = seq * len(kvs) + p
        masks.append((taken == prompt) & (spot < plen[prompt]))
        scores.append(dot_nt(queries, kv[:, :HD]))
        values.append(kv[:, HD:])
    other = lax.broadcasted_iota(jnp.int32, (1, dec_rows), 1)
    first = jnp.where(seq == 0, 1, 0)
    masks.append(
        (lax.rem(other, slots) == slot) & (other // slots <= step) & (first + 0 * other > 0)
    )
    scores.append(dot_nt(queries, new_key))
    values.append(new_value)

    top = jnp.full((count, 1), NEG, F32)
    scores = [jnp.where(mask, score, NEG) for mask, score in zip(masks, scores)]
    for score in scores:
        top = jnp.maximum(top, jnp.max(score, axis=-1, keepdims=True))
    total = jnp.zeros((count, 1), F32)
    acc = jnp.zeros((count, HD), F32)
    for mask, score, value in zip(masks, scores, values):
        expo = jnp.where(mask, jnp.exp2((score - top) * C2), 0.0)
        total = total + jnp.sum(expo, axis=-1, keepdims=True)
        acc = acc + dot(expo.astype(BF), value)
    some = total > 0.0
    safe = jnp.where(some, total, 1.0)
    part[:count, :] = acc * (1.0 / safe)
    level = jnp.where(some, top * C2 + jnp.log2(safe), NEG)
    part[count : count + 1, :] = jnp.sum(jnp.where(unit(count), level, 0.0), axis=0, keepdims=True)


def project_kernel(n_head, n_seq, *refs):
    plen_h, adm_h, clen_h, qg_h, kg_h, table_h, x_hbm, dec_hbm, wq_hbm, wk_hbm, wv_hbm, wo_hbm = refs[:12]
    send_h, pack_h, blocks_h, leave_h = refs[12:16]
    x_v, dec_v, flat_v, wkv_v, wq_v, wo_v, raw, raw_kv, send, pack, blocks = refs[16:27]
    plen, adm, clen, qg, kg, table = refs[27:33]
    bias_v, s_v, w_v, values, q_v = refs[33:38]
    x_sem, dec_sem, wkv_sem, wq_sem, wo_sem, small_sem, out_sem = refs[38:]
    prompts, rows, width = x_hbm.shape
    steps, slots, _ = dec_hbm.shape
    dec_rows = steps * slots
    local = wq_v.shape[1]
    nb = width // n_head
    lead = prompts - 1
    seq = lax.axis_index("seq")
    first, _ = partners()
    diag = 3 - lax.axis_index("head")
    front = rows + dec_rows

    cuts = cut_points(width)
    queue = []
    for c in range(len(cuts) - 1):
        at = pl.ds(cuts[c], cuts[c + 1] - cuts[c])
        queue.append(
            [
                pltpu.make_async_copy(
                    x_hbm.at[lead, :, at], x_v.at[pl.ds(0, rows), at], x_sem.at[0, c]
                ),
                pltpu.make_async_copy(
                    x_hbm.at[0, :, at], x_v.at[pl.ds(front, rows), at], x_sem.at[1, c]
                ),
                pltpu.make_async_copy(wk_hbm.at[at], wkv_v.at[at, pl.ds(0, HD)], wkv_sem.at[0, c]),
                pltpu.make_async_copy(wv_hbm.at[at], wkv_v.at[at, pl.ds(HD, HD)], wkv_sem.at[1, c]),
                pltpu.make_async_copy(wq_hbm.at[at], wq_v.at[at], wq_sem.at[c]),
            ]
        )
    small = [
        pltpu.make_async_copy(src, dst, small_sem.at[i])
        for i, (src, dst) in enumerate(
            [(plen_h, plen), (qg_h, qg), (kg_h, kg), (table_h, table), (adm_h, adm), (clen_h, clen)]
        )
    ]
    dec_copy = pltpu.make_async_copy(dec_hbm, dec_v, dec_sem)
    o_copies = [
        out_copy(wo_hbm, block, nb, wo_v.at[j], wo_sem.at[j]) for j, block in enumerate((diag, first))
    ]
    ahead = 3
    for copy in [dec_copy] + queue[0] + small:
        copy.start()
    for group in queue[1:ahead]:
        for copy in group:
            copy.start()
    for copy in small:
        copy.wait()
    bias_v[...] = mask_bias(rows, plen[seq * prompts + lead])
    dec_copy.wait()
    for t in range(steps):
        flat_v[t * slots : (t + 1) * slots, :] = dec_v[t].astype(F32)
    x_v[rows:front, :] = flat_v[...].astype(BF)
    for c in range(len(cuts) - 1):
        for copy in queue[c]:
            copy.wait()
        if c + ahead < len(queue):
            for copy in queue[c + ahead]:
                copy.start()
        at = slice(cuts[c], cuts[c + 1])
        kv_part = dot(x_v[:, at], wkv_v[at, :])
        q_part = dot(x_v[:front, at], wq_v[at, :])
        if c == 0:
            raw_kv[...] = kv_part
            raw[...] = q_part
        else:
            raw_kv[...] += kv_part
            raw[...] += q_part
    for copy in o_copies:
        copy.start()
    cos2, sin2 = table[:, :HD], table[:, HD:]
    both = 2 * HD
    base = prompts * both
    whole = pl.ds(0, rows)
    kvs = [pack.at[whole, pl.ds(p * both, both)] for p in range(prompts)]
    for p, start in ((lead, 0), (0, front)):
        at = slice(start, start + rows)
        kvs[p][:, :HD] = rope(norm(raw_kv[at, :HD], kg[...]), cos2, sin2).astype(BF)
        kvs[p][:, HD:] = raw_kv[at, HD:].astype(BF)
    values[:, :HD] = kvs[lead][:, HD:]
    values[:, HD:] = jnp.ones((rows, HD), BF)
    each = rows // n_seq
    to_row = lax.broadcasted_iota(jnp.int32, (rows, rows), 0)
    from_row = lax.broadcasted_iota(jnp.int32, (rows, rows), 1)
    move = jnp.where(from_row == lax.rem(to_row, each) * n_seq + to_row // each, 1.0, 0.0).astype(BF)
    for p, kv in enumerate(kvs):
        moved = dot(move, kv[...]).astype(BF)
        for d in range(n_seq):
            blocks[d, p * each : (p + 1) * each] = moved[d * each : (d + 1) * each]
    half = n_seq // 2
    away = (1 - seq // half) * half
    outs = [
        pltpu.make_async_copy(blocks, blocks_h, out_sem.at[0]),
        pltpu.make_async_copy(blocks.at[pl.ds(away, half)], leave_h, out_sem.at[1]),
    ]
    for copy in outs:
        copy.start()
    places = decode_places(plen, adm, clen, slots, dec_rows)
    dcos2, dsin2 = cos_sin(places, turns(places))
    new_at = slice(rows, front)
    pack[new_at, :] = jnp.zeros((dec_rows, pack.shape[1]), BF)
    pack[new_at, :HD] = rope(norm(raw_kv[new_at, :HD], kg[...]), dcos2, dsin2).astype(BF)
    pack[new_at, HD:both] = raw_kv[new_at, HD:].astype(BF)
    for h in range(local // HD):
        piece = raw[new_at, h * HD : (h + 1) * HD]
        col = base + h * HD
        pack[new_at, col : col + HD] = rope(norm(piece, qg[...]), dcos2, dsin2).astype(BF)
    mine = pack.at[whole, pl.ds(base, local)]
    wide = 4 * HD
    for j in range(local // wide):
        later = dot(x_v[front:, :], wq_v[:, j * wide : (j + 1) * wide])
        heads = range(4 * j, 4 * j + 4)
        for h in heads:
            piece = raw[:rows, h * HD : (h + 1) * HD]
            q_v[h] = rope(norm(piece, qg[...]), cos2, sin2).astype(BF)
        attention(heads, q_v, kvs[lead], values, bias_v, s_v, w_v, mine)
        for i, h in enumerate(heads):
            col = base + local + h * HD
            piece = later[:, i * HD : (i + 1) * HD]
            pack[:rows, col : col + HD] = rope(norm(piece, qg[...]), cos2, sin2).astype(BF)
    outs.append(pltpu.make_async_copy(pack, pack_h, out_sem.at[2]))
    outs[-1].start()
    for copy in o_copies:
        copy.wait()
    for j in range(2):
        at = pl.ds(j * nb, nb)
        send[:, at] = dot(mine[...], wo_v[j]).astype(BF)
        outs.append(pltpu.make_async_copy(send.at[:, at], send_h.at[:, at], out_sem.at[3 + j]))
        outs[-1].start()
    for copy in outs:
        copy.wait()


def cut_points(width):
    step = width // 16
    return [step * i for i in (0, 2, 6, 10, 13, 15, 16)]


def project(n_head, n_seq, plen, adm, clen, qg, kg, table, x, dec, wq, wk, wv, wo):
    prompts, rows, width = x.shape
    dec_rows = dec.shape[0] * dec.shape[1]
    local = wq.shape[1]
    nb = width // n_head
    every = prompts * rows + dec_rows
    send = (rows, 2 * nb)
    pack = (rows + dec_rows, 2 * prompts * HD + prompts * local)
    blocks = (n_seq, prompts * rows // n_seq, 2 * HD)
    chunks = len(cut_points(width)) - 1
    return pl.pallas_call(
        functools.partial(project_kernel, n_head, n_seq),
        out_shape=[
            jax.ShapeDtypeStruct(send, BF),
            jax.ShapeDtypeStruct(pack, BF),
            jax.ShapeDtypeStruct(blocks, BF),
            jax.ShapeDtypeStruct((n_seq // 2,) + blocks[1:], BF),
        ],
        in_specs=[HB] * 12,
        out_specs=[HB] * 4,
        scratch_shapes=[
            pltpu.VMEM((every, width), BF),
            pltpu.VMEM(dec.shape, BF),
            pltpu.VMEM((dec_rows, width), F32),
            pltpu.VMEM((width, 2 * HD), BF),
            pltpu.VMEM((width, local), BF),
            pltpu.VMEM((2, local, nb), BF),
            pltpu.VMEM((rows + dec_rows, local), F32),
            pltpu.VMEM((every, 2 * HD), F32),
            pltpu.VMEM(send, BF),
            pltpu.VMEM(pack, BF),
            pltpu.VMEM(blocks, BF),
            pltpu.SMEM(plen.shape, jnp.int32),
            pltpu.SMEM(adm.shape, jnp.int32),
            pltpu.SMEM(clen.shape, jnp.int32),
            pltpu.VMEM(qg.shape, F32),
            pltpu.VMEM(kg.shape, F32),
            pltpu.VMEM(table.shape, F32),
        ]
        + attention_scratch(rows, local // HD)
        + [
            pltpu.SemaphoreType.DMA((2, chunks)),
            pltpu.SemaphoreType.DMA,
            pltpu.SemaphoreType.DMA((2, chunks)),
            pltpu.SemaphoreType.DMA((chunks,)),
            pltpu.SemaphoreType.DMA((2,)),
            pltpu.SemaphoreType.DMA((6,)),
            pltpu.SemaphoreType.DMA((5,)),
        ],
        compiler_params=pltpu.CompilerParams(vmem_limit_bytes=LIMIT_A * MIB),
        cost_estimate=BRIEF,
        name="project",
    )(plen, adm, clen, qg, kg, table, x, dec, wq, wk, wv, wo)


def second_kernel(n_seq, prompts, *refs):
    plen_h, adm_h, clen_h, pack_h, cache_h, wo_hbm = refs[:6]
    send, attn, own1, part = refs[6:10]
    pack, cache, wo_v, plen, adm, clen = refs[10:16]
    bias_v, s_v, w_v, values, q_v = refs[16:21]
    pack_sem, small_sem, wo_sem, cache_sem = refs[21:]
    rows = attn.shape[0]
    dec_rows = pack.shape[0] - rows
    _, local, nb = wo_v.shape
    seq = lax.axis_index("seq")
    first, second = partners()
    head = lax.axis_index("head")
    pack_copy = pltpu.make_async_copy(pack_h, pack, pack_sem)
    cache_copy = pltpu.make_async_copy(cache_h, cache, cache_sem)
    small = [
        pltpu.make_async_copy(src, dst, small_sem.at[i])
        for i, (src, dst) in enumerate([(plen_h, plen), (adm_h, adm), (clen_h, clen)])
    ]
    copies = [
        out_copy(wo_hbm, block, nb, wo_v.at[j], wo_sem.at[j])
        for j, block in enumerate((head, second, 3 - head, first))
    ]
    for copy in small + [pack_copy] + copies[:2] + [cache_copy] + copies[2:]:
        copy.start()
    for copy in small:
        copy.wait()
    bias_v[...] = mask_bias(rows, plen[seq * prompts])
    pack_copy.wait()
    both = 2 * HD
    base = prompts * both
    whole = pl.ds(0, rows)
    kvs = [pack.at[whole, pl.ds(p * both, both)] for p in range(prompts)]
    other = pack.at[whole, pl.ds(base, local)]
    queries = pack.at[whole, pl.ds(base + local, local)]
    values[:, :HD] = kvs[0][:, HD:]
    values[:, HD:] = jnp.ones((rows, HD), BF)
    for h in range(local // HD):
        q_v[h] = queries[:, h * HD : (h + 1) * HD]
    for j in range(local // (4 * HD)):
        if j == 1:
            for i in range(2):
                copies[i].wait()
                own1[:, i * nb : (i + 1) * nb] = dot(other[...], wo_v[i]).astype(BF)
        attention(range(4 * j, 4 * j + 4), q_v, kvs[0], values, bias_v, s_v, w_v, attn)
    cache_copy.wait()
    for copy in copies[2:]:
        copy.wait()
    for j in range(2):
        send[:, j * nb : (j + 1) * nb] = dot(attn[...], wo_v[2 + j]).astype(BF)
    decode_attention(
        n_seq, cache.shape[0], plen, adm, clen, pack.at[pl.ds(rows, dec_rows), pl.ds(base, local)],
        pack.at[pl.ds(rows, dec_rows), pl.ds(0, both)], kvs, cache, part,
    )


def second(n_head, n_seq, prompts, rows, plen, adm, clen, pack, cache, wo):
    local, width = wo.shape
    nb = width // n_head
    dec_rows = pack.shape[0] - rows
    return pl.pallas_call(
        functools.partial(second_kernel, n_seq, prompts),
        out_shape=[
            jax.ShapeDtypeStruct((rows, 2 * nb), BF),
            jax.ShapeDtypeStruct((rows, local), BF),
            jax.ShapeDtypeStruct((rows, 2 * nb), BF),
            jax.ShapeDtypeStruct((dec_rows * (local // HD) + 8, HD), F32),
        ],
        in_specs=[HB] * 6,
        out_specs=[VM] * 4,
        scratch_shapes=[
            pltpu.VMEM(pack.shape, BF),
            pltpu.VMEM(cache.shape, BF),
            pltpu.VMEM((4, local, nb), BF),
            pltpu.SMEM(plen.shape, jnp.int32),
            pltpu.SMEM(adm.shape, jnp.int32),
            pltpu.SMEM(clen.shape, jnp.int32),
        ]
        + attention_scratch(rows, local // HD)
        + [
            pltpu.SemaphoreType.DMA,
            pltpu.SemaphoreType.DMA((3,)),
            pltpu.SemaphoreType.DMA((4,)),
            pltpu.SemaphoreType.DMA,
        ],
        compiler_params=pltpu.CompilerParams(vmem_limit_bytes=LIMIT_B * MIB),
        cost_estimate=BRIEF,
        name="second",
    )(plen, adm, clen, pack, cache, wo)


def third_kernel(attn, wo_hbm, own, wo_a, wo_b, wo_sem):
    nb = wo_a.shape[2]
    first, second = partners()
    head = lax.axis_index("head")
    wo_v = [wo_a.at[0], wo_a.at[1], wo_b.at[0], wo_b.at[1]]
    copies = [
        out_copy(wo_hbm, block, nb, wo_v[j], wo_sem.at[j])
        for j, block in enumerate((head, second, 3 - head, first))
    ]
    for copy in copies:
        copy.start()
    for j in range(2):
        copies[j].wait()
        own[:, j * nb : (j + 1) * nb] = dot(attn[...], wo_v[j][...]).astype(BF)
    for copy in copies[2:]:
        copy.wait()


def third(n_head, attn, wo):
    rows = attn.shape[0]
    local, width = wo.shape
    nb = width // n_head
    return pl.pallas_call(
        third_kernel,
        out_shape=[jax.ShapeDtypeStruct((rows, 2 * nb), BF)]
        + [jax.ShapeDtypeStruct((2, local, nb), BF)] * 2,
        in_specs=[VM, HB],
        out_specs=[VM] * 3,
        scratch_shapes=[pltpu.SemaphoreType.DMA((4,))],
        compiler_params=pltpu.CompilerParams(vmem_limit_bytes=LIMIT_C * MIB),
        cost_estimate=BRIEF,
        name="third",
    )(attn, wo)


def joined(bit, mine, other):
    count = mine.shape[0] - 8
    swap = lax.rem(lax.axis_index("seq") // bit, 2) == 1
    one, two = mine[...], other[...]
    low = jnp.where(swap, two, one)
    high = jnp.where(swap, one, two)
    eye = unit(count)

    def column(row):
        return jnp.sum(jnp.where(eye, row, 0.0), axis=1, keepdims=True)

    row_a, row_b = low[count : count + 1, :], high[count : count + 1, :]
    best = jnp.maximum(row_a, row_b)
    scale_a, scale_b = jnp.exp2(row_a - best), jnp.exp2(row_b - best)
    total = scale_a + scale_b
    inverse = 1.0 / total
    mixed = low[:count] * column(scale_a * inverse) + high[:count] * column(scale_b * inverse)
    return mixed, best + jnp.log2(total)


def range_start(seq, size):
    return seq // size * size


def range_start(seq, size):
    return seq // size * size


def join_kernel(bit, mine, other, out):
    count = mine.shape[0] - 8
    mixed, level = joined(bit, mine, other)
    out[:count, :] = mixed
    out[count : count + 1, :] = level


def join(bit, mine, other):
    return pl.pallas_call(
        functools.partial(join_kernel, bit),
        out_shape=jax.ShapeDtypeStruct(mine.shape, F32),
        in_specs=[VM] * 2,
        out_specs=VM,
        compiler_params=pltpu.CompilerParams(vmem_limit_bytes=8 * MIB),
        cost_estimate=BRIEF,
        name="join_%d" % bit,
    )(mine, other)


def hop_kernel(bit, *refs):
    held, leave = refs[:-1], refs[-1]
    seq = lax.axis_index("seq")
    size = bit // 2
    target = range_start(seq, bit) + size * (1 - lax.rem(seq // size, 2))
    at = 0
    for array in held:
        sources, dests = array.shape[:2]
        skip = target - range_start(seq, dests)
        for k in range(sources):
            leave[at] = array[k, pl.ds(skip, size)]
            at += 1


def hop(bit, held):
    sources = sum(array.shape[0] for array in held)
    return pl.pallas_call(
        functools.partial(hop_kernel, bit),
        out_shape=jax.ShapeDtypeStruct((sources, bit // 2) + held[0].shape[2:], BF),
        in_specs=[VM] * len(held),
        out_specs=VM,
        compiler_params=pltpu.CompilerParams(vmem_limit_bytes=8 * MIB),
        cost_estimate=BRIEF,
        name="hop_%d" % bit,
    )(*held)


def pass_on_kernel(own, got, on):
    nb = on.shape[1]
    on[...] = (own[:, nb:].astype(F32) + got[:, :nb].astype(F32)).astype(BF)


def pass_on(p, own, got):
    rows, both = got.shape
    return pl.pallas_call(
        pass_on_kernel,
        out_shape=jax.ShapeDtypeStruct((rows, both // 2), BF),
        in_specs=[VM] * 2,
        out_specs=VM,
        compiler_params=pltpu.CompilerParams(vmem_limit_bytes=8 * MIB),
        cost_estimate=BRIEF,
        name="pass_on_%d" % p,
    )(own, got)


def decode_out_kernel(bit, mine, other, wo_a, wo_b, *outs):
    count = mine.shape[0] - 8
    rows = outs[0].shape[0]
    mixed, _ = joined(bit, mine, other)
    mixed = mixed.astype(BF)
    flat = jnp.concatenate([mixed[i * rows : (i + 1) * rows] for i in range(count // rows)], axis=1)
    for j, out in enumerate(outs):
        out[...] = dot(flat, (wo_a, wo_b)[j // 2][j % 2]).astype(BF)


def decode_project(bit, dec_rows, mine, other, wo_a, wo_b):
    nb = wo_a.shape[2]
    return pl.pallas_call(
        functools.partial(decode_out_kernel, bit),
        out_shape=[jax.ShapeDtypeStruct((dec_rows, nb), BF)] * 4,
        in_specs=[VM] * 4,
        out_specs=[VM] * 4,
        compiler_params=pltpu.CompilerParams(vmem_limit_bytes=16 * MIB),
        cost_estimate=BRIEF,
        name="decode_project",
    )(mine, other, wo_a, wo_b)


def sum_parts(stage, out, sems, own, got, last):
    rows, nb = last.shape
    step = rows // 4
    copies = []
    for i in range(4):
        at = pl.ds(i * step, step)
        stage[at] = (
            own[at, :nb].astype(F32) + got[at, nb:].astype(F32) + last[at].astype(F32)
        ).astype(BF)
        copies.append(pltpu.make_async_copy(stage.at[at], out.at[at], sems.at[i]))
        copies[-1].start()
    return copies


def finish_first_kernel(p, bits, own, got, last, *refs):
    held, (out, handed, stage, sems, keep_sem) = refs[: len(bits) + 1], refs[len(bits) + 1 :]
    seq = lax.axis_index("seq")
    copies = []
    sources = [0]
    for j, array in enumerate(held):
        if j:
            sources = sources + [bits[j - 1] ^ source for source in sources]
        for k in range(array.shape[0]):
            source = seq ^ sources[len(copies)]
            copies.append(
                pltpu.make_async_copy(
                    array.at[k, seq - range_start(seq, array.shape[1])],
                    handed.at[source],
                    keep_sem.at[len(copies)],
                )
            )
            copies[-1].start()
    for copy in sum_parts(stage, out.at[p], sems, own, got, last) + copies:
        copy.wait()


def finish_first(p, prompts, bits, own, got, last, held):
    rows, nb = last.shape
    n_seq = held[0].shape[1]
    return pl.pallas_call(
        functools.partial(finish_first_kernel, p, bits),
        out_shape=[
            jax.ShapeDtypeStruct((prompts, rows, nb), BF),
            jax.ShapeDtypeStruct((n_seq,) + held[0].shape[2:], BF),
        ],
        in_specs=[VM] * (3 + len(held)),
        out_specs=[HB] * 2,
        scratch_shapes=[
            pltpu.VMEM((rows, nb), BF),
            pltpu.SemaphoreType.DMA((4,)),
            pltpu.SemaphoreType.DMA((n_seq,)),
        ],
        compiler_params=pltpu.CompilerParams(vmem_limit_bytes=8 * MIB),
        cost_estimate=BRIEF,
        name="finish_%d" % p,
    )(own, got, last, *held)


def finish_last_kernel(p, own, got, last, _, out, stage, sems):
    for copy in sum_parts(stage, out.at[p], sems, own, got, last):
        copy.wait()


def finish_last(p, own, got, last, partial):
    rows, nb = last.shape
    return pl.pallas_call(
        functools.partial(finish_last_kernel, p),
        out_shape=jax.ShapeDtypeStruct(partial.shape, BF),
        in_specs=[VM] * 3 + [HB],
        out_specs=HB,
        scratch_shapes=[pltpu.VMEM((rows, nb), BF), pltpu.SemaphoreType.DMA((4,))],
        input_output_aliases={3: 0},
        compiler_params=pltpu.CompilerParams(vmem_limit_bytes=8 * MIB),
        cost_estimate=BRIEF,
        name="finish_%d" % p,
    )(own, got, last, partial)


def decode_sum_kernel(slots, *refs):
    pieces, out = refs[:-1], refs[-1]
    total = pieces[0][...].astype(F32)
    for piece in pieces[1:]:
        total = total + piece[...].astype(F32)
    for t in range(out.shape[0]):
        out[t] = total[t * slots : (t + 1) * slots].astype(BF)


def decode_sum(steps, slots, pieces):
    return pl.pallas_call(
        functools.partial(decode_sum_kernel, slots),
        out_shape=jax.ShapeDtypeStruct((steps, slots, pieces[0].shape[1]), BF),
        in_specs=[VM] * len(pieces),
        out_specs=VM,
        compiler_params=pltpu.CompilerParams(vmem_limit_bytes=8 * MIB),
        cost_estimate=BRIEF,
        name="decode_sum",
    )(*pieces)


def after(value, other):
    return lax.optimization_barrier((value, other))[0]


def local(
    prompts, prompt_len, admitted, cache_len, cache_kv, dec_tokens, w_query, w_key, w_value, w_out, q_gain, k_gain
):
    n_seq = lax.axis_size("seq")
    n_head = lax.axis_size("head")
    pr_dev, rows, width = prompts.shape
    steps, slots, _ = dec_tokens.shape
    dec_rows = steps * slots
    each = rows // n_seq
    qg, kg = q_gain.reshape(1, HD), k_gain.reshape(1, HD)
    def head_move(value, masks):
        pairs = [
            (h * n_seq + s, (h ^ masks[s % 2]) * n_seq + s)
            for h in range(n_head)
            for s in range(n_seq)
        ]
        return lax.ppermute(value, ("head", "seq"), pairs)

    def seq_move(value, bit):
        return lax.ppermute(value, "seq", [(i, i ^ bit) for i in range(n_seq)])

    bits = []
    while 2 ** len(bits) < n_seq:
        bits.append(2 ** len(bits))
    bits = bits[::-1]

    table = jnp.asarray(prompt_table(rows))
    scalars = (prompt_len, admitted, cache_len)
    send1, pack, blocks, leave = project(
        n_head, n_seq, *scalars, qg, kg, table, prompts, dec_tokens, w_query, w_key, w_value, w_out
    )
    got1 = head_move(send1, (1, 2))
    arrived = seq_move(leave, bits[0])
    send0, attn0, own1, part = second(
        n_head, n_seq, pr_dev, rows, *scalars, pack, cache_kv[0], w_out
    )
    send0, arrived = lax.optimization_barrier((send0, arrived))
    got0 = head_move(send0, (1, 2))
    other = seq_move(part, bits[0])
    own0, *wo = third(n_head, attn0, w_out)
    other, got1 = lax.optimization_barrier((other, got1, own0))[:2]
    for i, bit in enumerate(bits[:-1]):
        part = join(bit, part, other)
        other = seq_move(part, bits[i + 1])
    held = [blocks[None], after(arrived, part)[None]]
    leave = hop(bits[0], held)
    held.append(seq_move(leave, bits[1]))
    on1 = pass_on(1, own1, after(got1, part))
    last1 = head_move(on1, (2, 1))
    got0, other, held[-1] = lax.optimization_barrier((got0, other, held[-1], on1))[:3]
    on0 = pass_on(0, own0, got0)
    last0 = head_move(on0, (2, 1))
    held[-1] = after(held[-1], on0)
    for i, bit in enumerate(bits[1:-1]):
        leave = hop(bit, held)
        held.append(seq_move(leave, bits[i + 2]))
    other = lax.optimization_barrier((other, on0, leave))[0]
    pieces = decode_project(bits[-1], dec_rows, part, other, *wo)
    pieces = [
        pieces[0],
        head_move(pieces[1], (2, 1)),
        head_move(pieces[2], (3, 3)),
        head_move(pieces[3], (1, 2)),
    ]
    partial, handed = finish_first(1, pr_dev, bits, own1, got1, last1, held)
    pieces = list(lax.optimization_barrier((*pieces, partial))[:-1])
    decode_out = decode_sum(steps, slots, pieces)
    prefill_out = finish_last(0, own0, got0, after(last0, decode_out), partial)
    return (prefill_out, handed.reshape(1, pr_dev * n_seq, each, 2 * HD), decode_out)


def solution(mesh):
    placed = (
        P("seq", None, None),
        P(),
        P(),
        P(),
        P("head", None, "seq", None),
        P(),
        P(None, "head"),
        P(None, "head"),
        P(None, "head"),
        P("head", None),
        P(),
        P(),
    )
    return jax.shard_map(
        local,
        mesh=mesh,
        in_specs=placed,
        out_specs=(P("seq", None, "head"), P("head", None, "seq", None), P(None, None, "head")),
        check_vma=False,
    )
```
